32 devices in a mesh: dp: 32 (over z, y, x, core).
Axes of the slice: x: 2, y: 2, z: 4, core: 2. Of those that a mesh axis runs over, the one named last changes fastest.
Arguments:
- images: bfloat16 [2, 32, 784, 512], P(None, 'dp'), may hold values from -6 to 6
- cotangent: bfloat16 [2, 32, 784, 512], P(None, 'dp'), may hold values from -0.23925781 to 0.23925781
- w_reduce: float32 [32, 65536], P('dp'), may hold values from -0.5 to 0.5
- w_spatial: float32 [32, 147456], P('dp'), may hold values from -0.3125 to 0.3125
- w_expand: float32 [32, 65536], P('dp'), may hold values from -1 to 1
- norm_gain: float32 [32, 768], P('dp'), may hold values from 0.5 to 1.5
- norm_bias: float32 [32, 768], P('dp'), may hold values from -1.2 to 1.2
- round_index: int32 [1], replicated, may hold values from 0 to 63
Outputs:
- avg_reduce: float32 [65536], P('dp')
- avg_spatial: float32 [147456], P('dp')
- avg_expand: float32 [65536], P('dp')
- avg_norm: float32 [1536], P('dp')
- moment_reduce: bfloat16 [32, 65536], P('dp')
- moment_spatial: bfloat16 [32, 147456], P('dp')
- moment_expand: bfloat16 [32, 65536], P('dp')
- moment_norm: bfloat16 [32, 1536], P('dp')
The draws below stay inside these ranges and needn't reach their ends.
All inputs are finite; a program needn't handle non-finite values.
Results may differ from the reference program's by a relative error of at most 0.017.
Values sent between devices are 32-bit elements; how exact they have to be, the bound alone decides.
No kernel may reach another device: no remote copies, remote signals or barrier semaphores. Data moves between devices by JAX's collectives and lax.ppermute only.
A program may use at most 64 MiB of HBM per device.

```python
import jax
import jax.numpy as jnp
from jax import lax

C_IN = 512
C_MID = 128
HEIGHT = 28
WIDTH = 28
KSIZE = 3
STEPS = 2
IMG_DEV = 1
PIXELS = 784
REPLICAS = 32
IMAGES = 32
NORM_CH = 768
N_DP = 32


def raised(values, key, source, target, blocks, factor):
    owner, partner = [(jnp.arange(values.shape[dim]) // (values.shape[dim] // blocks)).reshape([-1 if axis == dim else 1 for axis in range(values.ndim)]) for dim in (source, target)]
    chosen = jax.random.permutation(key, blocks)[partner]
    strong = (owner == chosen) | (owner == (partner + blocks // 2) % blocks)
    return jnp.where(strong, factor * values, values)


def shard_levels(key, extent, shards, low, high):
    factor_of, own = 1.0, jax.random.fold_in(key, 6)
    for axis_at, shards_of in shards:
        heights = jnp.exp(jax.random.uniform(jax.random.fold_in(own, axis_at), (shards_of,), jnp.float32, low / len(shards), high / len(shards)))
        factor_of = factor_of * jnp.repeat(heights, extent[axis_at] // shards_of).reshape([-1 if axis == axis_at else 1 for axis in range(len(extent))])
    return factor_of


def centred(rng, shape, spread, most, shards=(), kind=jnp.bfloat16):
    array = spread * jax.random.normal(rng, shape, jnp.float32)
    if shards:
        array = array * shard_levels(rng, shape, shards, -0.22, 0.18)
    return jnp.clip(array, -most, most).astype(kind)


def heavy_noise(own_key, shape, scale, reach, shards, heavy, kind=jnp.bfloat16):
    values = scale * jax.random.normal(own_key, shape, jnp.float32)
    if shards:
        values = values * shard_levels(own_key, shape, shards, -0.22, 0.18)
    return jnp.clip(raised(values, jax.random.fold_in(own_key, 3), *heavy), -reach, reach).astype(kind)


def setup_inputs(seed: int = 0) -> dict:
    arg_keys = jax.random.split(jax.random.key(seed), 9)
    images = centred(arg_keys[0], (STEPS, IMAGES, PIXELS, C_IN), 1.0, 6.0, ((1, 32),))
    cotangent = centred(arg_keys[1], (STEPS, IMAGES, PIXELS, C_IN), 0.04, 0.23925781, ((1, 32),))
    w_reduce = heavy_noise(arg_keys[2], (REPLICAS, C_IN * C_MID), C_IN ** -0.5, 0.5, ((0, 32),), (0, 1, 32, 2.75), jnp.float32)
    w_spatial = heavy_noise(arg_keys[3], (REPLICAS, KSIZE * KSIZE * C_MID * C_MID), (KSIZE * KSIZE * C_MID) ** -0.5, 0.3125, ((0, 32),), (0, 1, 32, 2.75), jnp.float32)
    w_expand = heavy_noise(arg_keys[4], (REPLICAS, C_MID * C_IN), C_MID ** -0.5, 1.0, ((0, 32),), (0, 1, 32, 2.75), jnp.float32)
    norm_gain = jnp.clip(1.0 + 0.1 * jax.random.normal(arg_keys[5], (REPLICAS, NORM_CH), jnp.float32), 0.5, 1.5)
    norm_bias = centred(arg_keys[6], (REPLICAS, NORM_CH), 0.3, 1.2, ((0, 32),), jnp.float32)
    round_index = jax.random.randint(arg_keys[7], (1,), 0, 64).astype(jnp.int32)
    return dict(images=images, cotangent=cotangent, w_reduce=w_reduce, w_spatial=w_spatial, w_expand=w_expand, norm_gain=norm_gain, norm_bias=norm_bias, round_index=round_index)


LEARN_RATE = 0.01
MOMENTUM = 0.9
EPSILON = 1e-05

def contract_rows(left, right):
    return lax.dot_general(left, right, (((0,), (0,)), ((), ())), preferred_element_type=jnp.float32)

def contract_cols(left, right):
    return lax.dot_general(left, right, (((1,), (1,)), ((), ())), preferred_element_type=jnp.float32)

def activate(values):
    return values * jax.nn.sigmoid(values)

def act_slope(values):
    sigma = jax.nn.sigmoid(values)
    return sigma * (1.0 + values * (1.0 - sigma))

def patches(source):
    channels = source.shape[1]
    margin = KSIZE // 2
    grid_view = source.reshape(-1, HEIGHT, WIDTH, channels)
    padded = jnp.pad(grid_view, ((0, 0), (margin, margin), (margin, margin), (0, 0)))
    pieces = [padded[:, row_off:row_off + HEIGHT, col_off:col_off + WIDTH, :] for row_off in range(KSIZE) for col_off in range(KSIZE)]
    return jnp.concatenate(pieces, axis=3).reshape(-1, KSIZE * KSIZE * channels)

def normalize(values, gains, shifts):
    center = values - lax.optimization_barrier(jnp.mean(values, axis=0))
    inv_scale = lax.rsqrt(lax.optimization_barrier(jnp.mean(center * center, axis=0)) + EPSILON)
    normed = center * inv_scale
    return (normed, inv_scale, normed * gains + shifts)

def normalize_back(grad_out, normed, inv_scale, gains):
    grad_gain = lax.optimization_barrier(jnp.sum(grad_out * normed, axis=0))
    grad_shift = lax.optimization_barrier(jnp.sum(grad_out, axis=0))
    grad_normed = grad_out * gains
    grad_in = (grad_normed - lax.optimization_barrier(jnp.mean(grad_normed, axis=0)) - normed * lax.optimization_barrier(jnp.mean(grad_normed * normed, axis=0))) * inv_scale
    return (grad_in, grad_gain, grad_shift)

def replica_grads(pixels_in, upstream, reduce_flat, spatial_flat, expand_flat, gain_all, shift_all):
    in_ch = pixels_in.shape[1]
    mid_ch = reduce_flat.shape[0] // in_ch
    taps = KSIZE * KSIZE
    reduce_w = reduce_flat.reshape(in_ch, mid_ch).astype(jnp.bfloat16)
    spatial_w = spatial_flat.reshape(taps * mid_ch, mid_ch).astype(jnp.bfloat16)
    expand_w = expand_flat.reshape(mid_ch, in_ch).astype(jnp.bfloat16)
    gain_a, gain_b, gain_c = (gain_all[:mid_ch], gain_all[mid_ch:2 * mid_ch], gain_all[2 * mid_ch:])
    shift_a, shift_b, shift_c = (shift_all[:mid_ch], shift_all[mid_ch:2 * mid_ch], shift_all[2 * mid_ch:])
    first = jnp.dot(pixels_in, reduce_w, preferred_element_type=jnp.float32)
    normed_a, scale_a, out_a = normalize(first, gain_a, shift_a)
    hidden_a = activate(out_a).astype(jnp.bfloat16)
    patch_a = patches(hidden_a)
    second = jnp.dot(patch_a, spatial_w, preferred_element_type=jnp.float32)
    normed_b, scale_b, out_b = normalize(second, gain_b, shift_b)
    hidden_b = activate(out_b).astype(jnp.bfloat16)
    third = jnp.dot(hidden_b, expand_w, preferred_element_type=jnp.float32)
    normed_c, scale_c, out_c = normalize(third, gain_c, shift_c)
    summed = out_c + pixels_in.astype(jnp.float32)
    grad_sum = upstream.astype(jnp.float32) * act_slope(summed)
    grad_third, dgain_c, dshift_c = normalize_back(grad_sum, normed_c, scale_c, gain_c)
    grad_third = grad_third.astype(jnp.bfloat16)
    grad_expand = contract_rows(hidden_b, grad_third)
    grad_hidden_b = contract_cols(grad_third, expand_w)
    grad_out_b = grad_hidden_b * act_slope(out_b)
    grad_second, dgain_b, dshift_b = normalize_back(grad_out_b, normed_b, scale_b, gain_b)
    grad_second = grad_second.astype(jnp.bfloat16)
    grad_spatial = contract_rows(patch_a, grad_second)
    flipped = spatial_w.reshape(taps, mid_ch, mid_ch)[::-1].transpose(0, 2, 1).reshape(taps * mid_ch, mid_ch)
    grad_hidden_a = jnp.dot(patches(grad_second), flipped, preferred_element_type=jnp.float32)
    grad_out_a = grad_hidden_a * act_slope(out_a)
    grad_first, dgain_a, dshift_a = normalize_back(grad_out_a, normed_a, scale_a, gain_a)
    grad_reduce = contract_rows(pixels_in, grad_first.astype(jnp.bfloat16))
    return (grad_reduce.reshape(-1), grad_spatial.reshape(-1), grad_expand.reshape(-1), jnp.concatenate([dgain_a, dgain_b, dgain_c]), jnp.concatenate([dshift_a, dshift_b, dshift_c]))

def reference(images, cotangent, w_reduce, w_spatial, w_expand, norm_gain, norm_bias, round_index):
    levels = N_DP.bit_length() - 1
    replicas = jnp.arange(N_DP, dtype=jnp.int32)
    params = (w_reduce, w_spatial, w_expand, norm_gain, norm_bias)
    moments = tuple((jnp.zeros_like(member) for member in params))
    for step_index in range(STEPS):
        bit_now = ((round_index[0] + step_index) % levels).astype(jnp.int32)
        partner = jnp.bitwise_xor(replicas, jnp.left_shift(jnp.int32(1), bit_now)).astype(jnp.int32)
        blended = tuple(((member + jnp.take(member, partner, axis=0)) * 0.5 for member in params))
        batch_rows = images[step_index].reshape(N_DP, IMG_DEV * PIXELS, C_IN)
        target = cotangent[step_index].reshape(N_DP, IMG_DEV * PIXELS, C_IN)
        gradients = lax.map(lambda packed: replica_grads(*packed), (batch_rows, target) + blended)
        moments = tuple((MOMENTUM * held + newest for held, newest in zip(moments, gradients)))
        params = tuple((member - LEARN_RATE * held for member, held in zip(blended, moments)))
    averaged = tuple((lax.optimization_barrier(jnp.sum(member, axis=0)) / N_DP for member in params))
    avg_norm = jnp.concatenate([averaged[3], averaged[4]])
    moment_norm = jnp.concatenate([moments[3], moments[4]], axis=1)
    return (averaged[0], averaged[1], averaged[2], avg_norm, moments[0].astype(jnp.bfloat16), moments[1].astype(jnp.bfloat16), moments[2].astype(jnp.bfloat16), moment_norm.astype(jnp.bfloat16))
```

```python
import functools

import jax
import jax.numpy as jnp
from jax import lax
from jax.sharding import PartitionSpec as P

HEIGHT = 28
WIDTH = 28
KSIZE = 3


LEARN_RATE = 0.01
MOMENTUM = 0.9
EPSILON = 1e-05


def partner_2(value, axis, distance):
    mask = 2**distance
    pairs = [(source, source ^ mask) for source in range(lax.axis_size(axis))]
    return lax.ppermute(value, axis, pairs)


def contract_rows(left, right):
    return lax.dot_general(
        left, right, (((0,), (0,)), ((), ())), preferred_element_type=jnp.float32
    )


def contract_cols(left, right):
    return lax.dot_general(
        left, right, (((1,), (1,)), ((), ())), preferred_element_type=jnp.float32
    )


def activate(values):
    return values * jax.nn.sigmoid(values)


def act_slope(values):
    sigma = jax.nn.sigmoid(values)
    return sigma * (1.0 + values * (1.0 - sigma))


def patches(source):
    channels = source.shape[1]
    margin = KSIZE // 2
    grid_view = source.reshape(-1, HEIGHT, WIDTH, channels)
    padded = jnp.pad(grid_view, ((0, 0), (margin, margin), (margin, margin), (0, 0)))
    pieces = [
        padded[:, row_off : row_off + HEIGHT, col_off : col_off + WIDTH, :]
        for row_off in range(KSIZE)
        for col_off in range(KSIZE)
    ]
    return jnp.concatenate(pieces, axis=3).reshape(-1, KSIZE * KSIZE * channels)


def normalize(values, gains, shifts):
    center = values - jnp.mean(values, axis=0)
    inv_scale = lax.rsqrt(jnp.mean(center * center, axis=0) + EPSILON)
    normed = center * inv_scale
    return (normed, inv_scale, normed * gains + shifts)


def normalize_back(grad_out, normed, inv_scale, gains):
    grad_gain = jnp.sum(grad_out * normed, axis=0)
    grad_shift = jnp.sum(grad_out, axis=0)
    grad_normed = grad_out * gains
    grad_in = (
        grad_normed
        - jnp.mean(grad_normed, axis=0)
        - normed * jnp.mean(grad_normed * normed, axis=0)
    ) * inv_scale
    return (grad_in, grad_gain, grad_shift)


def replica_grads(pixels_in, upstream, reduce_flat, spatial_flat, expand_flat, gain_all, shift_all):
    in_ch = pixels_in.shape[1]
    mid_ch = reduce_flat.shape[0] // in_ch
    taps = KSIZE * KSIZE
    reduce_w = reduce_flat.reshape(in_ch, mid_ch).astype(jnp.bfloat16)
    spatial_w = spatial_flat.reshape(taps * mid_ch, mid_ch).astype(jnp.bfloat16)
    expand_w = expand_flat.reshape(mid_ch, in_ch).astype(jnp.bfloat16)
    gain_a, gain_b, gain_c = (
        gain_all[:mid_ch],
        gain_all[mid_ch : 2 * mid_ch],
        gain_all[2 * mid_ch :],
    )
    shift_a, shift_b, shift_c = (
        shift_all[:mid_ch],
        shift_all[mid_ch : 2 * mid_ch],
        shift_all[2 * mid_ch :],
    )
    first = jnp.dot(pixels_in, reduce_w, preferred_element_type=jnp.float32)
    normed_a, scale_a, out_a = normalize(first, gain_a, shift_a)
    hidden_a = activate(out_a).astype(jnp.bfloat16)
    patch_a = patches(hidden_a)
    second = jnp.dot(patch_a, spatial_w, preferred_element_type=jnp.float32)
    normed_b, scale_b, out_b = normalize(second, gain_b, shift_b)
    hidden_b = activate(out_b).astype(jnp.bfloat16)
    third = jnp.dot(hidden_b, expand_w, preferred_element_type=jnp.float32)
    normed_c, scale_c, out_c = normalize(third, gain_c, shift_c)
    summed = out_c + pixels_in.astype(jnp.float32)
    grad_sum = upstream.astype(jnp.float32) * act_slope(summed)
    grad_third, dgain_c, dshift_c = normalize_back(grad_sum, normed_c, scale_c, gain_c)
    grad_third = grad_third.astype(jnp.bfloat16)
    grad_expand = contract_rows(hidden_b, grad_third)
    grad_hidden_b = contract_cols(grad_third, expand_w)
    grad_out_b = grad_hidden_b * act_slope(out_b)
    grad_second, dgain_b, dshift_b = normalize_back(grad_out_b, normed_b, scale_b, gain_b)
    grad_second = grad_second.astype(jnp.bfloat16)
    grad_spatial = contract_rows(patch_a, grad_second)
    flipped = (
        spatial_w.reshape(taps, mid_ch, mid_ch)[::-1]
        .transpose(0, 2, 1)
        .reshape(taps * mid_ch, mid_ch)
    )
    grad_hidden_a = jnp.dot(patches(grad_second), flipped, preferred_element_type=jnp.float32)
    grad_out_a = grad_hidden_a * act_slope(out_a)
    grad_first, dgain_a, dshift_a = normalize_back(grad_out_a, normed_a, scale_a, gain_a)
    grad_reduce = contract_rows(pixels_in, grad_first.astype(jnp.bfloat16))
    return (
        grad_reduce.reshape(-1),
        grad_spatial.reshape(-1),
        grad_expand.reshape(-1),
        jnp.concatenate([dgain_a, dgain_b, dgain_c]),
        jnp.concatenate([dshift_a, dshift_b, dshift_c]),
    )


def swap_front(values, bit_at):
    return partner_2(values, "dp", bit_at)


def swap_middle(values, bit_at):
    return partner_2(values, "dp", bit_at)


def swap_back(values, bit_at):
    return partner_2(values, "dp", bit_at)


def by_bit(mover, bit_choice, levels, values):
    branches = [functools.partial(mover, bit_at=bit_level) for bit_level in range(levels)]
    return lax.switch(bit_choice, branches, values)


def scatter_mean(arrays):
    replicas = lax.axis_size("dp")
    core = lax.axis_index("dp") % 2
    widths = [member.shape[0] // replicas for member in arrays]
    table = jnp.concatenate([member.reshape(replicas, -1) for member in arrays], axis=1)
    table = table.reshape(replicas // 2, 2, -1)
    kept = lax.dynamic_index_in_dim(table, core, 1, keepdims=False)
    sent = lax.dynamic_index_in_dim(table, 1 - core, 1, keepdims=False)
    halved = kept + partner_2(sent, "dp", 0)
    groups = [list(range(parity, replicas, 2)) for parity in range(2)]
    pieces = lax.all_to_all(halved, "dp", 0, 0, axis_index_groups=groups, tiled=True)
    mean = jnp.sum(pieces, axis=0) / replicas
    bounds = [sum(widths[:at]) for at in range(len(widths) + 1)]
    return tuple(mean[low:high] for low, high in zip(bounds[:-1], bounds[1:]))


def shards(images, cotangent, w_reduce, w_spatial, w_expand, norm_gain, norm_bias, round_index):
    replicas = lax.axis_size("dp")
    levels = replicas.bit_length() - 1
    params = (w_reduce[0], w_spatial[0], w_expand[0], norm_gain[0], norm_bias[0])
    moments = tuple((jnp.zeros_like(member) for member in params))
    for step_index in range(images.shape[0]):
        bit_choice = (round_index[0] + step_index) % levels
        front_part = by_bit(swap_front, bit_choice, levels, (params[0], params[3], params[4]))
        middle = by_bit(swap_middle, bit_choice, levels, params[1])
        back_part = by_bit(swap_back, bit_choice, levels, params[2])
        partner = (front_part[0], middle, back_part, front_part[1], front_part[2])
        blended = tuple(((member + theirs) * 0.5 for member, theirs in zip(params, partner)))
        pixels_in = images[step_index].reshape(-1, images.shape[-1])
        upstream = cotangent[step_index].reshape(-1, cotangent.shape[-1])
        gradients = replica_grads(pixels_in, upstream, *blended)
        moments = tuple((MOMENTUM * held + newest for held, newest in zip(moments, gradients)))
        params = tuple((member - LEARN_RATE * held for member, held in zip(blended, moments)))
    norm_params = jnp.concatenate([params[3], params[4]])
    averaged = scatter_mean((params[0], params[1], params[2], norm_params))
    norm_moment = jnp.concatenate([moments[3], moments[4]])
    momenta = (moments[0], moments[1], moments[2], norm_moment)
    return tuple(averaged) + tuple((member.astype(jnp.bfloat16)[None] for member in momenta))


def solution(mesh):
    in_specs = (
        P(None, "dp", None, None),
        P(None, "dp", None, None),
        P("dp", None),
        P("dp", None),
        P("dp", None),
        P("dp", None),
        P("dp", None),
        P(),
    )
    out_specs = (
        P("dp"),
        P("dp"),
        P("dp"),
        P("dp"),
        P("dp", None),
        P("dp", None),
        P("dp", None),
        P("dp", None),
    )
    return jax.shard_map(shards, mesh=mesh, in_specs=in_specs, out_specs=out_specs, check_vma=False)
```

```python
import functools

import jax
import jax.numpy as jnp
from jax import lax
from jax.experimental import pallas as pl
from jax.experimental.pallas import tpu as pltpu
from jax.sharding import PartitionSpec as P

HEIGHT = 28
WIDTH = 28
KSIZE = 3

LEARN_RATE = 0.01
MOMENTUM = 0.9
EPSILON = 1e-05

LANES = 128
PITCH = 32
VMEM_BYTES = 40 * 1024 * 1024


def round_up(value, unit):
    return (value + unit - 1) // unit * unit


def partner_2(value, axis, distance):
    mask = 2**distance
    pairs = [(source, source ^ mask) for source in range(lax.axis_size(axis))]
    return lax.ppermute(value, axis, pairs)


def matmul(left, right):
    return jnp.dot(left, right, preferred_element_type=jnp.float32)


def contract_cols(left, right):
    return lax.dot_general(left, right, (((1,), (1,)), ((), ())), preferred_element_type=jnp.float32)


def sigmoid(values):
    return 0.5 * jnp.tanh(0.5 * values) + 0.5


def activate(values):
    return values * sigmoid(values)


def act_slope(values):
    sigma = sigmoid(values)
    return sigma * (1.0 + values * (1.0 - sigma))


def column_sum(values):
    return jnp.sum(values, axis=0, keepdims=True)


def normalize(values):
    count = values.shape[0]
    center = values - column_sum(values) / count
    inv_scale = lax.rsqrt(column_sum(center * center) / count + EPSILON)
    return center * inv_scale, inv_scale


def normalize_back(grad_out, normed, inv_scale, gains):
    count = grad_out.shape[0]
    grad_gain = column_sum(grad_out * normed)
    grad_shift = column_sum(grad_out)
    grad_in = (grad_out - grad_shift / count - normed * (grad_gain / count)) * (inv_scale * gains)
    return grad_in, grad_gain, grad_shift


def spread(flat_ref, pad_ref, out_ref, top):
    pad_ref[...] = jnp.zeros_like(pad_ref)
    for row in range(HEIGHT):
        start = 8 + top + row * PITCH
        pad_ref[start : start + WIDTH, :] = flat_ref[row * WIDTH : (row + 1) * WIDTH, :]
    rows = out_ref.shape[0]
    for col_off in range(KSIZE):
        start = 8 + col_off - KSIZE // 2
        out_ref[:, col_off * LANES : (col_off + 1) * LANES] = pad_ref[start : start + rows, :].astype(jnp.bfloat16)


def convolve(wide_ref, weights_ref, top, pitched_ref, flat_ref):
    span = KSIZE * LANES
    rows = HEIGHT * PITCH
    total = None
    for row_off in range(KSIZE):
        start = top + (row_off - KSIZE // 2) * PITCH
        piece = matmul(wide_ref[start : start + rows, :], weights_ref[row_off * span : (row_off + 1) * span, :])
        total = piece if total is None else total + piece
    pitched_ref[...] = total
    for row in range(HEIGHT):
        flat_ref[row * WIDTH : (row + 1) * WIDTH, :] = pitched_ref[row * PITCH : row * PITCH + WIDTH, :]


TOP = PITCH
TOP_BACK = 2 * PITCH
ROWS = round_up(HEIGHT * PITCH + 2 * PITCH, LANES)
ROWS_BACK = ROWS + 2 * PITCH


def lead_kernel(x_ref, own_ref, theirs_ref, norm_own_ref, norm_theirs_ref,
                mixed_ref, norm_ref, normed_ref, scale_ref, wide_ref, wide_t_ref, x_t_ref,
                flat, pad):
    mixed = (own_ref[...] + theirs_ref[...]) * 0.5
    mixed_ref[...] = mixed
    norm = (norm_own_ref[...] + norm_theirs_ref[...]) * 0.5
    norm_ref[...] = norm
    first = matmul(x_ref[0, 0], mixed.astype(jnp.bfloat16))
    normed, inv_scale = normalize(first)
    normed_ref[...] = normed
    scale_ref[...] = inv_scale
    flat[...] = activate(normed * norm[0:1] + norm[6:7])
    spread(flat, pad, wide_ref, TOP)
    wide_t_ref[...] = wide_ref[...].T
    pixels = x_ref.shape[2]
    x_t_ref[:, :pixels] = x_ref[0, 0].T
    x_t_ref[:, pixels:] = jnp.zeros((x_t_ref.shape[0], x_t_ref.shape[1] - pixels), jnp.bfloat16)


def middle_kernel(own_ref, theirs_ref, wide_ref, norm_ref,
                  mixed_ref, normed_ref, scale_ref, hidden_ref, hidden_t_ref, flipped_ref,
                  weights, pitched, flat):
    mixed = (own_ref[...] + theirs_ref[...]) * 0.5
    mixed_ref[...] = mixed
    weights[...] = mixed.astype(jnp.bfloat16)
    convolve(wide_ref, weights, TOP, pitched, flat)
    normed, inv_scale = normalize(flat[...])
    normed_ref[...] = normed
    scale_ref[...] = inv_scale
    hidden = activate(normed * norm_ref[1:2] + norm_ref[7:8]).astype(jnp.bfloat16)
    hidden_ref[...] = hidden
    hidden_t_ref[...] = hidden.T
    taps = KSIZE * KSIZE
    for tap in range(taps):
        back = taps - 1 - tap
        flipped_ref[tap * LANES : (tap + 1) * LANES, :] = weights[back * LANES : (back + 1) * LANES, :].T


def tail_kernel(chunk, has_held, *refs):
    own_ref, theirs_ref, hidden_ref, hidden_t_ref, x_ref, upstream_ref, norm_ref = refs[:7]
    refs = refs[7:]
    held_ref = refs[0] if has_held else None
    refs = refs[1:] if has_held else refs
    param_ref, moment_ref, dnorm_ref, grad_hidden_ref, third, grad_sum, weights, grad_third, mixed = refs
    count, wide = third.shape
    blocks = wide // LANES
    mid = weights.shape[0]
    mixed[...] = (own_ref[...] + theirs_ref[...]) * 0.5
    for block in range(blocks):
        weights[:, block * LANES : (block + 1) * LANES] = mixed[pl.ds(block, mid, stride=blocks), :].astype(jnp.bfloat16)
    gains = jnp.concatenate([norm_ref[2 + block : 3 + block] for block in range(blocks)], axis=1)
    shifts = jnp.concatenate([norm_ref[8 + block : 9 + block] for block in range(blocks)], axis=1)
    steps = count // chunk
    zero = jnp.zeros((1, wide), jnp.float32)

    def rows_of(at):
        return pl.ds(pl.multiple_of(at * chunk, chunk), chunk)

    def make_third(at, total):
        values = matmul(hidden_ref[rows_of(at), :], weights[...])
        third[rows_of(at), :] = values
        return total + column_sum(values)

    mean = lax.fori_loop(0, steps, make_third, zero) / count

    def spread_of(at, total):
        center = third[rows_of(at), :] - mean
        return total + column_sum(center * center)

    inv_scale = lax.rsqrt(lax.fori_loop(0, steps, spread_of, zero) / count + EPSILON)

    def make_sum(at, totals):
        normed = (third[rows_of(at), :] - mean) * inv_scale
        summed = normed * gains + shifts + x_ref[0, 0, rows_of(at), :].astype(jnp.float32)
        grad = upstream_ref[0, 0, rows_of(at), :].astype(jnp.float32) * act_slope(summed)
        grad_sum[rows_of(at), :] = grad
        third[rows_of(at), :] = normed
        return totals[0] + column_sum(grad * normed), totals[1] + column_sum(grad)

    grad_gain, grad_shift = lax.fori_loop(0, steps, make_sum, (zero, zero))
    for block in range(blocks):
        dnorm_ref[block : block + 1, :] = grad_gain[:, block * LANES : (block + 1) * LANES]
        dnorm_ref[blocks + block : blocks + block + 1, :] = grad_shift[:, block * LANES : (block + 1) * LANES]
    slope_mean, slope_proj, factor = grad_shift / count, grad_gain / count, inv_scale * gains

    def make_back(at, carry):
        grad = (grad_sum[rows_of(at), :] - slope_mean - third[rows_of(at), :] * slope_proj) * factor
        grad = grad.astype(jnp.bfloat16)
        grad_third[rows_of(at), :] = grad
        grad_hidden_ref[rows_of(at), :] = contract_cols(grad, weights[...])
        return carry

    lax.fori_loop(0, steps, make_back, 0)
    grad = matmul(hidden_t_ref[...], grad_third[...])
    for block in range(blocks):
        moment_ref[pl.ds(block, mid, stride=blocks), :] = grad[:, block * LANES : (block + 1) * LANES]
    update(moment_ref[...], held_ref, mixed[...], moment_ref, param_ref)


def update(grad, held_ref, mixed, moment_ref, param_ref):
    moment = grad if held_ref is None else MOMENTUM * held_ref[...] + grad
    moment_ref[...] = moment
    param_ref[...] = mixed - LEARN_RATE * moment


def second_back(grad_hidden_ref, normed_ref, scale_ref, norm_ref, dnorm_ref, wide_ref, flat, pad):
    normed = normed_ref[...]
    gains = norm_ref[1:2]
    grad_out = grad_hidden_ref[...] * act_slope(normed * gains + norm_ref[7:8])
    grad_in, grad_gain, grad_shift = normalize_back(grad_out, normed, scale_ref[...], gains)
    dnorm_ref[0:1, :] = grad_gain
    dnorm_ref[1:2, :] = grad_shift
    flat[...] = grad_in
    spread(flat, pad, wide_ref, TOP_BACK)


def spatial_back(wide_ref, wide_t_ref, mixed_ref, held_ref, moment_ref, param_ref):
    for row_off in range(KSIZE):
        start = TOP_BACK - row_off * PITCH
        grad = matmul(wide_t_ref[...], wide_ref[start : start + ROWS, LANES : 2 * LANES])
        span = slice(row_off * KSIZE * LANES, (row_off + 1) * KSIZE * LANES)
        moment = grad if held_ref is None else MOMENTUM * held_ref[span, :] + grad
        moment_ref[span, :] = moment
        param_ref[span, :] = mixed_ref[span, :] - LEARN_RATE * moment


def first_back(wide_ref, flipped_ref, normed_ref, scale_ref, x_t_ref, mixed_ref, held_ref, norm_ref, norm_held_ref,
               dnorm_tail_ref, dnorm_mid_ref, moment_ref, param_ref, norm_moment_ref, norm_param_ref,
               pitched, flat, grad_first):
    convolve(wide_ref, flipped_ref, TOP_BACK, pitched, flat)
    normed = normed_ref[...]
    gains = norm_ref[0:1]
    grad_out = flat[...] * act_slope(normed * gains + norm_ref[6:7])
    grad_in, grad_gain, grad_shift = normalize_back(grad_out, normed, scale_ref[...], gains)
    count = normed.shape[0]
    grad_first[:count, :] = grad_in.astype(jnp.bfloat16)
    grad_first[count:, :] = jnp.zeros((grad_first.shape[0] - count, LANES), jnp.bfloat16)
    update(matmul(x_t_ref[...], grad_first[...]), held_ref, mixed_ref[...], moment_ref, param_ref)
    dnorm = jnp.concatenate(
        [grad_gain, dnorm_mid_ref[0:1], dnorm_tail_ref[0:4], grad_shift, dnorm_mid_ref[1:2], dnorm_tail_ref[4:8]], axis=0
    )
    update(dnorm, norm_held_ref, norm_ref[...], norm_moment_ref, norm_param_ref)


def front_grad_kernel(grad_hidden_ref, normed_b_ref, scale_b_ref, norm_ref, flipped_ref, normed_a_ref, scale_a_ref,
                      x_t_ref, mixed_ref, dnorm_tail_ref, wide_ref, moment_ref, param_ref, norm_moment_ref,
                      norm_param_ref, flat, pad, pitched, grad_first, dnorm_mid):
    second_back(grad_hidden_ref, normed_b_ref, scale_b_ref, norm_ref, dnorm_mid, wide_ref, flat, pad)
    first_back(wide_ref, flipped_ref, normed_a_ref, scale_a_ref, x_t_ref, mixed_ref, None, norm_ref, None,
               dnorm_tail_ref, dnorm_mid, moment_ref, param_ref, norm_moment_ref, norm_param_ref,
               pitched, flat, grad_first)


def spatial_grad_kernel(wide_ref, wide_t_ref, mixed_ref, moment_ref, param_ref):
    spatial_back(wide_ref, wide_t_ref, mixed_ref, None, moment_ref, param_ref)


def last_spatial_kernel(grad_hidden_ref, normed_ref, scale_ref, norm_ref, wide_t_ref, mixed_ref, held_ref,
                        dnorm_ref, wide_ref, moment_ref, param_ref, flat, pad):
    second_back(grad_hidden_ref, normed_ref, scale_ref, norm_ref, dnorm_ref, wide_ref, flat, pad)
    spatial_back(wide_ref, wide_t_ref, mixed_ref, held_ref, moment_ref, param_ref)


def last_front_kernel(wide_ref, flipped_ref, normed_ref, scale_ref, x_t_ref, mixed_ref, held_ref, norm_ref,
                      norm_held_ref, dnorm_tail_ref, dnorm_mid_ref, moment_ref, param_ref, norm_moment_ref,
                      norm_param_ref, pitched, flat, grad_first):
    first_back(wide_ref, flipped_ref, normed_ref, scale_ref, x_t_ref, mixed_ref, held_ref, norm_ref, norm_held_ref,
               dnorm_tail_ref, dnorm_mid_ref, moment_ref, param_ref, norm_moment_ref, norm_param_ref,
               pitched, flat, grad_first)


def run_kernel(body, name, operands, outs, scratch, flops):
    def spec(operand):
        if isinstance(operand, tuple):
            array, step = operand
            return pl.BlockSpec((1,) + array.shape[1:], lambda at: (step, 0, 0, 0))
        rank = operand.ndim
        return pl.BlockSpec(operand.shape, lambda at: (0,) * rank)

    arrays = [operand[0] if isinstance(operand, tuple) else operand for operand in operands]
    moved = sum(array.size * array.dtype.itemsize for array in arrays)
    return pl.pallas_call(
        body,
        grid=(1,),
        in_specs=[spec(operand) for operand in operands],
        out_specs=[pl.BlockSpec(shape, functools.partial(lambda rank, at: (0,) * rank, len(shape))) for shape, _ in outs],
        out_shape=[jax.ShapeDtypeStruct(shape, kind) for shape, kind in outs],
        scratch_shapes=[pltpu.VMEM(shape, kind) for shape, kind in scratch],
        compiler_params=pltpu.CompilerParams(vmem_limit_bytes=VMEM_BYTES),
        cost_estimate=pl.CostEstimate(flops=flops, bytes_accessed=moved, transcendentals=0),
        name=name,
    )(*arrays)


def scatter_mean(arrays):
    replicas = lax.axis_size("dp")
    core = lax.axis_index("dp") % 2
    widths = [member.size // replicas for member in arrays]
    halves = []
    for member in arrays:
        table = member.reshape(replicas // 2, 2, -1)
        kept = lax.dynamic_index_in_dim(table, core, 1, keepdims=False)
        sent = lax.dynamic_index_in_dim(table, 1 - core, 1, keepdims=False)
        halves.append(kept + partner_2(sent, "dp", 0))
    halved = jnp.concatenate(halves, axis=1)
    groups = [list(range(parity, replicas, 2)) for parity in range(2)]
    pieces = lax.all_to_all(halved, "dp", 0, 0, axis_index_groups=groups, tiled=True)
    mean = jnp.sum(pieces, axis=0) / replicas
    bounds = [sum(widths[:at]) for at in range(len(widths) + 1)]
    return tuple(mean[low:high] for low, high in zip(bounds[:-1], bounds[1:]))


def train(first_bit, levels, images, cotangent, reduce_w, spatial_w, expand_w, norm):
    f32, bf16 = jnp.float32, jnp.bfloat16
    steps, _, pixels, in_ch = images.shape
    pixels_up = round_up(pixels, LANES)
    moments = None
    flat_map = ((pixels, LANES), f32)
    pitched_map = ((HEIGHT * PITCH, LANES), f32)
    wide_map = ((ROWS, KSIZE * LANES), bf16)
    wide_back = ((ROWS_BACK, KSIZE * LANES), bf16)
    pad_map = ((ROWS + 16, LANES), f32)
    pad_back = ((ROWS_BACK + 16, LANES), f32)
    row = ((1, LANES), f32)
    size_r, size_s, size_e, size_n = [(member.shape, f32) for member in (reduce_w, spatial_w, expand_w, norm)]
    flops_1 = 2 * pixels * in_ch * LANES
    flops_3 = 2 * pixels * KSIZE * KSIZE * LANES * LANES
    for step in range(steps):
        bit = (first_bit + step) % levels
        last = step == steps - 1
        swap = functools.partial(partner_2, axis="dp", distance=bit)
        reduce_p, norm_p = swap(reduce_w), swap(norm)
        if step == 0:
            spatial_w, reduce_p = lax.optimization_barrier((spatial_w, reduce_p))
        spatial_p = swap(spatial_w)
        if step == 0:
            expand_w, spatial_p = lax.optimization_barrier((expand_w, spatial_p))
        expand_p = swap(expand_w)
        x, upstream = (images, step), (cotangent, step)
        mixed_r, mixed_n, normed_a, scale_a, wide, wide_t, x_t = run_kernel(
            lead_kernel, "lead", [x, reduce_w, reduce_p, norm, norm_p],
            [size_r, size_n, flat_map, row, wide_map, (wide_map[0][::-1], bf16), ((in_ch, pixels_up), bf16)],
            [flat_map, pad_map], flops_1,
        )
        mixed_s, normed_b, scale_b, hidden, hidden_t, flipped = run_kernel(
            middle_kernel, "middle", [spatial_w, spatial_p, wide, mixed_n],
            [size_s, flat_map, row, ((pixels, LANES), bf16), ((LANES, pixels), bf16), (spatial_w.shape, bf16)],
            [(spatial_w.shape, bf16), pitched_map, flat_map], flops_3,
        )
        held = [] if moments is None else [moments[2]]
        expand_w, moment_e, dnorm_tail, grad_hidden = run_kernel(
            functools.partial(tail_kernel, pixels // 7, bool(held)), "tail",
            [expand_w, expand_p, hidden, hidden_t, x, upstream, mixed_n] + held,
            [size_e, size_e, ((8, LANES), f32), flat_map],
            [((pixels, in_ch), f32), ((pixels, in_ch), f32), ((LANES, in_ch), bf16), ((pixels, in_ch), bf16), size_e],
            3 * flops_1,
        )
        back_in = [grad_hidden, normed_b, scale_b, mixed_n]
        grad_first = ((pixels_up, LANES), bf16)
        if moments is None:
            wide_b, moment_r, reduce_w, moment_n, norm = run_kernel(
                front_grad_kernel, "front_grad",
                back_in + [flipped, normed_a, scale_a, x_t, mixed_r, dnorm_tail],
                [wide_back, size_r, size_r, size_n, size_n],
                [flat_map, pad_back, pitched_map, grad_first, ((2, LANES), f32)], flops_1 + flops_3,
            )
            moment_s, spatial_w = run_kernel(
                spatial_grad_kernel, "spatial_grad", [wide_b, wide_t, mixed_s], [size_s, size_s], [], flops_3
            )
        else:
            dnorm_mid, wide_b, moment_s, spatial_w = run_kernel(
                last_spatial_kernel, "last_spatial", back_in + [wide_t, mixed_s, moments[1]],
                [((2, LANES), f32), wide_back, size_s, size_s], [flat_map, pad_back], flops_3,
            )
            moment_r, reduce_w, moment_n, norm = run_kernel(
                last_front_kernel, "last_front",
                [wide_b, flipped, normed_a, scale_a, x_t, mixed_r, moments[0], mixed_n, moments[3], dnorm_tail, dnorm_mid],
                [size_r, size_r, size_n, size_n], [pitched_map, flat_map, grad_first], flops_1 + flops_3,
            )
        moments = (moment_r, moment_s, moment_e, moment_n)
    averaged = scatter_mean((reduce_w, spatial_w, expand_w, norm))
    return averaged + tuple(member.reshape(1, -1).astype(bf16) for member in moments)


def shards(images, cotangent, w_reduce, w_spatial, w_expand, norm_gain, norm_bias, round_index):
    levels = lax.axis_size("dp").bit_length() - 1
    reduce_w, spatial_w, expand_w = (member.reshape(-1, LANES) for member in (w_reduce, w_spatial, w_expand))
    norm = jnp.concatenate([norm_gain.reshape(-1, LANES), norm_bias.reshape(-1, LANES)])
    branches = [functools.partial(train, bit, levels) for bit in range(levels)]
    return lax.switch(
        round_index[0] % levels, branches, images, cotangent, reduce_w, spatial_w, expand_w, norm
    )


def solution(mesh):
    in_specs = (
        P(None, "dp", None, None),
        P(None, "dp", None, None),
        P("dp", None),
        P("dp", None),
        P("dp", None),
        P("dp", None),
        P("dp", None),
        P(),
    )
    out_specs = (
        P("dp"),
        P("dp"),
        P("dp"),
        P("dp"),
        P("dp", None),
        P("dp", None),
        P("dp", None),
        P("dp", None),
    )
    return jax.shard_map(shards, mesh=mesh, in_specs=in_specs, out_specs=out_specs, check_vma=False)
```

```python
import functools

import jax
import jax.numpy as jnp
from jax import lax
from jax.experimental import pallas as pl
from jax.experimental.pallas import tpu as pltpu
from jax.sharding import PartitionSpec as P

HEIGHT = 28
WIDTH = 28
KSIZE = 3

LEARN_RATE = 0.01
MOMENTUM = 0.9
EPSILON = 1e-05

LANES = 128
PITCH = 32
VMEM_BYTES = 40 * 1024 * 1024


def round_up(value, unit):
    return (value + unit - 1) // unit * unit


def partner_2(value, axis, distance):
    mask = 2**distance
    pairs = [(source, source ^ mask) for source in range(lax.axis_size(axis))]
    return lax.ppermute(value, axis, pairs)


def matmul(left, right):
    return jnp.dot(left, right, preferred_element_type=jnp.float32)


def contract_cols(left, right):
    return lax.dot_general(left, right, (((1,), (1,)), ((), ())), preferred_element_type=jnp.float32)


def sigmoid(values):
    return 0.5 * jnp.tanh(0.5 * values) + 0.5


def activate(values):
    return values * sigmoid(values)


def act_slope(values):
    sigma = sigmoid(values)
    return sigma * (1.0 + values * (1.0 - sigma))


def column_sum(values):
    return jnp.sum(values, axis=0, keepdims=True)


MAPS = 4
FLAT = MAPS * WIDTH
PITCHED = MAPS * PITCH
CHUNKS = HEIGHT // MAPS
SPAN = KSIZE * LANES
TOP = PITCH
TOP_BACK = 2 * PITCH
ROWS = round_up(HEIGHT * PITCH + 2 * PITCH, LANES)
ROWS_BACK = ROWS + 2 * PITCH


def flat_rows(at):
    return pl.ds(pl.multiple_of(at * FLAT, FLAT), FLAT)


def zero_row(width):
    return jnp.zeros((1, width), jnp.float32)


def sweep(body, init=0):
    return lax.fori_loop(0, CHUNKS, body, init)


def statistics(values_ref, total):
    count, width = values_ref.shape
    mean = total / count

    def add(at, held):
        center = values_ref[flat_rows(at), :] - mean
        return held + column_sum(center * center)

    return mean, lax.rsqrt(sweep(add, zero_row(width)) / count + EPSILON)


def pad_chunk(pad_ref, top, at, values):
    for row in range(MAPS):
        start = pl.multiple_of(at * PITCHED, PITCHED) + (8 + top + row * PITCH)
        pad_ref[pl.ds(start, WIDTH), :] = values[row * WIDTH : (row + 1) * WIDTH]


def shift_columns(pad_ref, out_ref):
    rows = out_ref.shape[0]
    for col_off in range(KSIZE):
        start = 8 + col_off - KSIZE // 2
        out_ref[:, col_off * LANES : (col_off + 1) * LANES] = pad_ref[start : start + rows, :].astype(jnp.bfloat16)


def conv_chunk(wide_ref, top, at, weight_of, multiply):
    total = None
    for row_off in range(KSIZE):
        start = pl.multiple_of(at * PITCHED, PITCHED) + (top + (row_off - KSIZE // 2) * PITCH)
        piece = multiply(wide_ref[pl.ds(start, PITCHED), :], weight_of(row_off))
        total = piece if total is None else total + piece
    return jnp.concatenate([total[row * PITCH : row * PITCH + WIDTH] for row in range(MAPS)], axis=0)


def mean_of(own, theirs):
    return (own + theirs) * 0.5


def step_kernel(step, last, split, *refs):
    it = iter(refs)
    take = lambda count: [next(it) for _ in range(count)]
    core_ref = next(it) if last else None
    x_ref, upstream_ref = take(2)
    own_r, own_s, own_e, own_g, own_b = take(5)
    theirs_r, theirs_s, theirs_e, theirs_g, theirs_b = take(5)
    held = take(5) if step else [None] * 5
    if last:
        kept_ref, sent_ref = take(2)
    else:
        param_r, param_s, param_e, param_g, param_b = take(5)
    moment_r, moment_s, moment_e, moment_g, moment_b = take(5)
    (normed_a, normed_b, hidden_b, wide, wide_t, wide_b, pad, pad_b, mixed_e, weight_e, weight_s, weight_f,
     third, grad_sum, grad_third, work, back) = take(17)
    if last:
        param_r, param_s, param_e = take(3)
    count, width = third.shape
    blocks = width // LANES
    bf16 = jnp.bfloat16
    gains = mean_of(own_g[...], theirs_g[...])
    shifts = mean_of(own_b[...], theirs_b[...])
    gain_a, gain_b, gain_c = gains[:, :LANES], gains[:, LANES : 2 * LANES], gains[:, 2 * LANES :]
    shift_a, shift_b, shift_c = shifts[:, :LANES], shifts[:, LANES : 2 * LANES], shifts[:, 2 * LANES :]

    pad[...] = jnp.zeros_like(pad)
    pad_b[...] = jnp.zeros_like(pad_b)
    reduce_w = mean_of(own_r[...], theirs_r[...]).astype(bf16)

    def make_first(at, total):
        values = matmul(x_ref[step, 0, flat_rows(at), :], reduce_w)
        normed_a[flat_rows(at), :] = values
        return total + column_sum(values)

    mean, scale_a = statistics(normed_a, sweep(make_first, zero_row(LANES)))

    def make_hidden_a(at, carry):
        normed = (normed_a[flat_rows(at), :] - mean) * scale_a
        normed_a[flat_rows(at), :] = normed
        pad_chunk(pad, TOP, at, activate(normed * gain_a + shift_a))
        return carry

    sweep(make_hidden_a)
    shift_columns(pad, wide)

    taps = KSIZE * KSIZE
    for tap in range(taps):
        span = slice(tap * LANES, (tap + 1) * LANES)
        weights = mean_of(own_s[span, :], theirs_s[span, :]).astype(bf16)
        weight_s[span, :] = weights
        other = taps - 1 - tap
        weight_f[:, other * LANES : (other + 1) * LANES] = weights

    def make_second(at, total):
        values = conv_chunk(wide, TOP, at, lambda row: weight_s[row * SPAN : (row + 1) * SPAN, :], matmul)
        normed_b[flat_rows(at), :] = values
        return total + column_sum(values)

    mean, scale_b = statistics(normed_b, sweep(make_second, zero_row(LANES)))

    def make_hidden_b(at, carry):
        normed = (normed_b[flat_rows(at), :] - mean) * scale_b
        normed_b[flat_rows(at), :] = normed
        hidden_b[flat_rows(at), :] = activate(normed * gain_b + shift_b).astype(bf16)
        return carry

    sweep(make_hidden_b)

    mixed_e[...] = mean_of(own_e[...], theirs_e[...])
    for block in range(blocks):
        weight_e[:, block * LANES : (block + 1) * LANES] = mixed_e[pl.ds(block, LANES, stride=blocks), :].astype(bf16)

    def make_third(at, total):
        values = matmul(hidden_b[flat_rows(at), :], weight_e[...])
        third[flat_rows(at), :] = values
        return total + column_sum(values)

    mean, scale_c = statistics(third, sweep(make_third, zero_row(width)))

    def make_sum(at, totals):
        normed = (third[flat_rows(at), :] - mean) * scale_c
        summed = normed * gain_c + shift_c + x_ref[step, 0, flat_rows(at), :].astype(jnp.float32)
        grad = upstream_ref[step, 0, flat_rows(at), :].astype(jnp.float32) * act_slope(summed)
        grad_sum[flat_rows(at), :] = grad
        third[flat_rows(at), :] = normed
        return totals[0] + column_sum(grad * normed), totals[1] + column_sum(grad)

    dgain_c, dshift_c = sweep(make_sum, (zero_row(width), zero_row(width)))
    level, slope, factor = dshift_c / count, dgain_c / count, scale_c * gain_c

    def make_back_c(at, totals):
        grad = (grad_sum[flat_rows(at), :] - level - third[flat_rows(at), :] * slope) * factor
        grad = grad.astype(bf16)
        grad_third[flat_rows(at), :] = grad
        normed = normed_b[flat_rows(at), :]
        grad_out = contract_cols(grad, weight_e[...]) * act_slope(normed * gain_b + shift_b)
        work[flat_rows(at), :] = grad_out
        return totals[0] + column_sum(grad_out * normed), totals[1] + column_sum(grad_out)

    dgain_b, dshift_b = sweep(make_back_c, (zero_row(LANES), zero_row(LANES)))
    grad = matmul(hidden_b[...].T, grad_third[...])
    for block in range(blocks):
        moment_e[pl.ds(block, LANES, stride=blocks), :] = grad[:, block * LANES : (block + 1) * LANES]
    update(moment_e[...], held[2], mixed_e[...], moment_e, param_e)

    level_b, slope_b, factor_b = dshift_b / count, dgain_b / count, scale_b * gain_b

    def make_back_b(at, carry):
        grad = (work[flat_rows(at), :] - level_b - normed_b[flat_rows(at), :] * slope_b) * factor_b
        pad_chunk(pad_b, TOP_BACK, at, grad)
        return carry

    sweep(make_back_b)
    shift_columns(pad_b, wide_b)

    for at in range(ROWS // LANES):
        wide_t[:, at * LANES : (at + 1) * LANES] = wide[at * LANES : (at + 1) * LANES, :].T

    def make_spatial(col_off, carry):
        start = pl.multiple_of(col_off * LANES, LANES)
        left = wide_t[pl.ds(start, LANES), :]
        for row_off in range(KSIZE):
            low = TOP_BACK - row_off * PITCH
            grad = matmul(left, wide_b[low : low + ROWS, LANES : 2 * LANES])
            span = pl.ds(start + row_off * SPAN, LANES)
            moment = grad if held[1] is None else MOMENTUM * held[1][span, :] + grad
            moment_s[span, :] = moment
            param_s[span, :] = mean_of(own_s[span, :], theirs_s[span, :]) - LEARN_RATE * moment
        return carry

    lax.fori_loop(0, KSIZE, make_spatial, 0)

    def make_back_a(at, totals):
        grad = conv_chunk(wide_b, TOP_BACK, at, lambda row: weight_f[:, row * SPAN : (row + 1) * SPAN], contract_cols)
        normed = normed_a[flat_rows(at), :]
        grad_out = grad * act_slope(normed * gain_a + shift_a)
        work[flat_rows(at), :] = grad_out
        return totals[0] + column_sum(grad_out * normed), totals[1] + column_sum(grad_out)

    dgain_a, dshift_a = sweep(make_back_a, (zero_row(LANES), zero_row(LANES)))
    level_a, slope_a, factor_a = dshift_a / count, dgain_a / count, scale_a * gain_a

    def make_first_grad(at, carry):
        grad = (work[flat_rows(at), :] - level_a - normed_a[flat_rows(at), :] * slope_a) * factor_a
        back[flat_rows(at), :] = grad.astype(bf16)
        return carry

    sweep(make_first_grad)
    grad = matmul(back[...].T, x_ref[step, 0])
    for block in range(blocks):
        span = slice(block * LANES, (block + 1) * LANES)
        moment = grad[:, span].T
        if held[0] is not None:
            moment = MOMENTUM * held[0][span, :] + moment
        moment_r[span, :] = moment
        param_r[span, :] = mean_of(own_r[span, :], theirs_r[span, :]) - LEARN_RATE * moment
    dgain = jnp.concatenate([dgain_a, dgain_b, dgain_c], axis=1)
    dshift = jnp.concatenate([dshift_a, dshift_b, dshift_c], axis=1)
    if held[3] is not None:
        dgain = MOMENTUM * held[3][...] + dgain
        dshift = MOMENTUM * held[4][...] + dshift
    moment_g[...] = dgain
    moment_b[...] = dshift
    gains = gains - LEARN_RATE * dgain
    shifts = shifts - LEARN_RATE * dshift
    if not last:
        param_g[...] = gains
        param_b[...] = shifts
        return

    norm = jnp.concatenate([gains, shifts], axis=1)
    is_odd = jnp.full((1, 1), core_ref[0], jnp.int32) == 1
    pairs, piece_s, piece_e, piece_r, piece_n = split
    at_e = round_up(piece_s + 1, 8)
    at_r = at_e + piece_e

    def place(pair, start, low, high):
        rows = low.shape[0]
        kept_ref[pair, start : start + rows, :] = jnp.where(is_odd, high, low)
        sent_ref[pair, start : start + rows, :] = jnp.where(is_odd, low, high)

    for pair in range(pairs):
        for ref, rows, start in ((param_s, piece_s, 0), (param_e, piece_e, at_e), (param_r, piece_r, at_r)):
            first = 2 * pair * rows
            place(pair, start, ref[first : first + rows, :], ref[first + rows : first + 2 * rows, :])
        low, high = [
            jnp.concatenate(
                [norm[:, at * piece_n : (at + 1) * piece_n], jnp.zeros((1, LANES - piece_n), jnp.float32)], axis=1
            )
            for at in (2 * pair, 2 * pair + 1)
        ]
        rest = jnp.zeros((at_e - piece_s - 1, LANES), jnp.float32)
        place(pair, piece_s, jnp.concatenate([low, rest]), jnp.concatenate([high, rest]))


def update(grad, held_ref, mixed, moment_ref, param_ref):
    moment = grad if held_ref is None else MOMENTUM * held_ref[...] + grad
    moment_ref[...] = moment
    param_ref[...] = mixed - LEARN_RATE * moment


def fold_kernel(bits, *refs):
    spot_ref, kept_ref = refs[:2]
    came, outs, total = refs[2 : 2 + bits[0]], refs[2 + bits[0] : -1], refs[-1]
    values = kept_ref[...]
    for ref in came:
        values = values + ref[...]
    total[...] = values
    ways = len(outs)
    for hop, out in enumerate(outs):
        for at in range(out.shape[0]):
            out[at] = total[at * ways + jnp.bitwise_xor(spot_ref[0], hop)]


def mean_kernel(replicas, *refs):
    kept_ref, came, out = refs[0], refs[1:-1], refs[-1]
    values = kept_ref[...]
    for ref in came:
        values = values + ref[...]
    out[...] = values * (1.0 / replicas)


def pack_kernel(*refs):
    half = len(refs) // 2
    for source, out in zip(refs[:half], refs[half:]):
        if source.shape[0] == 1:
            out[...] = source[...].astype(jnp.bfloat16)
            continue

        def lay(at, carry, source=source, out=out):
            values = source[pl.ds(pl.multiple_of(at * 8, 8), 8), :].astype(jnp.bfloat16)
            base = pl.multiple_of(at * 8 * LANES, 8 * LANES)
            for row in range(8):
                out[0:1, pl.ds(base + row * LANES, LANES)] = values[row : row + 1]
            return carry

        lax.fori_loop(0, source.shape[0] // 8, lay, 0)


def run_kernel(body, name, operands, outs, scratch=(), flops=0, scalars=0):
    moved = sum(array.size * array.dtype.itemsize for array in operands)
    spec = pl.BlockSpec(memory_space=pltpu.VMEM)
    return pl.pallas_call(
        body,
        in_specs=[pl.BlockSpec(memory_space=pltpu.SMEM)] * scalars + [spec] * (len(operands) - scalars),
        out_specs=[spec] * len(outs),
        out_shape=[jax.ShapeDtypeStruct(shape, kind) for shape, kind in outs],
        scratch_shapes=[pltpu.VMEM(shape, kind) for shape, kind in scratch],
        compiler_params=pltpu.CompilerParams(vmem_limit_bytes=VMEM_BYTES),
        cost_estimate=pl.CostEstimate(flops=flops, bytes_accessed=moved, transcendentals=0),
        name=name,
    )(*operands)


def swap_all(bit, values):
    return [partner_2(member, "dp", bit) for member in values]


def exchange(spot, first_bit, ways, sends):
    replicas = lax.axis_size("dp")
    return [
        lax.ppermute(sent, "dp", [(at, at ^ (hop << first_bit)) for at in range(replicas)])
        for hop, sent in zip(range(1, ways), sends)
    ]


def scatter_mean(kept, sent, split):
    f32 = jnp.float32
    replicas = lax.axis_size("dp")
    levels = replicas.bit_length() - 1
    place = lax.axis_index("dp")
    pairs, piece_s, piece_e, piece_r, piece_n = split
    rows = kept.shape[1]
    came = exchange(place, 0, 2, [sent])
    left, low = pairs, 1
    while left > 1:
        width = min(2, levels - low)
        ways = 1 << width
        spot = ((place >> low) % ways).astype(jnp.int32).reshape(1)
        kept, *sends = run_kernel(
            functools.partial(fold_kernel, (len(came),)), "fold", [spot, kept] + came,
            [((left // ways, rows, LANES), f32)] * ways, [((left, rows, LANES), f32)], scalars=1,
        )
        came = exchange(place, low, ways, sends)
        left, low = left // ways, low + width
    (mean,) = run_kernel(
        functools.partial(mean_kernel, replicas), "mean", [kept] + came, [((1, rows, LANES), f32)]
    )
    mean = mean[0]
    at_e = round_up(piece_s + 1, 8)
    at_r = at_e + piece_e
    return (
        mean[at_r : at_r + piece_r].reshape(-1), mean[:piece_s].reshape(-1), mean[at_e:at_r].reshape(-1),
        mean[piece_s, :piece_n],
    )


def scatter_mean_any(arrays):
    replicas = lax.axis_size("dp")
    tables = [member.reshape(replicas, -1) for member in arrays]
    pieces = lax.all_to_all(jnp.concatenate(tables, axis=1), "dp", 0, 0, tiled=True)
    mean = jnp.sum(pieces, axis=0) / replicas
    bounds = [sum(table.shape[1] for table in tables[:at]) for at in range(len(tables) + 1)]
    return tuple(mean[low:high] for low, high in zip(bounds[:-1], bounds[1:]))


def shards(images, cotangent, w_reduce, w_spatial, w_expand, norm_gain, norm_bias, round_index):
    f32, bf16 = jnp.float32, jnp.bfloat16
    replicas = lax.axis_size("dp")
    levels = replicas.bit_length() - 1
    steps, _, pixels, in_ch = images.shape
    params = [member.reshape(-1, LANES) for member in (w_reduce, w_spatial, w_expand)] + [norm_gain, norm_bias]
    sizes = [(member.shape, f32) for member in params]
    taps_rows = params[1].shape[0]
    flat_map = ((pixels, LANES), f32)
    wide_map = ((pixels, in_ch), f32)
    scratch = [
        flat_map, flat_map, ((pixels, LANES), bf16), ((ROWS, SPAN), bf16), ((SPAN, ROWS), bf16),
        ((ROWS_BACK, SPAN), bf16), ((ROWS + 16, LANES), f32), ((ROWS_BACK + 16, LANES), f32),
        sizes[2], ((LANES, in_ch), bf16), ((taps_rows, LANES), bf16), ((LANES, taps_rows), bf16),
        wide_map, wide_map, ((pixels, in_ch), bf16), flat_map, ((pixels, LANES), bf16),
    ]
    flops = 6 * pixels * LANES * (2 * in_ch + taps_rows)
    fine = replicas > 1 and all(member.shape[0] % replicas == 0 for member in params[:3])
    split = (replicas // 2, *(params[at].shape[0] // replicas for at in (1, 2, 0)), 2 * norm_gain.size // replicas)
    moments = []
    for step in range(steps):
        branches = [functools.partial(swap_all, bit) for bit in range(levels)]
        theirs = list(lax.switch((round_index[0] + step) % levels, branches, params))
        packed = step == steps - 1 and fine
        operands = [images, cotangent] + params + theirs + moments
        if packed:
            core = (lax.axis_index("dp") % 2).astype(jnp.int32).reshape(1)
            half = ((split[0], round_up(split[1] + 1, 8) + split[2] + split[3], LANES), f32)
            kept, sent, *moments = run_kernel(
                functools.partial(step_kernel, step, True, split), "last_step", [core] + operands,
                [half, half] + sizes, scratch + [sizes[0], sizes[1], sizes[2]], flops, scalars=1,
            )
        else:
            done = run_kernel(
                functools.partial(step_kernel, step, False, None), "step", operands, sizes + sizes, scratch, flops
            )
            params, moments = list(done[:5]), list(done[5:])
    if fine:
        averaged = scatter_mean(kept, sent, split)
    else:
        flat = [member.reshape(-1) for member in params]
        averaged = scatter_mean_any(flat[:3] + [jnp.concatenate(flat[3:])])
    norm_moment = jnp.concatenate(moments[3:], axis=1)
    sources = list(moments[:3]) + [norm_moment]
    out = run_kernel(pack_kernel, "pack", sources, [((1, member.size), bf16) for member in sources])
    return tuple(averaged) + tuple(out)


def solution(mesh):
    in_specs = (
        P(None, "dp", None, None),
        P(None, "dp", None, None),
        P("dp", None),
        P("dp", None),
        P("dp", None),
        P("dp", None),
        P("dp", None),
        P(),
    )
    out_specs = (
        P("dp"),
        P("dp"),
        P("dp"),
        P("dp"),
        P("dp", None),
        P("dp", None),
        P("dp", None),
        P("dp", None),
    )
    return jax.shard_map(shards, mesh=mesh, in_specs=in_specs, out_specs=out_specs, check_vma=False)
```

```python
import functools

import jax
import jax.numpy as jnp
from jax import lax
from jax.experimental import pallas as pl
from jax.experimental.pallas import tpu as pltpu
from jax.sharding import PartitionSpec as P

HEIGHT = 28
WIDTH = 28
KSIZE = 3

LEARN_RATE = 0.01
MOMENTUM = 0.9
EPSILON = 1e-05

LANES = 128
PITCH = 32
VMEM_BYTES = 28 * 1024 * 1024
SMALL_VMEM = 8 * 1024 * 1024


def round_up(value, unit):
    return (value + unit - 1) // unit * unit


def partner_2(value, axis, distance):
    mask = 2**distance
    pairs = [(source, source ^ mask) for source in range(lax.axis_size(axis))]
    return lax.ppermute(value, axis, pairs)


def matmul(left, right):
    return jnp.dot(left, right, preferred_element_type=jnp.float32)


def contract_cols(left, right):
    return lax.dot_general(left, right, (((1,), (1,)), ((), ())), preferred_element_type=jnp.float32)


def sigmoid(values):
    return 0.5 * jnp.tanh(0.5 * values) + 0.5


def activate(values):
    return values * sigmoid(values)


def act_slope(values):
    sigma = sigmoid(values)
    return sigma * (1.0 + values * (1.0 - sigma))


def column_sum(values):
    return jnp.sum(values, axis=0, keepdims=True)


MAPS = 4
FLAT = MAPS * WIDTH
PITCHED = MAPS * PITCH
CHUNKS = HEIGHT // MAPS
SPAN = KSIZE * LANES
TOP = PITCH
TOP_BACK = 2 * PITCH
ROWS = round_up(HEIGHT * PITCH + 2 * PITCH, LANES)
ROWS_BACK = ROWS + 2 * PITCH


def flat_rows(at):
    return pl.ds(pl.multiple_of(at * FLAT, FLAT), FLAT)


def zero_row(width):
    return jnp.zeros((1, width), jnp.float32)


def sweep(body, init=0, unroll=True):
    return lax.fori_loop(0, CHUNKS, body, init, unroll=unroll)


def statistics(values_ref, total):
    count, width = values_ref.shape
    mean = total / count

    def add(at, held):
        center = values_ref[flat_rows(at), :] - mean
        return held + column_sum(center * center)

    return mean, lax.rsqrt(sweep(add, zero_row(width), width == LANES) / count + EPSILON)


def pad_chunk(pad_ref, top, at, values):
    for row in range(MAPS):
        start = pl.multiple_of(at * PITCHED, PITCHED) + (8 + top + row * PITCH)
        pad_ref[pl.ds(start, WIDTH), :] = values[row * WIDTH : (row + 1) * WIDTH]


def shift_columns(pad_ref, out_ref):
    rows = out_ref.shape[0]
    for col_off in range(KSIZE):
        start = 8 + col_off - KSIZE // 2
        out_ref[:, col_off * LANES : (col_off + 1) * LANES] = pad_ref[start : start + rows, :].astype(jnp.bfloat16)


def conv_chunk(wide_ref, top, at, weight_of, multiply):
    total = None
    for row_off in range(KSIZE):
        start = pl.multiple_of(at * PITCHED, PITCHED) + (top + (row_off - KSIZE // 2) * PITCH)
        piece = multiply(wide_ref[pl.ds(start, PITCHED), :], weight_of(row_off))
        total = piece if total is None else total + piece
    return jnp.concatenate([total[row * PITCH : row * PITCH + WIDTH] for row in range(MAPS)], axis=0)


def mean_of(own, theirs):
    return (own + theirs) * 0.5


def rows_at(ref, start, rows):
    return ref.at[pl.ds(start, rows), :]


def step_kernel(step, last, split, *refs):
    it = iter(refs)
    take = lambda count: [next(it) for _ in range(count)]
    core_ref = next(it) if last else None
    images_ref, cotangent_ref = take(2)
    packed = step > 0
    own, theirs = (take(2) if packed else take(5)) , (take(2) if packed else take(5))
    held_out = take(4) if packed else []
    outs = take(2) if last else take(2)
    moment_out = take(3)
    norm_moment = next(it)
    (x_ref, upstream_ref, own_ref, theirs_ref, param_ref, moment_ref,
     normed_a, normed_b, hidden_b, wide, wide_t, wide_b, pad, pad_b, mixed_e, weight_e, weight_s, weight_f,
     third, grad_sum, grad_third, work, back, arrived, left) = take(25)
    held_ref = next(it) if packed else None
    count, width = third.shape
    blocks = width // LANES
    rows_r, rows_s, rows_e = (ref.shape[0] for ref in moment_out)
    spans = ((0, rows_r), (rows_r, rows_s), (rows_r + rows_s, rows_e))
    bf16 = jnp.bfloat16
    view = lambda ref, part: rows_at(ref, *spans[part])
    pending = {}

    def fetch(name, source, target):
        copy = pltpu.make_async_copy(source, target, arrived.at[len(pending)])
        copy.start()
        pending[name] = copy

    def fetch_part(part):
        source = (lambda sides: view(sides[0], part)) if packed else (lambda sides: sides[part])
        fetch(("own", part), source(own), view(own_ref, part))
        fetch(("theirs", part), source(theirs), view(theirs_ref, part))

    def ready(part):
        pending["own", part].wait()
        pending["theirs", part].wait()

    fetch("x", images_ref.at[step, 0], x_ref)
    for part in range(3):
        fetch_part(part)
    fetch("upstream", cotangent_ref.at[step, 0], upstream_ref)
    if packed:
        for part in range(3):
            fetch(("held", part), held_out[part], view(held_ref, part))
    stores = []

    def store(source, target):
        copy = pltpu.make_async_copy(source, target, left.at[len(stores)])
        copy.start()
        stores.append(copy)

    def settle(part):
        store(view(moment_ref, part), moment_out[part])
        if not last:
            store(view(param_ref, part), view(outs[0], part))

    if packed:
        rows_of = lambda ref, low: jnp.concatenate([ref[low + at : low + at + 1, :] for at in range(ref.shape[0] // 2)], axis=1)
        half = own[1].shape[0] // 2
        gains = mean_of(rows_of(own[1], 0), rows_of(theirs[1], 0))
        shifts = mean_of(rows_of(own[1], half), rows_of(theirs[1], half))
    else:
        gains = mean_of(own[3][...], theirs[3][...])
        shifts = mean_of(own[4][...], theirs[4][...])
    gain_a, gain_b, gain_c = gains[:, :LANES], gains[:, LANES : 2 * LANES], gains[:, 2 * LANES :]
    shift_a, shift_b, shift_c = shifts[:, :LANES], shifts[:, LANES : 2 * LANES], shifts[:, 2 * LANES :]

    def mixed(part, start, rows):
        span = pl.ds(spans[part][0] + start, rows)
        return mean_of(own_ref[span, :], theirs_ref[span, :])

    def learn(part, start, rows, moment):
        span = pl.ds(spans[part][0] + start, rows)
        if packed:
            moment = MOMENTUM * held_ref[span, :] + moment
        moment_ref[span, :] = moment
        param_ref[span, :] = mixed(part, start, rows) - LEARN_RATE * moment

    pad[...] = jnp.zeros_like(pad)
    pad_b[...] = jnp.zeros_like(pad_b)
    pending["x"].wait()
    ready(0)
    reduce_w = mixed(0, 0, rows_r).astype(bf16)

    def make_first(at, total):
        values = matmul(x_ref[flat_rows(at), :], reduce_w)
        normed_a[flat_rows(at), :] = values
        return total + column_sum(values)

    mean, scale_a = statistics(normed_a, sweep(make_first, zero_row(LANES)))

    def make_hidden_a(at, carry):
        normed = (normed_a[flat_rows(at), :] - mean) * scale_a
        normed_a[flat_rows(at), :] = normed
        pad_chunk(pad, TOP, at, activate(normed * gain_a + shift_a))
        return carry

    sweep(make_hidden_a)
    shift_columns(pad, wide)

    taps = KSIZE * KSIZE
    ready(1)
    for tap in range(taps):
        weights = mixed(1, tap * LANES, LANES).astype(bf16)
        weight_s[tap * LANES : (tap + 1) * LANES, :] = weights
        other = taps - 1 - tap
        weight_f[:, other * LANES : (other + 1) * LANES] = weights

    def make_second(at, total):
        values = conv_chunk(wide, TOP, at, lambda row: weight_s[row * SPAN : (row + 1) * SPAN, :], matmul)
        normed_b[flat_rows(at), :] = values
        return total + column_sum(values)

    mean, scale_b = statistics(normed_b, sweep(make_second, zero_row(LANES)))

    def make_hidden_b(at, carry):
        normed = (normed_b[flat_rows(at), :] - mean) * scale_b
        normed_b[flat_rows(at), :] = normed
        hidden_b[flat_rows(at), :] = activate(normed * gain_b + shift_b).astype(bf16)
        return carry

    sweep(make_hidden_b)

    ready(2)
    mixed_e[...] = mixed(2, 0, rows_e)
    for block in range(blocks):
        weight_e[:, block * LANES : (block + 1) * LANES] = mixed_e[pl.ds(block, LANES, stride=blocks), :].astype(bf16)

    def make_third(at, total):
        values = matmul(hidden_b[flat_rows(at), :], weight_e[...])
        third[flat_rows(at), :] = values
        return total + column_sum(values)

    mean, scale_c = statistics(third, sweep(make_third, zero_row(width)))

    def make_sum(at, totals):
        normed = (third[flat_rows(at), :] - mean) * scale_c
        summed = normed * gain_c + shift_c + x_ref[flat_rows(at), :].astype(jnp.float32)
        grad = upstream_ref[flat_rows(at), :].astype(jnp.float32) * act_slope(summed)
        grad_sum[flat_rows(at), :] = grad
        third[flat_rows(at), :] = normed
        return totals[0] + column_sum(grad * normed), totals[1] + column_sum(grad)

    pending["upstream"].wait()
    dgain_c, dshift_c = sweep(make_sum, (zero_row(width), zero_row(width)), False)
    level, slope, factor = dshift_c / count, dgain_c / count, scale_c * gain_c

    def make_back_c(at, totals):
        grad = (grad_sum[flat_rows(at), :] - level - third[flat_rows(at), :] * slope) * factor
        grad = grad.astype(bf16)
        grad_third[flat_rows(at), :] = grad
        normed = normed_b[flat_rows(at), :]
        grad_out = contract_cols(grad, weight_e[...]) * act_slope(normed * gain_b + shift_b)
        work[flat_rows(at), :] = grad_out
        return totals[0] + column_sum(grad_out * normed), totals[1] + column_sum(grad_out)

    dgain_b, dshift_b = sweep(make_back_c, (zero_row(LANES), zero_row(LANES)))
    grad = matmul(hidden_b[...].T, grad_third[...])
    for block in range(blocks):
        mixed_e[pl.ds(block, LANES, stride=blocks), :] = grad[:, block * LANES : (block + 1) * LANES]
    for part in range(3 if packed else 0):
        pending["held", part].wait()
    learn(2, 0, rows_e, mixed_e[...])
    settle(2)

    level_b, slope_b, factor_b = dshift_b / count, dgain_b / count, scale_b * gain_b

    def make_back_b(at, carry):
        grad = (work[flat_rows(at), :] - level_b - normed_b[flat_rows(at), :] * slope_b) * factor_b
        pad_chunk(pad_b, TOP_BACK, at, grad)
        return carry

    sweep(make_back_b)
    shift_columns(pad_b, wide_b)

    for at in range(ROWS // LANES):
        wide_t[:, at * LANES : (at + 1) * LANES] = wide[at * LANES : (at + 1) * LANES, :].T

    def make_spatial(col_off, carry):
        start = pl.multiple_of(col_off * LANES, LANES)
        left = wide_t[pl.ds(start, LANES), :]
        for row_off in range(KSIZE):
            low = TOP_BACK - row_off * PITCH
            grad = matmul(left, wide_b[low : low + ROWS, LANES : 2 * LANES])
            learn(1, start + row_off * SPAN, LANES, grad)
        return carry

    lax.fori_loop(0, KSIZE, make_spatial, 0, unroll=True)
    settle(1)

    def make_back_a(at, totals):
        grad = conv_chunk(wide_b, TOP_BACK, at, lambda row: weight_f[:, row * SPAN : (row + 1) * SPAN], contract_cols)
        normed = normed_a[flat_rows(at), :]
        grad_out = grad * act_slope(normed * gain_a + shift_a)
        work[flat_rows(at), :] = grad_out
        return totals[0] + column_sum(grad_out * normed), totals[1] + column_sum(grad_out)

    dgain_a, dshift_a = sweep(make_back_a, (zero_row(LANES), zero_row(LANES)))
    level_a, slope_a, factor_a = dshift_a / count, dgain_a / count, scale_a * gain_a

    def make_first_grad(at, carry):
        grad = (work[flat_rows(at), :] - level_a - normed_a[flat_rows(at), :] * slope_a) * factor_a
        back[flat_rows(at), :] = grad.astype(bf16)
        return carry

    sweep(make_first_grad)
    grad = matmul(back[...].T, x_ref[...])
    for block in range(blocks):
        learn(0, block * LANES, LANES, grad[:, block * LANES : (block + 1) * LANES].T)
    settle(0)
    grad = jnp.concatenate([dgain_a, dgain_b, dgain_c, dshift_a, dshift_b, dshift_c], axis=1)
    norm = jnp.concatenate([gains, shifts], axis=1)
    if packed:
        grad = MOMENTUM * held_out[3][...] + grad
    norm_moment[...] = grad
    norm = norm - LEARN_RATE * grad
    if not last:
        for at in range(norm.shape[1] // LANES):
            outs[1][at : at + 1, :] = norm[:, at * LANES : (at + 1) * LANES]
        for copy in stores:
            copy.wait()
        return

    kept_ref, sent_ref = outs
    is_odd = jnp.full((1, 1), core_ref[0], jnp.int32) == 1
    pairs, piece_s, piece_e, piece_r, piece_n = split
    at_e = round_up(piece_s + 1, 8)
    at_r = at_e + piece_e

    def place(pair, start, low, high):
        rows = low.shape[0]
        kept_ref[pair, start : start + rows, :] = jnp.where(is_odd, high, low)
        sent_ref[pair, start : start + rows, :] = jnp.where(is_odd, low, high)

    for pair in range(pairs):
        for part, rows, start in ((1, piece_s, 0), (2, piece_e, at_e), (0, piece_r, at_r)):
            first = spans[part][0] + 2 * pair * rows
            place(pair, start, param_ref[first : first + rows, :], param_ref[first + rows : first + 2 * rows, :])
        low, high = [
            jnp.concatenate(
                [norm[:, at * piece_n : (at + 1) * piece_n], jnp.zeros((1, LANES - piece_n), jnp.float32)], axis=1
            )
            for at in (2 * pair, 2 * pair + 1)
        ]
        rest = jnp.zeros((at_e - piece_s - 1, LANES), jnp.float32)
        place(pair, piece_s, jnp.concatenate([low, rest]), jnp.concatenate([high, rest]))
    for copy in stores:
        copy.wait()


def fold_kernel(bits, *refs):
    spot_ref, kept_ref = refs[:2]
    came, outs, total = refs[2 : 2 + bits[0]], refs[2 + bits[0] : -1], refs[-1]
    values = kept_ref[...]
    for ref in came:
        values = values + ref[...]
    total[...] = values
    ways = len(outs)
    for hop, out in enumerate(outs):
        for at in range(out.shape[0]):
            out[at] = total[at * ways + jnp.bitwise_xor(spot_ref[0], hop)]


def mean_kernel(replicas, *refs):
    kept_ref, came, out = refs[0], refs[1:-1], refs[-1]
    values = kept_ref[...]
    for ref in came:
        values = values + ref[...]
    out[...] = values * (1.0 / replicas)


def pack_kernel(*refs):
    half = len(refs) // 2
    for source, out in zip(refs[:half], refs[half:]):
        if source.shape[0] == 1:
            out[...] = source[...].astype(jnp.bfloat16)
            continue

        def lay(at, carry, source=source, out=out):
            values = source[pl.ds(pl.multiple_of(at * 8, 8), 8), :].astype(jnp.bfloat16)
            base = pl.multiple_of(at * 8 * LANES, 8 * LANES)
            for row in range(8):
                out[0:1, pl.ds(base + row * LANES, LANES)] = values[row : row + 1]
            return carry

        lax.fori_loop(0, source.shape[0] // 8, lay, 0)


def run_kernel(body, name, operands, outs, scratch=(), flops=0, vmem=SMALL_VMEM):
    def parts(entries, is_plain):
        plain = [entry if is_plain(entry) else entry[0] for entry in entries]
        return plain, [pl.BlockSpec(memory_space=pltpu.VMEM if is_plain(entry) else entry[1]) for entry in entries]

    arrays, in_specs = parts(operands, lambda entry: not isinstance(entry, tuple))
    shapes, out_specs = parts(outs, lambda entry: isinstance(entry[0], tuple) and not isinstance(entry[0][0], tuple))
    moved = sum(array.size * array.dtype.itemsize for array in arrays)
    return list(pl.pallas_call(
        body,
        in_specs=in_specs,
        out_specs=out_specs,
        out_shape=[jax.ShapeDtypeStruct(shape, kind) for shape, kind in shapes],
        scratch_shapes=[pltpu.VMEM(*entry) if isinstance(entry, tuple) else entry for entry in scratch],
        compiler_params=pltpu.CompilerParams(vmem_limit_bytes=vmem),
        cost_estimate=pl.CostEstimate(flops=flops, bytes_accessed=moved, transcendentals=0),
        name=name,
    )(*arrays))


def in_hbm(entry):
    return entry, pltpu.HBM


def in_smem(value):
    return value.astype(jnp.int32).reshape(1), pltpu.SMEM


def swap_all(bit, values):
    return [partner_2(member, "dp", bit) for member in values]


def exchange(spot, first_bit, ways, sends):
    replicas = lax.axis_size("dp")
    return [
        lax.ppermute(sent, "dp", [(at, at ^ (hop << first_bit)) for at in range(replicas)])
        for hop, sent in zip(range(1, ways), sends)
    ]


def scatter_mean(kept, sent, split, beside):
    f32 = jnp.float32
    replicas = lax.axis_size("dp")
    levels = replicas.bit_length() - 1
    place = lax.axis_index("dp")
    pairs, piece_s, piece_e, piece_r, piece_n = split
    rows = kept.shape[1]
    came = exchange(place, 0, 2, [sent])
    left, low = pairs, 1
    while left > 1:
        width = min(2, levels - low)
        ways = 1 << width
        spot = in_smem((place >> low) % ways)
        kept, *sends = run_kernel(
            functools.partial(fold_kernel, (len(came),)), "fold", [spot, kept] + came,
            [((left // ways, rows, LANES), f32)] * ways, [((left, rows, LANES), f32)],
        )
        came = exchange(place, low, ways, sends)
        if beside is not None:
            done = beside()
            beside = None
            came, done = lax.optimization_barrier((came, done))
        left, low = left // ways, low + width
    (mean,) = run_kernel(
        functools.partial(mean_kernel, replicas), "mean", [kept] + came, [((1, rows, LANES), f32)]
    )
    mean = mean[0]
    at_e = round_up(piece_s + 1, 8)
    at_r = at_e + piece_e
    if beside is not None:
        done = beside()
    return done, (
        mean[at_r : at_r + piece_r].reshape(-1), mean[:piece_s].reshape(-1), mean[at_e:at_r].reshape(-1),
        mean[piece_s, :piece_n],
    )


def scatter_mean_any(arrays):
    replicas = lax.axis_size("dp")
    tables = [member.reshape(replicas, -1) for member in arrays]
    pieces = lax.all_to_all(jnp.concatenate(tables, axis=1), "dp", 0, 0, tiled=True)
    mean = jnp.sum(pieces, axis=0) / replicas
    bounds = [sum(table.shape[1] for table in tables[:at]) for at in range(len(tables) + 1)]
    return tuple(mean[low:high] for low, high in zip(bounds[:-1], bounds[1:]))


def shards(images, cotangent, w_reduce, w_spatial, w_expand, norm_gain, norm_bias, round_index):
    f32, bf16 = jnp.float32, jnp.bfloat16
    replicas = lax.axis_size("dp")
    levels = replicas.bit_length() - 1
    steps, _, pixels, in_ch = images.shape
    weights = [member.reshape(-1, LANES) for member in (w_reduce, w_spatial, w_expand)]
    sizes = [(member.shape, f32) for member in weights]
    rows_r, rows_s, rows_e = (member.shape[0] for member in weights)
    rows = rows_r + rows_s + rows_e
    norm_size = 2 * norm_gain.size
    flat_map = ((pixels, LANES), f32)
    wide_map = ((pixels, in_ch), f32)
    whole = ((rows, LANES), f32)
    norm_rows = ((norm_size // LANES, LANES), f32)
    half_map = ((pixels, in_ch), bf16)
    scratch = [
        half_map, half_map, whole, whole, whole, whole,
        flat_map, flat_map, ((pixels, LANES), bf16), ((ROWS, SPAN), bf16), ((SPAN, ROWS), bf16),
        ((ROWS_BACK, SPAN), bf16), ((ROWS + 16, LANES), f32), ((ROWS_BACK + 16, LANES), f32),
        sizes[2], ((LANES, in_ch), bf16), ((rows_s, LANES), bf16), ((LANES, rows_s), bf16),
        wide_map, wide_map, half_map, flat_map, ((pixels, LANES), bf16),
        pltpu.SemaphoreType.DMA((11,)), pltpu.SemaphoreType.DMA((6,)),
    ]
    flops = 6 * pixels * LANES * (2 * in_ch + rows_s)
    fine = replicas > 1 and all(size[0][0] % replicas == 0 for size in sizes)
    split = (replicas // 2, rows_s // replicas, rows_e // replicas, rows_r // replicas, norm_size // replicas)
    half = ((split[0], round_up(split[1] + 1, 8) + split[2] + split[3], LANES), f32)
    params = [weights[1], weights[0], weights[2], norm_gain, norm_bias]
    moments = []
    for step in range(steps):
        branches = [functools.partial(swap_all, bit) for bit in range(levels)]
        theirs = list(lax.switch((round_index[0] + step) % levels, branches, params))
        if step == 0:
            sides = [[in_hbm(side[at]) for at in (1, 0, 2)] + side[3:] for side in (params, theirs)]
        else:
            sides = [[in_hbm(side[0]), side[1]] for side in (params, theirs)]
        operands = [in_hbm(images), in_hbm(cotangent)] + sides[0] + sides[1]
        operands += [in_hbm(member) for member in moments[:3]] + moments[3:]
        moment_outs = [in_hbm(size) for size in sizes] + [((1, norm_size), f32)]
        extra = [whole] if step else []
        if step == steps - 1 and fine:
            core = in_smem(lax.axis_index("dp") % 2)
            kept, sent, *moments = run_kernel(
                functools.partial(step_kernel, step, True, split), "last_step", [core] + operands,
                [half, half] + moment_outs, scratch + extra, flops, VMEM_BYTES,
            )
        else:
            *params, m_r, m_s, m_e, m_n = run_kernel(
                functools.partial(step_kernel, step, False, None), "step", operands,
                [in_hbm(whole), norm_rows] + moment_outs, scratch + extra, flops, VMEM_BYTES,
            )
            moments = [m_r, m_s, m_e, m_n]
    pack = lambda: run_kernel(pack_kernel, "pack", moments, [((1, member.size), bf16) for member in moments])
    if fine:
        out, averaged = scatter_mean(kept, sent, split, pack)
    else:
        flat = [params[0][low:high].reshape(-1) for low, high in ((0, rows_r), (rows_r, rows_r + rows_s), (rows_r + rows_s, rows))]
        out, averaged = pack(), scatter_mean_any(flat + [params[1].reshape(-1)])
    return tuple(averaged) + tuple(out)


def solution(mesh):
    in_specs = (
        P(None, "dp", None, None),
        P(None, "dp", None, None),
        P("dp", None),
        P("dp", None),
        P("dp", None),
        P("dp", None),
        P("dp", None),
        P(),
    )
    out_specs = (
        P("dp"),
        P("dp"),
        P("dp"),
        P("dp"),
        P("dp", None),
        P("dp", None),
        P("dp", None),
        P("dp", None),
    )
    return jax.shard_map(shards, mesh=mesh, in_specs=in_specs, out_specs=out_specs, check_vma=False)
```

```python
import functools

import jax
import jax.numpy as jnp
from jax import lax
from jax.experimental import pallas as pl
from jax.experimental.pallas import tpu as pltpu
from jax.sharding import PartitionSpec as P

HEIGHT = 28
WIDTH = 28
KSIZE = 3

LEARN_RATE = 0.01
MOMENTUM = 0.9
EPSILON = 1e-05

LANES = 128
PITCH = 32
VMEM_BYTES = 60 * 1024 * 1024
SMALL_VMEM = 8 * 1024 * 1024


def round_up(value, unit):
    return (value + unit - 1) // unit * unit


def partner_2(value, axis, distance):
    mask = 2**distance
    pairs = [(source, source ^ mask) for source in range(lax.axis_size(axis))]
    return lax.ppermute(value, axis, pairs)


def matmul(left, right):
    return jnp.dot(left, right, preferred_element_type=jnp.float32)


def contract_cols(left, right):
    return lax.dot_general(left, right, (((1,), (1,)), ((), ())), preferred_element_type=jnp.float32)


def sigmoid(values):
    return 0.5 * jnp.tanh(0.5 * values) + 0.5


def activate(values):
    return values * sigmoid(values)


def act_slope(values):
    sigma = sigmoid(values)
    return sigma * (1.0 + values * (1.0 - sigma))


def column_sum(values):
    return jnp.sum(values, axis=0, keepdims=True)


MAPS = 4
FLAT = MAPS * WIDTH
PITCHED = MAPS * PITCH
CHUNKS = HEIGHT // MAPS
SPAN = KSIZE * LANES
TOP = PITCH
TOP_BACK = 2 * PITCH
ROWS = round_up(HEIGHT * PITCH + 2 * PITCH, LANES)
ROWS_BACK = ROWS + 2 * PITCH


def flat_rows(at):
    return pl.ds(pl.multiple_of(at * FLAT, FLAT), FLAT)


def zero_row(width):
    return jnp.zeros((1, width), jnp.float32)


def sweep(body, init=0, unroll=True):
    return lax.fori_loop(0, CHUNKS, body, init, unroll=unroll)


def statistics(values_ref, total):
    count, width = values_ref.shape
    mean = total / count

    def add(at, held):
        center = values_ref[flat_rows(at), :] - mean
        return held + column_sum(center * center)

    return mean, lax.rsqrt(sweep(add, zero_row(width), width == LANES) / count + EPSILON)


def pad_chunk(pad_ref, top, at, values):
    for row in range(MAPS):
        start = pl.multiple_of(at * PITCHED, PITCHED) + (8 + top + row * PITCH)
        pad_ref[pl.ds(start, WIDTH), :] = values[row * WIDTH : (row + 1) * WIDTH]


def shift_columns(pad_ref, out_ref):
    rows = out_ref.shape[0]
    for col_off in range(KSIZE):
        start = 8 + col_off - KSIZE // 2
        out_ref[:, col_off * LANES : (col_off + 1) * LANES] = pad_ref[start : start + rows, :].astype(jnp.bfloat16)


def conv_chunk(wide_ref, top, at, weight_of, multiply):
    total = None
    for row_off in range(KSIZE):
        start = pl.multiple_of(at * PITCHED, PITCHED) + (top + (row_off - KSIZE // 2) * PITCH)
        piece = multiply(wide_ref[pl.ds(start, PITCHED), :], weight_of(row_off))
        total = piece if total is None else total + piece
    return jnp.concatenate([total[row * PITCH : row * PITCH + WIDTH] for row in range(MAPS)], axis=0)


def mean_of(own, theirs):
    return (own + theirs) * 0.5


def rows_at(ref, start, rows):
    return ref.at[pl.ds(start, rows), :]


def step_kernel(step, last, split, *refs):
    it = iter(refs)
    take = lambda count: [next(it) for _ in range(count)]
    core_ref = next(it) if last else None
    images_ref, cotangent_ref = take(2)
    packed = step > 0
    own, theirs = (take(2) if packed else take(5)) , (take(2) if packed else take(5))
    held_out = take(4) if packed else []
    outs = take(2) if last else take(2)
    moment_out = take(3)
    norm_moment = next(it)
    (x_ref, upstream_ref, own_ref, theirs_ref, param_ref, moment_ref,
     normed_a, normed_b, hidden_b, wide, wide_t, wide_b, pad, pad_b, mixed_e, weight_e, weight_s, weight_f,
     third, grad_sum, grad_third, work, back, arrived, left) = take(25)
    held_ref = next(it) if packed else None
    count, width = third.shape
    blocks = width // LANES
    rows_r, rows_s, rows_e = (ref.shape[0] for ref in moment_out)
    spans = ((0, rows_r), (rows_r, rows_s), (rows_r + rows_s, rows_e))
    bf16 = jnp.bfloat16
    view = lambda ref, part: rows_at(ref, *spans[part])
    pending = {}

    def fetch(name, source, target):
        copy = pltpu.make_async_copy(source, target, arrived.at[len(pending)])
        copy.start()
        pending[name] = copy

    def fetch_part(part):
        source = (lambda sides: view(sides[0], part)) if packed else (lambda sides: sides[part])
        fetch(("own", part), source(own), view(own_ref, part))
        fetch(("theirs", part), source(theirs), view(theirs_ref, part))

    def ready(part):
        pending["own", part].wait()
        pending["theirs", part].wait()

    fetch("x", images_ref.at[step, 0], x_ref)
    for part in range(3):
        fetch_part(part)
    fetch("upstream", cotangent_ref.at[step, 0], upstream_ref)
    if packed:
        for part in range(3):
            fetch(("held", part), held_out[part], view(held_ref, part))
    stores = []

    def store(source, target):
        copy = pltpu.make_async_copy(source, target, left.at[len(stores)])
        copy.start()
        stores.append(copy)

    def settle(part):
        store(view(moment_ref, part), moment_out[part])
        if not last:
            store(view(param_ref, part), view(outs[0], part))

    if packed:
        rows_of = lambda ref, low: jnp.concatenate([ref[low + at : low + at + 1, :] for at in range(ref.shape[0] // 2)], axis=1)
        half = own[1].shape[0] // 2
        gains = mean_of(rows_of(own[1], 0), rows_of(theirs[1], 0))
        shifts = mean_of(rows_of(own[1], half), rows_of(theirs[1], half))
    else:
        gains = mean_of(own[3][...], theirs[3][...])
        shifts = mean_of(own[4][...], theirs[4][...])
    gain_a, gain_b, gain_c = gains[:, :LANES], gains[:, LANES : 2 * LANES], gains[:, 2 * LANES :]
    shift_a, shift_b, shift_c = shifts[:, :LANES], shifts[:, LANES : 2 * LANES], shifts[:, 2 * LANES :]

    def mixed(part, start, rows):
        span = pl.ds(spans[part][0] + start, rows)
        return mean_of(own_ref[span, :], theirs_ref[span, :])

    def learn(part, start, rows, moment):
        span = pl.ds(spans[part][0] + start, rows)
        if packed:
            moment = MOMENTUM * held_ref[span, :] + moment
        moment_ref[span, :] = moment
        param_ref[span, :] = mixed(part, start, rows) - LEARN_RATE * moment

    pad[...] = jnp.zeros_like(pad)
    pad_b[...] = jnp.zeros_like(pad_b)
    pending["x"].wait()
    ready(0)
    reduce_w = mixed(0, 0, rows_r).astype(bf16)

    def make_first(at, total):
        values = matmul(x_ref[flat_rows(at), :], reduce_w)
        normed_a[flat_rows(at), :] = values
        return total + column_sum(values)

    mean, scale_a = statistics(normed_a, sweep(make_first, zero_row(LANES)))

    def make_hidden_a(at, carry):
        normed = (normed_a[flat_rows(at), :] - mean) * scale_a
        normed_a[flat_rows(at), :] = normed
        pad_chunk(pad, TOP, at, activate(normed * gain_a + shift_a))
        return carry

    sweep(make_hidden_a)
    shift_columns(pad, wide)

    taps = KSIZE * KSIZE
    ready(1)
    for tap in range(taps):
        weights = mixed(1, tap * LANES, LANES).astype(bf16)
        weight_s[tap * LANES : (tap + 1) * LANES, :] = weights
        other = taps - 1 - tap
        weight_f[:, other * LANES : (other + 1) * LANES] = weights

    def make_second(at, total):
        values = conv_chunk(wide, TOP, at, lambda row: weight_s[row * SPAN : (row + 1) * SPAN, :], matmul)
        normed_b[flat_rows(at), :] = values
        return total + column_sum(values)

    mean, scale_b = statistics(normed_b, sweep(make_second, zero_row(LANES)))

    def make_hidden_b(at, carry):
        normed = (normed_b[flat_rows(at), :] - mean) * scale_b
        normed_b[flat_rows(at), :] = normed
        hidden_b[flat_rows(at), :] = activate(normed * gain_b + shift_b).astype(bf16)
        return carry

    sweep(make_hidden_b)

    ready(2)
    mixed_e[...] = mixed(2, 0, rows_e)
    for block in range(blocks):
        weight_e[:, block * LANES : (block + 1) * LANES] = mixed_e[pl.ds(block, LANES, stride=blocks), :].astype(bf16)

    def make_third(at, total):
        values = matmul(hidden_b[flat_rows(at), :], weight_e[...])
        third[flat_rows(at), :] = values
        return total + column_sum(values)

    mean, scale_c = statistics(third, sweep(make_third, zero_row(width)))

    def make_sum(at, totals):
        normed = (third[flat_rows(at), :] - mean) * scale_c
        summed = normed * gain_c + shift_c + x_ref[flat_rows(at), :].astype(jnp.float32)
        grad = upstream_ref[flat_rows(at), :].astype(jnp.float32) * act_slope(summed)
        grad_sum[flat_rows(at), :] = grad
        third[flat_rows(at), :] = normed
        return totals[0] + column_sum(grad * normed), totals[1] + column_sum(grad)

    pending["upstream"].wait()
    dgain_c, dshift_c = sweep(make_sum, (zero_row(width), zero_row(width)), False)
    level, slope, factor = dshift_c / count, dgain_c / count, scale_c * gain_c

    def make_back_c(at, totals):
        grad = (grad_sum[flat_rows(at), :] - level - third[flat_rows(at), :] * slope) * factor
        grad = grad.astype(bf16)
        grad_third[flat_rows(at), :] = grad
        normed = normed_b[flat_rows(at), :]
        grad_out = contract_cols(grad, weight_e[...]) * act_slope(normed * gain_b + shift_b)
        work[flat_rows(at), :] = grad_out
        return totals[0] + column_sum(grad_out * normed), totals[1] + column_sum(grad_out)

    dgain_b, dshift_b = sweep(make_back_c, (zero_row(LANES), zero_row(LANES)))
    grad = matmul(hidden_b[...].T, grad_third[...])
    for block in range(blocks):
        mixed_e[pl.ds(block, LANES, stride=blocks), :] = grad[:, block * LANES : (block + 1) * LANES]
    for part in range(3 if packed else 0):
        pending["held", part].wait()
    learn(2, 0, rows_e, mixed_e[...])
    settle(2)

    level_b, slope_b, factor_b = dshift_b / count, dgain_b / count, scale_b * gain_b

    def make_back_b(at, carry):
        grad = (work[flat_rows(at), :] - level_b - normed_b[flat_rows(at), :] * slope_b) * factor_b
        pad_chunk(pad_b, TOP_BACK, at, grad)
        return carry

    sweep(make_back_b)
    shift_columns(pad_b, wide_b)

    for at in range(ROWS // LANES):
        wide_t[:, at * LANES : (at + 1) * LANES] = wide[at * LANES : (at + 1) * LANES, :].T

    shifted = [
        wide_b[TOP_BACK - row_off * PITCH : TOP_BACK - row_off * PITCH + ROWS, LANES : 2 * LANES]
        for row_off in range(KSIZE)
    ]
    grad = matmul(wide_t[...], jnp.concatenate(shifted, axis=1))
    for row_off in range(KSIZE):
        learn(1, row_off * SPAN, SPAN, grad[:, row_off * LANES : (row_off + 1) * LANES])
    settle(1)

    def make_back_a(at, totals):
        grad = conv_chunk(wide_b, TOP_BACK, at, lambda row: weight_f[:, row * SPAN : (row + 1) * SPAN], contract_cols)
        normed = normed_a[flat_rows(at), :]
        grad_out = grad * act_slope(normed * gain_a + shift_a)
        work[flat_rows(at), :] = grad_out
        return totals[0] + column_sum(grad_out * normed), totals[1] + column_sum(grad_out)

    dgain_a, dshift_a = sweep(make_back_a, (zero_row(LANES), zero_row(LANES)))
    level_a, slope_a, factor_a = dshift_a / count, dgain_a / count, scale_a * gain_a

    def make_first_grad(at, carry):
        grad = (work[flat_rows(at), :] - level_a - normed_a[flat_rows(at), :] * slope_a) * factor_a
        back[flat_rows(at), :] = grad.astype(bf16)
        return carry

    sweep(make_first_grad)
    grad = matmul(back[...].T, x_ref[...])
    for block in range(blocks):
        learn(0, block * LANES, LANES, grad[:, block * LANES : (block + 1) * LANES].T)
    settle(0)
    grad = jnp.concatenate([dgain_a, dgain_b, dgain_c, dshift_a, dshift_b, dshift_c], axis=1)
    norm = jnp.concatenate([gains, shifts], axis=1)
    if packed:
        grad = MOMENTUM * held_out[3][...] + grad
    norm_moment[...] = grad
    norm = norm - LEARN_RATE * grad
    if not last:
        for at in range(norm.shape[1] // LANES):
            outs[1][at : at + 1, :] = norm[:, at * LANES : (at + 1) * LANES]
        for copy in stores:
            copy.wait()
        return

    kept_ref, sent_ref = outs
    is_odd = jnp.full((1, 1), core_ref[0], jnp.int32) == 1
    pairs, piece_s, piece_e, piece_r, piece_n = split
    at_e = round_up(piece_s + 1, 8)
    at_r = at_e + piece_e

    def place(pair, start, low, high):
        rows = low.shape[0]
        kept_ref[pair, start : start + rows, :] = jnp.where(is_odd, high, low)
        sent_ref[pair, start : start + rows, :] = jnp.where(is_odd, low, high)

    for pair in range(pairs):
        for part, rows, start in ((1, piece_s, 0), (2, piece_e, at_e), (0, piece_r, at_r)):
            first = spans[part][0] + 2 * pair * rows
            place(pair, start, param_ref[first : first + rows, :], param_ref[first + rows : first + 2 * rows, :])
        low, high = [
            jnp.concatenate(
                [norm[:, at * piece_n : (at + 1) * piece_n], jnp.zeros((1, LANES - piece_n), jnp.float32)], axis=1
            )
            for at in (2 * pair, 2 * pair + 1)
        ]
        rest = jnp.zeros((at_e - piece_s - 1, LANES), jnp.float32)
        place(pair, piece_s, jnp.concatenate([low, rest]), jnp.concatenate([high, rest]))
    for copy in stores:
        copy.wait()


def fold_kernel(bits, *refs):
    spot_ref, kept_ref = refs[:2]
    came, outs, total = refs[2 : 2 + bits[0]], refs[2 + bits[0] : -1], refs[-1]
    values = kept_ref[...]
    for ref in came:
        values = values + ref[...]
    total[...] = values
    ways = len(outs)
    for hop, out in enumerate(outs):
        for at in range(out.shape[0]):
            out[at] = total[at * ways + jnp.bitwise_xor(spot_ref[0], hop)]


def mean_kernel(replicas, spans, *refs):
    outs = refs[-len(spans) :]
    kept_ref, came = refs[0], refs[1 : -len(spans)]
    values = kept_ref[0]
    for ref in came:
        values = values + ref[0]
    values = values * (1.0 / replicas)
    for (start, rows), out in zip(spans, outs):
        width = out.shape[0] // rows
        for at in range(rows):
            out[at * width : (at + 1) * width] = values[start + at, :width]


def pack_kernel(*refs):
    half = len(refs) // 2
    for source, out in zip(refs[:half], refs[half:]):
        if source.shape[0] == 1:
            out[...] = source[...].astype(jnp.bfloat16)
            continue

        def lay(at, carry, source=source, out=out):
            values = source[pl.ds(pl.multiple_of(at * 8, 8), 8), :].astype(jnp.bfloat16)
            base = pl.multiple_of(at * 8 * LANES, 8 * LANES)
            for row in range(8):
                out[0:1, pl.ds(base + row * LANES, LANES)] = values[row : row + 1]
            return carry

        lax.fori_loop(0, source.shape[0] // 8, lay, 0)


def run_kernel(body, name, operands, outs, scratch=(), flops=0, vmem=SMALL_VMEM):
    def parts(entries, is_plain):
        plain = [entry if is_plain(entry) else entry[0] for entry in entries]
        return plain, [pl.BlockSpec(memory_space=pltpu.VMEM if is_plain(entry) else entry[1]) for entry in entries]

    arrays, in_specs = parts(operands, lambda entry: not isinstance(entry, tuple))
    shapes, out_specs = parts(outs, lambda entry: isinstance(entry[0], tuple) and not isinstance(entry[0][0], tuple))
    moved = sum(array.size * array.dtype.itemsize for array in arrays)
    return list(pl.pallas_call(
        body,
        in_specs=in_specs,
        out_specs=out_specs,
        out_shape=[jax.ShapeDtypeStruct(shape, kind) for shape, kind in shapes],
        scratch_shapes=[pltpu.VMEM(*entry) if isinstance(entry, tuple) else entry for entry in scratch],
        compiler_params=pltpu.CompilerParams(vmem_limit_bytes=vmem),
        cost_estimate=pl.CostEstimate(flops=flops, bytes_accessed=moved, transcendentals=0),
        name=name,
    )(*arrays))


def in_hbm(entry):
    return entry, pltpu.HBM


def in_smem(value):
    return value.astype(jnp.int32).reshape(1), pltpu.SMEM


def swap_all(bit, values):
    return [partner_2(member, "dp", bit) for member in values]


def exchange(spot, first_bit, ways, sends):
    replicas = lax.axis_size("dp")
    return [
        lax.ppermute(sent, "dp", [(at, at ^ (hop << first_bit)) for at in range(replicas)])
        for hop, sent in zip(range(1, ways), sends)
    ]


def scatter_mean(kept, sent, split, beside):
    f32 = jnp.float32
    replicas = lax.axis_size("dp")
    levels = replicas.bit_length() - 1
    place = lax.axis_index("dp")
    pairs, piece_s, piece_e, piece_r, piece_n = split
    rows = kept.shape[1]
    came = exchange(place, 0, 2, [sent])
    left, low = pairs, 1
    while left > 1:
        width = 2 if low == 1 and levels > 2 else 1
        ways = 1 << width
        spot = in_smem((place >> low) % ways)
        kept, *sends = run_kernel(
            functools.partial(fold_kernel, (len(came),)), "fold", [spot, kept] + came,
            [((left // ways, rows, LANES), f32)] * ways, [((left, rows, LANES), f32)],
        )
        came = exchange(place, low, ways, sends)
        if beside is not None:
            done = beside()
            beside = None
            came, done = lax.optimization_barrier((came, done))
        left, low = left // ways, low + width
    at_e = round_up(piece_s + 1, 8)
    spans = ((at_e + piece_e, piece_r), (0, piece_s), (at_e, piece_e), (piece_s, 1))
    sizes = [(rows_of * LANES,) for _, rows_of in spans[:3]] + [(piece_n,)]
    mean = run_kernel(
        functools.partial(mean_kernel, replicas, spans), "mean", [kept] + came, [(size, f32) for size in sizes]
    )
    if beside is not None:
        done = beside()
    return done, mean


def scatter_mean_any(arrays):
    replicas = lax.axis_size("dp")
    tables = [member.reshape(replicas, -1) for member in arrays]
    pieces = lax.all_to_all(jnp.concatenate(tables, axis=1), "dp", 0, 0, tiled=True)
    mean = jnp.sum(pieces, axis=0) / replicas
    bounds = [sum(table.shape[1] for table in tables[:at]) for at in range(len(tables) + 1)]
    return tuple(mean[low:high] for low, high in zip(bounds[:-1], bounds[1:]))


def shards(images, cotangent, w_reduce, w_spatial, w_expand, norm_gain, norm_bias, round_index):
    f32, bf16 = jnp.float32, jnp.bfloat16
    replicas = lax.axis_size("dp")
    levels = replicas.bit_length() - 1
    steps, _, pixels, in_ch = images.shape
    weights = [member.reshape(-1, LANES) for member in (w_reduce, w_spatial, w_expand)]
    sizes = [(member.shape, f32) for member in weights]
    rows_r, rows_s, rows_e = (member.shape[0] for member in weights)
    rows = rows_r + rows_s + rows_e
    norm_size = 2 * norm_gain.size
    flat_map = ((pixels, LANES), f32)
    wide_map = ((pixels, in_ch), f32)
    whole = ((rows, LANES), f32)
    norm_rows = ((norm_size // LANES, LANES), f32)
    half_map = ((pixels, in_ch), bf16)
    scratch = [
        half_map, half_map, whole, whole, whole, whole,
        flat_map, flat_map, ((pixels, LANES), bf16), ((ROWS, SPAN), bf16), ((SPAN, ROWS), bf16),
        ((ROWS_BACK, SPAN), bf16), ((ROWS + 16, LANES), f32), ((ROWS_BACK + 16, LANES), f32),
        sizes[2], ((LANES, in_ch), bf16), ((rows_s, LANES), bf16), ((LANES, rows_s), bf16),
        wide_map, wide_map, half_map, flat_map, ((pixels, LANES), bf16),
        pltpu.SemaphoreType.DMA((11,)), pltpu.SemaphoreType.DMA((6,)),
    ]
    flops = 6 * pixels * LANES * (2 * in_ch + rows_s)
    fine = replicas > 1 and all(size[0][0] % replicas == 0 for size in sizes)
    split = (replicas // 2, rows_s // replicas, rows_e // replicas, rows_r // replicas, norm_size // replicas)
    half = ((split[0], round_up(split[1] + 1, 8) + split[2] + split[3], LANES), f32)
    params = [weights[1], weights[0], weights[2], norm_gain, norm_bias]
    moments = []
    for step in range(steps):
        branches = [functools.partial(swap_all, bit) for bit in range(levels)]
        theirs = list(lax.switch((round_index[0] + step) % levels, branches, params))
        if step == 0:
            sides = [[in_hbm(side[at]) for at in (1, 0, 2)] + side[3:] for side in (params, theirs)]
        else:
            sides = [[in_hbm(side[0]), side[1]] for side in (params, theirs)]
        operands = [in_hbm(images), in_hbm(cotangent)] + sides[0] + sides[1]
        operands += [in_hbm(member) for member in moments[:3]] + moments[3:]
        moment_outs = [in_hbm(size) for size in sizes] + [((1, norm_size), f32)]
        extra = [whole] if step else []
        if step == steps - 1 and fine:
            core = in_smem(lax.axis_index("dp") % 2)
            kept, sent, *moments = run_kernel(
                functools.partial(step_kernel, step, True, split), "last_step", [core] + operands,
                [half, half] + moment_outs, scratch + extra, flops, VMEM_BYTES,
            )
        else:
            *params, m_r, m_s, m_e, m_n = run_kernel(
                functools.partial(step_kernel, step, False, None), "step", operands,
                [in_hbm(whole), norm_rows] + moment_outs, scratch + extra, flops, VMEM_BYTES,
            )
            moments = [m_r, m_s, m_e, m_n]
    pack = lambda: run_kernel(pack_kernel, "pack", moments, [((1, member.size), bf16) for member in moments])
    if fine:
        out, averaged = scatter_mean(kept, sent, split, pack)
    else:
        flat = [params[0][low:high].reshape(-1) for low, high in ((0, rows_r), (rows_r, rows_r + rows_s), (rows_r + rows_s, rows))]
        out, averaged = pack(), scatter_mean_any(flat + [params[1].reshape(-1)])
    return tuple(averaged) + tuple(out)


def solution(mesh):
    in_specs = (
        P(None, "dp", None, None),
        P(None, "dp", None, None),
        P("dp", None),
        P("dp", None),
        P("dp", None),
        P("dp", None),
        P("dp", None),
        P(),
    )
    out_specs = (
        P("dp"),
        P("dp"),
        P("dp"),
        P("dp"),
        P("dp", None),
        P("dp", None),
        P("dp", None),
        P("dp", None),
    )
    return jax.shard_map(shards, mesh=mesh, in_specs=in_specs, out_specs=out_specs, check_vma=False)
```

```python
import functools

import jax
import jax.numpy as jnp
from jax import lax
from jax.experimental import pallas as pl
from jax.experimental.pallas import tpu as pltpu
from jax.sharding import PartitionSpec as P

HEIGHT = 28
WIDTH = 28
KSIZE = 3

LEARN_RATE = 0.01
MOMENTUM = 0.9
EPSILON = 1e-05

LANES = 128
PITCH = 32
VMEM_BYTES = 60 * 1024 * 1024
SMALL_VMEM = 8 * 1024 * 1024


def round_up(value, unit):
    return (value + unit - 1) // unit * unit


def partner_2(value, axis, distance):
    mask = 2**distance
    pairs = [(source, source ^ mask) for source in range(lax.axis_size(axis))]
    return lax.ppermute(value, axis, pairs)


def matmul(left, right):
    return jnp.dot(left, right, preferred_element_type=jnp.float32)


def contract_cols(left, right):
    return lax.dot_general(left, right, (((1,), (1,)), ((), ())), preferred_element_type=jnp.float32)


def sigmoid(values):
    return 0.5 * jnp.tanh(0.5 * values) + 0.5


def activate(values):
    return values * sigmoid(values)


def act_slope(values):
    sigma = sigmoid(values)
    return sigma * (1.0 + values * (1.0 - sigma))


def column_sum(values):
    return jnp.sum(values, axis=0, keepdims=True)


MAPS = 4
THIN = 16
FLAT = MAPS * WIDTH
PITCHED = MAPS * PITCH
CHUNKS = HEIGHT // MAPS
SPAN = KSIZE * LANES
TOP = PITCH
TOP_BACK = 2 * PITCH
ROWS = round_up(HEIGHT * PITCH + 2 * PITCH, LANES)
ROWS_BACK = ROWS + 2 * PITCH


def flat_rows(at):
    return slice(at * FLAT, (at + 1) * FLAT)


def zero_rows(width):
    return jnp.zeros((8, width), jnp.float32)


def fold_rows(values):
    rows, width = values.shape
    return jnp.sum(values.reshape(rows // 8, 8, width), axis=0)


def sweep(body, init=0):
    carry = init
    for at in range(CHUNKS):
        carry = body(at, carry)
    return carry


def sweep_thin(count, body, init=0):
    def step(at, carry):
        return body(pl.ds(pl.multiple_of(at * THIN, THIN), THIN), carry)

    return lax.fori_loop(0, count // THIN, step, init, unroll=CHUNKS)


def pad_chunk(pad_ref, top, at, values):
    for row in range(MAPS):
        start = at * PITCHED + 8 + top + row * PITCH
        pad_ref[start : start + WIDTH, :] = values[row * WIDTH : (row + 1) * WIDTH]


def shift_columns(pad_ref, out_ref):
    rows = out_ref.shape[0]
    for col_off in range(KSIZE):
        start = 8 + col_off - KSIZE // 2
        out_ref[:, col_off * LANES : (col_off + 1) * LANES] = pad_ref[start : start + rows, :].astype(jnp.bfloat16)


def convolve(wide_ref, top, weights, multiply, pitched_ref):
    starts = [top + (row_off - KSIZE // 2) * PITCH for row_off in range(KSIZE)]
    taps = [wide_ref[start : start + HEIGHT * PITCH, :] for start in starts]
    pitched_ref[...] = multiply(jnp.concatenate(taps, axis=1), weights)


def compact(pitched_ref, at):
    starts = [at * PITCHED + row * PITCH for row in range(MAPS)]
    return jnp.concatenate([pitched_ref[start : start + WIDTH, :] for start in starts], axis=0)


def mean_of(own, theirs):
    return (own + theirs) * 0.5


def rows_at(ref, start, rows):
    return ref.at[pl.ds(start, rows), :]


def step_kernel(step, last, split, *refs):
    it = iter(refs)
    take = lambda count: [next(it) for _ in range(count)]
    core_ref = next(it) if last else None
    images_ref, cotangent_ref = take(2)
    packed = step > 0
    own, theirs = (take(2) if packed else take(5)) , (take(2) if packed else take(5))
    held_out = take(4) if packed else []
    outs = take(2) if last else take(2)
    moment_out = take(3)
    norm_moment = next(it)
    (x_ref, upstream_ref, own_ref, theirs_ref, param_ref, moment_ref,
     normed_a, normed_b, hidden_b, wide, wide_t, wide_b, pad, pad_b, mixed_e, weight_e, weight_s, weight_f,
     third, grad_sum, grad_third, work, back, pitched, arrived, left) = take(26)
    held_ref = next(it) if packed else None
    count, width = third.shape
    blocks = width // LANES
    rows_r, rows_s, rows_e = (ref.shape[0] for ref in moment_out)
    spans = ((0, rows_r), (rows_r, rows_s), (rows_r + rows_s, rows_e))
    bf16 = jnp.bfloat16
    view = lambda ref, part: rows_at(ref, *spans[part])
    pending = {}

    def fetch(name, source, target):
        copy = pltpu.make_async_copy(source, target, arrived.at[len(pending)])
        copy.start()
        pending[name] = copy

    def fetch_part(part):
        source = (lambda sides: view(sides[0], part)) if packed else (lambda sides: sides[part])
        fetch(("own", part), source(own), view(own_ref, part))
        fetch(("theirs", part), source(theirs), view(theirs_ref, part))

    def ready(part):
        pending["own", part].wait()
        pending["theirs", part].wait()

    fetch("x", images_ref.at[step, 0], x_ref)
    for part in range(3):
        fetch_part(part)
    fetch("upstream", cotangent_ref.at[step, 0], upstream_ref)
    if packed:
        for part in range(3):
            fetch(("held", part), held_out[part], view(held_ref, part))
    stores = []

    def store(source, target):
        copy = pltpu.make_async_copy(source, target, left.at[len(stores)])
        copy.start()
        stores.append(copy)

    def settle(part):
        store(view(moment_ref, part), moment_out[part])
        if not last:
            store(view(param_ref, part), view(outs[0], part))

    if packed:
        rows_of = lambda ref, low: jnp.concatenate([ref[low + at : low + at + 1, :] for at in range(ref.shape[0] // 2)], axis=1)
        half = own[1].shape[0] // 2
        gains = mean_of(rows_of(own[1], 0), rows_of(theirs[1], 0))
        shifts = mean_of(rows_of(own[1], half), rows_of(theirs[1], half))
    else:
        gains = mean_of(own[3][...], theirs[3][...])
        shifts = mean_of(own[4][...], theirs[4][...])
    gain_a, gain_b, gain_c = gains[:, :LANES], gains[:, LANES : 2 * LANES], gains[:, 2 * LANES :]
    shift_a, shift_b, shift_c = shifts[:, :LANES], shifts[:, LANES : 2 * LANES], shifts[:, 2 * LANES :]

    def mixed(part, start, rows):
        span = pl.ds(spans[part][0] + start, rows)
        return mean_of(own_ref[span, :], theirs_ref[span, :])

    def learn(part, start, rows, moment):
        span = pl.ds(spans[part][0] + start, rows)
        if packed:
            moment = MOMENTUM * held_ref[span, :] + moment
        moment_ref[span, :] = moment
        param_ref[span, :] = mixed(part, start, rows) - LEARN_RATE * moment

    pad[...] = jnp.zeros_like(pad)
    pad_b[...] = jnp.zeros_like(pad_b)
    pending["x"].wait()
    ready(0)
    normed_a[...] = matmul(x_ref[...], mixed(0, 0, rows_r).astype(bf16))

    def center(values_ref):
        mean = column_sum(sweep(lambda at, held: held + fold_rows(values_ref[flat_rows(at), :]), zero_rows(LANES))) / count

        def square(at, held):
            values = values_ref[flat_rows(at), :] - mean
            values_ref[flat_rows(at), :] = values
            return held + fold_rows(values * values)

        return lax.rsqrt(column_sum(sweep(square, zero_rows(LANES))) / count + EPSILON)

    scale_a = center(normed_a)
    for at in range(CHUNKS):
        normed = normed_a[flat_rows(at), :] * scale_a
        normed_a[flat_rows(at), :] = normed
        pad_chunk(pad, TOP, at, activate(normed * gain_a + shift_a))
    shift_columns(pad, wide)

    taps = KSIZE * KSIZE
    ready(1)
    for tap in range(taps):
        weights = mixed(1, tap * LANES, LANES).astype(bf16)
        weight_s[tap * LANES : (tap + 1) * LANES, :] = weights
        other = taps - 1 - tap
        weight_f[:, other * LANES : (other + 1) * LANES] = weights
    convolve(wide, TOP, weight_s[...], matmul, pitched)
    for at in range(CHUNKS):
        normed_b[flat_rows(at), :] = compact(pitched, at)
    scale_b = center(normed_b)
    for at in range(CHUNKS):
        normed = normed_b[flat_rows(at), :] * scale_b
        normed_b[flat_rows(at), :] = normed
        hidden_b[flat_rows(at), :] = activate(normed * gain_b + shift_b).astype(bf16)

    ready(2)
    mixed_e[...] = mixed(2, 0, rows_e)
    for block in range(blocks):
        weight_e[:, block * LANES : (block + 1) * LANES] = mixed_e[pl.ds(block, LANES, stride=blocks), :].astype(bf16)
    total = zero_rows(width)
    for at in range(CHUNKS):
        values = matmul(hidden_b[flat_rows(at), :], weight_e[...])
        third[flat_rows(at), :] = values
        total = total + fold_rows(values)
    mean = column_sum(total) / count

    def square(rows, held):
        values = third[rows, :] - mean
        third[rows, :] = values
        return held + fold_rows(values * values)

    scale_c = lax.rsqrt(column_sum(sweep_thin(count, square, zero_rows(width))) / count + EPSILON)
    pending["upstream"].wait()
    stretch = scale_c * gain_c

    def make_sum(rows, totals):
        values = third[rows, :]
        half_sum = 0.5 * (values * stretch + (shift_c + x_ref[rows, :].astype(jnp.float32)))
        bend = jnp.tanh(half_sum)
        slope = (1.0 + bend) * (1.0 + half_sum * (1.0 - bend))
        grad = upstream_ref[rows, :].astype(jnp.float32) * slope
        grad_sum[rows, :] = grad
        return totals[0] + fold_rows(grad * values), totals[1] + fold_rows(grad)

    dgain_c, dshift_c = sweep_thin(count, make_sum, (zero_rows(width), zero_rows(width)))
    dgain_c, dshift_c = 0.5 * column_sum(dgain_c) * scale_c, 0.5 * column_sum(dshift_c)
    level, slope, factor = 2.0 * dshift_c / count, 2.0 * scale_c * dgain_c / count, 0.5 * stretch

    def make_back_c(rows, carry):
        grad_third[rows, :] = ((grad_sum[rows, :] - level - third[rows, :] * slope) * factor).astype(bf16)
        return carry

    sweep_thin(count, make_back_c)
    work[...] = contract_cols(grad_third[...], weight_e[...])
    grad = matmul(hidden_b[...].T, grad_third[...])
    for block in range(blocks):
        mixed_e[pl.ds(block, LANES, stride=blocks), :] = grad[:, block * LANES : (block + 1) * LANES]
    for part in range(3 if packed else 0):
        pending["held", part].wait()
    learn(2, 0, rows_e, mixed_e[...])
    settle(2)

    def through_act(grad_of, normed_ref, gain, shift):
        totals = zero_rows(LANES), zero_rows(LANES)
        for at in range(CHUNKS):
            normed = normed_ref[flat_rows(at), :]
            grad = grad_of(at) * act_slope(normed * gain + shift)
            work[flat_rows(at), :] = grad
            totals = totals[0] + fold_rows(grad * normed), totals[1] + fold_rows(grad)
        return column_sum(totals[0]), column_sum(totals[1])

    def through_norm(at, normed_ref, dgain, dshift, factor):
        grad = work[flat_rows(at), :] - dshift / count - normed_ref[flat_rows(at), :] * (dgain / count)
        return grad * factor

    dgain_b, dshift_b = through_act(lambda at: work[flat_rows(at), :], normed_b, gain_b, shift_b)
    for at in range(CHUNKS):
        pad_chunk(pad_b, TOP_BACK, at, through_norm(at, normed_b, dgain_b, dshift_b, scale_b * gain_b))
    shift_columns(pad_b, wide_b)

    for at in range(ROWS // LANES):
        wide_t[:, at * LANES : (at + 1) * LANES] = wide[at * LANES : (at + 1) * LANES, :].T

    shifted = [
        wide_b[TOP_BACK - row_off * PITCH : TOP_BACK - row_off * PITCH + ROWS, LANES : 2 * LANES]
        for row_off in range(KSIZE)
    ]
    grad = matmul(wide_t[...], jnp.concatenate(shifted, axis=1))
    for row_off in range(KSIZE):
        learn(1, row_off * SPAN, SPAN, grad[:, row_off * LANES : (row_off + 1) * LANES])
    settle(1)

    convolve(wide_b, TOP_BACK, weight_f[...], contract_cols, pitched)
    dgain_a, dshift_a = through_act(lambda at: compact(pitched, at), normed_a, gain_a, shift_a)
    for at in range(CHUNKS):
        back[flat_rows(at), :] = through_norm(at, normed_a, dgain_a, dshift_a, scale_a * gain_a).astype(bf16)
    grad = matmul(back[...].T, x_ref[...])
    for block in range(blocks):
        learn(0, block * LANES, LANES, grad[:, block * LANES : (block + 1) * LANES].T)
    settle(0)
    grad = jnp.concatenate([dgain_a, dgain_b, dgain_c, dshift_a, dshift_b, dshift_c], axis=1)
    norm = jnp.concatenate([gains, shifts], axis=1)
    if packed:
        grad = MOMENTUM * held_out[3][...] + grad
    norm_moment[...] = grad
    norm = norm - LEARN_RATE * grad
    if not last:
        for at in range(norm.shape[1] // LANES):
            outs[1][at : at + 1, :] = norm[:, at * LANES : (at + 1) * LANES]
        for copy in stores:
            copy.wait()
        return

    kept_ref, sent_ref = outs
    is_odd = jnp.full((1, 1), core_ref[0], jnp.int32) == 1
    pairs, piece_s, piece_e, piece_r, piece_n = split
    at_e = round_up(piece_s + 1, 8)
    at_r = at_e + piece_e

    def place(pair, start, low, high):
        rows = low.shape[0]
        kept_ref[pair, start : start + rows, :] = jnp.where(is_odd, high, low)
        sent_ref[pair, start : start + rows, :] = jnp.where(is_odd, low, high)

    for pair in range(pairs):
        for part, rows, start in ((1, piece_s, 0), (2, piece_e, at_e), (0, piece_r, at_r)):
            first = spans[part][0] + 2 * pair * rows
            place(pair, start, param_ref[first : first + rows, :], param_ref[first + rows : first + 2 * rows, :])
        low, high = [
            jnp.concatenate(
                [norm[:, at * piece_n : (at + 1) * piece_n], jnp.zeros((1, LANES - piece_n), jnp.float32)], axis=1
            )
            for at in (2 * pair, 2 * pair + 1)
        ]
        rest = jnp.zeros((at_e - piece_s - 1, LANES), jnp.float32)
        place(pair, piece_s, jnp.concatenate([low, rest]), jnp.concatenate([high, rest]))
    for copy in stores:
        copy.wait()


def fold_kernel(bits, *refs):
    spot_ref, kept_ref = refs[:2]
    came, outs, total = refs[2 : 2 + bits[0]], refs[2 + bits[0] : -1], refs[-1]
    values = kept_ref[...]
    for ref in came:
        values = values + ref[...]
    total[...] = values
    ways = len(outs)
    for hop, out in enumerate(outs):
        for at in range(out.shape[0]):
            out[at] = total[at * ways + jnp.bitwise_xor(spot_ref[0], hop)]


def mean_kernel(replicas, spans, *refs):
    outs = refs[-len(spans) :]
    kept_ref, came = refs[0], refs[1 : -len(spans)]
    values = kept_ref[0]
    for ref in came:
        values = values + ref[0]
    values = values * (1.0 / replicas)
    for (start, rows), out in zip(spans, outs):
        width = out.shape[0] // rows
        for at in range(rows):
            out[at * width : (at + 1) * width] = values[start + at, :width]


def pack_kernel(*refs):
    half = len(refs) // 2
    for source, out in zip(refs[:half], refs[half:]):
        if source.shape[0] == 1:
            out[...] = source[...].astype(jnp.bfloat16)
            continue

        def lay(at, carry, source=source, out=out):
            values = source[pl.ds(pl.multiple_of(at * 8, 8), 8), :].astype(jnp.bfloat16)
            base = pl.multiple_of(at * 8 * LANES, 8 * LANES)
            for row in range(8):
                out[0:1, pl.ds(base + row * LANES, LANES)] = values[row : row + 1]
            return carry

        lax.fori_loop(0, source.shape[0] // 8, lay, 0)


def run_kernel(body, name, operands, outs, scratch=(), flops=0, vmem=SMALL_VMEM):
    def parts(entries, is_plain):
        plain = [entry if is_plain(entry) else entry[0] for entry in entries]
        return plain, [pl.BlockSpec(memory_space=pltpu.VMEM if is_plain(entry) else entry[1]) for entry in entries]

    arrays, in_specs = parts(operands, lambda entry: not isinstance(entry, tuple))
    shapes, out_specs = parts(outs, lambda entry: isinstance(entry[0], tuple) and not isinstance(entry[0][0], tuple))
    moved = sum(array.size * array.dtype.itemsize for array in arrays)
    return list(pl.pallas_call(
        body,
        in_specs=in_specs,
        out_specs=out_specs,
        out_shape=[jax.ShapeDtypeStruct(shape, kind) for shape, kind in shapes],
        scratch_shapes=[pltpu.VMEM(*entry) if isinstance(entry, tuple) else entry for entry in scratch],
        compiler_params=pltpu.CompilerParams(vmem_limit_bytes=vmem),
        cost_estimate=pl.CostEstimate(flops=flops, bytes_accessed=moved, transcendentals=0),
        name=name,
    )(*arrays))


def in_hbm(entry):
    return entry, pltpu.HBM


def in_smem(value):
    return value.astype(jnp.int32).reshape(1), pltpu.SMEM


def swap_all(bit, values):
    return [partner_2(member, "dp", bit) for member in values]


def exchange(spot, first_bit, ways, sends):
    replicas = lax.axis_size("dp")
    return [
        lax.ppermute(sent, "dp", [(at, at ^ (hop << first_bit)) for at in range(replicas)])
        for hop, sent in zip(range(1, ways), sends)
    ]


def scatter_mean(kept, sent, split, beside):
    f32 = jnp.float32
    replicas = lax.axis_size("dp")
    levels = replicas.bit_length() - 1
    place = lax.axis_index("dp")
    pairs, piece_s, piece_e, piece_r, piece_n = split
    rows = kept.shape[1]
    came = exchange(place, 0, 2, [sent])
    left, low = pairs, 1
    while left > 1:
        width = 2 if low == 1 and levels > 2 else 1
        ways = 1 << width
        spot = in_smem((place >> low) % ways)
        kept, *sends = run_kernel(
            functools.partial(fold_kernel, (len(came),)), "fold", [spot, kept] + came,
            [((left // ways, rows, LANES), f32)] * ways, [((left, rows, LANES), f32)],
        )
        came = exchange(place, low, ways, sends)
        if beside is not None:
            done = beside()
            beside = None
            came, done = lax.optimization_barrier((came, done))
        left, low = left // ways, low + width
    at_e = round_up(piece_s + 1, 8)
    spans = ((at_e + piece_e, piece_r), (0, piece_s), (at_e, piece_e), (piece_s, 1))
    sizes = [(rows_of * LANES,) for _, rows_of in spans[:3]] + [(piece_n,)]
    mean = run_kernel(
        functools.partial(mean_kernel, replicas, spans), "mean", [kept] + came, [(size, f32) for size in sizes]
    )
    if beside is not None:
        done = beside()
    return done, mean


def scatter_mean_any(arrays):
    replicas = lax.axis_size("dp")
    tables = [member.reshape(replicas, -1) for member in arrays]
    pieces = lax.all_to_all(jnp.concatenate(tables, axis=1), "dp", 0, 0, tiled=True)
    mean = jnp.sum(pieces, axis=0) / replicas
    bounds = [sum(table.shape[1] for table in tables[:at]) for at in range(len(tables) + 1)]
    return tuple(mean[low:high] for low, high in zip(bounds[:-1], bounds[1:]))


def shards(images, cotangent, w_reduce, w_spatial, w_expand, norm_gain, norm_bias, round_index):
    f32, bf16 = jnp.float32, jnp.bfloat16
    replicas = lax.axis_size("dp")
    levels = replicas.bit_length() - 1
    steps, _, pixels, in_ch = images.shape
    weights = [member.reshape(-1, LANES) for member in (w_reduce, w_spatial, w_expand)]
    sizes = [(member.shape, f32) for member in weights]
    rows_r, rows_s, rows_e = (member.shape[0] for member in weights)
    rows = rows_r + rows_s + rows_e
    norm_size = 2 * norm_gain.size
    flat_map = ((pixels, LANES), f32)
    wide_map = ((pixels, in_ch), f32)
    whole = ((rows, LANES), f32)
    norm_rows = ((norm_size // LANES, LANES), f32)
    half_map = ((pixels, in_ch), bf16)
    scratch = [
        half_map, half_map, whole, whole, whole, whole,
        flat_map, flat_map, ((pixels, LANES), bf16), ((ROWS, SPAN), bf16), ((SPAN, ROWS), bf16),
        ((ROWS_BACK, SPAN), bf16), ((ROWS + 16, LANES), f32), ((ROWS_BACK + 16, LANES), f32),
        sizes[2], ((LANES, in_ch), bf16), ((rows_s, LANES), bf16), ((LANES, rows_s), bf16),
        wide_map, wide_map, half_map, flat_map, ((pixels, LANES), bf16), ((HEIGHT * PITCH, LANES), f32),
        pltpu.SemaphoreType.DMA((11,)), pltpu.SemaphoreType.DMA((6,)),
    ]
    flops = 6 * pixels * LANES * (2 * in_ch + rows_s)
    fine = replicas > 1 and all(size[0][0] % replicas == 0 for size in sizes)
    split = (replicas // 2, rows_s // replicas, rows_e // replicas, rows_r // replicas, norm_size // replicas)
    half = ((split[0], round_up(split[1] + 1, 8) + split[2] + split[3], LANES), f32)
    params = [weights[1], weights[0], weights[2], norm_gain, norm_bias]
    moments = []
    for step in range(steps):
        branches = [functools.partial(swap_all, bit) for bit in range(levels)]
        theirs = list(lax.switch((round_index[0] + step) % levels, branches, params))
        if step == 0:
            sides = [[in_hbm(side[at]) for at in (1, 0, 2)] + side[3:] for side in (params, theirs)]
        else:
            sides = [[in_hbm(side[0]), side[1]] for side in (params, theirs)]
        operands = [in_hbm(images), in_hbm(cotangent)] + sides[0] + sides[1]
        operands += [in_hbm(member) for member in moments[:3]] + moments[3:]
        moment_outs = [in_hbm(size) for size in sizes] + [((1, norm_size), f32)]
        extra = [whole] if step else []
        if step == steps - 1 and fine:
            core = in_smem(lax.axis_index("dp") % 2)
            kept, sent, *moments = run_kernel(
                functools.partial(step_kernel, step, True, split), "last_step", [core] + operands,
                [half, half] + moment_outs, scratch + extra, flops, VMEM_BYTES,
            )
        else:
            *params, m_r, m_s, m_e, m_n = run_kernel(
                functools.partial(step_kernel, step, False, None), "step", operands,
                [in_hbm(whole), norm_rows] + moment_outs, scratch + extra, flops, VMEM_BYTES,
            )
            moments = [m_r, m_s, m_e, m_n]
    pack = lambda: run_kernel(pack_kernel, "pack", moments, [((1, member.size), bf16) for member in moments])
    if fine:
        out, averaged = scatter_mean(kept, sent, split, pack)
    else:
        flat = [params[0][low:high].reshape(-1) for low, high in ((0, rows_r), (rows_r, rows_r + rows_s), (rows_r + rows_s, rows))]
        out, averaged = pack(), scatter_mean_any(flat + [params[1].reshape(-1)])
    return tuple(averaged) + tuple(out)


def solution(mesh):
    in_specs = (
        P(None, "dp", None, None),
        P(None, "dp", None, None),
        P("dp", None),
        P("dp", None),
        P("dp", None),
        P("dp", None),
        P("dp", None),
        P(),
    )
    out_specs = (
        P("dp"),
        P("dp"),
        P("dp"),
        P("dp"),
        P("dp", None),
        P("dp", None),
        P("dp", None),
        P("dp", None),
    )
    return jax.shard_map(shards, mesh=mesh, in_specs=in_specs, out_specs=out_specs, check_vma=False)
```

```python
import functools

import jax
import jax.numpy as jnp
from jax import lax
from jax.experimental import pallas as pl
from jax.experimental.pallas import tpu as pltpu
from jax.sharding import PartitionSpec as P

HEIGHT = 28
WIDTH = 28
KSIZE = 3

LEARN_RATE = 0.01
MOMENTUM = 0.9
EPSILON = 1e-05

LANES = 128
PITCH = 32
VMEM_BYTES = 60 * 1024 * 1024
SMALL_VMEM = 8 * 1024 * 1024


def round_up(value, unit):
    return (value + unit - 1) // unit * unit


def partner_2(value, axis, distance):
    mask = 2**distance
    pairs = [(source, source ^ mask) for source in range(lax.axis_size(axis))]
    return lax.ppermute(value, axis, pairs)


def matmul(left, right):
    return jnp.dot(left, right, preferred_element_type=jnp.float32)


def contract_cols(left, right):
    return lax.dot_general(left, right, (((1,), (1,)), ((), ())), preferred_element_type=jnp.float32)


def sigmoid(values):
    return 0.5 * jnp.tanh(0.5 * values) + 0.5


def activate(values):
    return values * sigmoid(values)


def act_slope(values):
    sigma = sigmoid(values)
    return sigma * (1.0 + values * (1.0 - sigma))


def column_sum(values):
    return jnp.sum(values, axis=0, keepdims=True)


MAPS = 4
THIN = 16
FLAT = MAPS * WIDTH
PITCHED = MAPS * PITCH
CHUNKS = HEIGHT // MAPS
SPAN = KSIZE * LANES
TOP = PITCH
TOP_BACK = 2 * PITCH
ROWS = round_up(HEIGHT * PITCH + 2 * PITCH, LANES)
ROWS_BACK = ROWS + 2 * PITCH


def flat_rows(at):
    return slice(at * FLAT, (at + 1) * FLAT)


def zero_rows(width):
    return jnp.zeros((8, width), jnp.float32)


def fold_rows(values):
    rows, width = values.shape
    return jnp.sum(values.reshape(rows // 8, 8, width), axis=0)


def sweep(body, init=0):
    carry = init
    for at in range(CHUNKS):
        carry = body(at, carry)
    return carry


def sweep_wide(count, body, init, thin):
    rows = THIN if thin else FLAT

    def step(at, carry):
        return body(pl.ds(pl.multiple_of(at * rows, rows), rows), carry)

    return lax.fori_loop(0, count // rows, step, init, unroll=CHUNKS if thin else 1)


def pad_chunk(pad_ref, top, at, values):
    for row in range(MAPS):
        start = at * PITCHED + 8 + top + row * PITCH
        pad_ref[start : start + WIDTH, :] = values[row * WIDTH : (row + 1) * WIDTH]


def shift_columns(pad_ref, out_ref):
    rows = out_ref.shape[0]
    for col_off in range(KSIZE):
        start = 8 + col_off - KSIZE // 2
        out_ref[:, col_off * LANES : (col_off + 1) * LANES] = pad_ref[start : start + rows, :].astype(jnp.bfloat16)


def convolve(wide_ref, top, weights, multiply, pitched_ref, by_row):
    if by_row:
        total = None
        for row_off in range(KSIZE):
            start = top + (row_off - KSIZE // 2) * PITCH
            piece = multiply(wide_ref[start : start + HEIGHT * PITCH, :], weights(row_off))
            total = piece if total is None else total + piece
        pitched_ref[...] = total
        return
    weights = weights(None)
    starts = [top + (row_off - KSIZE // 2) * PITCH for row_off in range(KSIZE)]
    taps = [wide_ref[start : start + HEIGHT * PITCH, :] for start in starts]
    pitched_ref[...] = multiply(jnp.concatenate(taps, axis=1), weights)


def compact(pitched_ref, at):
    starts = [at * PITCHED + row * PITCH for row in range(MAPS)]
    return jnp.concatenate([pitched_ref[start : start + WIDTH, :] for start in starts], axis=0)


def mean_of(own, theirs):
    return (own + theirs) * 0.5


def rows_at(ref, start, rows):
    return ref.at[pl.ds(start, rows), :]


def step_kernel(step, last, split, *refs):
    it = iter(refs)
    take = lambda count: [next(it) for _ in range(count)]
    core_ref = next(it) if last else None
    images_ref, cotangent_ref = take(2)
    packed = step > 0
    own, theirs = (take(2) if packed else take(5)) , (take(2) if packed else take(5))
    held_out = take(4) if packed else []
    outs = take(2) if last else take(2)
    moment_out = take(3)
    norm_moment = next(it)
    (x_ref, upstream_ref, own_ref, theirs_ref, param_ref, moment_ref,
     normed_a, normed_b, hidden_b, wide, wide_t, wide_b, pad, pad_b, mixed_e, weight_e, weight_s, weight_f,
     third, grad_sum, grad_third, work, back, pitched, arrived, left) = take(26)
    held_ref = next(it) if packed else None
    count, width = third.shape
    blocks = width // LANES
    rows_r, rows_s, rows_e = (ref.shape[0] for ref in moment_out)
    spans = ((0, rows_r), (rows_r, rows_s), (rows_r + rows_s, rows_e))
    bf16 = jnp.bfloat16
    view = lambda ref, part: rows_at(ref, *spans[part])
    pending = {}

    def fetch(name, source, target):
        copy = pltpu.make_async_copy(source, target, arrived.at[len(pending)])
        copy.start()
        pending[name] = copy

    def fetch_part(part):
        source = (lambda sides: view(sides[0], part)) if packed else (lambda sides: sides[part])
        fetch(("own", part), source(own), view(own_ref, part))
        fetch(("theirs", part), source(theirs), view(theirs_ref, part))

    def ready(part):
        pending["own", part].wait()
        pending["theirs", part].wait()

    fetch("x", images_ref.at[step, 0], x_ref)
    for part in range(3):
        fetch_part(part)
    fetch("upstream", cotangent_ref.at[step, 0], upstream_ref)
    if packed:
        for part in range(3):
            fetch(("held", part), held_out[part], view(held_ref, part))
    stores = []

    def store(source, target):
        copy = pltpu.make_async_copy(source, target, left.at[len(stores)])
        copy.start()
        stores.append(copy)

    def settle(part):
        store(view(moment_ref, part), moment_out[part])
        if not last:
            store(view(param_ref, part), view(outs[0], part))

    if packed:
        rows_of = lambda ref, low: jnp.concatenate([ref[low + at : low + at + 1, :] for at in range(ref.shape[0] // 2)], axis=1)
        half = own[1].shape[0] // 2
        gains = mean_of(rows_of(own[1], 0), rows_of(theirs[1], 0))
        shifts = mean_of(rows_of(own[1], half), rows_of(theirs[1], half))
    else:
        gains = mean_of(own[3][...], theirs[3][...])
        shifts = mean_of(own[4][...], theirs[4][...])
    gain_a, gain_b, gain_c = gains[:, :LANES], gains[:, LANES : 2 * LANES], gains[:, 2 * LANES :]
    shift_a, shift_b, shift_c = shifts[:, :LANES], shifts[:, LANES : 2 * LANES], shifts[:, 2 * LANES :]

    def mixed(part, start, rows):
        span = pl.ds(spans[part][0] + start, rows)
        return mean_of(own_ref[span, :], theirs_ref[span, :])

    def learn(part, start, rows, moment):
        span = pl.ds(spans[part][0] + start, rows)
        if packed:
            moment = MOMENTUM * held_ref[span, :] + moment
        moment_ref[span, :] = moment
        param_ref[span, :] = mixed(part, start, rows) - LEARN_RATE * moment

    pad[...] = jnp.zeros_like(pad)
    pad_b[...] = jnp.zeros_like(pad_b)
    pending["x"].wait()
    ready(0)
    normed_a[...] = matmul(x_ref[...], mixed(0, 0, rows_r).astype(bf16))

    def center(values_ref):
        mean = column_sum(sweep(lambda at, held: held + fold_rows(values_ref[flat_rows(at), :]), zero_rows(LANES))) / count

        def square(at, held):
            values = values_ref[flat_rows(at), :] - mean
            values_ref[flat_rows(at), :] = values
            return held + fold_rows(values * values)

        return lax.rsqrt(column_sum(sweep(square, zero_rows(LANES))) / count + EPSILON)

    scale_a = center(normed_a)
    for at in range(CHUNKS):
        normed = normed_a[flat_rows(at), :] * scale_a
        normed_a[flat_rows(at), :] = normed
        pad_chunk(pad, TOP, at, activate(normed * gain_a + shift_a))
    shift_columns(pad, wide)

    taps = KSIZE * KSIZE
    ready(1)
    for tap in range(taps):
        weights = mixed(1, tap * LANES, LANES).astype(bf16)
        weight_s[tap * LANES : (tap + 1) * LANES, :] = weights
        other = taps - 1 - tap
        weight_f[:, other * LANES : (other + 1) * LANES] = weights
    by_row, thin = step == 0, step == 0
    pick_s = lambda row: weight_s[...] if row is None else weight_s[row * SPAN : (row + 1) * SPAN, :]
    pick_f = lambda row: weight_f[...] if row is None else weight_f[:, row * SPAN : (row + 1) * SPAN]
    convolve(wide, TOP, pick_s, matmul, pitched, by_row)
    for at in range(CHUNKS):
        normed_b[flat_rows(at), :] = compact(pitched, at)
    scale_b = center(normed_b)
    for at in range(CHUNKS):
        normed = normed_b[flat_rows(at), :] * scale_b
        normed_b[flat_rows(at), :] = normed
        hidden_b[flat_rows(at), :] = activate(normed * gain_b + shift_b).astype(bf16)

    ready(2)
    mixed_e[...] = mixed(2, 0, rows_e)
    for block in range(blocks):
        weight_e[:, block * LANES : (block + 1) * LANES] = mixed_e[pl.ds(block, LANES, stride=blocks), :].astype(bf16)
    total = zero_rows(width)
    for at in range(CHUNKS):
        values = matmul(hidden_b[flat_rows(at), :], weight_e[...])
        third[flat_rows(at), :] = values
        total = total + fold_rows(values)
    mean = column_sum(total) / count

    def square(rows, held):
        values = third[rows, :] - mean
        third[rows, :] = values
        return held + fold_rows(values * values)

    scale_c = lax.rsqrt(column_sum(sweep_wide(count, square, zero_rows(width), thin)) / count + EPSILON)
    pending["upstream"].wait()
    stretch = scale_c * gain_c

    def make_sum(rows, totals):
        values = third[rows, :]
        half_sum = 0.5 * (values * stretch + (shift_c + x_ref[rows, :].astype(jnp.float32)))
        bend = jnp.tanh(half_sum)
        slope = (1.0 + bend) * (1.0 + half_sum * (1.0 - bend))
        grad = upstream_ref[rows, :].astype(jnp.float32) * slope
        grad_sum[rows, :] = grad
        return totals[0] + fold_rows(grad * values), totals[1] + fold_rows(grad)

    dgain_c, dshift_c = sweep_wide(count, make_sum, (zero_rows(width), zero_rows(width)), thin)
    dgain_c, dshift_c = 0.5 * column_sum(dgain_c) * scale_c, 0.5 * column_sum(dshift_c)
    level, slope, factor = 2.0 * dshift_c / count, 2.0 * scale_c * dgain_c / count, 0.5 * stretch

    def make_back_c(rows, carry):
        grad = ((grad_sum[rows, :] - level - third[rows, :] * slope) * factor).astype(bf16)
        grad_third[rows, :] = grad
        if not thin:
            work[rows, :] = contract_cols(grad, weight_e[...])
        return carry

    sweep_wide(count, make_back_c, 0, thin)
    if thin:
        work[...] = contract_cols(grad_third[...], weight_e[...])
    grad = matmul(hidden_b[...].T, grad_third[...])
    for block in range(blocks):
        mixed_e[pl.ds(block, LANES, stride=blocks), :] = grad[:, block * LANES : (block + 1) * LANES]
    for part in range(3 if packed else 0):
        pending["held", part].wait()
    learn(2, 0, rows_e, mixed_e[...])
    settle(2)

    def through_act(grad_of, normed_ref, gain, shift):
        totals = zero_rows(LANES), zero_rows(LANES)
        for at in range(CHUNKS):
            normed = normed_ref[flat_rows(at), :]
            grad = grad_of(at) * act_slope(normed * gain + shift)
            work[flat_rows(at), :] = grad
            totals = totals[0] + fold_rows(grad * normed), totals[1] + fold_rows(grad)
        return column_sum(totals[0]), column_sum(totals[1])

    def through_norm(at, normed_ref, dgain, dshift, factor):
        grad = work[flat_rows(at), :] - dshift / count - normed_ref[flat_rows(at), :] * (dgain / count)
        return grad * factor

    dgain_b, dshift_b = through_act(lambda at: work[flat_rows(at), :], normed_b, gain_b, shift_b)
    for at in range(CHUNKS):
        pad_chunk(pad_b, TOP_BACK, at, through_norm(at, normed_b, dgain_b, dshift_b, scale_b * gain_b))
    shift_columns(pad_b, wide_b)

    for at in range(ROWS // LANES):
        wide_t[:, at * LANES : (at + 1) * LANES] = wide[at * LANES : (at + 1) * LANES, :].T

    shifted = [
        wide_b[TOP_BACK - row_off * PITCH : TOP_BACK - row_off * PITCH + ROWS, LANES : 2 * LANES]
        for row_off in range(KSIZE)
    ]
    grad = matmul(wide_t[...], jnp.concatenate(shifted, axis=1))
    for row_off in range(KSIZE):
        learn(1, row_off * SPAN, SPAN, grad[:, row_off * LANES : (row_off + 1) * LANES])
    settle(1)

    convolve(wide_b, TOP_BACK, pick_f, contract_cols, pitched, by_row)
    dgain_a, dshift_a = through_act(lambda at: compact(pitched, at), normed_a, gain_a, shift_a)
    for at in range(CHUNKS):
        back[flat_rows(at), :] = through_norm(at, normed_a, dgain_a, dshift_a, scale_a * gain_a).astype(bf16)
    grad = matmul(back[...].T, x_ref[...])
    for block in range(blocks):
        learn(0, block * LANES, LANES, grad[:, block * LANES : (block + 1) * LANES].T)
    settle(0)
    grad = jnp.concatenate([dgain_a, dgain_b, dgain_c, dshift_a, dshift_b, dshift_c], axis=1)
    norm = jnp.concatenate([gains, shifts], axis=1)
    if packed:
        grad = MOMENTUM * held_out[3][...] + grad
    norm_moment[...] = grad
    norm = norm - LEARN_RATE * grad
    if not last:
        for at in range(norm.shape[1] // LANES):
            outs[1][at : at + 1, :] = norm[:, at * LANES : (at + 1) * LANES]
        for copy in stores:
            copy.wait()
        return

    kept_ref, sent_ref = outs
    is_odd = jnp.full((1, 1), core_ref[0], jnp.int32) == 1
    pairs, piece_s, piece_e, piece_r, piece_n = split
    at_e = round_up(piece_s + 1, 8)
    at_r = at_e + piece_e

    def place(pair, start, low, high):
        rows = low.shape[0]
        kept_ref[pair, start : start + rows, :] = jnp.where(is_odd, high, low)
        sent_ref[pair, start : start + rows, :] = jnp.where(is_odd, low, high)

    for pair in range(pairs):
        for part, rows, start in ((1, piece_s, 0), (2, piece_e, at_e), (0, piece_r, at_r)):
            first = spans[part][0] + 2 * pair * rows
            place(pair, start, param_ref[first : first + rows, :], param_ref[first + rows : first + 2 * rows, :])
        low, high = [
            jnp.concatenate(
                [norm[:, at * piece_n : (at + 1) * piece_n], jnp.zeros((1, LANES - piece_n), jnp.float32)], axis=1
            )
            for at in (2 * pair, 2 * pair + 1)
        ]
        rest = jnp.zeros((at_e - piece_s - 1, LANES), jnp.float32)
        place(pair, piece_s, jnp.concatenate([low, rest]), jnp.concatenate([high, rest]))
    for copy in stores:
        copy.wait()


def fold_kernel(bits, *refs):
    spot_ref, kept_ref = refs[:2]
    came, outs, total = refs[2 : 2 + bits[0]], refs[2 + bits[0] : -1], refs[-1]
    values = kept_ref[...]
    for ref in came:
        values = values + ref[...]
    total[...] = values
    ways = len(outs)
    for hop, out in enumerate(outs):
        for at in range(out.shape[0]):
            out[at] = total[at * ways + jnp.bitwise_xor(spot_ref[0], hop)]


def mean_kernel(replicas, spans, *refs):
    outs = refs[-len(spans) :]
    kept_ref, came = refs[0], refs[1 : -len(spans)]
    values = kept_ref[0]
    for ref in came:
        values = values + ref[0]
    values = values * (1.0 / replicas)
    for (start, rows), out in zip(spans, outs):
        width = out.shape[0] // rows
        for at in range(rows):
            out[at * width : (at + 1) * width] = values[start + at, :width]


def pack_kernel(*refs):
    half = len(refs) // 2
    for source, out in zip(refs[:half], refs[half:]):
        if source.shape[0] == 1:
            out[...] = source[...].astype(jnp.bfloat16)
            continue

        def lay(at, carry, source=source, out=out):
            values = source[pl.ds(pl.multiple_of(at * 8, 8), 8), :].astype(jnp.bfloat16)
            base = pl.multiple_of(at * 8 * LANES, 8 * LANES)
            for row in range(8):
                out[0:1, pl.ds(base + row * LANES, LANES)] = values[row : row + 1]
            return carry

        lax.fori_loop(0, source.shape[0] // 8, lay, 0)


def run_kernel(body, name, operands, outs, scratch=(), flops=0, vmem=SMALL_VMEM):
    def parts(entries, is_plain):
        plain = [entry if is_plain(entry) else entry[0] for entry in entries]
        return plain, [pl.BlockSpec(memory_space=pltpu.VMEM if is_plain(entry) else entry[1]) for entry in entries]

    arrays, in_specs = parts(operands, lambda entry: not isinstance(entry, tuple))
    shapes, out_specs = parts(outs, lambda entry: isinstance(entry[0], tuple) and not isinstance(entry[0][0], tuple))
    moved = sum(array.size * array.dtype.itemsize for array in arrays)
    return list(pl.pallas_call(
        body,
        in_specs=in_specs,
        out_specs=out_specs,
        out_shape=[jax.ShapeDtypeStruct(shape, kind) for shape, kind in shapes],
        scratch_shapes=[pltpu.VMEM(*entry) if isinstance(entry, tuple) else entry for entry in scratch],
        compiler_params=pltpu.CompilerParams(vmem_limit_bytes=vmem),
        cost_estimate=pl.CostEstimate(flops=flops, bytes_accessed=moved, transcendentals=0),
        name=name,
    )(*arrays))


def in_hbm(entry):
    return entry, pltpu.HBM


def in_smem(value):
    return value.astype(jnp.int32).reshape(1), pltpu.SMEM


def swap_all(bit, values):
    return [partner_2(member, "dp", bit) for member in values]


def exchange(spot, first_bit, ways, sends):
    replicas = lax.axis_size("dp")
    return [
        lax.ppermute(sent, "dp", [(at, at ^ (hop << first_bit)) for at in range(replicas)])
        for hop, sent in zip(range(1, ways), sends)
    ]


def scatter_mean(kept, sent, split, beside):
    f32 = jnp.float32
    replicas = lax.axis_size("dp")
    levels = replicas.bit_length() - 1
    place = lax.axis_index("dp")
    pairs, piece_s, piece_e, piece_r, piece_n = split
    rows = kept.shape[1]
    came = exchange(place, 0, 2, [sent])
    left, low = pairs, 1
    while left > 1:
        width = 2 if low == 1 and levels > 2 else 1
        ways = 1 << width
        spot = in_smem((place >> low) % ways)
        kept, *sends = run_kernel(
            functools.partial(fold_kernel, (len(came),)), "fold", [spot, kept] + came,
            [((left // ways, rows, LANES), f32)] * ways, [((left, rows, LANES), f32)],
        )
        came = exchange(place, low, ways, sends)
        if beside is not None:
            done = beside()
            beside = None
            came, done = lax.optimization_barrier((came, done))
        left, low = left // ways, low + width
    at_e = round_up(piece_s + 1, 8)
    spans = ((at_e + piece_e, piece_r), (0, piece_s), (at_e, piece_e), (piece_s, 1))
    sizes = [(rows_of * LANES,) for _, rows_of in spans[:3]] + [(piece_n,)]
    mean = run_kernel(
        functools.partial(mean_kernel, replicas, spans), "mean", [kept] + came, [(size, f32) for size in sizes]
    )
    if beside is not None:
        done = beside()
    return done, mean


def scatter_mean_any(arrays):
    replicas = lax.axis_size("dp")
    tables = [member.reshape(replicas, -1) for member in arrays]
    pieces = lax.all_to_all(jnp.concatenate(tables, axis=1), "dp", 0, 0, tiled=True)
    mean = jnp.sum(pieces, axis=0) / replicas
    bounds = [sum(table.shape[1] for table in tables[:at]) for at in range(len(tables) + 1)]
    return tuple(mean[low:high] for low, high in zip(bounds[:-1], bounds[1:]))


def shards(images, cotangent, w_reduce, w_spatial, w_expand, norm_gain, norm_bias, round_index):
    f32, bf16 = jnp.float32, jnp.bfloat16
    replicas = lax.axis_size("dp")
    levels = replicas.bit_length() - 1
    steps, _, pixels, in_ch = images.shape
    weights = [member.reshape(-1, LANES) for member in (w_reduce, w_spatial, w_expand)]
    sizes = [(member.shape, f32) for member in weights]
    rows_r, rows_s, rows_e = (member.shape[0] for member in weights)
    rows = rows_r + rows_s + rows_e
    norm_size = 2 * norm_gain.size
    flat_map = ((pixels, LANES), f32)
    wide_map = ((pixels, in_ch), f32)
    whole = ((rows, LANES), f32)
    norm_rows = ((norm_size // LANES, LANES), f32)
    half_map = ((pixels, in_ch), bf16)
    scratch = [
        half_map, half_map, whole, whole, whole, whole,
        flat_map, flat_map, ((pixels, LANES), bf16), ((ROWS, SPAN), bf16), ((SPAN, ROWS), bf16),
        ((ROWS_BACK, SPAN), bf16), ((ROWS + 16, LANES), f32), ((ROWS_BACK + 16, LANES), f32),
        sizes[2], ((LANES, in_ch), bf16), ((rows_s, LANES), bf16), ((LANES, rows_s), bf16),
        wide_map, wide_map, half_map, flat_map, ((pixels, LANES), bf16), ((HEIGHT * PITCH, LANES), f32),
        pltpu.SemaphoreType.DMA((11,)), pltpu.SemaphoreType.DMA((6,)),
    ]
    flops = 6 * pixels * LANES * (2 * in_ch + rows_s)
    fine = replicas > 1 and all(size[0][0] % replicas == 0 for size in sizes)
    split = (replicas // 2, rows_s // replicas, rows_e // replicas, rows_r // replicas, norm_size // replicas)
    half = ((split[0], round_up(split[1] + 1, 8) + split[2] + split[3], LANES), f32)
    params = [weights[1], weights[0], weights[2], norm_gain, norm_bias]
    moments = []
    for step in range(steps):
        branches = [functools.partial(swap_all, bit) for bit in range(levels)]
        theirs = list(lax.switch((round_index[0] + step) % levels, branches, params))
        if step == 0:
            sides = [[in_hbm(side[at]) for at in (1, 0, 2)] + side[3:] for side in (params, theirs)]
        else:
            sides = [[in_hbm(side[0]), side[1]] for side in (params, theirs)]
        operands = [in_hbm(images), in_hbm(cotangent)] + sides[0] + sides[1]
        operands += [in_hbm(member) for member in moments[:3]] + moments[3:]
        moment_outs = [in_hbm(size) for size in sizes] + [((1, norm_size), f32)]
        extra = [whole] if step else []
        if step == steps - 1 and fine:
            core = in_smem(lax.axis_index("dp") % 2)
            kept, sent, *moments = run_kernel(
                functools.partial(step_kernel, step, True, split), "last_step", [core] + operands,
                [half, half] + moment_outs, scratch + extra, flops, VMEM_BYTES,
            )
        else:
            *params, m_r, m_s, m_e, m_n = run_kernel(
                functools.partial(step_kernel, step, False, None), "step", operands,
                [in_hbm(whole), norm_rows] + moment_outs, scratch + extra, flops, VMEM_BYTES,
            )
            moments = [m_r, m_s, m_e, m_n]
    pack = lambda: run_kernel(pack_kernel, "pack", moments, [((1, member.size), bf16) for member in moments])
    if fine:
        out, averaged = scatter_mean(kept, sent, split, pack)
    else:
        flat = [params[0][low:high].reshape(-1) for low, high in ((0, rows_r), (rows_r, rows_r + rows_s), (rows_r + rows_s, rows))]
        out, averaged = pack(), scatter_mean_any(flat + [params[1].reshape(-1)])
    return tuple(averaged) + tuple(out)


def solution(mesh):
    in_specs = (
        P(None, "dp", None, None),
        P(None, "dp", None, None),
        P("dp", None),
        P("dp", None),
        P("dp", None),
        P("dp", None),
        P("dp", None),
        P(),
    )
    out_specs = (
        P("dp"),
        P("dp"),
        P("dp"),
        P("dp"),
        P("dp", None),
        P("dp", None),
        P("dp", None),
        P("dp", None),
    )
    return jax.shard_map(shards, mesh=mesh, in_specs=in_specs, out_specs=out_specs, check_vma=False)
```

```python
import functools

import jax
import jax.numpy as jnp
from jax import lax
from jax.experimental import pallas as pl
from jax.experimental.pallas import tpu as pltpu
from jax.sharding import PartitionSpec as P

HEIGHT = 28
WIDTH = 28
KSIZE = 3

LEARN_RATE = 0.01
MOMENTUM = 0.9
EPSILON = 1e-05

LANES = 128
PITCH = 32
VMEM_BYTES = 60 * 1024 * 1024
SMALL_VMEM = 8 * 1024 * 1024


def round_up(value, unit):
    return (value + unit - 1) // unit * unit


def partner_2(value, axis, distance):
    mask = 2**distance
    pairs = [(source, source ^ mask) for source in range(lax.axis_size(axis))]
    return lax.ppermute(value, axis, pairs)


def matmul(left, right):
    return jnp.dot(left, right, preferred_element_type=jnp.float32)


def contract_cols(left, right):
    return lax.dot_general(left, right, (((1,), (1,)), ((), ())), preferred_element_type=jnp.float32)


def sigmoid(values):
    return 0.5 * jnp.tanh(0.5 * values) + 0.5


def activate(values):
    return values * sigmoid(values)


def act_slope(values):
    sigma = sigmoid(values)
    return sigma * (1.0 + values * (1.0 - sigma))


def column_sum(values):
    return jnp.sum(values, axis=0, keepdims=True)


MAPS = 4
THIN = 16
FLAT = MAPS * WIDTH
PITCHED = MAPS * PITCH
CHUNKS = HEIGHT // MAPS
SPAN = KSIZE * LANES
TOP = PITCH
TOP_BACK = 2 * PITCH
ROWS = round_up(HEIGHT * PITCH + 2 * PITCH, LANES)
ROWS_BACK = ROWS + 2 * PITCH


def flat_rows(at):
    return slice(at * FLAT, (at + 1) * FLAT)


def zero_rows(width):
    return jnp.zeros((8, width), jnp.float32)


def fold_rows(values):
    rows, width = values.shape
    return jnp.sum(values.reshape(rows // 8, 8, width), axis=0)


def sweep(body, init=0):
    carry = init
    for at in range(CHUNKS):
        carry = body(at, carry)
    return carry


def sweep_wide(body, init=0, beside=None):
    def step(at, carry):
        if beside is not None:
            beside(at)
        for piece in range(FLAT // THIN):
            carry = body(pl.ds(pl.multiple_of(at * FLAT + piece * THIN, THIN), THIN), carry)
        return carry

    return lax.fori_loop(0, CHUNKS, step, init)


def pad_chunk(pad_ref, top, at, values):
    for row in range(MAPS):
        start = at * PITCHED + 8 + top + row * PITCH
        pad_ref[start : start + WIDTH, :] = values[row * WIDTH : (row + 1) * WIDTH]


def shift_columns(pad_ref, out_ref):
    rows = out_ref.shape[0]
    for col_off in range(KSIZE):
        start = 8 + col_off - KSIZE // 2
        out_ref[:, col_off * LANES : (col_off + 1) * LANES] = pad_ref[start : start + rows, :].astype(jnp.bfloat16)


def conv_chunk(wide_ref, top, at, weights, multiply, by_row):
    starts = [at * PITCHED + top + (row_off - KSIZE // 2) * PITCH for row_off in range(KSIZE)]
    taps = [wide_ref[start : start + PITCHED, :] for start in starts]
    if by_row:
        total = multiply(taps[0], weights(0))
        for row_off in range(1, KSIZE):
            total = total + multiply(taps[row_off], weights(row_off))
    else:
        total = multiply(jnp.concatenate(taps, axis=1), weights(None))
    return jnp.concatenate([total[row * PITCH : row * PITCH + WIDTH] for row in range(MAPS)], axis=0)


def mean_of(own, theirs):
    return (own + theirs) * 0.5


def rows_at(ref, start, rows):
    return ref.at[pl.ds(start, rows), :]


def step_kernel(step, last, split, *refs):
    it = iter(refs)
    take = lambda count: [next(it) for _ in range(count)]
    core_ref = next(it) if last else None
    images_ref, cotangent_ref = take(2)
    packed = step > 0
    own, theirs = (take(2) if packed else take(5)) , (take(2) if packed else take(5))
    held_out = take(4) if packed else []
    outs = take(2) if last else take(2)
    moment_out = take(3)
    norm_moment = next(it)
    (x_ref, upstream_ref, own_ref, theirs_ref, param_ref, moment_ref,
     normed_a, normed_b, hidden_b, wide, wide_t, wide_b, pad, pad_b, mixed_e, weight_e, weight_s, weight_f,
     third, grad_sum, grad_third, work, back, hidden_t, arrived, left) = take(26)
    held_ref = next(it) if packed else None
    count, width = third.shape
    blocks = width // LANES
    rows_r, rows_s, rows_e = (ref.shape[0] for ref in moment_out)
    spans = ((0, rows_r), (rows_r, rows_s), (rows_r + rows_s, rows_e))
    bf16 = jnp.bfloat16
    view = lambda ref, part: rows_at(ref, *spans[part])
    pending = {}

    def fetch(name, source, target):
        copy = pltpu.make_async_copy(source, target, arrived.at[len(pending)])
        copy.start()
        pending[name] = copy

    def fetch_part(part):
        source = (lambda sides: view(sides[0], part)) if packed else (lambda sides: sides[part])
        fetch(("own", part), source(own), view(own_ref, part))
        fetch(("theirs", part), source(theirs), view(theirs_ref, part))

    def ready(part):
        pending["own", part].wait()
        pending["theirs", part].wait()

    fetch("x", images_ref.at[step, 0], x_ref)
    for part in range(3):
        fetch_part(part)
    fetch("upstream", cotangent_ref.at[step, 0], upstream_ref)
    if packed:
        for part in range(3):
            fetch(("held", part), held_out[part], view(held_ref, part))
    stores = []

    def store(source, target):
        copy = pltpu.make_async_copy(source, target, left.at[len(stores)])
        copy.start()
        stores.append(copy)

    def settle(part):
        store(view(moment_ref, part), moment_out[part])
        if not last:
            store(view(param_ref, part), view(outs[0], part))

    if packed:
        rows_of = lambda ref, low: jnp.concatenate([ref[low + at : low + at + 1, :] for at in range(ref.shape[0] // 2)], axis=1)
        half = own[1].shape[0] // 2
        gains = mean_of(rows_of(own[1], 0), rows_of(theirs[1], 0))
        shifts = mean_of(rows_of(own[1], half), rows_of(theirs[1], half))
    else:
        gains = mean_of(own[3][...], theirs[3][...])
        shifts = mean_of(own[4][...], theirs[4][...])
    gain_a, gain_b, gain_c = gains[:, :LANES], gains[:, LANES : 2 * LANES], gains[:, 2 * LANES :]
    shift_a, shift_b, shift_c = shifts[:, :LANES], shifts[:, LANES : 2 * LANES], shifts[:, 2 * LANES :]

    def mixed(part, start, rows):
        span = pl.ds(spans[part][0] + start, rows)
        return mean_of(own_ref[span, :], theirs_ref[span, :])

    def learn(part, start, rows, moment):
        span = pl.ds(spans[part][0] + start, rows)
        if packed:
            moment = MOMENTUM * held_ref[span, :] + moment
        moment_ref[span, :] = moment
        param_ref[span, :] = mixed(part, start, rows) - LEARN_RATE * moment

    pad[...] = jnp.zeros_like(pad)
    pad_b[...] = jnp.zeros_like(pad_b)
    pending["x"].wait()
    ready(0)
    reduce_w = mixed(0, 0, rows_r).astype(bf16)

    def center(values_ref, make):
        total = zero_rows(LANES)
        for at in range(CHUNKS):
            values = make(at)
            values_ref[flat_rows(at), :] = values
            total = total + fold_rows(values)
        mean = column_sum(total) / count

        def square(at, held):
            values = values_ref[flat_rows(at), :] - mean
            values_ref[flat_rows(at), :] = values
            return held + fold_rows(values * values)

        return lax.rsqrt(column_sum(sweep(square, zero_rows(LANES))) / count + EPSILON)

    scale_a = center(normed_a, lambda at: matmul(x_ref[flat_rows(at), :], reduce_w))
    for at in range(CHUNKS):
        normed = normed_a[flat_rows(at), :] * scale_a
        normed_a[flat_rows(at), :] = normed
        pad_chunk(pad, TOP, at, activate(normed * gain_a + shift_a))
    shift_columns(pad, wide)

    taps = KSIZE * KSIZE
    ready(1)
    for tap in range(taps):
        weights = mixed(1, tap * LANES, LANES).astype(bf16)
        weight_s[tap * LANES : (tap + 1) * LANES, :] = weights
        other = taps - 1 - tap
        weight_f[:, other * LANES : (other + 1) * LANES] = weights
    by_row = step == 0
    pick_s = lambda row: weight_s[...] if row is None else weight_s[row * SPAN : (row + 1) * SPAN, :]
    pick_f = lambda row: weight_f[...] if row is None else weight_f[:, row * SPAN : (row + 1) * SPAN]
    scale_b = center(normed_b, lambda at: conv_chunk(wide, TOP, at, pick_s, matmul, by_row))
    for at in range(CHUNKS):
        normed = normed_b[flat_rows(at), :] * scale_b
        normed_b[flat_rows(at), :] = normed
        hidden_b[flat_rows(at), :] = activate(normed * gain_b + shift_b).astype(bf16)
    hidden_b[count:, :] = jnp.zeros((hidden_b.shape[0] - count, LANES), bf16)
    grad_third[count:, :] = jnp.zeros((grad_third.shape[0] - count, width), bf16)

    ready(2)
    mixed_e[...] = mixed(2, 0, rows_e)
    for block in range(blocks):
        weight_e[:, block * LANES : (block + 1) * LANES] = mixed_e[pl.ds(block, LANES, stride=blocks), :].astype(bf16)
    total = zero_rows(width)
    for at in range(CHUNKS):
        values = matmul(hidden_b[flat_rows(at), :], weight_e[...])
        third[flat_rows(at), :] = values
        total = total + fold_rows(values)
    mean = column_sum(total) / count

    def square(rows, held):
        values = third[rows, :] - mean
        third[rows, :] = values
        return held + fold_rows(values * values)

    def turn(source, target):
        def block(at):
            start = pl.multiple_of(at * LANES, LANES)
            target[:, pl.ds(start, LANES)] = source[pl.ds(start, LANES), :].T

        return block

    scale_c = lax.rsqrt(column_sum(sweep_wide(square, zero_rows(width), turn(hidden_b, hidden_t))) / count + EPSILON)
    pending["upstream"].wait()
    stretch = scale_c * gain_c

    def make_sum(rows, totals):
        values = third[rows, :]
        half_sum = 0.5 * (values * stretch + (shift_c + x_ref[rows, :].astype(jnp.float32)))
        bend = jnp.tanh(half_sum)
        slope = (1.0 + bend) * (1.0 + half_sum * (1.0 - bend))
        grad = upstream_ref[rows, :].astype(jnp.float32) * slope
        grad_sum[rows, :] = grad
        return totals[0] + fold_rows(grad * values), totals[1] + fold_rows(grad)

    dgain_c, dshift_c = sweep_wide(make_sum, (zero_rows(width), zero_rows(width)), turn(wide, wide_t))
    for at in range(CHUNKS, ROWS // LANES):
        turn(wide, wide_t)(at)
    dgain_c, dshift_c = 0.5 * column_sum(dgain_c) * scale_c, 0.5 * column_sum(dshift_c)
    level, slope, factor = 2.0 * dshift_c / count, 2.0 * scale_c * dgain_c / count, 0.5 * stretch

    def make_back_c(rows, carry):
        grad = ((grad_sum[rows, :] - level - third[rows, :] * slope) * factor).astype(bf16)
        grad_third[rows, :] = grad
        return carry

    sweep_wide(make_back_c)
    for block in range(blocks):
        grad = matmul(hidden_t[...], grad_third[:, block * LANES : (block + 1) * LANES])
        mixed_e[pl.ds(block, LANES, stride=blocks), :] = grad
    for part in range(3 if packed else 0):
        pending["held", part].wait()
    learn(2, 0, rows_e, mixed_e[...])
    settle(2)

    def through_act(grad_of, normed_ref, gain, shift):
        totals = zero_rows(LANES), zero_rows(LANES)
        for at in range(CHUNKS):
            normed = normed_ref[flat_rows(at), :]
            grad = grad_of(at) * act_slope(normed * gain + shift)
            work[flat_rows(at), :] = grad
            totals = totals[0] + fold_rows(grad * normed), totals[1] + fold_rows(grad)
        return column_sum(totals[0]), column_sum(totals[1])

    def through_norm(at, normed_ref, dgain, dshift, factor):
        grad = work[flat_rows(at), :] - dshift / count - normed_ref[flat_rows(at), :] * (dgain / count)
        return grad * factor

    dgain_b, dshift_b = through_act(
        lambda at: contract_cols(grad_third[flat_rows(at), :], weight_e[...]), normed_b, gain_b, shift_b
    )
    for at in range(CHUNKS):
        pad_chunk(pad_b, TOP_BACK, at, through_norm(at, normed_b, dgain_b, dshift_b, scale_b * gain_b))
    shift_columns(pad_b, wide_b)

    shifted = [
        wide_b[TOP_BACK - row_off * PITCH : TOP_BACK - row_off * PITCH + ROWS, LANES : 2 * LANES]
        for row_off in range(KSIZE)
    ]
    shifted = jnp.concatenate(shifted, axis=1)
    for col_off in range(KSIZE):
        grad = matmul(wide_t[col_off * LANES : (col_off + 1) * LANES, :], shifted)
        for row_off in range(KSIZE):
            learn(1, row_off * SPAN + col_off * LANES, LANES, grad[:, row_off * LANES : (row_off + 1) * LANES])
    settle(1)

    dgain_a, dshift_a = through_act(
        lambda at: conv_chunk(wide_b, TOP_BACK, at, pick_f, contract_cols, by_row), normed_a, gain_a, shift_a
    )
    for at in range(CHUNKS):
        back[flat_rows(at), :] = through_norm(at, normed_a, dgain_a, dshift_a, scale_a * gain_a).astype(bf16)
    back_t = back[...].T
    for block in range(blocks):
        span = slice(block * LANES, (block + 1) * LANES)
        learn(0, block * LANES, LANES, matmul(back_t, x_ref[:, span]).T)
    settle(0)
    grad = jnp.concatenate([dgain_a, dgain_b, dgain_c, dshift_a, dshift_b, dshift_c], axis=1)
    norm = jnp.concatenate([gains, shifts], axis=1)
    if packed:
        grad = MOMENTUM * held_out[3][...] + grad
    norm_moment[...] = grad
    norm = norm - LEARN_RATE * grad
    if not last:
        for at in range(norm.shape[1] // LANES):
            outs[1][at : at + 1, :] = norm[:, at * LANES : (at + 1) * LANES]
        for copy in stores:
            copy.wait()
        return

    kept_ref, sent_ref = outs
    is_odd = jnp.full((1, 1), core_ref[0], jnp.int32) == 1
    pairs, piece_s, piece_e, piece_r, piece_n = split
    at_e = round_up(piece_s + 1, 8)
    at_r = at_e + piece_e

    def place(pair, start, low, high):
        rows = low.shape[0]
        kept_ref[pair, start : start + rows, :] = jnp.where(is_odd, high, low)
        sent_ref[pair, start : start + rows, :] = jnp.where(is_odd, low, high)

    for pair in range(pairs):
        for part, rows, start in ((1, piece_s, 0), (2, piece_e, at_e), (0, piece_r, at_r)):
            first = spans[part][0] + 2 * pair * rows
            place(pair, start, param_ref[first : first + rows, :], param_ref[first + rows : first + 2 * rows, :])
        low, high = [
            jnp.concatenate(
                [norm[:, at * piece_n : (at + 1) * piece_n], jnp.zeros((1, LANES - piece_n), jnp.float32)], axis=1
            )
            for at in (2 * pair, 2 * pair + 1)
        ]
        rest = jnp.zeros((at_e - piece_s - 1, LANES), jnp.float32)
        place(pair, piece_s, jnp.concatenate([low, rest]), jnp.concatenate([high, rest]))
    for copy in stores:
        copy.wait()


def fold_kernel(bits, *refs):
    spot_ref, kept_ref = refs[:2]
    came, outs, total = refs[2 : 2 + bits[0]], refs[2 + bits[0] : -1], refs[-1]
    values = kept_ref[...]
    for ref in came:
        values = values + ref[...]
    total[...] = values
    ways = len(outs)
    for hop, out in enumerate(outs):
        for at in range(out.shape[0]):
            out[at] = total[at * ways + jnp.bitwise_xor(spot_ref[0], hop)]


def mean_kernel(replicas, spans, *refs):
    outs = refs[-len(spans) :]
    kept_ref, came = refs[0], refs[1 : -len(spans)]
    values = kept_ref[0]
    for ref in came:
        values = values + ref[0]
    values = values * (1.0 / replicas)
    for (start, rows), out in zip(spans, outs):
        width = out.shape[0] // rows
        for at in range(rows):
            out[at * width : (at + 1) * width] = values[start + at, :width]


def pack_kernel(*refs):
    half = len(refs) // 2
    for source, out in zip(refs[:half], refs[half:]):
        if source.shape[0] == 1:
            out[...] = source[...].astype(jnp.bfloat16)
            continue

        def lay(at, carry, source=source, out=out):
            values = source[pl.ds(pl.multiple_of(at * 8, 8), 8), :].astype(jnp.bfloat16)
            base = pl.multiple_of(at * 8 * LANES, 8 * LANES)
            for row in range(8):
                out[0:1, pl.ds(base + row * LANES, LANES)] = values[row : row + 1]
            return carry

        lax.fori_loop(0, source.shape[0] // 8, lay, 0)


def run_kernel(body, name, operands, outs, scratch=(), flops=0, vmem=SMALL_VMEM):
    def parts(entries, is_plain):
        plain = [entry if is_plain(entry) else entry[0] for entry in entries]
        return plain, [pl.BlockSpec(memory_space=pltpu.VMEM if is_plain(entry) else entry[1]) for entry in entries]

    arrays, in_specs = parts(operands, lambda entry: not isinstance(entry, tuple))
    shapes, out_specs = parts(outs, lambda entry: isinstance(entry[0], tuple) and not isinstance(entry[0][0], tuple))
    moved = sum(array.size * array.dtype.itemsize for array in arrays)
    return list(pl.pallas_call(
        body,
        in_specs=in_specs,
        out_specs=out_specs,
        out_shape=[jax.ShapeDtypeStruct(shape, kind) for shape, kind in shapes],
        scratch_shapes=[pltpu.VMEM(*entry) if isinstance(entry, tuple) else entry for entry in scratch],
        compiler_params=pltpu.CompilerParams(vmem_limit_bytes=vmem),
        cost_estimate=pl.CostEstimate(flops=flops, bytes_accessed=moved, transcendentals=0),
        name=name,
    )(*arrays))


def in_hbm(entry):
    return entry, pltpu.HBM


def in_smem(value):
    return value.astype(jnp.int32).reshape(1), pltpu.SMEM


def swap_all(bit, values):
    return [partner_2(member, "dp", bit) for member in values]


def exchange(spot, first_bit, ways, sends):
    replicas = lax.axis_size("dp")
    return [
        lax.ppermute(sent, "dp", [(at, at ^ (hop << first_bit)) for at in range(replicas)])
        for hop, sent in zip(range(1, ways), sends)
    ]


def scatter_mean(kept, sent, split, beside):
    f32 = jnp.float32
    replicas = lax.axis_size("dp")
    levels = replicas.bit_length() - 1
    place = lax.axis_index("dp")
    pairs, piece_s, piece_e, piece_r, piece_n = split
    rows = kept.shape[1]
    came = exchange(place, 0, 2, [sent])
    left, low = pairs, 1
    while left > 1:
        width = 2 if low == 1 and levels > 2 else 1
        ways = 1 << width
        spot = in_smem((place >> low) % ways)
        kept, *sends = run_kernel(
            functools.partial(fold_kernel, (len(came),)), "fold", [spot, kept] + came,
            [((left // ways, rows, LANES), f32)] * ways, [((left, rows, LANES), f32)],
        )
        came = exchange(place, low, ways, sends)
        if beside is not None:
            done = beside()
            beside = None
            came, done = lax.optimization_barrier((came, done))
        left, low = left // ways, low + width
    at_e = round_up(piece_s + 1, 8)
    spans = ((at_e + piece_e, piece_r), (0, piece_s), (at_e, piece_e), (piece_s, 1))
    sizes = [(rows_of * LANES,) for _, rows_of in spans[:3]] + [(piece_n,)]
    mean = run_kernel(
        functools.partial(mean_kernel, replicas, spans), "mean", [kept] + came, [(size, f32) for size in sizes]
    )
    if beside is not None:
        done = beside()
    return done, mean


def scatter_mean_any(arrays):
    replicas = lax.axis_size("dp")
    tables = [member.reshape(replicas, -1) for member in arrays]
    pieces = lax.all_to_all(jnp.concatenate(tables, axis=1), "dp", 0, 0, tiled=True)
    mean = jnp.sum(pieces, axis=0) / replicas
    bounds = [sum(table.shape[1] for table in tables[:at]) for at in range(len(tables) + 1)]
    return tuple(mean[low:high] for low, high in zip(bounds[:-1], bounds[1:]))


def shards(images, cotangent, w_reduce, w_spatial, w_expand, norm_gain, norm_bias, round_index):
    f32, bf16 = jnp.float32, jnp.bfloat16
    replicas = lax.axis_size("dp")
    levels = replicas.bit_length() - 1
    steps, _, pixels, in_ch = images.shape
    weights = [member.reshape(-1, LANES) for member in (w_reduce, w_spatial, w_expand)]
    sizes = [(member.shape, f32) for member in weights]
    rows_r, rows_s, rows_e = (member.shape[0] for member in weights)
    rows = rows_r + rows_s + rows_e
    norm_size = 2 * norm_gain.size
    pixels_up = round_up(pixels, LANES)
    flat_map = ((pixels, LANES), f32)
    wide_map = ((pixels, in_ch), f32)
    whole = ((rows, LANES), f32)
    norm_rows = ((norm_size // LANES, LANES), f32)
    half_map = ((pixels, in_ch), bf16)
    scratch = [
        half_map, half_map, whole, whole, whole, whole,
        flat_map, flat_map, ((pixels_up, LANES), bf16), ((ROWS, SPAN), bf16), ((SPAN, ROWS), bf16),
        ((ROWS_BACK, SPAN), bf16), ((ROWS + 16, LANES), f32), ((ROWS_BACK + 16, LANES), f32),
        sizes[2], ((LANES, in_ch), bf16), ((rows_s, LANES), bf16), ((LANES, rows_s), bf16),
        wide_map, wide_map, ((pixels_up, in_ch), bf16), flat_map, ((pixels, LANES), bf16), ((LANES, pixels_up), bf16),
        pltpu.SemaphoreType.DMA((11,)), pltpu.SemaphoreType.DMA((6,)),
    ]
    flops = 6 * pixels * LANES * (2 * in_ch + rows_s)
    fine = replicas > 1 and all(size[0][0] % replicas == 0 for size in sizes)
    split = (replicas // 2, rows_s // replicas, rows_e // replicas, rows_r // replicas, norm_size // replicas)
    half = ((split[0], round_up(split[1] + 1, 8) + split[2] + split[3], LANES), f32)
    params = [weights[1], weights[0], weights[2], norm_gain, norm_bias]
    moments = []
    for step in range(steps):
        branches = [functools.partial(swap_all, bit) for bit in range(levels)]
        theirs = list(lax.switch((round_index[0] + step) % levels, branches, params))
        if step == 0:
            sides = [[in_hbm(side[at]) for at in (1, 0, 2)] + side[3:] for side in (params, theirs)]
        else:
            sides = [[in_hbm(side[0]), side[1]] for side in (params, theirs)]
        operands = [in_hbm(images), in_hbm(cotangent)] + sides[0] + sides[1]
        operands += [in_hbm(member) for member in moments[:3]] + moments[3:]
        moment_outs = [in_hbm(size) for size in sizes] + [((1, norm_size), f32)]
        extra = [whole] if step else []
        if step == steps - 1 and fine:
            core = in_smem(lax.axis_index("dp") % 2)
            kept, sent, *moments = run_kernel(
                functools.partial(step_kernel, step, True, split), "last_step", [core] + operands,
                [half, half] + moment_outs, scratch + extra, flops, VMEM_BYTES,
            )
        else:
            *params, m_r, m_s, m_e, m_n = run_kernel(
                functools.partial(step_kernel, step, False, None), "step", operands,
                [in_hbm(whole), norm_rows] + moment_outs, scratch + extra, flops, VMEM_BYTES,
            )
            moments = [m_r, m_s, m_e, m_n]
    pack = lambda: run_kernel(pack_kernel, "pack", moments, [((1, member.size), bf16) for member in moments])
    if fine:
        out, averaged = scatter_mean(kept, sent, split, pack)
    else:
        flat = [params[0][low:high].reshape(-1) for low, high in ((0, rows_r), (rows_r, rows_r + rows_s), (rows_r + rows_s, rows))]
        out, averaged = pack(), scatter_mean_any(flat + [params[1].reshape(-1)])
    return tuple(averaged) + tuple(out)


def solution(mesh):
    in_specs = (
        P(None, "dp", None, None),
        P(None, "dp", None, None),
        P("dp", None),
        P("dp", None),
        P("dp", None),
        P("dp", None),
        P("dp", None),
        P(),
    )
    out_specs = (
        P("dp"),
        P("dp"),
        P("dp"),
        P("dp"),
        P("dp", None),
        P("dp", None),
        P("dp", None),
        P("dp", None),
    )
    return jax.shard_map(shards, mesh=mesh, in_specs=in_specs, out_specs=out_specs, check_vma=False)
```

```python
import functools

import jax
import jax.numpy as jnp
from jax import lax
from jax.experimental import pallas as pl
from jax.experimental.pallas import tpu as pltpu
from jax.sharding import PartitionSpec as P

HEIGHT = 28
WIDTH = 28
KSIZE = 3

LEARN_RATE = 0.01
MOMENTUM = 0.9
EPSILON = 1e-05

LANES = 128
PITCH = 32
VMEM_BYTES = 60 * 1024 * 1024
SMALL_VMEM = 8 * 1024 * 1024


def round_up(value, unit):
    return (value + unit - 1) // unit * unit


def partner_2(value, axis, distance):
    mask = 2**distance
    pairs = [(source, source ^ mask) for source in range(lax.axis_size(axis))]
    return lax.ppermute(value, axis, pairs)


def matmul(left, right):
    return jnp.dot(left, right, preferred_element_type=jnp.float32)


def contract_cols(left, right):
    return lax.dot_general(left, right, (((1,), (1,)), ((), ())), preferred_element_type=jnp.float32)


def sigmoid(values):
    return 0.5 * jnp.tanh(0.5 * values) + 0.5


def activate(values):
    return values * sigmoid(values)


def act_slope(values):
    sigma = sigmoid(values)
    return sigma * (1.0 + values * (1.0 - sigma))


def column_sum(values):
    return jnp.sum(values, axis=0, keepdims=True)


MAPS = 4
THIN = 16
FLAT = MAPS * WIDTH
PITCHED = MAPS * PITCH
CHUNKS = HEIGHT // MAPS
SPAN = KSIZE * LANES
TOP = PITCH
TOP_BACK = 2 * PITCH
ROWS = round_up(HEIGHT * PITCH + 2 * PITCH, LANES)
ROWS_BACK = ROWS + 2 * PITCH


def flat_rows(at):
    return pl.ds(pl.multiple_of(at * FLAT, FLAT), FLAT)


def zero_row(width):
    return jnp.zeros((1, width), jnp.float32)


def sweep(body, init=0, unroll=True):
    return lax.fori_loop(0, CHUNKS, body, init, unroll=unroll)


def fold_rows(values):
    rows, width = values.shape
    return jnp.sum(values.reshape(rows // 8, 8, width), axis=0)


def zero_rows(width):
    return jnp.zeros((8, width), jnp.float32)


def sweep_wide(count, body, init=0, beside=None):
    def step(at, carry):
        if beside is not None:
            beside(at)
        for piece in range(FLAT // THIN):
            carry = body(pl.ds(pl.multiple_of(at * FLAT + piece * THIN, THIN), THIN), carry)
        return carry

    return lax.fori_loop(0, count // FLAT, step, init)


def statistics(values_ref, total):
    count, width = values_ref.shape
    mean = total / count

    def add(at, held):
        center = values_ref[flat_rows(at), :] - mean
        return held + column_sum(center * center)

    return mean, lax.rsqrt(sweep(add, zero_row(width), width == LANES) / count + EPSILON)


def pad_chunk(pad_ref, top, at, values):
    for row in range(MAPS):
        start = pl.multiple_of(at * PITCHED, PITCHED) + (8 + top + row * PITCH)
        pad_ref[pl.ds(start, WIDTH), :] = values[row * WIDTH : (row + 1) * WIDTH]


def shift_columns(pad_ref, out_ref):
    rows = out_ref.shape[0]
    for col_off in range(KSIZE):
        start = 8 + col_off - KSIZE // 2
        out_ref[:, col_off * LANES : (col_off + 1) * LANES] = pad_ref[start : start + rows, :].astype(jnp.bfloat16)


def conv_chunk(wide_ref, top, at, weight_of, multiply):
    total = None
    for row_off in range(KSIZE):
        start = pl.multiple_of(at * PITCHED, PITCHED) + (top + (row_off - KSIZE // 2) * PITCH)
        piece = multiply(wide_ref[pl.ds(start, PITCHED), :], weight_of(row_off))
        total = piece if total is None else total + piece
    return jnp.concatenate([total[row * PITCH : row * PITCH + WIDTH] for row in range(MAPS)], axis=0)


def mean_of(own, theirs):
    return (own + theirs) * 0.5


def rows_at(ref, start, rows):
    return ref.at[pl.ds(start, rows), :]


def step_kernel(step, last, split, *refs):
    it = iter(refs)
    take = lambda count: [next(it) for _ in range(count)]
    core_ref = next(it) if last else None
    images_ref, cotangent_ref = take(2)
    packed = step > 0
    own, theirs = (take(2) if packed else take(5)) , (take(2) if packed else take(5))
    held_out = take(4) if packed else []
    outs = take(2) if last else take(2)
    moment_out = take(3)
    norm_moment = next(it)
    (x_ref, upstream_ref, own_ref, theirs_ref, param_ref, moment_ref,
     normed_a, normed_b, hidden_b, wide, wide_t, wide_b, pad, pad_b, mixed_e, weight_e, weight_s, weight_f,
     third, grad_sum, grad_third, work, back, arrived, left) = take(25)
    held_ref = next(it) if packed else None
    count, width = third.shape
    blocks = width // LANES
    rows_r, rows_s, rows_e = (ref.shape[0] for ref in moment_out)
    spans = ((0, rows_r), (rows_r, rows_s), (rows_r + rows_s, rows_e))
    bf16 = jnp.bfloat16
    view = lambda ref, part: rows_at(ref, *spans[part])
    pending = {}

    def fetch(name, source, target):
        copy = pltpu.make_async_copy(source, target, arrived.at[len(pending)])
        copy.start()
        pending[name] = copy

    def fetch_part(part):
        source = (lambda sides: view(sides[0], part)) if packed else (lambda sides: sides[part])
        fetch(("own", part), source(own), view(own_ref, part))
        fetch(("theirs", part), source(theirs), view(theirs_ref, part))

    def ready(part):
        pending["own", part].wait()
        pending["theirs", part].wait()

    fetch("x", images_ref.at[step, 0], x_ref)
    fetch_part(0)

    def fetch_rest():
        fetch_part(1)
        fetch_part(2)
        fetch("upstream", cotangent_ref.at[step, 0], upstream_ref)
        if packed:
            for part in range(3):
                fetch(("held", part), held_out[part], view(held_ref, part))

    stores = []

    def store(source, target):
        copy = pltpu.make_async_copy(source, target, left.at[len(stores)])
        copy.start()
        stores.append(copy)

    def settle(part):
        store(view(moment_ref, part), moment_out[part])
        if not last:
            store(view(param_ref, part), view(outs[0], part))

    if packed:
        rows_of = lambda ref, low: jnp.concatenate([ref[low + at : low + at + 1, :] for at in range(ref.shape[0] // 2)], axis=1)
        half = own[1].shape[0] // 2
        gains = mean_of(rows_of(own[1], 0), rows_of(theirs[1], 0))
        shifts = mean_of(rows_of(own[1], half), rows_of(theirs[1], half))
    else:
        gains = mean_of(own[3][...], theirs[3][...])
        shifts = mean_of(own[4][...], theirs[4][...])
    gain_a, gain_b, gain_c = gains[:, :LANES], gains[:, LANES : 2 * LANES], gains[:, 2 * LANES :]
    shift_a, shift_b, shift_c = shifts[:, :LANES], shifts[:, LANES : 2 * LANES], shifts[:, 2 * LANES :]

    def mixed(part, start, rows):
        span = pl.ds(spans[part][0] + start, rows)
        return mean_of(own_ref[span, :], theirs_ref[span, :])

    def learn(part, start, rows, moment):
        span = pl.ds(spans[part][0] + start, rows)
        if packed:
            moment = MOMENTUM * held_ref[span, :] + moment
        moment_ref[span, :] = moment
        param_ref[span, :] = mixed(part, start, rows) - LEARN_RATE * moment

    pad[...] = jnp.zeros_like(pad)
    pad_b[...] = jnp.zeros_like(pad_b)
    pending["x"].wait()
    ready(0)
    fetch_rest()
    reduce_w = mixed(0, 0, rows_r).astype(bf16)

    def make_first(at, total):
        values = matmul(x_ref[flat_rows(at), :], reduce_w)
        normed_a[flat_rows(at), :] = values
        return total + column_sum(values)

    mean, scale_a = statistics(normed_a, sweep(make_first, zero_row(LANES)))

    def make_hidden_a(at, carry):
        normed = (normed_a[flat_rows(at), :] - mean) * scale_a
        normed_a[flat_rows(at), :] = normed
        pad_chunk(pad, TOP, at, activate(normed * gain_a + shift_a))
        return carry

    sweep(make_hidden_a)
    shift_columns(pad, wide)

    taps = KSIZE * KSIZE
    ready(1)
    for tap in range(taps):
        weights = mixed(1, tap * LANES, LANES).astype(bf16)
        weight_s[tap * LANES : (tap + 1) * LANES, :] = weights
        other = taps - 1 - tap
        weight_f[:, other * LANES : (other + 1) * LANES] = weights

    def make_second(at, total):
        values = conv_chunk(wide, TOP, at, lambda row: weight_s[row * SPAN : (row + 1) * SPAN, :], matmul)
        normed_b[flat_rows(at), :] = values
        return total + column_sum(values)

    mean, scale_b = statistics(normed_b, sweep(make_second, zero_row(LANES)))

    def make_hidden_b(at, carry):
        normed = (normed_b[flat_rows(at), :] - mean) * scale_b
        normed_b[flat_rows(at), :] = normed
        hidden_b[flat_rows(at), :] = activate(normed * gain_b + shift_b).astype(bf16)
        return carry

    sweep(make_hidden_b)

    ready(2)
    mixed_e[...] = mixed(2, 0, rows_e)
    for block in range(blocks):
        weight_e[:, block * LANES : (block + 1) * LANES] = mixed_e[pl.ds(block, LANES, stride=blocks), :].astype(bf16)

    def make_third(at, total):
        values = matmul(hidden_b[flat_rows(at), :], weight_e[...])
        third[flat_rows(at), :] = values
        return total + column_sum(values)

    mean = sweep(make_third, zero_row(width)) / count

    def square(rows, held):
        values = third[rows, :] - mean
        third[rows, :] = values
        return held + fold_rows(values * values)

    def turn(at):
        start = pl.multiple_of(at * LANES, LANES)
        wide_t[:, pl.ds(start, LANES)] = wide[pl.ds(start, LANES), :].T

    beside = turn if step == 0 else None
    scale_c = lax.rsqrt(column_sum(sweep_wide(count, square, zero_rows(width))) / count + EPSILON)
    pending["upstream"].wait()
    stretch = scale_c * gain_c

    def make_sum(rows, totals):
        values = third[rows, :]
        half_sum = 0.5 * (values * stretch + (shift_c + x_ref[rows, :].astype(jnp.float32)))
        bend = jnp.tanh(half_sum)
        slope = (1.0 + bend) * (1.0 + half_sum * (1.0 - bend))
        grad = upstream_ref[rows, :].astype(jnp.float32) * slope
        grad_sum[rows, :] = grad
        return totals[0] + fold_rows(grad * values), totals[1] + fold_rows(grad)

    dgain_c, dshift_c = sweep_wide(count, make_sum, (zero_rows(width), zero_rows(width)), beside)
    dgain_c, dshift_c = 0.5 * column_sum(dgain_c) * scale_c, 0.5 * column_sum(dshift_c)
    level, slope, factor = 2.0 * dshift_c / count, 2.0 * scale_c * dgain_c / count, 0.5 * stretch

    def make_third_grad(rows, carry):
        grad_third[rows, :] = ((grad_sum[rows, :] - level - third[rows, :] * slope) * factor).astype(bf16)
        return carry

    sweep_wide(count, make_third_grad)

    def make_back_c(at, totals):
        normed = normed_b[flat_rows(at), :]
        grad_out = contract_cols(grad_third[flat_rows(at), :], weight_e[...]) * act_slope(normed * gain_b + shift_b)
        work[flat_rows(at), :] = grad_out
        return totals[0] + column_sum(grad_out * normed), totals[1] + column_sum(grad_out)

    dgain_b, dshift_b = sweep(make_back_c, (zero_row(LANES), zero_row(LANES)))
    grad = matmul(hidden_b[...].T, grad_third[...])
    for block in range(blocks):
        mixed_e[pl.ds(block, LANES, stride=blocks), :] = grad[:, block * LANES : (block + 1) * LANES]
    for part in range(3 if packed else 0):
        pending["held", part].wait()
    learn(2, 0, rows_e, mixed_e[...])
    settle(2)

    level_b, slope_b, factor_b = dshift_b / count, dgain_b / count, scale_b * gain_b

    def make_back_b(at, carry):
        grad = (work[flat_rows(at), :] - level_b - normed_b[flat_rows(at), :] * slope_b) * factor_b
        pad_chunk(pad_b, TOP_BACK, at, grad)
        return carry

    sweep(make_back_b)
    shift_columns(pad_b, wide_b)

    for at in range(CHUNKS if step == 0 else 0, ROWS // LANES):
        wide_t[:, at * LANES : (at + 1) * LANES] = wide[at * LANES : (at + 1) * LANES, :].T

    shifted = [
        wide_b[TOP_BACK - row_off * PITCH : TOP_BACK - row_off * PITCH + ROWS, LANES : 2 * LANES]
        for row_off in range(KSIZE)
    ]
    grad = matmul(wide_t[...], jnp.concatenate(shifted, axis=1))
    for row_off in range(KSIZE):
        learn(1, row_off * SPAN, SPAN, grad[:, row_off * LANES : (row_off + 1) * LANES])
    settle(1)

    def make_back_a(at, totals):
        grad = conv_chunk(wide_b, TOP_BACK, at, lambda row: weight_f[:, row * SPAN : (row + 1) * SPAN], contract_cols)
        normed = normed_a[flat_rows(at), :]
        grad_out = grad * act_slope(normed * gain_a + shift_a)
        work[flat_rows(at), :] = grad_out
        return totals[0] + column_sum(grad_out * normed), totals[1] + column_sum(grad_out)

    dgain_a, dshift_a = sweep(make_back_a, (zero_row(LANES), zero_row(LANES)))
    level_a, slope_a, factor_a = dshift_a / count, dgain_a / count, scale_a * gain_a

    def make_first_grad(at, carry):
        grad = (work[flat_rows(at), :] - level_a - normed_a[flat_rows(at), :] * slope_a) * factor_a
        back[flat_rows(at), :] = grad.astype(bf16)
        return carry

    sweep(make_first_grad)
    grad = matmul(back[...].T, x_ref[...])
    for block in range(blocks):
        learn(0, block * LANES, LANES, grad[:, block * LANES : (block + 1) * LANES].T)
    settle(0)
    grad = jnp.concatenate([dgain_a, dgain_b, dgain_c, dshift_a, dshift_b, dshift_c], axis=1)
    norm = jnp.concatenate([gains, shifts], axis=1)
    if packed:
        grad = MOMENTUM * held_out[3][...] + grad
    norm_moment[...] = grad
    norm = norm - LEARN_RATE * grad
    if not last:
        for at in range(norm.shape[1] // LANES):
            outs[1][at : at + 1, :] = norm[:, at * LANES : (at + 1) * LANES]
        for copy in stores:
            copy.wait()
        return

    kept_ref, sent_ref = outs
    is_odd = jnp.full((1, 1), core_ref[0], jnp.int32) == 1
    pairs, piece_s, piece_e, piece_r, piece_n = split
    at_e = round_up(piece_s + 1, 8)
    at_r = at_e + piece_e

    def place(pair, start, low, high):
        rows = low.shape[0]
        kept_ref[pair, start : start + rows, :] = jnp.where(is_odd, high, low)
        sent_ref[pair, start : start + rows, :] = jnp.where(is_odd, low, high)

    for pair in range(pairs):
        for part, rows, start in ((1, piece_s, 0), (2, piece_e, at_e), (0, piece_r, at_r)):
            first = spans[part][0] + 2 * pair * rows
            place(pair, start, param_ref[first : first + rows, :], param_ref[first + rows : first + 2 * rows, :])
        low, high = [
            jnp.concatenate(
                [norm[:, at * piece_n : (at + 1) * piece_n], jnp.zeros((1, LANES - piece_n), jnp.float32)], axis=1
            )
            for at in (2 * pair, 2 * pair + 1)
        ]
        rest = jnp.zeros((at_e - piece_s - 1, LANES), jnp.float32)
        place(pair, piece_s, jnp.concatenate([low, rest]), jnp.concatenate([high, rest]))
    for copy in stores:
        copy.wait()


def fold_kernel(bits, *refs):
    spot_ref, kept_ref = refs[:2]
    came, outs, total = refs[2 : 2 + bits[0]], refs[2 + bits[0] : -1], refs[-1]
    values = kept_ref[...]
    for ref in came:
        values = values + ref[...]
    total[...] = values
    ways = len(outs)
    for hop, out in enumerate(outs):
        for at in range(out.shape[0]):
            out[at] = total[at * ways + jnp.bitwise_xor(spot_ref[0], hop)]


def mean_kernel(replicas, spans, *refs):
    outs = refs[-len(spans) :]
    kept_ref, came = refs[0], refs[1 : -len(spans)]
    values = kept_ref[0]
    for ref in came:
        values = values + ref[0]
    values = values * (1.0 / replicas)
    for (start, rows), out in zip(spans, outs):
        width = out.shape[0] // rows
        for at in range(rows):
            out[at * width : (at + 1) * width] = values[start + at, :width]


def pack_kernel(*refs):
    half = len(refs) // 2
    for source, out in zip(refs[:half], refs[half:]):
        if source.shape[0] == 1:
            out[...] = source[...].astype(jnp.bfloat16)
            continue

        def lay(at, carry, source=source, out=out):
            values = source[pl.ds(pl.multiple_of(at * 8, 8), 8), :].astype(jnp.bfloat16)
            base = pl.multiple_of(at * 8 * LANES, 8 * LANES)
            for row in range(8):
                out[0:1, pl.ds(base + row * LANES, LANES)] = values[row : row + 1]
            return carry

        lax.fori_loop(0, source.shape[0] // 8, lay, 0)


def run_kernel(body, name, operands, outs, scratch=(), flops=0, vmem=SMALL_VMEM):
    def parts(entries, is_plain):
        plain = [entry if is_plain(entry) else entry[0] for entry in entries]
        return plain, [pl.BlockSpec(memory_space=pltpu.VMEM if is_plain(entry) else entry[1]) for entry in entries]

    arrays, in_specs = parts(operands, lambda entry: not isinstance(entry, tuple))
    shapes, out_specs = parts(outs, lambda entry: isinstance(entry[0], tuple) and not isinstance(entry[0][0], tuple))
    moved = sum(array.size * array.dtype.itemsize for array in arrays)
    return list(pl.pallas_call(
        body,
        in_specs=in_specs,
        out_specs=out_specs,
        out_shape=[jax.ShapeDtypeStruct(shape, kind) for shape, kind in shapes],
        scratch_shapes=[pltpu.VMEM(*entry) if isinstance(entry, tuple) else entry for entry in scratch],
        compiler_params=pltpu.CompilerParams(vmem_limit_bytes=vmem),
        cost_estimate=pl.CostEstimate(flops=flops, bytes_accessed=moved, transcendentals=0),
        name=name,
    )(*arrays))


def in_hbm(entry):
    return entry, pltpu.HBM


def in_smem(value):
    return value.astype(jnp.int32).reshape(1), pltpu.SMEM


def swap_all(bit, values):
    return [partner_2(member, "dp", bit) for member in values]


def exchange(spot, first_bit, ways, sends):
    replicas = lax.axis_size("dp")
    return [
        lax.ppermute(sent, "dp", [(at, at ^ (hop << first_bit)) for at in range(replicas)])
        for hop, sent in zip(range(1, ways), sends)
    ]


def scatter_mean(kept, sent, split, beside):
    f32 = jnp.float32
    replicas = lax.axis_size("dp")
    levels = replicas.bit_length() - 1
    place = lax.axis_index("dp")
    pairs, piece_s, piece_e, piece_r, piece_n = split
    rows = kept.shape[1]
    came = exchange(place, 0, 2, [sent])
    left, low = pairs, 1
    while left > 1:
        width = 2 if low == 1 and levels > 2 else 1
        ways = 1 << width
        spot = in_smem((place >> low) % ways)
        kept, *sends = run_kernel(
            functools.partial(fold_kernel, (len(came),)), "fold", [spot, kept] + came,
            [((left // ways, rows, LANES), f32)] * ways, [((left, rows, LANES), f32)],
        )
        came = exchange(place, low, ways, sends)
        if beside is not None:
            done = beside()
            beside = None
            came, done = lax.optimization_barrier((came, done))
        left, low = left // ways, low + width
    at_e = round_up(piece_s + 1, 8)
    spans = ((at_e + piece_e, piece_r), (0, piece_s), (at_e, piece_e), (piece_s, 1))
    sizes = [(rows_of * LANES,) for _, rows_of in spans[:3]] + [(piece_n,)]
    mean = run_kernel(
        functools.partial(mean_kernel, replicas, spans), "mean", [kept] + came, [(size, f32) for size in sizes]
    )
    if beside is not None:
        done = beside()
    return done, mean


def scatter_mean_any(arrays):
    replicas = lax.axis_size("dp")
    tables = [member.reshape(replicas, -1) for member in arrays]
    pieces = lax.all_to_all(jnp.concatenate(tables, axis=1), "dp", 0, 0, tiled=True)
    mean = jnp.sum(pieces, axis=0) / replicas
    bounds = [sum(table.shape[1] for table in tables[:at]) for at in range(len(tables) + 1)]
    return tuple(mean[low:high] for low, high in zip(bounds[:-1], bounds[1:]))


def shards(images, cotangent, w_reduce, w_spatial, w_expand, norm_gain, norm_bias, round_index):
    f32, bf16 = jnp.float32, jnp.bfloat16
    replicas = lax.axis_size("dp")
    levels = replicas.bit_length() - 1
    steps, _, pixels, in_ch = images.shape
    weights = [member.reshape(-1, LANES) for member in (w_reduce, w_spatial, w_expand)]
    sizes = [(member.shape, f32) for member in weights]
    rows_r, rows_s, rows_e = (member.shape[0] for member in weights)
    rows = rows_r + rows_s + rows_e
    norm_size = 2 * norm_gain.size
    flat_map = ((pixels, LANES), f32)
    wide_map = ((pixels, in_ch), f32)
    whole = ((rows, LANES), f32)
    norm_rows = ((norm_size // LANES, LANES), f32)
    half_map = ((pixels, in_ch), bf16)
    scratch = [
        half_map, half_map, whole, whole, whole, whole,
        flat_map, flat_map, ((pixels, LANES), bf16), ((ROWS, SPAN), bf16), ((SPAN, ROWS), bf16),
        ((ROWS_BACK, SPAN), bf16), ((ROWS + 16, LANES), f32), ((ROWS_BACK + 16, LANES), f32),
        sizes[2], ((LANES, in_ch), bf16), ((rows_s, LANES), bf16), ((LANES, rows_s), bf16),
        wide_map, wide_map, half_map, flat_map, ((pixels, LANES), bf16),
        pltpu.SemaphoreType.DMA((11,)), pltpu.SemaphoreType.DMA((6,)),
    ]
    flops = 6 * pixels * LANES * (2 * in_ch + rows_s)
    fine = replicas > 1 and all(size[0][0] % replicas == 0 for size in sizes)
    split = (replicas // 2, rows_s // replicas, rows_e // replicas, rows_r // replicas, norm_size // replicas)
    half = ((split[0], round_up(split[1] + 1, 8) + split[2] + split[3], LANES), f32)
    params = [weights[1], weights[0], weights[2], norm_gain, norm_bias]
    moments = []
    for step in range(steps):
        branches = [functools.partial(swap_all, bit) for bit in range(levels)]
        theirs = list(lax.switch((round_index[0] + step) % levels, branches, params))
        if step == 0:
            sides = [[in_hbm(side[at]) for at in (1, 0, 2)] + side[3:] for side in (params, theirs)]
        else:
            sides = [[in_hbm(side[0]), side[1]] for side in (params, theirs)]
        operands = [in_hbm(images), in_hbm(cotangent)] + sides[0] + sides[1]
        operands += [in_hbm(member) for member in moments[:3]] + moments[3:]
        moment_outs = [in_hbm(size) for size in sizes] + [((1, norm_size), f32)]
        extra = [whole] if step else []
        if step == steps - 1 and fine:
            core = in_smem(lax.axis_index("dp") % 2)
            kept, sent, *moments = run_kernel(
                functools.partial(step_kernel, step, True, split), "last_step", [core] + operands,
                [half, half] + moment_outs, scratch + extra, flops, VMEM_BYTES,
            )
        else:
            *params, m_r, m_s, m_e, m_n = run_kernel(
                functools.partial(step_kernel, step, False, None), "step", operands,
                [in_hbm(whole), norm_rows] + moment_outs, scratch + extra, flops, VMEM_BYTES,
            )
            moments = [m_r, m_s, m_e, m_n]
    pack = lambda: run_kernel(pack_kernel, "pack", moments, [((1, member.size), bf16) for member in moments])
    if fine:
        out, averaged = scatter_mean(kept, sent, split, pack)
    else:
        flat = [params[0][low:high].reshape(-1) for low, high in ((0, rows_r), (rows_r, rows_r + rows_s), (rows_r + rows_s, rows))]
        out, averaged = pack(), scatter_mean_any(flat + [params[1].reshape(-1)])
    return tuple(averaged) + tuple(out)


def solution(mesh):
    in_specs = (
        P(None, "dp", None, None),
        P(None, "dp", None, None),
        P("dp", None),
        P("dp", None),
        P("dp", None),
        P("dp", None),
        P("dp", None),
        P(),
    )
    out_specs = (
        P("dp"),
        P("dp"),
        P("dp"),
        P("dp"),
        P("dp", None),
        P("dp", None),
        P("dp", None),
        P("dp", None),
    )
    return jax.shard_map(shards, mesh=mesh, in_specs=in_specs, out_specs=out_specs, check_vma=False)
```

```python
import functools

import jax
import jax.numpy as jnp
from jax import lax
from jax.experimental import pallas as pl
from jax.experimental.pallas import tpu as pltpu
from jax.sharding import PartitionSpec as P

HEIGHT = 28
WIDTH = 28
KSIZE = 3

LEARN_RATE = 0.01
MOMENTUM = 0.9
EPSILON = 1e-05

LANES = 128
PITCH = 32
VMEM_BYTES = 60 * 1024 * 1024
SMALL_VMEM = 8 * 1024 * 1024
PHASE_VMEM = 20 * 1024 * 1024


def round_up(value, unit):
    return (value + unit - 1) // unit * unit


def partner_2(value, axis, distance):
    mask = 2**distance
    pairs = [(source, source ^ mask) for source in range(lax.axis_size(axis))]
    return lax.ppermute(value, axis, pairs)


def matmul(left, right):
    return jnp.dot(left, right, preferred_element_type=jnp.float32)


def contract_cols(left, right):
    return lax.dot_general(left, right, (((1,), (1,)), ((), ())), preferred_element_type=jnp.float32)


def sigmoid(values):
    return 0.5 * jnp.tanh(0.5 * values) + 0.5


def activate(values):
    return values * sigmoid(values)


def act_slope(values):
    sigma = sigmoid(values)
    return sigma * (1.0 + values * (1.0 - sigma))


def column_sum(values):
    return jnp.sum(values, axis=0, keepdims=True)


MAPS = 4
FLAT = MAPS * WIDTH
PITCHED = MAPS * PITCH
CHUNKS = HEIGHT // MAPS
SPAN = KSIZE * LANES
TOP = PITCH
TOP_BACK = 2 * PITCH
ROWS = round_up(HEIGHT * PITCH + 2 * PITCH, LANES)
ROWS_BACK = ROWS + 2 * PITCH


def flat_rows(at):
    return pl.ds(pl.multiple_of(at * FLAT, FLAT), FLAT)


def zero_row(width):
    return jnp.zeros((1, width), jnp.float32)


def sweep(body, init=0, unroll=True):
    return lax.fori_loop(0, CHUNKS, body, init, unroll=unroll)


def statistics(values_ref, total):
    count, width = values_ref.shape
    mean = total / count

    def add(at, held):
        center = values_ref[flat_rows(at), :] - mean
        return held + column_sum(center * center)

    return mean, lax.rsqrt(sweep(add, zero_row(width), width == LANES) / count + EPSILON)


def pad_chunk(pad_ref, top, at, values):
    for row in range(MAPS):
        start = pl.multiple_of(at * PITCHED, PITCHED) + (8 + top + row * PITCH)
        pad_ref[pl.ds(start, WIDTH), :] = values[row * WIDTH : (row + 1) * WIDTH]


def shift_columns(pad_ref, out_ref):
    rows = out_ref.shape[0]
    for col_off in range(KSIZE):
        start = 8 + col_off - KSIZE // 2
        out_ref[:, col_off * LANES : (col_off + 1) * LANES] = pad_ref[start : start + rows, :].astype(jnp.bfloat16)


def conv_chunk(wide_ref, top, at, weight_of, multiply):
    total = None
    for row_off in range(KSIZE):
        start = pl.multiple_of(at * PITCHED, PITCHED) + (top + (row_off - KSIZE // 2) * PITCH)
        piece = multiply(wide_ref[pl.ds(start, PITCHED), :], weight_of(row_off))
        total = piece if total is None else total + piece
    return jnp.concatenate([total[row * PITCH : row * PITCH + WIDTH] for row in range(MAPS)], axis=0)


def mean_of(own, theirs):
    return (own + theirs) * 0.5


def rows_at(ref, start, rows):
    return ref.at[pl.ds(start, rows), :]


def step_kernel(step, last, split, *refs):
    it = iter(refs)
    take = lambda count: [next(it) for _ in range(count)]
    core_ref = next(it) if last else None
    images_ref, cotangent_ref = take(2)
    packed = step > 0
    own, theirs = (take(2) if packed else take(5)) , (take(2) if packed else take(5))
    held_out = take(4) if packed else []
    outs = take(2) if last else take(2)
    moment_out = take(3)
    norm_moment = next(it)
    (x_ref, upstream_ref, own_ref, theirs_ref, param_ref, moment_ref,
     normed_a, normed_b, hidden_b, wide, wide_t, wide_b, pad, pad_b, mixed_e, weight_e, weight_s, weight_f,
     third, grad_sum, grad_third, work, back, weight_t, arrived, left) = take(26)
    held_ref = next(it) if packed else None
    count, width = third.shape
    blocks = width // LANES
    rows_r, rows_s, rows_e = (ref.shape[0] for ref in moment_out)
    spans = ((0, rows_r), (rows_r, rows_s), (rows_r + rows_s, rows_e))
    bf16 = jnp.bfloat16
    view = lambda ref, part: rows_at(ref, *spans[part])
    pending = {}

    def fetch(name, source, target):
        copy = pltpu.make_async_copy(source, target, arrived.at[len(pending)])
        copy.start()
        pending[name] = copy

    def fetch_part(part):
        source = (lambda sides: view(sides[0], part)) if packed else (lambda sides: sides[part])
        fetch(("own", part), source(own), view(own_ref, part))
        fetch(("theirs", part), source(theirs), view(theirs_ref, part))

    def ready(part):
        pending["own", part].wait()
        pending["theirs", part].wait()

    fetch("x", images_ref.at[step, 0], x_ref)
    for part in range(3):
        fetch_part(part)
    fetch("upstream", cotangent_ref.at[step, 0], upstream_ref)
    if packed:
        for part in range(3):
            fetch(("held", part), held_out[part], view(held_ref, part))
    stores = []

    def store(source, target):
        copy = pltpu.make_async_copy(source, target, left.at[len(stores)])
        copy.start()
        stores.append(copy)

    def settle(part):
        store(view(moment_ref, part), moment_out[part])
        if not last:
            store(view(param_ref, part), view(outs[0], part))

    if packed:
        rows_of = lambda ref, low: jnp.concatenate([ref[low + at : low + at + 1, :] for at in range(ref.shape[0] // 2)], axis=1)
        half = own[1].shape[0] // 2
        gains = mean_of(rows_of(own[1], 0), rows_of(theirs[1], 0))
        shifts = mean_of(rows_of(own[1], half), rows_of(theirs[1], half))
    else:
        gains = mean_of(own[3][...], theirs[3][...])
        shifts = mean_of(own[4][...], theirs[4][...])
    gain_a, gain_b, gain_c = gains[:, :LANES], gains[:, LANES : 2 * LANES], gains[:, 2 * LANES :]
    shift_a, shift_b, shift_c = shifts[:, :LANES], shifts[:, LANES : 2 * LANES], shifts[:, 2 * LANES :]

    def mixed(part, start, rows):
        span = pl.ds(spans[part][0] + start, rows)
        return mean_of(own_ref[span, :], theirs_ref[span, :])

    def learn(part, start, rows, moment):
        span = pl.ds(spans[part][0] + start, rows)
        if packed:
            moment = MOMENTUM * held_ref[span, :] + moment
        moment_ref[span, :] = moment
        param_ref[span, :] = mixed(part, start, rows) - LEARN_RATE * moment

    pad[...] = jnp.zeros_like(pad)
    pad_b[...] = jnp.zeros_like(pad_b)
    pending["x"].wait()
    ready(0)
    reduce_w = mixed(0, 0, rows_r).astype(bf16)

    def make_first(at, total):
        values = matmul(x_ref[flat_rows(at), :], reduce_w)
        normed_a[flat_rows(at), :] = values
        return total + column_sum(values)

    mean, scale_a = statistics(normed_a, sweep(make_first, zero_row(LANES)))

    def make_hidden_a(at, carry):
        normed = (normed_a[flat_rows(at), :] - mean) * scale_a
        normed_a[flat_rows(at), :] = normed
        pad_chunk(pad, TOP, at, activate(normed * gain_a + shift_a))
        return carry

    sweep(make_hidden_a)
    shift_columns(pad, wide)

    taps = KSIZE * KSIZE
    ready(1)
    for tap in range(taps):
        weights = mixed(1, tap * LANES, LANES).astype(bf16)
        weight_s[tap * LANES : (tap + 1) * LANES, :] = weights
        other = taps - 1 - tap
        weight_f[other * LANES : (other + 1) * LANES, :] = weights.T

    def make_second(at, total):
        values = conv_chunk(wide, TOP, at, lambda row: weight_s[row * SPAN : (row + 1) * SPAN, :], matmul)
        normed_b[flat_rows(at), :] = values
        return total + column_sum(values)

    mean, scale_b = statistics(normed_b, sweep(make_second, zero_row(LANES)))

    def make_hidden_b(at, carry):
        normed = (normed_b[flat_rows(at), :] - mean) * scale_b
        normed_b[flat_rows(at), :] = normed
        hidden_b[flat_rows(at), :] = activate(normed * gain_b + shift_b).astype(bf16)
        return carry

    sweep(make_hidden_b)

    ready(2)
    mixed_e[...] = mixed(2, 0, rows_e)
    for block in range(blocks):
        weights = mixed_e[pl.ds(block, LANES, stride=blocks), :].astype(bf16)
        weight_e[:, block * LANES : (block + 1) * LANES] = weights
        weight_t[block * LANES : (block + 1) * LANES, :] = weights.T

    def make_third(at, total):
        values = matmul(hidden_b[flat_rows(at), :], weight_e[...])
        third[flat_rows(at), :] = values
        return total + column_sum(values)

    mean, scale_c = statistics(third, sweep(make_third, zero_row(width)))

    def make_sum(at, totals):
        normed = (third[flat_rows(at), :] - mean) * scale_c
        summed = normed * gain_c + shift_c + x_ref[flat_rows(at), :].astype(jnp.float32)
        grad = upstream_ref[flat_rows(at), :].astype(jnp.float32) * act_slope(summed)
        grad_sum[flat_rows(at), :] = grad
        third[flat_rows(at), :] = normed
        return totals[0] + column_sum(grad * normed), totals[1] + column_sum(grad)

    pending["upstream"].wait()
    dgain_c, dshift_c = sweep(make_sum, (zero_row(width), zero_row(width)), False)
    level, slope, factor = dshift_c / count, dgain_c / count, scale_c * gain_c

    def make_back_c(at, totals):
        grad = (grad_sum[flat_rows(at), :] - level - third[flat_rows(at), :] * slope) * factor
        grad = grad.astype(bf16)
        grad_third[flat_rows(at), :] = grad
        normed = normed_b[flat_rows(at), :]
        grad_out = matmul(grad, weight_t[...]) * act_slope(normed * gain_b + shift_b)
        work[flat_rows(at), :] = grad_out
        return totals[0] + column_sum(grad_out * normed), totals[1] + column_sum(grad_out)

    dgain_b, dshift_b = sweep(make_back_c, (zero_row(LANES), zero_row(LANES)))
    grad = matmul(hidden_b[...].T, grad_third[...])
    for block in range(blocks):
        mixed_e[pl.ds(block, LANES, stride=blocks), :] = grad[:, block * LANES : (block + 1) * LANES]
    for part in range(3 if packed else 0):
        pending["held", part].wait()
    learn(2, 0, rows_e, mixed_e[...])
    settle(2)

    level_b, slope_b, factor_b = dshift_b / count, dgain_b / count, scale_b * gain_b

    def make_back_b(at, carry):
        grad = (work[flat_rows(at), :] - level_b - normed_b[flat_rows(at), :] * slope_b) * factor_b
        pad_chunk(pad_b, TOP_BACK, at, grad)
        return carry

    sweep(make_back_b)
    shift_columns(pad_b, wide_b)

    for at in range(ROWS // LANES):
        wide_t[:, at * LANES : (at + 1) * LANES] = wide[at * LANES : (at + 1) * LANES, :].T

    shifted = [
        wide_b[TOP_BACK - row_off * PITCH : TOP_BACK - row_off * PITCH + ROWS, LANES : 2 * LANES]
        for row_off in range(KSIZE)
    ]
    grad = matmul(wide_t[...], jnp.concatenate(shifted, axis=1))
    for row_off in range(KSIZE):
        learn(1, row_off * SPAN, SPAN, grad[:, row_off * LANES : (row_off + 1) * LANES])
    settle(1)

    def make_back_a(at, totals):
        grad = conv_chunk(wide_b, TOP_BACK, at, lambda row: weight_f[row * SPAN : (row + 1) * SPAN, :], matmul)
        normed = normed_a[flat_rows(at), :]
        grad_out = grad * act_slope(normed * gain_a + shift_a)
        work[flat_rows(at), :] = grad_out
        return totals[0] + column_sum(grad_out * normed), totals[1] + column_sum(grad_out)

    dgain_a, dshift_a = sweep(make_back_a, (zero_row(LANES), zero_row(LANES)))
    level_a, slope_a, factor_a = dshift_a / count, dgain_a / count, scale_a * gain_a

    def make_first_grad(at, carry):
        grad = (work[flat_rows(at), :] - level_a - normed_a[flat_rows(at), :] * slope_a) * factor_a
        back[flat_rows(at), :] = grad.astype(bf16)
        return carry

    sweep(make_first_grad)
    grad = matmul(back[...].T, x_ref[...])
    for block in range(blocks):
        learn(0, block * LANES, LANES, grad[:, block * LANES : (block + 1) * LANES].T)
    settle(0)
    grad = jnp.concatenate([dgain_a, dgain_b, dgain_c, dshift_a, dshift_b, dshift_c], axis=1)
    norm = jnp.concatenate([gains, shifts], axis=1)
    if packed:
        grad = MOMENTUM * held_out[3][...] + grad
    norm_moment[...] = grad
    norm = norm - LEARN_RATE * grad
    if not last:
        for at in range(norm.shape[1] // LANES):
            outs[1][at : at + 1, :] = norm[:, at * LANES : (at + 1) * LANES]
        for copy in stores:
            copy.wait()
        return

    kept_ref, sent_ref = outs
    is_odd = jnp.full((1, 1), core_ref[0], jnp.int32) == 1
    pairs, piece_s, piece_e, piece_r, piece_n = split
    at_e = round_up(piece_s + 1, 8)
    at_r = at_e + piece_e

    def place(pair, start, low, high):
        rows = low.shape[0]
        kept_ref[pair, start : start + rows, :] = jnp.where(is_odd, high, low)
        sent_ref[pair, start : start + rows, :] = jnp.where(is_odd, low, high)

    for pair in range(pairs):
        for part, rows, start in ((1, piece_s, 0), (2, piece_e, at_e), (0, piece_r, at_r)):
            first = spans[part][0] + 2 * pair * rows
            place(pair, start, param_ref[first : first + rows, :], param_ref[first + rows : first + 2 * rows, :])
        low, high = [
            jnp.concatenate(
                [norm[:, at * piece_n : (at + 1) * piece_n], jnp.zeros((1, LANES - piece_n), jnp.float32)], axis=1
            )
            for at in (2 * pair, 2 * pair + 1)
        ]
        rest = jnp.zeros((at_e - piece_s - 1, LANES), jnp.float32)
        place(pair, piece_s, jnp.concatenate([low, rest]), jnp.concatenate([high, rest]))
    for copy in stores:
        copy.wait()


def put_sums(ref, sums):
    for at, values in enumerate(sums):
        ref[at : at + 1, :] = values


def lead_kernel(images_ref, own_ref, theirs_ref, gain_own, gain_theirs, shift_own, shift_theirs,
                normed_ref, scale_ref, wide, pad):
    gain, shift = mean_of(gain_own[:, :LANES], gain_theirs[:, :LANES]), mean_of(shift_own[:, :LANES], shift_theirs[:, :LANES])
    pad[...] = jnp.zeros_like(pad)
    weights = mean_of(own_ref[...], theirs_ref[...]).astype(jnp.bfloat16)

    def make_first(at, total):
        values = matmul(images_ref[0, 0, flat_rows(at), :], weights)
        normed_ref[flat_rows(at), :] = values
        return total + column_sum(values)

    mean, scale = statistics(normed_ref, sweep(make_first, zero_row(LANES)))
    scale_ref[...] = scale

    def make_hidden(at, carry):
        normed = (normed_ref[flat_rows(at), :] - mean) * scale
        normed_ref[flat_rows(at), :] = normed
        pad_chunk(pad, TOP, at, activate(normed * gain + shift))
        return carry

    sweep(make_hidden)
    shift_columns(pad, wide)


def middle_kernel(own_ref, theirs_ref, wide, gain_own, gain_theirs, shift_own, shift_theirs,
                  normed_ref, scale_ref, hidden, weight_f, weight_s):
    span = slice(LANES, 2 * LANES)
    gain, shift = mean_of(gain_own[:, span], gain_theirs[:, span]), mean_of(shift_own[:, span], shift_theirs[:, span])
    taps = KSIZE * KSIZE
    for tap in range(taps):
        rows = slice(tap * LANES, (tap + 1) * LANES)
        weights = mean_of(own_ref[rows, :], theirs_ref[rows, :]).astype(jnp.bfloat16)
        weight_s[rows, :] = weights
        weight_f[(taps - 1 - tap) * LANES : (taps - tap) * LANES, :] = weights.T

    def make_second(at, total):
        values = conv_chunk(wide, TOP, at, lambda row: weight_s[row * SPAN : (row + 1) * SPAN, :], matmul)
        normed_ref[flat_rows(at), :] = values
        return total + column_sum(values)

    mean, scale = statistics(normed_ref, sweep(make_second, zero_row(LANES)))
    scale_ref[...] = scale

    def make_hidden(at, carry):
        normed = (normed_ref[flat_rows(at), :] - mean) * scale
        normed_ref[flat_rows(at), :] = normed
        hidden[flat_rows(at), :] = activate(normed * gain + shift).astype(jnp.bfloat16)
        return carry

    sweep(make_hidden)


def tail_kernel(images_ref, cotangent_ref, own_ref, theirs_ref, hidden, normed_b, gain_own, gain_theirs, shift_own,
                shift_theirs, param_ref, moment_ref, work, sums_b, sums_c, third, grad_sum, grad_third, mixed, weight_e, weight_t):
    count, width = third.shape
    blocks = width // LANES
    gains, shifts = mean_of(gain_own[...], gain_theirs[...]), mean_of(shift_own[...], shift_theirs[...])
    gain_b, gain_c = gains[:, LANES : 2 * LANES], gains[:, 2 * LANES :]
    shift_b, shift_c = shifts[:, LANES : 2 * LANES], shifts[:, 2 * LANES :]
    mixed[...] = mean_of(own_ref[...], theirs_ref[...])
    for block in range(blocks):
        weights = mixed[pl.ds(block, LANES, stride=blocks), :].astype(jnp.bfloat16)
        weight_e[:, block * LANES : (block + 1) * LANES] = weights
        weight_t[block * LANES : (block + 1) * LANES, :] = weights.T

    def make_third(at, total):
        values = matmul(hidden[flat_rows(at), :], weight_e[...])
        third[flat_rows(at), :] = values
        return total + column_sum(values)

    mean, scale = statistics(third, sweep(make_third, zero_row(width)))

    def make_sum(at, totals):
        normed = (third[flat_rows(at), :] - mean) * scale
        summed = normed * gain_c + shift_c + images_ref[0, 0, flat_rows(at), :].astype(jnp.float32)
        grad = cotangent_ref[0, 0, flat_rows(at), :].astype(jnp.float32) * act_slope(summed)
        grad_sum[flat_rows(at), :] = grad
        third[flat_rows(at), :] = normed
        return totals[0] + column_sum(grad * normed), totals[1] + column_sum(grad)

    dgain, dshift = sweep(make_sum, (zero_row(width), zero_row(width)), False)
    put_sums(sums_c, (dgain, dshift))
    level, slope, factor = dshift / count, dgain / count, scale * gain_c

    def make_back(at, totals):
        grad = (grad_sum[flat_rows(at), :] - level - third[flat_rows(at), :] * slope) * factor
        grad = grad.astype(jnp.bfloat16)
        grad_third[flat_rows(at), :] = grad
        normed = normed_b[flat_rows(at), :]
        grad_out = matmul(grad, weight_t[...]) * act_slope(normed * gain_b + shift_b)
        work[flat_rows(at), :] = grad_out
        return totals[0] + column_sum(grad_out * normed), totals[1] + column_sum(grad_out)

    put_sums(sums_b, sweep(make_back, (zero_row(LANES), zero_row(LANES))))
    grad = matmul(hidden[...].T, grad_third[...])
    for block in range(blocks):
        moment_ref[pl.ds(block, LANES, stride=blocks), :] = grad[:, block * LANES : (block + 1) * LANES]
    param_ref[...] = mixed[...] - LEARN_RATE * moment_ref[...]


def spatial_kernel(own_ref, theirs_ref, work, normed_b, scale_ref, sums_b, wide, gain_own, gain_theirs,
                   param_ref, moment_ref, wide_b, pad_b, wide_t):
    gain = mean_of(gain_own[:, LANES : 2 * LANES], gain_theirs[:, LANES : 2 * LANES])
    count = work.shape[0]
    pad_b[...] = jnp.zeros_like(pad_b)
    level, slope, factor = sums_b[1:2, :] / count, sums_b[0:1, :] / count, scale_ref[...] * gain

    def make_back(at, carry):
        grad = (work[flat_rows(at), :] - level - normed_b[flat_rows(at), :] * slope) * factor
        pad_chunk(pad_b, TOP_BACK, at, grad)
        return carry

    sweep(make_back)
    shift_columns(pad_b, wide_b)
    for at in range(ROWS // LANES):
        wide_t[:, at * LANES : (at + 1) * LANES] = wide[at * LANES : (at + 1) * LANES, :].T
    shifted = [
        wide_b[TOP_BACK - row_off * PITCH : TOP_BACK - row_off * PITCH + ROWS, LANES : 2 * LANES]
        for row_off in range(KSIZE)
    ]
    grad = matmul(wide_t[...], jnp.concatenate(shifted, axis=1))
    for row_off in range(KSIZE):
        rows = slice(row_off * SPAN, (row_off + 1) * SPAN)
        moment = grad[:, row_off * LANES : (row_off + 1) * LANES]
        moment_ref[rows, :] = moment
        param_ref[rows, :] = mean_of(own_ref[rows, :], theirs_ref[rows, :]) - LEARN_RATE * moment


def front_kernel(images_ref, own_ref, theirs_ref, wide_b, weight_f, normed_a, scale_ref, sums_b, sums_c,
                 gain_own, gain_theirs, shift_own, shift_theirs, param_ref, moment_ref, norm_ref, norm_moment, work, back):
    gains, shifts = mean_of(gain_own[...], gain_theirs[...]), mean_of(shift_own[...], shift_theirs[...])
    gain, shift = gains[:, :LANES], shifts[:, :LANES]
    count = work.shape[0]

    def make_back(at, totals):
        grad = conv_chunk(wide_b, TOP_BACK, at, lambda row: weight_f[row * SPAN : (row + 1) * SPAN, :], matmul)
        normed = normed_a[flat_rows(at), :]
        grad_out = grad * act_slope(normed * gain + shift)
        work[flat_rows(at), :] = grad_out
        return totals[0] + column_sum(grad_out * normed), totals[1] + column_sum(grad_out)

    dgain, dshift = sweep(make_back, (zero_row(LANES), zero_row(LANES)))
    level, slope, factor = dshift / count, dgain / count, scale_ref[...] * gain

    def make_first_grad(at, carry):
        grad = (work[flat_rows(at), :] - level - normed_a[flat_rows(at), :] * slope) * factor
        back[flat_rows(at), :] = grad.astype(jnp.bfloat16)
        return carry

    sweep(make_first_grad)
    grad = matmul(back[...].T, images_ref[0, 0])
    for block in range(grad.shape[1] // LANES):
        span = slice(block * LANES, (block + 1) * LANES)
        moment = grad[:, span].T
        moment_ref[span, :] = moment
        param_ref[span, :] = mean_of(own_ref[span, :], theirs_ref[span, :]) - LEARN_RATE * moment
    grad = jnp.concatenate([dgain, sums_b[0:1, :], sums_c[0:1, :], dshift, sums_b[1:2, :], sums_c[1:2, :]], axis=1)
    norm_moment[...] = grad
    norm = jnp.concatenate([gains, shifts], axis=1) - LEARN_RATE * grad
    for at in range(norm.shape[1] // LANES):
        norm_ref[at : at + 1, :] = norm[:, at * LANES : (at + 1) * LANES]


def first_step(images, cotangent, own, theirs):
    f32, bf16 = jnp.float32, jnp.bfloat16
    pixels, in_ch = images.shape[2:]
    norms = [own[3], theirs[3], own[4], theirs[4]]
    size_r, size_s, size_e = ((member.shape, f32) for member in own[:3])
    flat_map, half_map, row, pair = ((pixels, LANES), f32), ((pixels, LANES), bf16), ((1, LANES), f32), ((2, LANES), f32)
    wide_map, wide_half = ((pixels, in_ch), f32), ((pixels, in_ch), bf16)
    map_in, map_back = ((ROWS, SPAN), bf16), ((ROWS_BACK, SPAN), bf16)
    x, upstream = images[:1], cotangent[:1]
    run = functools.partial(run_kernel, vmem=PHASE_VMEM)
    normed_a, scale_a, wide = run(
        lead_kernel, "lead", [x, own[0], theirs[0]] + norms, [flat_map, row, map_in], [((ROWS + 16, LANES), f32)]
    )
    normed_b, scale_b, hidden, weight_f = run(
        middle_kernel, "middle", [own[1], theirs[1], wide] + norms,
        [flat_map, row, half_map, (size_s[0], bf16)], [(size_s[0], bf16)],
    )
    param_e, moment_e, work, sums_b, sums_c = run(
        tail_kernel, "tail", [x, upstream, own[2], theirs[2], hidden, normed_b] + norms,
        [size_e, size_e, flat_map, pair, ((2, in_ch), f32)],
        [wide_map, wide_map, wide_half, size_e, ((LANES, in_ch), bf16), ((in_ch, LANES), bf16)],
    )
    param_s, moment_s, wide_b = run(
        spatial_kernel, "spatial", [own[1], theirs[1], work, normed_b, scale_b, sums_b, wide] + norms[:2],
        [size_s, size_s, map_back], [((ROWS_BACK + 16, LANES), f32), (map_in[0][::-1], bf16)],
    )
    param_r, moment_r, norm, norm_moment = run(
        front_kernel, "front", [x, own[0], theirs[0], wide_b, weight_f, normed_a, scale_a, sums_b, sums_c] + norms,
        [size_r, size_r, ((2 * own[3].size // LANES, LANES), f32), ((1, 2 * own[3].size), f32)], [flat_map, half_map],
    )
    return [jnp.concatenate([param_r, param_s, param_e]), norm], [moment_r, moment_s, moment_e, norm_moment]


def fold_kernel(bits, *refs):
    spot_ref, kept_ref = refs[:2]
    came, outs, total = refs[2 : 2 + bits[0]], refs[2 + bits[0] : -1], refs[-1]
    values = kept_ref[...]
    for ref in came:
        values = values + ref[...]
    total[...] = values
    ways = len(outs)
    for hop, out in enumerate(outs):
        for at in range(out.shape[0]):
            out[at] = total[at * ways + jnp.bitwise_xor(spot_ref[0], hop)]


def add_kernel(*refs):
    values = refs[0][...]
    for ref in refs[1:-1]:
        values = values + ref[...]
    refs[-1][...] = values


def mean_kernel(replicas, spans, *refs):
    outs = refs[-len(spans) :]
    kept_ref = refs[0]
    values = jnp.sum(kept_ref[...], axis=0) * (1.0 / replicas)
    for (start, rows), out in zip(spans, outs):
        width = out.shape[0] // rows
        for at in range(rows):
            out[at * width : (at + 1) * width] = values[start + at, :width]


def pack_kernel(*refs):
    half = len(refs) // 2
    for source, out in zip(refs[:half], refs[half:]):
        if source.shape[0] == 1:
            out[...] = source[...].astype(jnp.bfloat16)
            continue

        def lay(at, carry, source=source, out=out):
            values = source[pl.ds(pl.multiple_of(at * 8, 8), 8), :].astype(jnp.bfloat16)
            base = pl.multiple_of(at * 8 * LANES, 8 * LANES)
            for row in range(8):
                out[0:1, pl.ds(base + row * LANES, LANES)] = values[row : row + 1]
            return carry

        lax.fori_loop(0, source.shape[0] // 8, lay, 0)


def run_kernel(body, name, operands, outs, scratch=(), flops=0, vmem=SMALL_VMEM):
    def parts(entries, is_plain):
        plain = [entry if is_plain(entry) else entry[0] for entry in entries]
        return plain, [pl.BlockSpec(memory_space=pltpu.VMEM if is_plain(entry) else entry[1]) for entry in entries]

    arrays, in_specs = parts(operands, lambda entry: not isinstance(entry, tuple))
    shapes, out_specs = parts(outs, lambda entry: isinstance(entry[0], tuple) and not isinstance(entry[0][0], tuple))
    moved = sum(array.size * array.dtype.itemsize for array in arrays)
    return list(pl.pallas_call(
        body,
        in_specs=in_specs,
        out_specs=out_specs,
        out_shape=[jax.ShapeDtypeStruct(shape, kind) for shape, kind in shapes],
        scratch_shapes=[pltpu.VMEM(*entry) if isinstance(entry, tuple) else entry for entry in scratch],
        compiler_params=pltpu.CompilerParams(vmem_limit_bytes=vmem),
        cost_estimate=pl.CostEstimate(flops=flops, bytes_accessed=moved, transcendentals=0),
        name=name,
    )(*arrays))


def in_hbm(entry):
    return entry, pltpu.HBM


def in_smem(value):
    return value.astype(jnp.int32).reshape(1), pltpu.SMEM


def swap_all(bit, values):
    return [partner_2(member, "dp", bit) for member in values]


def exchange(spot, first_bit, ways, sends):
    replicas = lax.axis_size("dp")
    return [
        lax.ppermute(sent, "dp", [(at, at ^ (hop << first_bit)) for at in range(replicas)])
        for hop, sent in zip(range(1, ways), sends)
    ]


def scatter_mean(kept, sent, split, beside):
    f32 = jnp.float32
    replicas = lax.axis_size("dp")
    levels = replicas.bit_length() - 1
    place = lax.axis_index("dp")
    pairs, piece_s, piece_e, piece_r, piece_n = split
    rows = kept.shape[1]
    came = exchange(place, 0, 2, [sent])
    left, low = pairs, 1
    ways = 4
    spot = in_smem((place >> low) % ways)
    kept, *sends = run_kernel(
        functools.partial(fold_kernel, (len(came),)), "fold", [spot, kept] + came,
        [((left // ways, rows, LANES), f32)] * ways, [((left, rows, LANES), f32)],
    )
    came = exchange(place, low, ways, sends)
    done = beside()
    came, done = lax.optimization_barrier((came, done))
    left, low = left // ways, low + 2
    (total,) = run_kernel(add_kernel, "add", [kept] + came, [((left, rows, LANES), f32)])
    stride = 1 << low
    groups = [list(range(first, replicas, stride)) for first in range(stride)]
    pieces = lax.all_to_all(total, "dp", 0, 0, axis_index_groups=groups, tiled=True)
    at_e = round_up(piece_s + 1, 8)
    spans = ((at_e + piece_e, piece_r), (0, piece_s), (at_e, piece_e), (piece_s, 1))
    sizes = [(rows_of * LANES,) for _, rows_of in spans[:3]] + [(piece_n,)]
    mean = run_kernel(
        functools.partial(mean_kernel, replicas, spans), "mean", [pieces], [(size, f32) for size in sizes]
    )
    return done, mean


def scatter_mean_any(arrays):
    replicas = lax.axis_size("dp")
    tables = [member.reshape(replicas, -1) for member in arrays]
    pieces = lax.all_to_all(jnp.concatenate(tables, axis=1), "dp", 0, 0, tiled=True)
    mean = jnp.sum(pieces, axis=0) / replicas
    bounds = [sum(table.shape[1] for table in tables[:at]) for at in range(len(tables) + 1)]
    return tuple(mean[low:high] for low, high in zip(bounds[:-1], bounds[1:]))


def shards(images, cotangent, w_reduce, w_spatial, w_expand, norm_gain, norm_bias, round_index):
    f32, bf16 = jnp.float32, jnp.bfloat16
    replicas = lax.axis_size("dp")
    levels = replicas.bit_length() - 1
    steps, _, pixels, in_ch = images.shape
    weights = [member.reshape(-1, LANES) for member in (w_reduce, w_spatial, w_expand)]
    sizes = [(member.shape, f32) for member in weights]
    rows_r, rows_s, rows_e = (member.shape[0] for member in weights)
    rows = rows_r + rows_s + rows_e
    norm_size = 2 * norm_gain.size
    flat_map = ((pixels, LANES), f32)
    wide_map = ((pixels, in_ch), f32)
    whole = ((rows, LANES), f32)
    norm_rows = ((norm_size // LANES, LANES), f32)
    half_map = ((pixels, in_ch), bf16)
    scratch = [
        half_map, half_map, whole, whole, whole, whole,
        flat_map, flat_map, ((pixels, LANES), bf16), ((ROWS, SPAN), bf16), ((SPAN, ROWS), bf16),
        ((ROWS_BACK, SPAN), bf16), ((ROWS + 16, LANES), f32), ((ROWS_BACK + 16, LANES), f32),
        sizes[2], ((LANES, in_ch), bf16), ((rows_s, LANES), bf16), ((rows_s, LANES), bf16),
        wide_map, wide_map, half_map, flat_map, ((pixels, LANES), bf16), ((in_ch, LANES), bf16),
        pltpu.SemaphoreType.DMA((11,)), pltpu.SemaphoreType.DMA((6,)),
    ]
    flops = 6 * pixels * LANES * (2 * in_ch + rows_s)
    fine = replicas >= 8 and all(size[0][0] % replicas == 0 for size in sizes)
    split = (replicas // 2, rows_s // replicas, rows_e // replicas, rows_r // replicas, norm_size // replicas)
    half = ((split[0], round_up(split[1] + 1, 8) + split[2] + split[3], LANES), f32)
    params = [weights[1], weights[0], weights[2], norm_gain, norm_bias]
    moments = []
    for step in range(steps):
        branches = [functools.partial(swap_all, bit) for bit in range(levels)]
        theirs = list(lax.switch((round_index[0] + step) % levels, branches, params))
        if step == 0 and fine and steps > 1:
            order = (1, 0, 2, 3, 4)
            params, moments = first_step(images, cotangent, [params[at] for at in order], [theirs[at] for at in order])
            continue
        if step == 0:
            sides = [[in_hbm(side[at]) for at in (1, 0, 2)] + side[3:] for side in (params, theirs)]
        else:
            sides = [[in_hbm(side[0]), side[1]] for side in (params, theirs)]
        operands = [in_hbm(images), in_hbm(cotangent)] + sides[0] + sides[1]
        operands += [in_hbm(member) for member in moments[:3]] + moments[3:]
        moment_outs = [in_hbm(size) for size in sizes] + [((1, norm_size), f32)]
        extra = [whole] if step else []
        if step == steps - 1 and fine:
            core = in_smem(lax.axis_index("dp") % 2)
            kept, sent, *moments = run_kernel(
                functools.partial(step_kernel, step, True, split), "last_step", [core] + operands,
                [half, half] + moment_outs, scratch + extra, flops, VMEM_BYTES,
            )
        else:
            *params, m_r, m_s, m_e, m_n = run_kernel(
                functools.partial(step_kernel, step, False, None), "step", operands,
                [in_hbm(whole), norm_rows] + moment_outs, scratch + extra, flops, VMEM_BYTES,
            )
            moments = [m_r, m_s, m_e, m_n]
    pack = lambda: run_kernel(pack_kernel, "pack", moments, [((1, member.size), bf16) for member in moments])
    if fine:
        out, averaged = scatter_mean(kept, sent, split, pack)
    else:
        flat = [params[0][low:high].reshape(-1) for low, high in ((0, rows_r), (rows_r, rows_r + rows_s), (rows_r + rows_s, rows))]
        out, averaged = pack(), scatter_mean_any(flat + [params[1].reshape(-1)])
    return tuple(averaged) + tuple(out)


def solution(mesh):
    in_specs = (
        P(None, "dp", None, None),
        P(None, "dp", None, None),
        P("dp", None),
        P("dp", None),
        P("dp", None),
        P("dp", None),
        P("dp", None),
        P(),
    )
    out_specs = (
        P("dp"),
        P("dp"),
        P("dp"),
        P("dp"),
        P("dp", None),
        P("dp", None),
        P("dp", None),
        P("dp", None),
    )
    return jax.shard_map(shards, mesh=mesh, in_specs=in_specs, out_specs=out_specs, check_vma=False)
```

```python
import functools

import jax
import jax.numpy as jnp
from jax import lax
from jax.experimental import pallas as pl
from jax.experimental.pallas import tpu as pltpu
from jax.sharding import PartitionSpec as P

HEIGHT = 28
WIDTH = 28
KSIZE = 3

LEARN_RATE = 0.01
MOMENTUM = 0.9
EPSILON = 1e-05

LANES = 128
PITCH = 32
VMEM_BYTES = 60 * 1024 * 1024
SMALL_VMEM = 8 * 1024 * 1024


def round_up(value, unit):
    return (value + unit - 1) // unit * unit


def partner_2(value, axis, distance):
    mask = 2**distance
    pairs = [(source, source ^ mask) for source in range(lax.axis_size(axis))]
    return lax.ppermute(value, axis, pairs)


def matmul(left, right):
    return jnp.dot(left, right, preferred_element_type=jnp.float32)


def contract_cols(left, right):
    return lax.dot_general(left, right, (((1,), (1,)), ((), ())), preferred_element_type=jnp.float32)


def sigmoid(values):
    return 0.5 * jnp.tanh(0.5 * values) + 0.5


def activate(values):
    return values * sigmoid(values)


def act_slope(values):
    sigma = sigmoid(values)
    return sigma * (1.0 + values * (1.0 - sigma))


def column_sum(values):
    return jnp.sum(values, axis=0, keepdims=True)


MAPS = 4
THIN = 16
FLAT = MAPS * WIDTH
PITCHED = MAPS * PITCH
CHUNKS = HEIGHT // MAPS
SPAN = KSIZE * LANES
TOP = PITCH
TOP_BACK = 2 * PITCH
ROWS = round_up(HEIGHT * PITCH + 2 * PITCH, LANES)
ROWS_BACK = ROWS + 2 * PITCH


def flat_rows(at):
    return pl.ds(pl.multiple_of(at * FLAT, FLAT), FLAT)


def zero_row(width):
    return jnp.zeros((1, width), jnp.float32)


def sweep(body, init=0, unroll=True):
    return lax.fori_loop(0, CHUNKS, body, init, unroll=unroll)


def statistics(values_ref, total):
    count, width = values_ref.shape
    mean = total / count

    def add(at, held):
        center = values_ref[flat_rows(at), :] - mean
        return held + column_sum(center * center)

    return mean, lax.rsqrt(sweep(add, zero_row(width), width == LANES) / count + EPSILON)


def fold_rows(values):
    rows, width = values.shape
    return jnp.sum(values.reshape(rows // 8, 8, width), axis=0)


def sweep_wide(count, body, init, thin):
    rows = THIN if thin else FLAT

    def step(at, carry):
        for piece in range(FLAT // rows):
            carry = body(pl.ds(pl.multiple_of(at * FLAT + piece * rows, rows), rows), carry)
        return carry

    return lax.fori_loop(0, count // FLAT, step, init)


def normalize(values):
    count = values.shape[0]
    center = values - column_sum(values) / count
    inv_scale = lax.rsqrt(column_sum(center * center) / count + EPSILON)
    return center * inv_scale, inv_scale


def normalize_back(grad_out, normed, inv_scale, gains):
    count = grad_out.shape[0]
    grad_gain = column_sum(grad_out * normed)
    grad_shift = column_sum(grad_out)
    grad_in = (grad_out - grad_shift / count - normed * (grad_gain / count)) * (inv_scale * gains)
    return grad_in, grad_gain, grad_shift


def spread(flat_ref, pad_ref, out_ref, top):
    for row in range(HEIGHT):
        start = 8 + top + row * PITCH
        pad_ref[start : start + WIDTH, :] = flat_ref[row * WIDTH : (row + 1) * WIDTH, :]
    rows = out_ref.shape[0]
    for col_off in range(KSIZE):
        start = 8 + col_off - KSIZE // 2
        out_ref[:, col_off * LANES : (col_off + 1) * LANES] = pad_ref[start : start + rows, :].astype(jnp.bfloat16)


def convolve(wide_ref, weights_ref, top, pitched_ref, flat_ref):
    rows = HEIGHT * PITCH
    total = None
    for row_off in range(KSIZE):
        start = top + (row_off - KSIZE // 2) * PITCH
        piece = matmul(wide_ref[start : start + rows, :], weights_ref[row_off * SPAN : (row_off + 1) * SPAN, :])
        total = piece if total is None else total + piece
    pitched_ref[...] = total
    for row in range(HEIGHT):
        flat_ref[row * WIDTH : (row + 1) * WIDTH, :] = pitched_ref[row * PITCH : row * PITCH + WIDTH, :]


def mean_of(own, theirs):
    return (own + theirs) * 0.5


def rows_at(ref, start, rows):
    return ref.at[pl.ds(start, rows), :]


def step_kernel(step, last, split, *refs):
    it = iter(refs)
    take = lambda count: [next(it) for _ in range(count)]
    core_ref = next(it) if last else None
    images_ref, cotangent_ref = take(2)
    packed = step > 0
    own, theirs = (take(2) if packed else take(5)) , (take(2) if packed else take(5))
    held_out = take(4) if packed else []
    outs = take(2) if last else take(2)
    moment_out = take(3)
    norm_moment = next(it)
    (x_ref, upstream_ref, own_ref, theirs_ref, param_ref, moment_ref,
     normed_a, normed_b, hidden_b, wide, wide_t, wide_b, pad, pad_b, mixed_e, weight_e, weight_s, weight_f,
     third, grad_sum, grad_third, work, back, weight_t, pitched, arrived, left) = take(27)
    held_ref = next(it) if packed else None
    count, width = third.shape
    blocks = width // LANES
    rows_r, rows_s, rows_e = (ref.shape[0] for ref in moment_out)
    spans = ((0, rows_r), (rows_r, rows_s), (rows_r + rows_s, rows_e))
    bf16 = jnp.bfloat16
    view = lambda ref, part: rows_at(ref, *spans[part])
    pending = {}

    def fetch(name, source, target):
        copy = pltpu.make_async_copy(source, target, arrived.at[len(pending)])
        copy.start()
        pending[name] = copy

    def fetch_part(part):
        source = (lambda sides: view(sides[0], part)) if packed else (lambda sides: sides[part])
        fetch(("own", part), source(own), view(own_ref, part))
        fetch(("theirs", part), source(theirs), view(theirs_ref, part))

    def ready(part):
        pending["own", part].wait()
        pending["theirs", part].wait()

    fetch("x", images_ref.at[step, 0], x_ref)
    fetch_part(0)

    def fetch_rest():
        fetch_part(1)
        fetch_part(2)
        fetch("upstream", cotangent_ref.at[step, 0], upstream_ref)
        if packed:
            for part in range(3):
                fetch(("held", part), held_out[part], view(held_ref, part))

    stores = []

    def store(source, target):
        copy = pltpu.make_async_copy(source, target, left.at[len(stores)])
        copy.start()
        stores.append(copy)

    def settle(part):
        store(view(moment_ref, part), moment_out[part])
        if not last:
            store(view(param_ref, part), view(outs[0], part))

    if packed:
        rows_of = lambda ref, low: jnp.concatenate([ref[low + at : low + at + 1, :] for at in range(ref.shape[0] // 2)], axis=1)
        half = own[1].shape[0] // 2
        gains = mean_of(rows_of(own[1], 0), rows_of(theirs[1], 0))
        shifts = mean_of(rows_of(own[1], half), rows_of(theirs[1], half))
    else:
        gains = mean_of(own[3][...], theirs[3][...])
        shifts = mean_of(own[4][...], theirs[4][...])
    gain_a, gain_b, gain_c = gains[:, :LANES], gains[:, LANES : 2 * LANES], gains[:, 2 * LANES :]
    shift_a, shift_b, shift_c = shifts[:, :LANES], shifts[:, LANES : 2 * LANES], shifts[:, 2 * LANES :]

    def mixed(part, start, rows):
        span = pl.ds(spans[part][0] + start, rows)
        return mean_of(own_ref[span, :], theirs_ref[span, :])

    def learn(part, start, rows, moment):
        span = pl.ds(spans[part][0] + start, rows)
        if packed:
            moment = MOMENTUM * held_ref[span, :] + moment
        moment_ref[span, :] = moment
        param_ref[span, :] = mixed(part, start, rows) - LEARN_RATE * moment

    pad[...] = jnp.zeros_like(pad)
    pad_b[...] = jnp.zeros_like(pad_b)
    pending["x"].wait()
    ready(0)
    fetch_rest()
    normed, scale_a = normalize(matmul(x_ref[...], mixed(0, 0, rows_r).astype(bf16)))
    normed_a[...] = normed
    work[...] = activate(normed * gain_a + shift_a)
    spread(work, pad, wide, TOP)

    taps = KSIZE * KSIZE
    ready(1)
    for tap in range(taps):
        weights = mixed(1, tap * LANES, LANES).astype(bf16)
        weight_s[tap * LANES : (tap + 1) * LANES, :] = weights
        other = taps - 1 - tap
        weight_f[other * LANES : (other + 1) * LANES, :] = weights.T

    convolve(wide, weight_s, TOP, pitched, work)
    normed, scale_b = normalize(work[...])
    normed_b[...] = normed
    hidden_b[...] = activate(normed * gain_b + shift_b).astype(bf16)
    for at in range(ROWS // LANES):
        wide_t[:, at * LANES : (at + 1) * LANES] = wide[at * LANES : (at + 1) * LANES, :].T

    ready(2)
    mixed_e[...] = mixed(2, 0, rows_e)
    for block in range(blocks):
        weights = mixed_e[pl.ds(block, LANES, stride=blocks), :].astype(bf16)
        weight_e[:, block * LANES : (block + 1) * LANES] = weights
        weight_t[block * LANES : (block + 1) * LANES, :] = weights.T

    def make_third(at, total):
        values = matmul(hidden_b[flat_rows(at), :], weight_e[...])
        third[flat_rows(at), :] = values
        return total + column_sum(values)

    mean = sweep(make_third, zero_row(width)) / count
    thin = step > 0
    zero = jnp.zeros((8, width), jnp.float32)

    def square(rows, held):
        center = third[rows, :] - mean
        return held + fold_rows(center * center)

    scale_c = lax.rsqrt(column_sum(sweep_wide(count, square, zero, thin)) / count + EPSILON)
    pending["upstream"].wait()

    def make_sum(rows, totals):
        normed = (third[rows, :] - mean) * scale_c
        half_sum = 0.5 * (normed * gain_c + (shift_c + x_ref[rows, :].astype(jnp.float32)))
        bend = jnp.tanh(half_sum)
        slope = (1.0 + bend) * (1.0 + half_sum * (1.0 - bend))
        grad = upstream_ref[rows, :].astype(jnp.float32) * slope
        grad_sum[rows, :] = grad
        third[rows, :] = normed
        return totals[0] + fold_rows(grad * normed), totals[1] + fold_rows(grad)

    dgain_c, dshift_c = sweep_wide(count, make_sum, (zero, zero), thin)
    dgain_c, dshift_c = 0.5 * column_sum(dgain_c), 0.5 * column_sum(dshift_c)
    level, slope, factor = 2.0 * dshift_c / count, 2.0 * dgain_c / count, 0.5 * scale_c * gain_c

    def make_back_c(at, totals):
        grad = (grad_sum[flat_rows(at), :] - level - third[flat_rows(at), :] * slope) * factor
        grad = grad.astype(bf16)
        grad_third[flat_rows(at), :] = grad
        normed = normed_b[flat_rows(at), :]
        grad_out = matmul(grad, weight_t[...]) * act_slope(normed * gain_b + shift_b)
        work[flat_rows(at), :] = grad_out
        return totals[0] + column_sum(grad_out * normed), totals[1] + column_sum(grad_out)

    dgain_b, dshift_b = sweep(make_back_c, (zero_row(LANES), zero_row(LANES)))
    grad = matmul(hidden_b[...].T, grad_third[...])
    for block in range(blocks):
        mixed_e[pl.ds(block, LANES, stride=blocks), :] = grad[:, block * LANES : (block + 1) * LANES]
    for part in range(3 if packed else 0):
        pending["held", part].wait()
    learn(2, 0, rows_e, mixed_e[...])
    settle(2)

    work[...] = (work[...] - dshift_b / count - normed_b[...] * (dgain_b / count)) * (scale_b * gain_b)
    spread(work, pad_b, wide_b, TOP_BACK)
    shifted = [
        wide_b[TOP_BACK - row_off * PITCH : TOP_BACK - row_off * PITCH + ROWS, LANES : 2 * LANES]
        for row_off in range(KSIZE)
    ]
    grad = matmul(wide_t[...], jnp.concatenate(shifted, axis=1))
    for row_off in range(KSIZE):
        learn(1, row_off * SPAN, SPAN, grad[:, row_off * LANES : (row_off + 1) * LANES])
    settle(1)

    convolve(wide_b, weight_f, TOP_BACK, pitched, work)
    normed = normed_a[...]
    grad_out = work[...] * act_slope(normed * gain_a + shift_a)
    grad_in, dgain_a, dshift_a = normalize_back(grad_out, normed, scale_a, gain_a)
    back[...] = grad_in.astype(bf16)
    grad = matmul(back[...].T, x_ref[...])
    for block in range(blocks):
        learn(0, block * LANES, LANES, grad[:, block * LANES : (block + 1) * LANES].T)
    settle(0)
    grad = jnp.concatenate([dgain_a, dgain_b, dgain_c, dshift_a, dshift_b, dshift_c], axis=1)
    norm = jnp.concatenate([gains, shifts], axis=1)
    if packed:
        grad = MOMENTUM * held_out[3][...] + grad
    norm_moment[...] = grad
    norm = norm - LEARN_RATE * grad
    if not last:
        for at in range(norm.shape[1] // LANES):
            outs[1][at : at + 1, :] = norm[:, at * LANES : (at + 1) * LANES]
        for copy in stores:
            copy.wait()
        return

    kept_ref, sent_ref = outs
    is_odd = jnp.full((1, 1), core_ref[0], jnp.int32) == 1
    pairs, piece_s, piece_e, piece_r, piece_n = split
    at_e = round_up(piece_s + 1, 8)
    at_r = at_e + piece_e

    def place(pair, start, low, high):
        rows = low.shape[0]
        kept_ref[pair, start : start + rows, :] = jnp.where(is_odd, high, low)
        sent_ref[pair, start : start + rows, :] = jnp.where(is_odd, low, high)

    for pair in range(pairs):
        for part, rows, start in ((1, piece_s, 0), (2, piece_e, at_e), (0, piece_r, at_r)):
            first = spans[part][0] + 2 * pair * rows
            place(pair, start, param_ref[first : first + rows, :], param_ref[first + rows : first + 2 * rows, :])
        low, high = [
            jnp.concatenate(
                [norm[:, at * piece_n : (at + 1) * piece_n], jnp.zeros((1, LANES - piece_n), jnp.float32)], axis=1
            )
            for at in (2 * pair, 2 * pair + 1)
        ]
        rest = jnp.zeros((at_e - piece_s - 1, LANES), jnp.float32)
        place(pair, piece_s, jnp.concatenate([low, rest]), jnp.concatenate([high, rest]))
    for copy in stores:
        copy.wait()


def fold_kernel(bits, *refs):
    spot_ref, kept_ref = refs[:2]
    came, outs, total = refs[2 : 2 + bits[0]], refs[2 + bits[0] : -1], refs[-1]
    values = kept_ref[...]
    for ref in came:
        values = values + ref[...]
    total[...] = values
    ways = len(outs)
    for hop, out in enumerate(outs):
        for at in range(out.shape[0]):
            out[at] = total[at * ways + jnp.bitwise_xor(spot_ref[0], hop)]


def mean_kernel(replicas, spans, *refs):
    outs = refs[-len(spans) :]
    kept_ref, came = refs[0], refs[1 : -len(spans)]
    values = kept_ref[0]
    for ref in came:
        values = values + ref[0]
    values = values * (1.0 / replicas)
    for (start, rows), out in zip(spans, outs):
        width = out.shape[0] // rows
        for at in range(rows):
            out[at * width : (at + 1) * width] = values[start + at, :width]


def pack_kernel(*refs):
    half = len(refs) // 2
    for source, out in zip(refs[:half], refs[half:]):
        if source.shape[0] == 1:
            out[...] = source[...].astype(jnp.bfloat16)
            continue

        def lay(at, carry, source=source, out=out):
            values = source[pl.ds(pl.multiple_of(at * 8, 8), 8), :].astype(jnp.bfloat16)
            base = pl.multiple_of(at * 8 * LANES, 8 * LANES)
            for row in range(8):
                out[0:1, pl.ds(base + row * LANES, LANES)] = values[row : row + 1]
            return carry

        lax.fori_loop(0, source.shape[0] // 8, lay, 0)


def run_kernel(body, name, operands, outs, scratch=(), flops=0, vmem=SMALL_VMEM):
    def parts(entries, is_plain):
        plain = [entry if is_plain(entry) else entry[0] for entry in entries]
        return plain, [pl.BlockSpec(memory_space=pltpu.VMEM if is_plain(entry) else entry[1]) for entry in entries]

    arrays, in_specs = parts(operands, lambda entry: not isinstance(entry, tuple))
    shapes, out_specs = parts(outs, lambda entry: isinstance(entry[0], tuple) and not isinstance(entry[0][0], tuple))
    moved = sum(array.size * array.dtype.itemsize for array in arrays)
    return list(pl.pallas_call(
        body,
        in_specs=in_specs,
        out_specs=out_specs,
        out_shape=[jax.ShapeDtypeStruct(shape, kind) for shape, kind in shapes],
        scratch_shapes=[pltpu.VMEM(*entry) if isinstance(entry, tuple) else entry for entry in scratch],
        compiler_params=pltpu.CompilerParams(vmem_limit_bytes=vmem),
        cost_estimate=pl.CostEstimate(flops=flops, bytes_accessed=moved, transcendentals=0),
        name=name,
    )(*arrays))


def in_hbm(entry):
    return entry, pltpu.HBM


def in_smem(value):
    return value.astype(jnp.int32).reshape(1), pltpu.SMEM


def swap_all(bit, values):
    return [partner_2(member, "dp", bit) for member in values]


def exchange(spot, first_bit, ways, sends):
    replicas = lax.axis_size("dp")
    return [
        lax.ppermute(sent, "dp", [(at, at ^ (hop << first_bit)) for at in range(replicas)])
        for hop, sent in zip(range(1, ways), sends)
    ]


def scatter_mean(kept, sent, split, beside):
    f32 = jnp.float32
    replicas = lax.axis_size("dp")
    levels = replicas.bit_length() - 1
    place = lax.axis_index("dp")
    pairs, piece_s, piece_e, piece_r, piece_n = split
    rows = kept.shape[1]
    came = exchange(place, 0, 2, [sent])
    left, low = pairs, 1
    while left > 1:
        width = 2 if low == 1 and levels > 2 else 1
        ways = 1 << width
        spot = in_smem((place >> low) % ways)
        kept, *sends = run_kernel(
            functools.partial(fold_kernel, (len(came),)), "fold", [spot, kept] + came,
            [((left // ways, rows, LANES), f32)] * ways, [((left, rows, LANES), f32)],
        )
        came = exchange(place, low, ways, sends)
        if beside is not None:
            done = beside()
            beside = None
            came, done = lax.optimization_barrier((came, done))
        left, low = left // ways, low + width
    at_e = round_up(piece_s + 1, 8)
    spans = ((at_e + piece_e, piece_r), (0, piece_s), (at_e, piece_e), (piece_s, 1))
    sizes = [(rows_of * LANES,) for _, rows_of in spans[:3]] + [(piece_n,)]
    mean = run_kernel(
        functools.partial(mean_kernel, replicas, spans), "mean", [kept] + came, [(size, f32) for size in sizes]
    )
    if beside is not None:
        done = beside()
    return done, mean


def scatter_mean_any(arrays):
    replicas = lax.axis_size("dp")
    tables = [member.reshape(replicas, -1) for member in arrays]
    pieces = lax.all_to_all(jnp.concatenate(tables, axis=1), "dp", 0, 0, tiled=True)
    mean = jnp.sum(pieces, axis=0) / replicas
    bounds = [sum(table.shape[1] for table in tables[:at]) for at in range(len(tables) + 1)]
    return tuple(mean[low:high] for low, high in zip(bounds[:-1], bounds[1:]))


def shards(images, cotangent, w_reduce, w_spatial, w_expand, norm_gain, norm_bias, round_index):
    f32, bf16 = jnp.float32, jnp.bfloat16
    replicas = lax.axis_size("dp")
    levels = replicas.bit_length() - 1
    steps, _, pixels, in_ch = images.shape
    weights = [member.reshape(-1, LANES) for member in (w_reduce, w_spatial, w_expand)]
    sizes = [(member.shape, f32) for member in weights]
    rows_r, rows_s, rows_e = (member.shape[0] for member in weights)
    rows = rows_r + rows_s + rows_e
    norm_size = 2 * norm_gain.size
    flat_map = ((pixels, LANES), f32)
    wide_map = ((pixels, in_ch), f32)
    whole = ((rows, LANES), f32)
    norm_rows = ((norm_size // LANES, LANES), f32)
    half_map = ((pixels, in_ch), bf16)
    scratch = [
        half_map, half_map, whole, whole, whole, whole,
        flat_map, flat_map, ((pixels, LANES), bf16), ((ROWS, SPAN), bf16), ((SPAN, ROWS), bf16),
        ((ROWS_BACK, SPAN), bf16), ((ROWS + 16, LANES), f32), ((ROWS_BACK + 16, LANES), f32),
        sizes[2], ((LANES, in_ch), bf16), ((rows_s, LANES), bf16), ((rows_s, LANES), bf16),
        wide_map, wide_map, half_map, flat_map, ((pixels, LANES), bf16), ((in_ch, LANES), bf16), ((HEIGHT * PITCH, LANES), f32),
        pltpu.SemaphoreType.DMA((11,)), pltpu.SemaphoreType.DMA((6,)),
    ]
    flops = 6 * pixels * LANES * (2 * in_ch + rows_s)
    fine = replicas > 1 and all(size[0][0] % replicas == 0 for size in sizes)
    split = (replicas // 2, rows_s // replicas, rows_e // replicas, rows_r // replicas, norm_size // replicas)
    half = ((split[0], round_up(split[1] + 1, 8) + split[2] + split[3], LANES), f32)
    params = [weights[1], weights[0], weights[2], norm_gain, norm_bias]
    moments = []
    for step in range(steps):
        branches = [functools.partial(swap_all, bit) for bit in range(levels)]
        theirs = list(lax.switch((round_index[0] + step) % levels, branches, params))
        if step == 0:
            sides = [[in_hbm(side[at]) for at in (1, 0, 2)] + side[3:] for side in (params, theirs)]
        else:
            sides = [[in_hbm(side[0]), side[1]] for side in (params, theirs)]
        operands = [in_hbm(images), in_hbm(cotangent)] + sides[0] + sides[1]
        operands += [in_hbm(member) for member in moments[:3]] + moments[3:]
        moment_outs = [in_hbm(size) for size in sizes] + [((1, norm_size), f32)]
        extra = [whole] if step else []
        if step == steps - 1 and fine:
            core = in_smem(lax.axis_index("dp") % 2)
            kept, sent, *moments = run_kernel(
                functools.partial(step_kernel, step, True, split), "last_step", [core] + operands,
                [half, half] + moment_outs, scratch + extra, flops, VMEM_BYTES,
            )
        else:
            *params, m_r, m_s, m_e, m_n = run_kernel(
                functools.partial(step_kernel, step, False, None), "step", operands,
                [in_hbm(whole), norm_rows] + moment_outs, scratch + extra, flops, VMEM_BYTES,
            )
            moments = [m_r, m_s, m_e, m_n]
    pack = lambda: run_kernel(pack_kernel, "pack", moments, [((1, member.size), bf16) for member in moments])
    if fine:
        out, averaged = scatter_mean(kept, sent, split, pack)
    else:
        flat = [params[0][low:high].reshape(-1) for low, high in ((0, rows_r), (rows_r, rows_r + rows_s), (rows_r + rows_s, rows))]
        out, averaged = pack(), scatter_mean_any(flat + [params[1].reshape(-1)])
    return tuple(averaged) + tuple(out)


def solution(mesh):
    in_specs = (
        P(None, "dp", None, None),
        P(None, "dp", None, None),
        P("dp", None),
        P("dp", None),
        P("dp", None),
        P("dp", None),
        P("dp", None),
        P(),
    )
    out_specs = (
        P("dp"),
        P("dp"),
        P("dp"),
        P("dp"),
        P("dp", None),
        P("dp", None),
        P("dp", None),
        P("dp", None),
    )
    return jax.shard_map(shards, mesh=mesh, in_specs=in_specs, out_specs=out_specs, check_vma=False)
```

```python
import functools

import jax
import jax.numpy as jnp
from jax import lax
from jax.experimental import pallas as pl
from jax.experimental.pallas import tpu as pltpu
from jax.sharding import PartitionSpec as P

HEIGHT = 28
WIDTH = 28
KSIZE = 3

LEARN_RATE = 0.01
MOMENTUM = 0.9
EPSILON = 1e-05

LANES = 128
PITCH = 32
VMEM_BYTES = 60 * 1024 * 1024
SMALL_VMEM = 8 * 1024 * 1024


def round_up(value, unit):
    return (value + unit - 1) // unit * unit


def partner_2(value, axis, distance):
    mask = 2**distance
    pairs = [(source, source ^ mask) for source in range(lax.axis_size(axis))]
    return lax.ppermute(value, axis, pairs)


def matmul(left, right):
    return jnp.dot(left, right, preferred_element_type=jnp.float32)


def contract_cols(left, right):
    return lax.dot_general(left, right, (((1,), (1,)), ((), ())), preferred_element_type=jnp.float32)


def sigmoid(values):
    return 0.5 * jnp.tanh(0.5 * values) + 0.5


def activate(values):
    return values * sigmoid(values)


def act_slope(values):
    sigma = sigmoid(values)
    return sigma * (1.0 + values * (1.0 - sigma))


def column_sum(values):
    return jnp.sum(values, axis=0, keepdims=True)


MAPS = 4
THIN = 16
FLAT = MAPS * WIDTH
PITCHED = MAPS * PITCH
CHUNKS = HEIGHT // MAPS
SPAN = KSIZE * LANES
TOP = PITCH
TOP_BACK = 2 * PITCH
ROWS = round_up(HEIGHT * PITCH + 2 * PITCH, LANES)
ROWS_BACK = ROWS + 2 * PITCH


def flat_rows(at):
    return pl.ds(pl.multiple_of(at * FLAT, FLAT), FLAT)


def zero_row(width):
    return jnp.zeros((1, width), jnp.float32)


def sweep(body, init=0, unroll=True):
    return lax.fori_loop(0, CHUNKS, body, init, unroll=unroll)


def statistics(values_ref, total):
    count, width = values_ref.shape
    mean = total / count

    def add(at, held):
        center = values_ref[flat_rows(at), :] - mean
        return held + column_sum(center * center)

    return mean, lax.rsqrt(sweep(add, zero_row(width), width == LANES) / count + EPSILON)


def fold_rows(values):
    rows, width = values.shape
    return jnp.sum(values.reshape(rows // 8, 8, width), axis=0)


def sweep_wide(count, body, init, thin):
    rows = THIN if thin else FLAT

    def step(at, carry):
        for piece in range(FLAT // rows):
            carry = body(pl.ds(pl.multiple_of(at * FLAT + piece * rows, rows), rows), carry)
        return carry

    return lax.fori_loop(0, count // FLAT, step, init)


def normalize(values):
    count = values.shape[0]
    center = values - column_sum(values) / count
    inv_scale = lax.rsqrt(column_sum(center * center) / count + EPSILON)
    return center * inv_scale, inv_scale


def normalize_back(grad_out, normed, inv_scale, gains):
    count = grad_out.shape[0]
    grad_gain = column_sum(grad_out * normed)
    grad_shift = column_sum(grad_out)
    grad_in = (grad_out - grad_shift / count - normed * (grad_gain / count)) * (inv_scale * gains)
    return grad_in, grad_gain, grad_shift


def spread(flat_ref, pad_ref, out_ref, top):
    for row in range(HEIGHT):
        start = 8 + top + row * PITCH
        pad_ref[start : start + WIDTH, :] = flat_ref[row * WIDTH : (row + 1) * WIDTH, :]
    rows = out_ref.shape[0]
    for col_off in range(KSIZE):
        start = 8 + col_off - KSIZE // 2
        out_ref[:, col_off * LANES : (col_off + 1) * LANES] = pad_ref[start : start + rows, :].astype(jnp.bfloat16)


def convolve(wide_ref, weights_ref, top, pitched_ref, flat_ref):
    rows = HEIGHT * PITCH
    total = None
    for row_off in range(KSIZE):
        start = top + (row_off - KSIZE // 2) * PITCH
        piece = matmul(wide_ref[start : start + rows, :], weights_ref[row_off * SPAN : (row_off + 1) * SPAN, :])
        total = piece if total is None else total + piece
    pitched_ref[...] = total
    for row in range(HEIGHT):
        flat_ref[row * WIDTH : (row + 1) * WIDTH, :] = pitched_ref[row * PITCH : row * PITCH + WIDTH, :]


def mean_of(own, theirs):
    return (own + theirs) * 0.5


def rows_at(ref, start, rows):
    return ref.at[pl.ds(start, rows), :]


def step_kernel(step, last, split, *refs):
    it = iter(refs)
    take = lambda count: [next(it) for _ in range(count)]
    core_ref = next(it) if last else None
    images_ref, cotangent_ref = take(2)
    packed = step > 0
    own, theirs = (take(2) if packed else take(5)) , (take(2) if packed else take(5))
    held_out = take(4) if packed else []
    outs = take(2) if last else take(2)
    moment_out = take(3)
    norm_moment = next(it)
    (x_ref, upstream_ref, own_ref, theirs_ref, param_ref, moment_ref,
     normed_a, normed_b, hidden_b, wide, wide_t, wide_b, pad, pad_b, mixed_e, weight_e, weight_s, weight_f,
     third, grad_sum, grad_third, work, back, weight_t, pitched, arrived, left) = take(27)
    held_ref = next(it) if packed else None
    count, width = third.shape
    blocks = width // LANES
    rows_r, rows_s, rows_e = (ref.shape[0] for ref in moment_out)
    spans = ((0, rows_r), (rows_r, rows_s), (rows_r + rows_s, rows_e))
    bf16 = jnp.bfloat16
    view = lambda ref, part: rows_at(ref, *spans[part])
    pending = {}

    def fetch(name, source, target):
        copy = pltpu.make_async_copy(source, target, arrived.at[len(pending)])
        copy.start()
        pending[name] = copy

    def fetch_part(part):
        source = (lambda sides: view(sides[0], part)) if packed else (lambda sides: sides[part])
        fetch(("own", part), source(own), view(own_ref, part))
        fetch(("theirs", part), source(theirs), view(theirs_ref, part))

    def ready(part):
        pending["own", part].wait()
        pending["theirs", part].wait()

    fetch("x", images_ref.at[step, 0], x_ref)
    for part in range(3):
        fetch_part(part)
    fetch("upstream", cotangent_ref.at[step, 0], upstream_ref)
    if packed:
        for part in range(3):
            fetch(("held", part), held_out[part], view(held_ref, part))

    stores = []

    def store(source, target):
        copy = pltpu.make_async_copy(source, target, left.at[len(stores)])
        copy.start()
        stores.append(copy)

    def settle(part):
        store(view(moment_ref, part), moment_out[part])
        if not last:
            store(view(param_ref, part), view(outs[0], part))

    if packed:
        rows_of = lambda ref, low: jnp.concatenate([ref[low + at : low + at + 1, :] for at in range(ref.shape[0] // 2)], axis=1)
        half = own[1].shape[0] // 2
        gains = mean_of(rows_of(own[1], 0), rows_of(theirs[1], 0))
        shifts = mean_of(rows_of(own[1], half), rows_of(theirs[1], half))
    else:
        gains = mean_of(own[3][...], theirs[3][...])
        shifts = mean_of(own[4][...], theirs[4][...])
    gain_a, gain_b, gain_c = gains[:, :LANES], gains[:, LANES : 2 * LANES], gains[:, 2 * LANES :]
    shift_a, shift_b, shift_c = shifts[:, :LANES], shifts[:, LANES : 2 * LANES], shifts[:, 2 * LANES :]

    def mixed(part, start, rows):
        span = pl.ds(spans[part][0] + start, rows)
        return mean_of(own_ref[span, :], theirs_ref[span, :])

    def learn(part, start, rows, moment):
        span = pl.ds(spans[part][0] + start, rows)
        if packed:
            moment = MOMENTUM * held_ref[span, :] + moment
        moment_ref[span, :] = moment
        param_ref[span, :] = mixed(part, start, rows) - LEARN_RATE * moment

    pad[...] = jnp.zeros_like(pad)
    pad_b[...] = jnp.zeros_like(pad_b)
    pending["x"].wait()
    ready(0)
    normed, scale_a = normalize(matmul(x_ref[...], mixed(0, 0, rows_r).astype(bf16)))
    normed_a[...] = normed
    work[...] = activate(normed * gain_a + shift_a)
    spread(work, pad, wide, TOP)

    taps = KSIZE * KSIZE
    ready(1)
    for tap in range(taps):
        weights = mixed(1, tap * LANES, LANES).astype(bf16)
        weight_s[tap * LANES : (tap + 1) * LANES, :] = weights
        other = taps - 1 - tap
        weight_f[other * LANES : (other + 1) * LANES, :] = weights.T

    convolve(wide, weight_s, TOP, pitched, work)
    normed, scale_b = normalize(work[...])
    normed_b[...] = normed
    hidden_b[...] = activate(normed * gain_b + shift_b).astype(bf16)
    for at in range(ROWS // LANES):
        wide_t[:, at * LANES : (at + 1) * LANES] = wide[at * LANES : (at + 1) * LANES, :].T

    ready(2)
    mixed_e[...] = mixed(2, 0, rows_e)
    for block in range(blocks):
        weights = mixed_e[pl.ds(block, LANES, stride=blocks), :].astype(bf16)
        weight_e[:, block * LANES : (block + 1) * LANES] = weights
        weight_t[block * LANES : (block + 1) * LANES, :] = weights.T

    def make_third(at, total):
        values = matmul(hidden_b[flat_rows(at), :], weight_e[...])
        third[flat_rows(at), :] = values
        return total + column_sum(values)

    mean = sweep(make_third, zero_row(width)) / count
    thin = step > 0
    zero = jnp.zeros((8, width), jnp.float32)

    def square(rows, held):
        center = third[rows, :] - mean
        return held + fold_rows(center * center)

    scale_c = lax.rsqrt(column_sum(sweep_wide(count, square, zero, thin)) / count + EPSILON)
    pending["upstream"].wait()

    def make_sum(rows, totals):
        normed = (third[rows, :] - mean) * scale_c
        half_sum = 0.5 * (normed * gain_c + (shift_c + x_ref[rows, :].astype(jnp.float32)))
        bend = jnp.tanh(half_sum)
        slope = (1.0 + bend) * (1.0 + half_sum * (1.0 - bend))
        grad = upstream_ref[rows, :].astype(jnp.float32) * slope
        grad_sum[rows, :] = grad
        third[rows, :] = normed
        return totals[0] + fold_rows(grad * normed), totals[1] + fold_rows(grad)

    dgain_c, dshift_c = sweep_wide(count, make_sum, (zero, zero), thin)
    dgain_c, dshift_c = 0.5 * column_sum(dgain_c), 0.5 * column_sum(dshift_c)
    level, slope, factor = 2.0 * dshift_c / count, 2.0 * dgain_c / count, 0.5 * scale_c * gain_c

    def make_back_c(at, totals):
        grad = (grad_sum[flat_rows(at), :] - level - third[flat_rows(at), :] * slope) * factor
        grad = grad.astype(bf16)
        grad_third[flat_rows(at), :] = grad
        normed = normed_b[flat_rows(at), :]
        grad_out = matmul(grad, weight_t[...]) * act_slope(normed * gain_b + shift_b)
        work[flat_rows(at), :] = grad_out
        return totals[0] + column_sum(grad_out * normed), totals[1] + column_sum(grad_out)

    dgain_b, dshift_b = sweep(make_back_c, (zero_row(LANES), zero_row(LANES)))
    grad = matmul(hidden_b[...].T, grad_third[...])
    for block in range(blocks):
        mixed_e[pl.ds(block, LANES, stride=blocks), :] = grad[:, block * LANES : (block + 1) * LANES]
    for part in range(3 if packed else 0):
        pending["held", part].wait()
    learn(2, 0, rows_e, mixed_e[...])
    settle(2)

    work[...] = (work[...] - dshift_b / count - normed_b[...] * (dgain_b / count)) * (scale_b * gain_b)
    spread(work, pad_b, wide_b, TOP_BACK)
    shifted = [
        wide_b[TOP_BACK - row_off * PITCH : TOP_BACK - row_off * PITCH + ROWS, LANES : 2 * LANES]
        for row_off in range(KSIZE)
    ]
    grad = matmul(wide_t[...], jnp.concatenate(shifted, axis=1))
    for row_off in range(KSIZE):
        learn(1, row_off * SPAN, SPAN, grad[:, row_off * LANES : (row_off + 1) * LANES])
    settle(1)

    convolve(wide_b, weight_f, TOP_BACK, pitched, work)
    normed = normed_a[...]
    grad_out = work[...] * act_slope(normed * gain_a + shift_a)
    grad_in, dgain_a, dshift_a = normalize_back(grad_out, normed, scale_a, gain_a)
    back[...] = grad_in.astype(bf16)
    grad = matmul(back[...].T, x_ref[...])
    for block in range(blocks):
        learn(0, block * LANES, LANES, grad[:, block * LANES : (block + 1) * LANES].T)
    settle(0)
    grad = jnp.concatenate([dgain_a, dgain_b, dgain_c, dshift_a, dshift_b, dshift_c], axis=1)
    norm = jnp.concatenate([gains, shifts], axis=1)
    if packed:
        grad = MOMENTUM * held_out[3][...] + grad
    norm_moment[...] = grad
    norm = norm - LEARN_RATE * grad
    if not last:
        for at in range(norm.shape[1] // LANES):
            outs[1][at : at + 1, :] = norm[:, at * LANES : (at + 1) * LANES]
        for copy in stores:
            copy.wait()
        return

    kept_ref, sent_ref = outs
    is_odd = jnp.full((1, 1), core_ref[0], jnp.int32) == 1
    pairs, piece_s, piece_e, piece_r, piece_n = split
    at_e = round_up(piece_s + 1, 8)
    at_r = at_e + piece_e

    def place(pair, start, low, high):
        rows = low.shape[0]
        kept_ref[pair, start : start + rows, :] = jnp.where(is_odd, high, low)
        sent_ref[pair, start : start + rows, :] = jnp.where(is_odd, low, high)

    for pair in range(pairs):
        for part, rows, start in ((1, piece_s, 0), (2, piece_e, at_e), (0, piece_r, at_r)):
            first = spans[part][0] + 2 * pair * rows
            place(pair, start, param_ref[first : first + rows, :], param_ref[first + rows : first + 2 * rows, :])
        low, high = [
            jnp.concatenate(
                [norm[:, at * piece_n : (at + 1) * piece_n], jnp.zeros((1, LANES - piece_n), jnp.float32)], axis=1
            )
            for at in (2 * pair, 2 * pair + 1)
        ]
        rest = jnp.zeros((at_e - piece_s - 1, LANES), jnp.float32)
        place(pair, piece_s, jnp.concatenate([low, rest]), jnp.concatenate([high, rest]))
    for copy in stores:
        copy.wait()


def fold_kernel(bits, *refs):
    spot_ref, kept_ref = refs[:2]
    came, outs, total = refs[2 : 2 + bits[0]], refs[2 + bits[0] : -1], refs[-1]
    values = kept_ref[...]
    for ref in came:
        values = values + ref[...]
    total[...] = values
    ways = len(outs)
    for hop, out in enumerate(outs):
        for at in range(out.shape[0]):
            out[at] = total[at * ways + jnp.bitwise_xor(spot_ref[0], hop)]


def mean_kernel(replicas, spans, *refs):
    outs = refs[-len(spans) :]
    kept_ref, came = refs[0], refs[1 : -len(spans)]
    values = kept_ref[0]
    for ref in came:
        values = values + ref[0]
    values = values * (1.0 / replicas)
    for (start, rows), out in zip(spans, outs):
        width = out.shape[0] // rows
        for at in range(rows):
            out[at * width : (at + 1) * width] = values[start + at, :width]


def pack_kernel(*refs):
    half = len(refs) // 2
    for source, out in zip(refs[:half], refs[half:]):
        if source.shape[0] == 1:
            out[...] = source[...].astype(jnp.bfloat16)
            continue

        def lay(at, carry, source=source, out=out):
            values = source[pl.ds(pl.multiple_of(at * 8, 8), 8), :].astype(jnp.bfloat16)
            base = pl.multiple_of(at * 8 * LANES, 8 * LANES)
            for row in range(8):
                out[0:1, pl.ds(base + row * LANES, LANES)] = values[row : row + 1]
            return carry

        lax.fori_loop(0, source.shape[0] // 8, lay, 0)


def run_kernel(body, name, operands, outs, scratch=(), flops=0, vmem=SMALL_VMEM):
    def parts(entries, is_plain):
        plain = [entry if is_plain(entry) else entry[0] for entry in entries]
        return plain, [pl.BlockSpec(memory_space=pltpu.VMEM if is_plain(entry) else entry[1]) for entry in entries]

    arrays, in_specs = parts(operands, lambda entry: not isinstance(entry, tuple))
    shapes, out_specs = parts(outs, lambda entry: isinstance(entry[0], tuple) and not isinstance(entry[0][0], tuple))
    moved = sum(array.size * array.dtype.itemsize for array in arrays)
    return list(pl.pallas_call(
        body,
        in_specs=in_specs,
        out_specs=out_specs,
        out_shape=[jax.ShapeDtypeStruct(shape, kind) for shape, kind in shapes],
        scratch_shapes=[pltpu.VMEM(*entry) if isinstance(entry, tuple) else entry for entry in scratch],
        compiler_params=pltpu.CompilerParams(vmem_limit_bytes=vmem),
        cost_estimate=pl.CostEstimate(flops=flops, bytes_accessed=moved, transcendentals=0),
        name=name,
    )(*arrays))


def in_hbm(entry):
    return entry, pltpu.HBM


def in_smem(value):
    return value.astype(jnp.int32).reshape(1), pltpu.SMEM


def swap_all(bit, values):
    return [partner_2(member, "dp", bit) for member in values]


def exchange(spot, first_bit, ways, sends):
    replicas = lax.axis_size("dp")
    return [
        lax.ppermute(sent, "dp", [(at, at ^ (hop << first_bit)) for at in range(replicas)])
        for hop, sent in zip(range(1, ways), sends)
    ]


def scatter_mean(kept, sent, split, beside):
    f32 = jnp.float32
    replicas = lax.axis_size("dp")
    levels = replicas.bit_length() - 1
    place = lax.axis_index("dp")
    pairs, piece_s, piece_e, piece_r, piece_n = split
    rows = kept.shape[1]
    kept, came = kept + exchange(place, 0, 2, [sent])[0], []
    left, low = pairs, 1
    while left > 1:
        width = 2 if low == 1 and levels > 2 else 1
        ways = 1 << width
        spot = in_smem((place >> low) % ways)
        kept, *sends = run_kernel(
            functools.partial(fold_kernel, (len(came),)), "fold", [spot, kept] + came,
            [((left // ways, rows, LANES), f32)] * ways, [((left, rows, LANES), f32)],
        )
        came = exchange(place, low, ways, sends)
        if beside is not None:
            done = beside()
            beside = None
            came, done = lax.optimization_barrier((came, done))
        left, low = left // ways, low + width
    at_e = round_up(piece_s + 1, 8)
    spans = ((at_e + piece_e, piece_r), (0, piece_s), (at_e, piece_e), (piece_s, 1))
    sizes = [(rows_of * LANES,) for _, rows_of in spans[:3]] + [(piece_n,)]
    mean = run_kernel(
        functools.partial(mean_kernel, replicas, spans), "mean", [kept] + came, [(size, f32) for size in sizes]
    )
    if beside is not None:
        done = beside()
    return done, mean


def scatter_mean_any(arrays):
    replicas = lax.axis_size("dp")
    tables = [member.reshape(replicas, -1) for member in arrays]
    pieces = lax.all_to_all(jnp.concatenate(tables, axis=1), "dp", 0, 0, tiled=True)
    mean = jnp.sum(pieces, axis=0) / replicas
    bounds = [sum(table.shape[1] for table in tables[:at]) for at in range(len(tables) + 1)]
    return tuple(mean[low:high] for low, high in zip(bounds[:-1], bounds[1:]))


def shards(images, cotangent, w_reduce, w_spatial, w_expand, norm_gain, norm_bias, round_index):
    f32, bf16 = jnp.float32, jnp.bfloat16
    replicas = lax.axis_size("dp")
    levels = replicas.bit_length() - 1
    steps, _, pixels, in_ch = images.shape
    weights = [member.reshape(-1, LANES) for member in (w_reduce, w_spatial, w_expand)]
    sizes = [(member.shape, f32) for member in weights]
    rows_r, rows_s, rows_e = (member.shape[0] for member in weights)
    rows = rows_r + rows_s + rows_e
    norm_size = 2 * norm_gain.size
    flat_map = ((pixels, LANES), f32)
    wide_map = ((pixels, in_ch), f32)
    whole = ((rows, LANES), f32)
    norm_rows = ((norm_size // LANES, LANES), f32)
    half_map = ((pixels, in_ch), bf16)
    scratch = [
        half_map, half_map, whole, whole, whole, whole,
        flat_map, flat_map, ((pixels, LANES), bf16), ((ROWS, SPAN), bf16), ((SPAN, ROWS), bf16),
        ((ROWS_BACK, SPAN), bf16), ((ROWS + 16, LANES), f32), ((ROWS_BACK + 16, LANES), f32),
        sizes[2], ((LANES, in_ch), bf16), ((rows_s, LANES), bf16), ((rows_s, LANES), bf16),
        wide_map, wide_map, half_map, flat_map, ((pixels, LANES), bf16), ((in_ch, LANES), bf16), ((HEIGHT * PITCH, LANES), f32),
        pltpu.SemaphoreType.DMA((11,)), pltpu.SemaphoreType.DMA((6,)),
    ]
    flops = 6 * pixels * LANES * (2 * in_ch + rows_s)
    fine = replicas > 1 and all(size[0][0] % replicas == 0 for size in sizes)
    split = (replicas // 2, rows_s // replicas, rows_e // replicas, rows_r // replicas, norm_size // replicas)
    half = ((split[0], round_up(split[1] + 1, 8) + split[2] + split[3], LANES), f32)
    params = [weights[1], weights[0], weights[2], norm_gain, norm_bias]
    moments = []
    for step in range(steps):
        branches = [functools.partial(swap_all, bit) for bit in range(levels)]
        theirs = list(lax.switch((round_index[0] + step) % levels, branches, params))
        if step == 0:
            sides = [[in_hbm(side[at]) for at in (1, 0, 2)] + side[3:] for side in (params, theirs)]
        else:
            sides = [[in_hbm(side[0]), side[1]] for side in (params, theirs)]
        operands = [in_hbm(images), in_hbm(cotangent)] + sides[0] + sides[1]
        operands += [in_hbm(member) for member in moments[:3]] + moments[3:]
        moment_outs = [in_hbm(size) for size in sizes] + [((1, norm_size), f32)]
        extra = [whole] if step else []
        if step == steps - 1 and fine:
            core = in_smem(lax.axis_index("dp") % 2)
            kept, sent, *moments = run_kernel(
                functools.partial(step_kernel, step, True, split), "last_step", [core] + operands,
                [half, half] + moment_outs, scratch + extra, flops, VMEM_BYTES,
            )
        else:
            *params, m_r, m_s, m_e, m_n = run_kernel(
                functools.partial(step_kernel, step, False, None), "step", operands,
                [in_hbm(whole), norm_rows] + moment_outs, scratch + extra, flops, VMEM_BYTES,
            )
            moments = [m_r, m_s, m_e, m_n]
    pack = lambda: run_kernel(pack_kernel, "pack", moments, [((1, member.size), bf16) for member in moments])
    if fine:
        out, averaged = scatter_mean(kept, sent, split, pack)
    else:
        flat = [params[0][low:high].reshape(-1) for low, high in ((0, rows_r), (rows_r, rows_r + rows_s), (rows_r + rows_s, rows))]
        out, averaged = pack(), scatter_mean_any(flat + [params[1].reshape(-1)])
    return tuple(averaged) + tuple(out)


def solution(mesh):
    in_specs = (
        P(None, "dp", None, None),
        P(None, "dp", None, None),
        P("dp", None),
        P("dp", None),
        P("dp", None),
        P("dp", None),
        P("dp", None),
        P(),
    )
    out_specs = (
        P("dp"),
        P("dp"),
        P("dp"),
        P("dp"),
        P("dp", None),
        P("dp", None),
        P("dp", None),
        P("dp", None),
    )
    return jax.shard_map(shards, mesh=mesh, in_specs=in_specs, out_specs=out_specs, check_vma=False)
```

```python
import functools

import jax
import jax.numpy as jnp
from jax import lax
from jax.experimental import pallas as pl
from jax.experimental.pallas import tpu as pltpu
from jax.sharding import PartitionSpec as P

HEIGHT = 28
WIDTH = 28
KSIZE = 3

LEARN_RATE = 0.01
MOMENTUM = 0.9
EPSILON = 1e-05

LANES = 128
PITCH = 32
VMEM_BYTES = 60 * 1024 * 1024
SMALL_VMEM = 8 * 1024 * 1024


def round_up(value, unit):
    return (value + unit - 1) // unit * unit


def partner_2(value, axis, distance):
    mask = 2**distance
    pairs = [(source, source ^ mask) for source in range(lax.axis_size(axis))]
    return lax.ppermute(value, axis, pairs)


def matmul(left, right):
    return jnp.dot(left, right, preferred_element_type=jnp.float32)


def contract_cols(left, right):
    return lax.dot_general(left, right, (((1,), (1,)), ((), ())), preferred_element_type=jnp.float32)


def sigmoid(values):
    return 0.5 * jnp.tanh(0.5 * values) + 0.5


def activate(values):
    return values * sigmoid(values)


def act_slope(values):
    sigma = sigmoid(values)
    return sigma * (1.0 + values * (1.0 - sigma))


def column_sum(values):
    return jnp.sum(values, axis=0, keepdims=True)


MAPS = 4
FLAT = MAPS * WIDTH
PITCHED = MAPS * PITCH
CHUNKS = HEIGHT // MAPS
SPAN = KSIZE * LANES
TOP = PITCH
TOP_BACK = 2 * PITCH
ROWS = round_up(HEIGHT * PITCH + 2 * PITCH, LANES)
ROWS_BACK = ROWS + 2 * PITCH


def flat_rows(at):
    return pl.ds(pl.multiple_of(at * FLAT, FLAT), FLAT)


def zero_row(width):
    return jnp.zeros((1, width), jnp.float32)


def sweep(body, init=0, unroll=True):
    return lax.fori_loop(0, CHUNKS, body, init, unroll=unroll)


def statistics(values_ref, total):
    count, width = values_ref.shape
    mean = total / count

    def add(at, held):
        center = values_ref[flat_rows(at), :] - mean
        return held + column_sum(center * center)

    return mean, lax.rsqrt(sweep(add, zero_row(width), width == LANES) / count + EPSILON)


def pad_chunk(pad_ref, top, at, values):
    for row in range(MAPS):
        start = pl.multiple_of(at * PITCHED, PITCHED) + (8 + top + row * PITCH)
        pad_ref[pl.ds(start, WIDTH), :] = values[row * WIDTH : (row + 1) * WIDTH]


def shift_columns(pad_ref, out_ref):
    rows = out_ref.shape[0]
    for col_off in range(KSIZE):
        start = 8 + col_off - KSIZE // 2
        out_ref[:, col_off * LANES : (col_off + 1) * LANES] = pad_ref[start : start + rows, :].astype(jnp.bfloat16)


def conv_chunk(wide_ref, top, at, weight_of, multiply):
    total = None
    for row_off in range(KSIZE):
        start = pl.multiple_of(at * PITCHED, PITCHED) + (top + (row_off - KSIZE // 2) * PITCH)
        piece = multiply(wide_ref[pl.ds(start, PITCHED), :], weight_of(row_off))
        total = piece if total is None else total + piece
    return jnp.concatenate([total[row * PITCH : row * PITCH + WIDTH] for row in range(MAPS)], axis=0)


def mean_of(own, theirs):
    return (own + theirs) * 0.5


def rows_at(ref, start, rows):
    return ref.at[pl.ds(start, rows), :]


def step_kernel(step, last, split, *refs):
    it = iter(refs)
    take = lambda count: [next(it) for _ in range(count)]
    core_ref = next(it) if last else None
    packed = step > 0
    if packed:
        x_ref, upstream_ref = take(2)
    images_ref, cotangent_ref = take(0 if last and packed else 2) or (None, None)
    own, theirs = (take(2) if packed else take(5)) , (take(2) if packed else take(5))
    held_out = take(4) if packed else []
    outs = take(2)
    next_refs = [] if last else take(2)
    moment_out = take(3)
    norm_moment = next(it)
    if not packed:
        x_ref, upstream_ref = take(2)
    (own_ref, theirs_ref, param_ref, moment_ref,
     normed_a, normed_b, hidden_b, wide, wide_t, wide_b, pad, pad_b, mixed_e, weight_e, weight_s, weight_f,
     third, grad_sum, grad_third, work, back, weight_t, arrived, left) = take(24)
    held_ref = next(it) if packed else None
    kept_part, sent_part = take(2) if last else (None, None)
    count, width = third.shape
    blocks = width // LANES
    rows_r, rows_s, rows_e = (ref.shape[0] for ref in moment_out)
    spans = ((0, rows_r), (rows_r, rows_s), (rows_r + rows_s, rows_e))
    bf16 = jnp.bfloat16
    view = lambda ref, part: rows_at(ref, *spans[part])
    pending = {}

    def fetch(name, source, target):
        copy = pltpu.make_async_copy(source, target, arrived.at[len(pending)])
        copy.start()
        pending[name] = copy

    def fetch_part(part):
        source = (lambda sides: view(sides[0], part)) if packed else (lambda sides: sides[part])
        fetch(("own", part), source(own), view(own_ref, part))
        fetch(("theirs", part), source(theirs), view(theirs_ref, part))

    def ready(part):
        pending["own", part].wait()
        pending["theirs", part].wait()

    if not packed:
        fetch("x", images_ref.at[step, 0], x_ref)
    for part in range(3):
        fetch_part(part)
    if not packed:
        fetch("upstream", cotangent_ref.at[step, 0], upstream_ref)
    if packed:
        for part in range(3):
            fetch(("held", part), held_out[part], view(held_ref, part))
    stores = []

    def store(source, target):
        copy = pltpu.make_async_copy(source, target, left.at[len(stores)])
        copy.start()
        stores.append(copy)

    def settle(part):
        store(view(moment_ref, part), moment_out[part])
        if not last:
            store(view(param_ref, part), view(outs[0], part))
        else:
            place_part(part)
            if part == 1:
                send(0, cut)
            if part == 2:
                send(start_of[2], split[2])

    if packed:
        rows_of = lambda ref, low: jnp.concatenate([ref[low + at : low + at + 1, :] for at in range(ref.shape[0] // 2)], axis=1)
        half = own[1].shape[0] // 2
        gains = mean_of(rows_of(own[1], 0), rows_of(theirs[1], 0))
        shifts = mean_of(rows_of(own[1], half), rows_of(theirs[1], half))
    else:
        gains = mean_of(own[3][...], theirs[3][...])
        shifts = mean_of(own[4][...], theirs[4][...])
    gain_a, gain_b, gain_c = gains[:, :LANES], gains[:, LANES : 2 * LANES], gains[:, 2 * LANES :]
    shift_a, shift_b, shift_c = shifts[:, :LANES], shifts[:, LANES : 2 * LANES], shifts[:, 2 * LANES :]

    def mixed(part, start, rows):
        span = pl.ds(spans[part][0] + start, rows)
        return mean_of(own_ref[span, :], theirs_ref[span, :])

    def learn(part, start, rows, moment):
        span = pl.ds(spans[part][0] + start, rows)
        if packed:
            moment = MOMENTUM * held_ref[span, :] + moment
        moment_ref[span, :] = moment
        param_ref[span, :] = mixed(part, start, rows) - LEARN_RATE * moment

    if last:
        is_odd = jnp.full((1, 1), core_ref[0], jnp.int32) == 1
        start_of, _ = starts_in_piece(split)
        cut = split[1] // 8 * 8

    def place(pair, start, low, high):
        rows = low.shape[0]
        kept_part[pair, start : start + rows, :] = jnp.where(is_odd, high, low)
        sent_part[pair, start : start + rows, :] = jnp.where(is_odd, low, high)

    def place_part(part):
        rows = split[(3, 1, 2)[part]]
        for pair in range(split[0]):
            first = spans[part][0] + 2 * pair * rows
            place(pair, start_of[part], param_ref[first : first + rows, :], param_ref[first + rows : first + 2 * rows, :])

    def send(start, rows):
        if rows == 0:
            return
        for source, target in zip((sent_part, kept_part), (outs[1], outs[0])):
            store(source.at[:, pl.ds(start, rows), :], target.at[:, pl.ds(start, rows), :])

    pad[...] = jnp.zeros_like(pad)
    pad_b[...] = jnp.zeros_like(pad_b)
    if not packed:
        pending["x"].wait()
    ready(0)
    reduce_w = mixed(0, 0, rows_r).astype(bf16)

    def make_first(at, total):
        values = matmul(x_ref[flat_rows(at), :], reduce_w)
        normed_a[flat_rows(at), :] = values
        return total + column_sum(values)

    mean, scale_a = statistics(normed_a, sweep(make_first, zero_row(LANES)))

    def make_hidden_a(at, carry):
        normed = (normed_a[flat_rows(at), :] - mean) * scale_a
        normed_a[flat_rows(at), :] = normed
        pad_chunk(pad, TOP, at, activate(normed * gain_a + shift_a))
        return carry

    sweep(make_hidden_a)
    shift_columns(pad, wide)

    taps = KSIZE * KSIZE
    ready(1)
    for tap in range(taps):
        weights = mixed(1, tap * LANES, LANES).astype(bf16)
        weight_s[tap * LANES : (tap + 1) * LANES, :] = weights
        other = taps - 1 - tap
        weight_f[other * LANES : (other + 1) * LANES, :] = weights.T

    def make_second(at, total):
        values = conv_chunk(wide, TOP, at, lambda row: weight_s[row * SPAN : (row + 1) * SPAN, :], matmul)
        normed_b[flat_rows(at), :] = values
        return total + column_sum(values)

    mean, scale_b = statistics(normed_b, sweep(make_second, zero_row(LANES)))

    def make_hidden_b(at, carry):
        normed = (normed_b[flat_rows(at), :] - mean) * scale_b
        normed_b[flat_rows(at), :] = normed
        hidden_b[flat_rows(at), :] = activate(normed * gain_b + shift_b).astype(bf16)
        return carry

    sweep(make_hidden_b)

    ready(2)
    mixed_e[...] = mixed(2, 0, rows_e)
    for block in range(blocks):
        weights = mixed_e[pl.ds(block, LANES, stride=blocks), :].astype(bf16)
        weight_e[:, block * LANES : (block + 1) * LANES] = weights
        weight_t[block * LANES : (block + 1) * LANES, :] = weights.T

    def make_third(at, total):
        values = matmul(hidden_b[flat_rows(at), :], weight_e[...])
        third[flat_rows(at), :] = values
        return total + column_sum(values)

    mean, scale_c = statistics(third, sweep(make_third, zero_row(width)))

    def make_sum(at, totals):
        normed = (third[flat_rows(at), :] - mean) * scale_c
        summed = normed * gain_c + shift_c + x_ref[flat_rows(at), :].astype(jnp.float32)
        grad = upstream_ref[flat_rows(at), :].astype(jnp.float32) * act_slope(summed)
        grad_sum[flat_rows(at), :] = grad
        third[flat_rows(at), :] = normed
        return totals[0] + column_sum(grad * normed), totals[1] + column_sum(grad)

    if not packed:
        pending["upstream"].wait()
    if not last:
        for ahead, (source, target) in enumerate(zip((images_ref, cotangent_ref), next_refs)):
            fetch(("next", ahead), source.at[step + 1, 0], target)
    dgain_c, dshift_c = sweep(make_sum, (zero_row(width), zero_row(width)), False)
    level, slope, factor = dshift_c / count, dgain_c / count, scale_c * gain_c

    def make_back_c(at, totals):
        grad = (grad_sum[flat_rows(at), :] - level - third[flat_rows(at), :] * slope) * factor
        grad = grad.astype(bf16)
        grad_third[flat_rows(at), :] = grad
        normed = normed_b[flat_rows(at), :]
        grad_out = matmul(grad, weight_t[...]) * act_slope(normed * gain_b + shift_b)
        work[flat_rows(at), :] = grad_out
        return totals[0] + column_sum(grad_out * normed), totals[1] + column_sum(grad_out)

    dgain_b, dshift_b = sweep(make_back_c, (zero_row(LANES), zero_row(LANES)))
    grad = matmul(hidden_b[...].T, grad_third[...])
    for block in range(blocks):
        mixed_e[pl.ds(block, LANES, stride=blocks), :] = grad[:, block * LANES : (block + 1) * LANES]
    for part in range(3 if packed else 0):
        pending["held", part].wait()
    learn(2, 0, rows_e, mixed_e[...])
    settle(2)

    level_b, slope_b, factor_b = dshift_b / count, dgain_b / count, scale_b * gain_b

    def make_back_b(at, carry):
        grad = (work[flat_rows(at), :] - level_b - normed_b[flat_rows(at), :] * slope_b) * factor_b
        pad_chunk(pad_b, TOP_BACK, at, grad)
        return carry

    sweep(make_back_b)
    shift_columns(pad_b, wide_b)

    for at in range(ROWS // LANES):
        wide_t[:, at * LANES : (at + 1) * LANES] = wide[at * LANES : (at + 1) * LANES, :].T

    shifted = [
        wide_b[TOP_BACK - row_off * PITCH : TOP_BACK - row_off * PITCH + ROWS, LANES : 2 * LANES]
        for row_off in range(KSIZE)
    ]
    grad = matmul(wide_t[...], jnp.concatenate(shifted, axis=1))
    for row_off in range(KSIZE):
        learn(1, row_off * SPAN, SPAN, grad[:, row_off * LANES : (row_off + 1) * LANES])
    settle(1)

    def make_back_a(at, totals):
        grad = conv_chunk(wide_b, TOP_BACK, at, lambda row: weight_f[row * SPAN : (row + 1) * SPAN, :], matmul)
        normed = normed_a[flat_rows(at), :]
        grad_out = grad * act_slope(normed * gain_a + shift_a)
        work[flat_rows(at), :] = grad_out
        return totals[0] + column_sum(grad_out * normed), totals[1] + column_sum(grad_out)

    dgain_a, dshift_a = sweep(make_back_a, (zero_row(LANES), zero_row(LANES)))
    level_a, slope_a, factor_a = dshift_a / count, dgain_a / count, scale_a * gain_a

    def make_first_grad(at, carry):
        grad = (work[flat_rows(at), :] - level_a - normed_a[flat_rows(at), :] * slope_a) * factor_a
        back[flat_rows(at), :] = grad.astype(bf16)
        return carry

    sweep(make_first_grad)
    grad = matmul(back[...].T, x_ref[...])
    for block in range(blocks):
        learn(0, block * LANES, LANES, grad[:, block * LANES : (block + 1) * LANES].T)
    settle(0)
    grad = jnp.concatenate([dgain_a, dgain_b, dgain_c, dshift_a, dshift_b, dshift_c], axis=1)
    norm = jnp.concatenate([gains, shifts], axis=1)
    if packed:
        grad = MOMENTUM * held_out[3][...] + grad
    norm_moment[...] = grad
    norm = norm - LEARN_RATE * grad
    if not last:
        for at in range(norm.shape[1] // LANES):
            outs[1][at : at + 1, :] = norm[:, at * LANES : (at + 1) * LANES]
        for copy in stores + [pending["next", 0], pending["next", 1]]:
            copy.wait()
        return

    piece_n = split[4]
    for pair in range(split[0]):
        low, high = [
            jnp.concatenate(
                [norm[:, at * piece_n : (at + 1) * piece_n], jnp.zeros((1, LANES - piece_n), jnp.float32)], axis=1
            )
            for at in (2 * pair, 2 * pair + 1)
        ]
        rest = jnp.zeros((start_of[2] - start_of[3] - 1, LANES), jnp.float32)
        place(pair, start_of[3], jnp.concatenate([low, rest]), jnp.concatenate([high, rest]))
    send(cut, start_of[2] - cut)
    send(start_of[0], split[3])
    for copy in stores:
        copy.wait()


def starts_in_piece(split):
    _, piece_s, piece_e, piece_r, _ = split
    at_e = round_up(piece_s + 1, 8)
    at_r = at_e + piece_e
    return (at_r, 0, at_e, piece_s), at_r + piece_r


def fold_kernel(bits, *refs):
    spot_ref, kept_ref = refs[:2]
    came, outs, total = refs[2 : 2 + bits[0]], refs[2 + bits[0] : -1], refs[-1]
    values = kept_ref[...]
    for ref in came:
        values = values + ref[...]
    total[...] = values
    ways = len(outs)
    for hop, out in enumerate(outs):
        for at in range(out.shape[0]):
            out[at] = total[at * ways + jnp.bitwise_xor(spot_ref[0], hop)]


def mean_kernel(replicas, spans, *refs):
    outs = refs[-len(spans) :]
    kept_ref, came = refs[0], refs[1 : -len(spans)]
    values = kept_ref[0]
    for ref in came:
        values = values + ref[0]
    values = values * (1.0 / replicas)
    for (start, rows), out in zip(spans, outs):
        width = out.shape[0] // rows
        for at in range(rows):
            out[at * width : (at + 1) * width] = values[start + at, :width]


def pack_kernel(*refs):
    half = len(refs) // 2
    for source, out in zip(refs[:half], refs[half:]):
        if source.shape[0] == 1:
            out[...] = source[...].astype(jnp.bfloat16)
            continue

        def lay(at, carry, source=source, out=out):
            values = source[pl.ds(pl.multiple_of(at * 8, 8), 8), :].astype(jnp.bfloat16)
            base = pl.multiple_of(at * 8 * LANES, 8 * LANES)
            for row in range(8):
                out[0:1, pl.ds(base + row * LANES, LANES)] = values[row : row + 1]
            return carry

        lax.fori_loop(0, source.shape[0] // 8, lay, 0)


def run_kernel(body, name, operands, outs, scratch=(), flops=0, vmem=SMALL_VMEM):
    def parts(entries, is_plain):
        plain = [entry if is_plain(entry) else entry[0] for entry in entries]
        return plain, [pl.BlockSpec(memory_space=pltpu.VMEM if is_plain(entry) else entry[1]) for entry in entries]

    arrays, in_specs = parts(operands, lambda entry: not isinstance(entry, tuple))
    shapes, out_specs = parts(outs, lambda entry: isinstance(entry[0], tuple) and not isinstance(entry[0][0], tuple))
    moved = sum(array.size * array.dtype.itemsize for array in arrays)
    return list(pl.pallas_call(
        body,
        in_specs=in_specs,
        out_specs=out_specs,
        out_shape=[jax.ShapeDtypeStruct(shape, kind) for shape, kind in shapes],
        scratch_shapes=[pltpu.VMEM(*entry) if isinstance(entry, tuple) else entry for entry in scratch],
        compiler_params=pltpu.CompilerParams(vmem_limit_bytes=vmem),
        cost_estimate=pl.CostEstimate(flops=flops, bytes_accessed=moved, transcendentals=0),
        name=name,
    )(*arrays))


def in_hbm(entry):
    return entry, pltpu.HBM


def in_smem(value):
    return value.astype(jnp.int32).reshape(1), pltpu.SMEM


def swap_all(bit, values):
    return [partner_2(member, "dp", bit) for member in values]


def exchange(spot, first_bit, ways, sends):
    replicas = lax.axis_size("dp")
    return [
        lax.ppermute(sent, "dp", [(at, at ^ (hop << first_bit)) for at in range(replicas)])
        for hop, sent in zip(range(1, ways), sends)
    ]


def scatter_mean(kept, sent, split, beside):
    f32 = jnp.float32
    replicas = lax.axis_size("dp")
    levels = replicas.bit_length() - 1
    place = lax.axis_index("dp")
    pairs, piece_s, piece_e, piece_r, piece_n = split
    rows = kept.shape[1]
    came = exchange(place, 0, 2, [sent])
    left, low = pairs, 1
    while left > 1:
        width = 2 if low == 1 and levels > 2 else 1
        ways = 1 << width
        spot = in_smem((place >> low) % ways)
        kept, *sends = run_kernel(
            functools.partial(fold_kernel, (len(came),)), "fold", [spot, kept] + came,
            [((left // ways, rows, LANES), f32)] * ways, [((left, rows, LANES), f32)],
        )
        came = exchange(place, low, ways, sends)
        if beside is not None:
            done = beside()
            beside = None
            came, done = lax.optimization_barrier((came, done))
        left, low = left // ways, low + width
    start_of, _ = starts_in_piece(split)
    spans = ((start_of[0], piece_r), (start_of[1], piece_s), (start_of[2], piece_e), (start_of[3], 1))
    sizes = [(rows_of * LANES,) for _, rows_of in spans[:3]] + [(piece_n,)]
    mean = run_kernel(
        functools.partial(mean_kernel, replicas, spans), "mean", [kept] + came, [(size, f32) for size in sizes]
    )
    if beside is not None:
        done = beside()
    return done, mean


def scatter_mean_any(arrays):
    replicas = lax.axis_size("dp")
    tables = [member.reshape(replicas, -1) for member in arrays]
    pieces = lax.all_to_all(jnp.concatenate(tables, axis=1), "dp", 0, 0, tiled=True)
    mean = jnp.sum(pieces, axis=0) / replicas
    bounds = [sum(table.shape[1] for table in tables[:at]) for at in range(len(tables) + 1)]
    return tuple(mean[low:high] for low, high in zip(bounds[:-1], bounds[1:]))


def shards(images, cotangent, w_reduce, w_spatial, w_expand, norm_gain, norm_bias, round_index):
    f32, bf16 = jnp.float32, jnp.bfloat16
    replicas = lax.axis_size("dp")
    levels = replicas.bit_length() - 1
    steps, _, pixels, in_ch = images.shape
    weights = [member.reshape(-1, LANES) for member in (w_reduce, w_spatial, w_expand)]
    sizes = [(member.shape, f32) for member in weights]
    rows_r, rows_s, rows_e = (member.shape[0] for member in weights)
    rows = rows_r + rows_s + rows_e
    norm_size = 2 * norm_gain.size
    flat_map = ((pixels, LANES), f32)
    wide_map = ((pixels, in_ch), f32)
    whole = ((rows, LANES), f32)
    norm_rows = ((norm_size // LANES, LANES), f32)
    half_map = ((pixels, in_ch), bf16)
    scratch = [
        whole, whole, whole, whole,
        flat_map, flat_map, ((pixels, LANES), bf16), ((ROWS, SPAN), bf16), ((SPAN, ROWS), bf16),
        ((ROWS_BACK, SPAN), bf16), ((ROWS + 16, LANES), f32), ((ROWS_BACK + 16, LANES), f32),
        sizes[2], ((LANES, in_ch), bf16), ((rows_s, LANES), bf16), ((rows_s, LANES), bf16),
        wide_map, wide_map, half_map, flat_map, ((pixels, LANES), bf16), ((in_ch, LANES), bf16),
        pltpu.SemaphoreType.DMA((13,)), pltpu.SemaphoreType.DMA((11,)),
    ]
    flops = 6 * pixels * LANES * (2 * in_ch + rows_s)
    fine = replicas > 1 and all(size[0][0] % replicas == 0 for size in sizes)
    split = (replicas // 2, rows_s // replicas, rows_e // replicas, rows_r // replicas, norm_size // replicas)
    half = ((split[0], starts_in_piece(split)[1], LANES), f32)
    params = [weights[1], weights[0], weights[2], norm_gain, norm_bias]
    moments, ahead = [], []
    for step in range(steps):
        branches = [functools.partial(swap_all, bit) for bit in range(levels)]
        theirs = list(lax.switch((round_index[0] + step) % levels, branches, params))
        if step == 0:
            sides = [[in_hbm(side[at]) for at in (1, 0, 2)] + side[3:] for side in (params, theirs)]
        else:
            sides = [[in_hbm(side[0]), side[1]] for side in (params, theirs)]
        last = step == steps - 1 and fine
        operands = ahead + ([] if last and step else [in_hbm(images), in_hbm(cotangent)]) + sides[0] + sides[1]
        operands += [in_hbm(member) for member in moments[:3]] + moments[3:]
        moment_outs = [in_hbm(size) for size in sizes] + [((1, norm_size), f32)]
        extra = [whole] if step else []
        before = [] if step else [half_map, half_map]
        if last:
            core = in_smem(lax.axis_index("dp") % 2)
            kept, sent, *moments = run_kernel(
                functools.partial(step_kernel, step, True, split), "last_step", [core] + operands,
                [in_hbm(half), in_hbm(half)] + moment_outs, before + scratch + extra + [half, half], flops, VMEM_BYTES,
            )
        else:
            *params, next_x, next_up, m_r, m_s, m_e, m_n = run_kernel(
                functools.partial(step_kernel, step, False, None), "step", operands,
                [in_hbm(whole), norm_rows, half_map, half_map] + moment_outs, before + scratch + extra, flops, VMEM_BYTES,
            )
            ahead = [next_x, next_up]
            moments = [m_r, m_s, m_e, m_n]
    pack = lambda: run_kernel(pack_kernel, "pack", moments, [((1, member.size), bf16) for member in moments])
    if fine:
        out, averaged = scatter_mean(kept, sent, split, pack)
    else:
        flat = [params[0][low:high].reshape(-1) for low, high in ((0, rows_r), (rows_r, rows_r + rows_s), (rows_r + rows_s, rows))]
        out, averaged = pack(), scatter_mean_any(flat + [params[1].reshape(-1)])
    return tuple(averaged) + tuple(out)


def solution(mesh):
    in_specs = (
        P(None, "dp", None, None),
        P(None, "dp", None, None),
        P("dp", None),
        P("dp", None),
        P("dp", None),
        P("dp", None),
        P("dp", None),
        P(),
    )
    out_specs = (
        P("dp"),
        P("dp"),
        P("dp"),
        P("dp"),
        P("dp", None),
        P("dp", None),
        P("dp", None),
        P("dp", None),
    )
    return jax.shard_map(shards, mesh=mesh, in_specs=in_specs, out_specs=out_specs, check_vma=False)
```

```python
import functools

import jax
import jax.numpy as jnp
from jax import lax
from jax.experimental import pallas as pl
from jax.experimental.pallas import tpu as pltpu
from jax.sharding import PartitionSpec as P

HEIGHT = 28
WIDTH = 28
KSIZE = 3

LEARN_RATE = 0.01
MOMENTUM = 0.9
EPSILON = 1e-05

LANES = 128
PITCH = 32
VMEM_BYTES = 60 * 1024 * 1024
SMALL_VMEM = 8 * 1024 * 1024


def round_up(value, unit):
    return (value + unit - 1) // unit * unit


def partner_2(value, axis, distance):
    mask = 2**distance
    pairs = [(source, source ^ mask) for source in range(lax.axis_size(axis))]
    return lax.ppermute(value, axis, pairs)


def matmul(left, right):
    return jnp.dot(left, right, preferred_element_type=jnp.float32)


def contract_cols(left, right):
    return lax.dot_general(left, right, (((1,), (1,)), ((), ())), preferred_element_type=jnp.float32)


def sigmoid(values):
    return 0.5 * jnp.tanh(0.5 * values) + 0.5


def activate(values):
    return values * sigmoid(values)


def act_slope(values):
    sigma = sigmoid(values)
    return sigma * (1.0 + values * (1.0 - sigma))


def column_sum(values):
    return jnp.sum(values, axis=0, keepdims=True)


MAPS = 4
FLAT = MAPS * WIDTH
PITCHED = MAPS * PITCH
CHUNKS = HEIGHT // MAPS
SPAN = KSIZE * LANES
TOP = PITCH
TOP_BACK = 2 * PITCH
ROWS = round_up(HEIGHT * PITCH + 2 * PITCH, LANES)
ROWS_BACK = ROWS + 2 * PITCH


def flat_rows(at):
    return pl.ds(pl.multiple_of(at * FLAT, FLAT), FLAT)


def zero_row(width):
    return jnp.zeros((1, width), jnp.float32)


def sweep(body, init=0, unroll=True):
    return lax.fori_loop(0, CHUNKS, body, init, unroll=unroll)


def statistics(values_ref, total):
    count, width = values_ref.shape
    mean = total / count

    def add(at, held):
        center = values_ref[flat_rows(at), :] - mean
        return held + column_sum(center * center)

    return mean, lax.rsqrt(sweep(add, zero_row(width), width == LANES) / count + EPSILON)


def pad_chunk(pad_ref, top, at, values):
    for row in range(MAPS):
        start = pl.multiple_of(at * PITCHED, PITCHED) + (8 + top + row * PITCH)
        pad_ref[pl.ds(start, WIDTH), :] = values[row * WIDTH : (row + 1) * WIDTH]


def shift_columns(pad_ref, out_ref):
    rows = out_ref.shape[0]
    for col_off in range(KSIZE):
        start = 8 + col_off - KSIZE // 2
        out_ref[:, col_off * LANES : (col_off + 1) * LANES] = pad_ref[start : start + rows, :].astype(jnp.bfloat16)


def conv_chunk(wide_ref, top, at, weight_of, multiply):
    total = None
    for row_off in range(KSIZE):
        start = pl.multiple_of(at * PITCHED, PITCHED) + (top + (row_off - KSIZE // 2) * PITCH)
        piece = multiply(wide_ref[pl.ds(start, PITCHED), :], weight_of(row_off))
        total = piece if total is None else total + piece
    return jnp.concatenate([total[row * PITCH : row * PITCH + WIDTH] for row in range(MAPS)], axis=0)


def mean_of(own, theirs):
    return (own + theirs) * 0.5


def rows_at(ref, start, rows):
    return ref.at[pl.ds(start, rows), :]


def step_kernel(step, last, split, *refs):
    it = iter(refs)
    take = lambda count: [next(it) for _ in range(count)]
    core_ref = next(it) if last else None
    images_ref, cotangent_ref = take(2)
    packed = step > 0
    own, theirs = (take(2) if packed else take(5)) , (take(2) if packed else take(5))
    held_out = take(4) if packed else []
    outs = take(2) if last else take(2)
    moment_out = take(3)
    norm_moment = next(it)
    (x_ref, upstream_ref, own_ref, theirs_ref, param_ref, moment_ref,
     normed_a, normed_b, hidden_b, wide, wide_t, wide_b, pad, pad_b, mixed_e, weight_e, weight_s, weight_f,
     third, grad_sum, grad_third, work, back, weight_t, arrived, left) = take(26)
    held_ref = next(it) if packed else None
    count, width = third.shape
    blocks = width // LANES
    rows_r, rows_s, rows_e = (ref.shape[0] for ref in moment_out)
    spans = ((0, rows_r), (rows_r, rows_s), (rows_r + rows_s, rows_e))
    bf16 = jnp.bfloat16
    view = lambda ref, part: rows_at(ref, *spans[part])
    pending = {}

    def fetch(name, source, target):
        copy = pltpu.make_async_copy(source, target, arrived.at[len(pending)])
        copy.start()
        pending[name] = copy

    def fetch_part(part):
        source = (lambda sides: view(sides[0], part)) if packed else (lambda sides: sides[part])
        fetch(("own", part), source(own), view(own_ref, part))
        fetch(("theirs", part), source(theirs), view(theirs_ref, part))

    def ready(part):
        pending["own", part].wait()
        pending["theirs", part].wait()

    fetch_part(0)
    for at in range(CHUNKS):
        rows = pl.ds(at * FLAT, FLAT)
        fetch(("x", at), images_ref.at[step, 0, rows, :], rows_at(x_ref, at * FLAT, FLAT))
    fetch_part(1)
    fetch_part(2)
    fetch("upstream", cotangent_ref.at[step, 0], upstream_ref)
    if packed:
        for part in range(3):
            fetch(("held", part), held_out[part], view(held_ref, part))
    stores = []

    def store(source, target):
        copy = pltpu.make_async_copy(source, target, left.at[len(stores)])
        copy.start()
        stores.append(copy)

    def settle(part):
        store(view(moment_ref, part), moment_out[part])
        if not last:
            store(view(param_ref, part), view(outs[0], part))

    if packed:
        rows_of = lambda ref, low: jnp.concatenate([ref[low + at : low + at + 1, :] for at in range(ref.shape[0] // 2)], axis=1)
        half = own[1].shape[0] // 2
        gains = mean_of(rows_of(own[1], 0), rows_of(theirs[1], 0))
        shifts = mean_of(rows_of(own[1], half), rows_of(theirs[1], half))
    else:
        gains = mean_of(own[3][...], theirs[3][...])
        shifts = mean_of(own[4][...], theirs[4][...])
    gain_a, gain_b, gain_c = gains[:, :LANES], gains[:, LANES : 2 * LANES], gains[:, 2 * LANES :]
    shift_a, shift_b, shift_c = shifts[:, :LANES], shifts[:, LANES : 2 * LANES], shifts[:, 2 * LANES :]

    def mixed(part, start, rows):
        span = pl.ds(spans[part][0] + start, rows)
        return mean_of(own_ref[span, :], theirs_ref[span, :])

    def learn(part, start, rows, moment):
        span = pl.ds(spans[part][0] + start, rows)
        if packed:
            moment = MOMENTUM * held_ref[span, :] + moment
        moment_ref[span, :] = moment
        param_ref[span, :] = mixed(part, start, rows) - LEARN_RATE * moment

    pad[...] = jnp.zeros_like(pad)
    pad_b[...] = jnp.zeros_like(pad_b)
    ready(0)
    reduce_w = mixed(0, 0, rows_r).astype(bf16)

    total = zero_row(LANES)
    for at in range(CHUNKS):
        pending["x", at].wait()
        rows = slice(at * FLAT, (at + 1) * FLAT)
        values = matmul(x_ref[rows, :], reduce_w)
        normed_a[rows, :] = values
        total = total + column_sum(values)
    mean, scale_a = statistics(normed_a, total)

    def make_hidden_a(at, carry):
        normed = (normed_a[flat_rows(at), :] - mean) * scale_a
        normed_a[flat_rows(at), :] = normed
        pad_chunk(pad, TOP, at, activate(normed * gain_a + shift_a))
        return carry

    sweep(make_hidden_a)
    shift_columns(pad, wide)

    taps = KSIZE * KSIZE
    ready(1)
    for tap in range(taps):
        weights = mixed(1, tap * LANES, LANES).astype(bf16)
        weight_s[tap * LANES : (tap + 1) * LANES, :] = weights
        other = taps - 1 - tap
        weight_f[other * LANES : (other + 1) * LANES, :] = weights.T

    def make_second(at, total):
        values = conv_chunk(wide, TOP, at, lambda row: weight_s[row * SPAN : (row + 1) * SPAN, :], matmul)
        normed_b[flat_rows(at), :] = values
        return total + column_sum(values)

    mean, scale_b = statistics(normed_b, sweep(make_second, zero_row(LANES)))

    def make_hidden_b(at, carry):
        normed = (normed_b[flat_rows(at), :] - mean) * scale_b
        normed_b[flat_rows(at), :] = normed
        hidden_b[flat_rows(at), :] = activate(normed * gain_b + shift_b).astype(bf16)
        return carry

    sweep(make_hidden_b)

    ready(2)
    mixed_e[...] = mixed(2, 0, rows_e)
    for block in range(blocks):
        weights = mixed_e[pl.ds(block, LANES, stride=blocks), :].astype(bf16)
        weight_e[:, block * LANES : (block + 1) * LANES] = weights
        weight_t[block * LANES : (block + 1) * LANES, :] = weights.T

    def make_third(at, total):
        values = matmul(hidden_b[flat_rows(at), :], weight_e[...])
        third[flat_rows(at), :] = values
        return total + column_sum(values)

    mean, scale_c = statistics(third, sweep(make_third, zero_row(width)))

    def make_sum(at, totals):
        normed = (third[flat_rows(at), :] - mean) * scale_c
        summed = normed * gain_c + shift_c + x_ref[flat_rows(at), :].astype(jnp.float32)
        grad = upstream_ref[flat_rows(at), :].astype(jnp.float32) * act_slope(summed)
        grad_sum[flat_rows(at), :] = grad
        third[flat_rows(at), :] = normed
        return totals[0] + column_sum(grad * normed), totals[1] + column_sum(grad)

    pending["upstream"].wait()
    dgain_c, dshift_c = sweep(make_sum, (zero_row(width), zero_row(width)), False)
    level, slope, factor = dshift_c / count, dgain_c / count, scale_c * gain_c

    def make_back_c(at, totals):
        grad = (grad_sum[flat_rows(at), :] - level - third[flat_rows(at), :] * slope) * factor
        grad = grad.astype(bf16)
        grad_third[flat_rows(at), :] = grad
        normed = normed_b[flat_rows(at), :]
        grad_out = matmul(grad, weight_t[...]) * act_slope(normed * gain_b + shift_b)
        work[flat_rows(at), :] = grad_out
        return totals[0] + column_sum(grad_out * normed), totals[1] + column_sum(grad_out)

    dgain_b, dshift_b = sweep(make_back_c, (zero_row(LANES), zero_row(LANES)))
    grad = matmul(hidden_b[...].T, grad_third[...])
    for block in range(blocks):
        mixed_e[pl.ds(block, LANES, stride=blocks), :] = grad[:, block * LANES : (block + 1) * LANES]
    for part in range(3 if packed else 0):
        pending["held", part].wait()
    learn(2, 0, rows_e, mixed_e[...])
    settle(2)

    level_b, slope_b, factor_b = dshift_b / count, dgain_b / count, scale_b * gain_b

    def make_back_b(at, carry):
        grad = (work[flat_rows(at), :] - level_b - normed_b[flat_rows(at), :] * slope_b) * factor_b
        pad_chunk(pad_b, TOP_BACK, at, grad)
        return carry

    sweep(make_back_b)
    shift_columns(pad_b, wide_b)

    for at in range(ROWS // LANES):
        wide_t[:, at * LANES : (at + 1) * LANES] = wide[at * LANES : (at + 1) * LANES, :].T

    shifted = [
        wide_b[TOP_BACK - row_off * PITCH : TOP_BACK - row_off * PITCH + ROWS, LANES : 2 * LANES]
        for row_off in range(KSIZE)
    ]
    grad = matmul(wide_t[...], jnp.concatenate(shifted, axis=1))
    for row_off in range(KSIZE):
        learn(1, row_off * SPAN, SPAN, grad[:, row_off * LANES : (row_off + 1) * LANES])
    settle(1)

    def make_back_a(at, totals):
        grad = conv_chunk(wide_b, TOP_BACK, at, lambda row: weight_f[row * SPAN : (row + 1) * SPAN, :], matmul)
        normed = normed_a[flat_rows(at), :]
        grad_out = grad * act_slope(normed * gain_a + shift_a)
        work[flat_rows(at), :] = grad_out
        return totals[0] + column_sum(grad_out * normed), totals[1] + column_sum(grad_out)

    dgain_a, dshift_a = sweep(make_back_a, (zero_row(LANES), zero_row(LANES)))
    level_a, slope_a, factor_a = dshift_a / count, dgain_a / count, scale_a * gain_a

    def make_first_grad(at, carry):
        grad = (work[flat_rows(at), :] - level_a - normed_a[flat_rows(at), :] * slope_a) * factor_a
        back[flat_rows(at), :] = grad.astype(bf16)
        return carry

    sweep(make_first_grad)
    grad = matmul(back[...].T, x_ref[...])
    for block in range(blocks):
        learn(0, block * LANES, LANES, grad[:, block * LANES : (block + 1) * LANES].T)
    settle(0)
    grad = jnp.concatenate([dgain_a, dgain_b, dgain_c, dshift_a, dshift_b, dshift_c], axis=1)
    norm = jnp.concatenate([gains, shifts], axis=1)
    if packed:
        grad = MOMENTUM * held_out[3][...] + grad
    norm_moment[...] = grad
    norm = norm - LEARN_RATE * grad
    if not last:
        for at in range(norm.shape[1] // LANES):
            outs[1][at : at + 1, :] = norm[:, at * LANES : (at + 1) * LANES]
        for copy in stores:
            copy.wait()
        return

    kept_ref, sent_ref = outs
    is_odd = jnp.full((1, 1), core_ref[0], jnp.int32) == 1
    pairs, piece_s, piece_e, piece_r, piece_n = split
    at_e = round_up(piece_s + 1, 8)
    at_r = at_e + piece_e

    def place(pair, start, low, high):
        rows = low.shape[0]
        kept_ref[pair, start : start + rows, :] = jnp.where(is_odd, high, low)
        sent_ref[pair, start : start + rows, :] = jnp.where(is_odd, low, high)

    for pair in range(pairs):
        for part, rows, start in ((1, piece_s, 0), (2, piece_e, at_e), (0, piece_r, at_r)):
            first = spans[part][0] + 2 * pair * rows
            place(pair, start, param_ref[first : first + rows, :], param_ref[first + rows : first + 2 * rows, :])
        low, high = [
            jnp.concatenate(
                [norm[:, at * piece_n : (at + 1) * piece_n], jnp.zeros((1, LANES - piece_n), jnp.float32)], axis=1
            )
            for at in (2 * pair, 2 * pair + 1)
        ]
        rest = jnp.zeros((at_e - piece_s - 1, LANES), jnp.float32)
        place(pair, piece_s, jnp.concatenate([low, rest]), jnp.concatenate([high, rest]))
    for copy in stores:
        copy.wait()


def fold_kernel(bits, *refs):
    spot_ref, kept_ref = refs[:2]
    came, outs, total = refs[2 : 2 + bits[0]], refs[2 + bits[0] : -1], refs[-1]
    values = kept_ref[...]
    for ref in came:
        values = values + ref[...]
    total[...] = values
    ways = len(outs)
    for hop, out in enumerate(outs):
        for at in range(out.shape[0]):
            out[at] = total[at * ways + jnp.bitwise_xor(spot_ref[0], hop)]


def mean_kernel(replicas, spans, *refs):
    outs = refs[-len(spans) :]
    kept_ref, came = refs[0], refs[1 : -len(spans)]
    values = kept_ref[0]
    for ref in came:
        values = values + ref[0]
    values = values * (1.0 / replicas)
    for (start, rows), out in zip(spans, outs):
        width = out.shape[0] // rows
        for at in range(rows):
            out[at * width : (at + 1) * width] = values[start + at, :width]


def copy_kernel(source, target, sem):
    copy = pltpu.make_async_copy(source, target, sem)
    copy.start()
    copy.wait()


def pack_kernel(*refs):
    half = len(refs) // 2
    for source, out in zip(refs[:half], refs[half:]):
        if source.shape[0] == 1:
            out[...] = source[...].astype(jnp.bfloat16)
            continue

        def lay(at, carry, source=source, out=out):
            values = source[pl.ds(pl.multiple_of(at * 8, 8), 8), :].astype(jnp.bfloat16)
            base = pl.multiple_of(at * 8 * LANES, 8 * LANES)
            for row in range(8):
                out[0:1, pl.ds(base + row * LANES, LANES)] = values[row : row + 1]
            return carry

        lax.fori_loop(0, source.shape[0] // 8, lay, 0)


def run_kernel(body, name, operands, outs, scratch=(), flops=0, vmem=SMALL_VMEM):
    def parts(entries, is_plain):
        plain = [entry if is_plain(entry) else entry[0] for entry in entries]
        return plain, [pl.BlockSpec(memory_space=pltpu.VMEM if is_plain(entry) else entry[1]) for entry in entries]

    arrays, in_specs = parts(operands, lambda entry: not isinstance(entry, tuple))
    shapes, out_specs = parts(outs, lambda entry: isinstance(entry[0], tuple) and not isinstance(entry[0][0], tuple))
    moved = sum(array.size * array.dtype.itemsize for array in arrays)
    return list(pl.pallas_call(
        body,
        in_specs=in_specs,
        out_specs=out_specs,
        out_shape=[jax.ShapeDtypeStruct(shape, kind) for shape, kind in shapes],
        scratch_shapes=[pltpu.VMEM(*entry) if isinstance(entry, tuple) else entry for entry in scratch],
        compiler_params=pltpu.CompilerParams(vmem_limit_bytes=vmem),
        cost_estimate=pl.CostEstimate(flops=flops, bytes_accessed=moved, transcendentals=0),
        name=name,
    )(*arrays))


def in_hbm(entry):
    return entry, pltpu.HBM


def in_smem(value):
    return value.astype(jnp.int32).reshape(1), pltpu.SMEM


def swap_all(bit, values):
    return [partner_2(member, "dp", bit) for member in values]


def exchange(spot, first_bit, ways, sends):
    replicas = lax.axis_size("dp")
    return [
        lax.ppermute(sent, "dp", [(at, at ^ (hop << first_bit)) for at in range(replicas)])
        for hop, sent in zip(range(1, ways), sends)
    ]


def scatter_mean(kept, sent, split, beside):
    f32 = jnp.float32
    replicas = lax.axis_size("dp")
    levels = replicas.bit_length() - 1
    place = lax.axis_index("dp")
    pairs, piece_s, piece_e, piece_r, piece_n = split
    rows = kept.shape[1]
    came = exchange(place, 0, 2, [sent])
    (kept,) = run_kernel(
        copy_kernel, "copy", [in_hbm(kept)], [(kept.shape, f32)], [pltpu.SemaphoreType.DMA(())]
    )
    came, kept = lax.optimization_barrier((came, kept))
    left, low, done = pairs, 1, []
    while left > 1:
        width = 2 if low == 1 and levels > 2 else 1
        ways = 1 << width
        spot = in_smem((place >> low) % ways)
        kept, *sends = run_kernel(
            functools.partial(fold_kernel, (len(came),)), "fold", [spot, kept] + came,
            [((left // ways, rows, LANES), f32)] * ways, [((left, rows, LANES), f32)],
        )
        came = exchange(place, low, ways, sends)
        if beside:
            work, *beside = beside
            came, ready = lax.optimization_barrier((came, work()))
            done.append(ready)
        left, low = left // ways, low + width
    at_e = round_up(piece_s + 1, 8)
    spans = ((at_e + piece_e, piece_r), (0, piece_s), (at_e, piece_e), (piece_s, 1))
    sizes = [(rows_of * LANES,) for _, rows_of in spans[:3]] + [(piece_n,)]
    mean = run_kernel(
        functools.partial(mean_kernel, replicas, spans), "mean", [kept] + came, [(size, f32) for size in sizes]
    )
    return done + [work() for work in beside], mean


def scatter_mean_any(arrays):
    replicas = lax.axis_size("dp")
    tables = [member.reshape(replicas, -1) for member in arrays]
    pieces = lax.all_to_all(jnp.concatenate(tables, axis=1), "dp", 0, 0, tiled=True)
    mean = jnp.sum(pieces, axis=0) / replicas
    bounds = [sum(table.shape[1] for table in tables[:at]) for at in range(len(tables) + 1)]
    return tuple(mean[low:high] for low, high in zip(bounds[:-1], bounds[1:]))


def shards(images, cotangent, w_reduce, w_spatial, w_expand, norm_gain, norm_bias, round_index):
    f32, bf16 = jnp.float32, jnp.bfloat16
    replicas = lax.axis_size("dp")
    levels = replicas.bit_length() - 1
    steps, _, pixels, in_ch = images.shape
    weights = [member.reshape(-1, LANES) for member in (w_reduce, w_spatial, w_expand)]
    sizes = [(member.shape, f32) for member in weights]
    rows_r, rows_s, rows_e = (member.shape[0] for member in weights)
    rows = rows_r + rows_s + rows_e
    norm_size = 2 * norm_gain.size
    flat_map = ((pixels, LANES), f32)
    wide_map = ((pixels, in_ch), f32)
    whole = ((rows, LANES), f32)
    norm_rows = ((norm_size // LANES, LANES), f32)
    half_map = ((pixels, in_ch), bf16)
    scratch = [
        half_map, half_map, whole, whole, whole, whole,
        flat_map, flat_map, ((pixels, LANES), bf16), ((ROWS, SPAN), bf16), ((SPAN, ROWS), bf16),
        ((ROWS_BACK, SPAN), bf16), ((ROWS + 16, LANES), f32), ((ROWS_BACK + 16, LANES), f32),
        sizes[2], ((LANES, in_ch), bf16), ((rows_s, LANES), bf16), ((rows_s, LANES), bf16),
        wide_map, wide_map, half_map, flat_map, ((pixels, LANES), bf16), ((in_ch, LANES), bf16),
        pltpu.SemaphoreType.DMA((17,)), pltpu.SemaphoreType.DMA((6,)),
    ]
    flops = 6 * pixels * LANES * (2 * in_ch + rows_s)
    fine = replicas > 1 and all(size[0][0] % replicas == 0 for size in sizes)
    split = (replicas // 2, rows_s // replicas, rows_e // replicas, rows_r // replicas, norm_size // replicas)
    half = ((split[0], round_up(split[1] + 1, 8) + split[2] + split[3], LANES), f32)
    params = [weights[1], weights[0], weights[2], norm_gain, norm_bias]
    moments = []
    for step in range(steps):
        branches = [functools.partial(swap_all, bit) for bit in range(levels)]
        theirs = list(lax.switch((round_index[0] + step) % levels, branches, params))
        if step == 0:
            sides = [[in_hbm(side[at]) for at in (1, 0, 2)] + side[3:] for side in (params, theirs)]
        else:
            sides = [[in_hbm(side[0]), side[1]] for side in (params, theirs)]
        operands = [in_hbm(images), in_hbm(cotangent)] + sides[0] + sides[1]
        operands += [in_hbm(member) for member in moments[:3]] + moments[3:]
        moment_outs = [in_hbm(size) for size in sizes] + [((1, norm_size), f32)]
        extra = [whole] if step else []
        if step == steps - 1 and fine:
            core = in_smem(lax.axis_index("dp") % 2)
            kept, sent, *moments = run_kernel(
                functools.partial(step_kernel, step, True, split), "last_step", [core] + operands,
                [half, half] + moment_outs, scratch + extra, flops, VMEM_BYTES,
            )
        else:
            *params, m_r, m_s, m_e, m_n = run_kernel(
                functools.partial(step_kernel, step, False, None), "step", operands,
                [in_hbm(whole), norm_rows] + moment_outs, scratch + extra, flops, VMEM_BYTES,
            )
            moments = [m_r, m_s, m_e, m_n]
    def pack(*which):
        sources = [moments[at] for at in which]
        return run_kernel(pack_kernel, "pack", sources, [((1, member.size), bf16) for member in sources])

    if fine:
        beside = [functools.partial(pack, 0, 1), functools.partial(pack, 2, 3)]
        (first, second), averaged = scatter_mean(kept, sent, split, beside)
        out = first + second
    else:
        flat = [params[0][low:high].reshape(-1) for low, high in ((0, rows_r), (rows_r, rows_r + rows_s), (rows_r + rows_s, rows))]
        out, averaged = pack(0, 1, 2, 3), scatter_mean_any(flat + [params[1].reshape(-1)])
    return tuple(averaged) + tuple(out)


def solution(mesh):
    in_specs = (
        P(None, "dp", None, None),
        P(None, "dp", None, None),
        P("dp", None),
        P("dp", None),
        P("dp", None),
        P("dp", None),
        P("dp", None),
        P(),
    )
    out_specs = (
        P("dp"),
        P("dp"),
        P("dp"),
        P("dp"),
        P("dp", None),
        P("dp", None),
        P("dp", None),
        P("dp", None),
    )
    return jax.shard_map(shards, mesh=mesh, in_specs=in_specs, out_specs=out_specs, check_vma=False)
```

```python
import functools

import jax
import jax.numpy as jnp
from jax import lax
from jax.experimental import pallas as pl
from jax.experimental.pallas import tpu as pltpu
from jax.sharding import PartitionSpec as P

HEIGHT = 28
WIDTH = 28
KSIZE = 3

LEARN_RATE = 0.01
MOMENTUM = 0.9
EPSILON = 1e-05

LANES = 128
PITCH = 32
VMEM_BYTES = 60 * 1024 * 1024
SMALL_VMEM = 8 * 1024 * 1024


def round_up(value, unit):
    return (value + unit - 1) // unit * unit


def partner_2(value, axis, distance):
    mask = 2**distance
    pairs = [(source, source ^ mask) for source in range(lax.axis_size(axis))]
    return lax.ppermute(value, axis, pairs)


def matmul(left, right):
    return jnp.dot(left, right, preferred_element_type=jnp.float32)


def contract_cols(left, right):
    return lax.dot_general(left, right, (((1,), (1,)), ((), ())), preferred_element_type=jnp.float32)


def sigmoid(values):
    return 0.5 * jnp.tanh(0.5 * values) + 0.5


def activate(values):
    return values * sigmoid(values)


def act_slope(values):
    sigma = sigmoid(values)
    return sigma * (1.0 + values * (1.0 - sigma))


def column_sum(values):
    return jnp.sum(values, axis=0, keepdims=True)


MAPS = 4
FLAT = MAPS * WIDTH
PITCHED = MAPS * PITCH
CHUNKS = HEIGHT // MAPS
SPAN = KSIZE * LANES
TOP = PITCH
TOP_BACK = 2 * PITCH
ROWS = round_up(HEIGHT * PITCH + 2 * PITCH, LANES)
ROWS_BACK = ROWS + 2 * PITCH


def flat_rows(at):
    return pl.ds(pl.multiple_of(at * FLAT, FLAT), FLAT)


def zero_row(width):
    return jnp.zeros((1, width), jnp.float32)


def sweep(body, init=0, unroll=True):
    return lax.fori_loop(0, CHUNKS, body, init, unroll=unroll)


def statistics(values_ref, total):
    count, width = values_ref.shape
    mean = total / count

    def add(at, held):
        center = values_ref[flat_rows(at), :] - mean
        return held + column_sum(center * center)

    return mean, lax.rsqrt(sweep(add, zero_row(width), width == LANES) / count + EPSILON)


def pad_chunk(pad_ref, top, at, values):
    for row in range(MAPS):
        start = pl.multiple_of(at * PITCHED, PITCHED) + (8 + top + row * PITCH)
        pad_ref[pl.ds(start, WIDTH), :] = values[row * WIDTH : (row + 1) * WIDTH]


def shift_columns(pad_ref, out_ref):
    rows = out_ref.shape[0]
    for col_off in range(KSIZE):
        start = 8 + col_off - KSIZE // 2
        out_ref[:, col_off * LANES : (col_off + 1) * LANES] = pad_ref[start : start + rows, :].astype(jnp.bfloat16)


def conv_chunk(wide_ref, top, at, weight_of, multiply):
    total = None
    for row_off in range(KSIZE):
        start = pl.multiple_of(at * PITCHED, PITCHED) + (top + (row_off - KSIZE // 2) * PITCH)
        piece = multiply(wide_ref[pl.ds(start, PITCHED), :], weight_of(row_off))
        total = piece if total is None else total + piece
    return jnp.concatenate([total[row * PITCH : row * PITCH + WIDTH] for row in range(MAPS)], axis=0)


def mean_of(own, theirs):
    return (own + theirs) * 0.5


def rows_at(ref, start, rows):
    return ref.at[pl.ds(start, rows), :]


def step_kernel(step, last, split, *refs):
    it = iter(refs)
    take = lambda count: [next(it) for _ in range(count)]
    core_ref = next(it) if last else None
    images_ref, cotangent_ref = take(2)
    packed = step > 0
    own, theirs = (take(2) if packed else take(5)) , (take(2) if packed else take(5))
    held_out = take(2) if packed else []
    outs = take(2) if last else take(2)
    moment_out = next(it)
    norm_moment = next(it)
    own_ref = own[0] if packed else next(it)
    (x_ref, upstream_ref, theirs_ref, param_ref, moment_ref,
     normed_a, normed_b, hidden_b, wide, wide_t, wide_b, pad, pad_b, mixed_e, weight_e, weight_s, weight_f,
     third, grad_sum, grad_third, work, back, weight_t, arrived, left) = take(25)
    held_ref = next(it) if packed else None
    count, width = third.shape
    blocks = width // LANES
    rows_r, rows_s, rows_e = width, weight_s.shape[0], width
    spans = ((0, rows_r), (rows_r, rows_s), (rows_r + rows_s, rows_e))
    bf16 = jnp.bfloat16
    view = lambda ref, part: rows_at(ref, *spans[part])
    pending = {}

    def fetch(name, source, target):
        copy = pltpu.make_async_copy(source, target, arrived.at[len(pending)])
        copy.start()
        pending[name] = copy

    def fetch_part(part):
        fetch(("own", part), own[part], view(own_ref, part))
        fetch(("theirs", part), theirs[part], view(theirs_ref, part))

    def ready(part):
        if not packed:
            pending["own", part].wait()
            pending["theirs", part].wait()
        elif part < 2:
            pending["others" if part else "reduce"].wait()

    fetch("x", images_ref.at[step, 0], x_ref)
    if packed:
        later = rows_s + rows_e
        fetch("reduce", rows_at(theirs[0], 0, rows_r), rows_at(theirs_ref, 0, rows_r))
        fetch("others", rows_at(theirs[0], rows_r, later), rows_at(theirs_ref, rows_r, later))
    else:
        for part in range(3):
            fetch_part(part)
    fetch("upstream", cotangent_ref.at[step, 0], upstream_ref)
    if packed:
        fetch("held", held_out[0], held_ref)
    stores = []

    def store(source, target):
        copy = pltpu.make_async_copy(source, target, left.at[len(stores)])
        copy.start()
        stores.append(copy)

    def settle(start, rows):
        store(rows_at(moment_ref, start, rows), rows_at(moment_out, start, rows))
        if not last:
            store(rows_at(param_ref, start, rows), rows_at(outs[0], start, rows))

    if packed:
        rows_of = lambda ref, low: jnp.concatenate([ref[low + at : low + at + 1, :] for at in range(ref.shape[0] // 2)], axis=1)
        half = own[1].shape[0] // 2
        gains = mean_of(rows_of(own[1], 0), rows_of(theirs[1], 0))
        shifts = mean_of(rows_of(own[1], half), rows_of(theirs[1], half))
    else:
        gains = mean_of(own[3][...], theirs[3][...])
        shifts = mean_of(own[4][...], theirs[4][...])
    gain_a, gain_b, gain_c = gains[:, :LANES], gains[:, LANES : 2 * LANES], gains[:, 2 * LANES :]
    shift_a, shift_b, shift_c = shifts[:, :LANES], shifts[:, LANES : 2 * LANES], shifts[:, 2 * LANES :]

    def mixed(part, start, rows):
        span = pl.ds(spans[part][0] + start, rows)
        return mean_of(own_ref[span, :], theirs_ref[span, :])

    def learn(part, start, rows, moment):
        span = pl.ds(spans[part][0] + start, rows)
        if packed:
            moment = MOMENTUM * held_ref[span, :] + moment
        moment_ref[span, :] = moment
        param_ref[span, :] = mixed(part, start, rows) - LEARN_RATE * moment

    pad[...] = jnp.zeros_like(pad)
    pad_b[...] = jnp.zeros_like(pad_b)
    pending["x"].wait()
    ready(0)
    reduce_w = mixed(0, 0, rows_r).astype(bf16)

    def make_first(at, total):
        values = matmul(x_ref[flat_rows(at), :], reduce_w)
        normed_a[flat_rows(at), :] = values
        return total + column_sum(values)

    mean, scale_a = statistics(normed_a, sweep(make_first, zero_row(LANES)))

    def make_hidden_a(at, carry):
        normed = (normed_a[flat_rows(at), :] - mean) * scale_a
        normed_a[flat_rows(at), :] = normed
        pad_chunk(pad, TOP, at, activate(normed * gain_a + shift_a))
        return carry

    sweep(make_hidden_a)
    shift_columns(pad, wide)

    taps = KSIZE * KSIZE
    ready(1)
    for tap in range(taps):
        weights = mixed(1, tap * LANES, LANES).astype(bf16)
        weight_s[tap * LANES : (tap + 1) * LANES, :] = weights
        other = taps - 1 - tap
        weight_f[other * LANES : (other + 1) * LANES, :] = weights.T

    def make_second(at, total):
        values = conv_chunk(wide, TOP, at, lambda row: weight_s[row * SPAN : (row + 1) * SPAN, :], matmul)
        normed_b[flat_rows(at), :] = values
        return total + column_sum(values)

    mean, scale_b = statistics(normed_b, sweep(make_second, zero_row(LANES)))

    def make_hidden_b(at, carry):
        normed = (normed_b[flat_rows(at), :] - mean) * scale_b
        normed_b[flat_rows(at), :] = normed
        hidden_b[flat_rows(at), :] = activate(normed * gain_b + shift_b).astype(bf16)
        return carry

    sweep(make_hidden_b)

    ready(2)
    mixed_e[...] = mixed(2, 0, rows_e)
    for block in range(blocks):
        weights = mixed_e[pl.ds(block, LANES, stride=blocks), :].astype(bf16)
        weight_e[:, block * LANES : (block + 1) * LANES] = weights
        weight_t[block * LANES : (block + 1) * LANES, :] = weights.T

    def make_third(at, total):
        values = matmul(hidden_b[flat_rows(at), :], weight_e[...])
        third[flat_rows(at), :] = values
        return total + column_sum(values)

    mean, scale_c = statistics(third, sweep(make_third, zero_row(width)))

    def make_sum(at, totals):
        normed = (third[flat_rows(at), :] - mean) * scale_c
        summed = normed * gain_c + shift_c + x_ref[flat_rows(at), :].astype(jnp.float32)
        grad = upstream_ref[flat_rows(at), :].astype(jnp.float32) * act_slope(summed)
        grad_sum[flat_rows(at), :] = grad
        third[flat_rows(at), :] = normed
        return totals[0] + column_sum(grad * normed), totals[1] + column_sum(grad)

    pending["upstream"].wait()
    dgain_c, dshift_c = sweep(make_sum, (zero_row(width), zero_row(width)), False)
    level, slope, factor = dshift_c / count, dgain_c / count, scale_c * gain_c

    def make_back_c(at, totals):
        grad = (grad_sum[flat_rows(at), :] - level - third[flat_rows(at), :] * slope) * factor
        grad = grad.astype(bf16)
        grad_third[flat_rows(at), :] = grad
        normed = normed_b[flat_rows(at), :]
        grad_out = matmul(grad, weight_t[...]) * act_slope(normed * gain_b + shift_b)
        work[flat_rows(at), :] = grad_out
        return totals[0] + column_sum(grad_out * normed), totals[1] + column_sum(grad_out)

    dgain_b, dshift_b = sweep(make_back_c, (zero_row(LANES), zero_row(LANES)))
    grad = matmul(hidden_b[...].T, grad_third[...])
    for block in range(blocks):
        mixed_e[pl.ds(block, LANES, stride=blocks), :] = grad[:, block * LANES : (block + 1) * LANES]
    if packed:
        pending["held"].wait()
    learn(2, 0, rows_e, mixed_e[...])

    level_b, slope_b, factor_b = dshift_b / count, dgain_b / count, scale_b * gain_b

    def make_back_b(at, carry):
        grad = (work[flat_rows(at), :] - level_b - normed_b[flat_rows(at), :] * slope_b) * factor_b
        pad_chunk(pad_b, TOP_BACK, at, grad)
        return carry

    sweep(make_back_b)
    shift_columns(pad_b, wide_b)

    for at in range(ROWS // LANES):
        wide_t[:, at * LANES : (at + 1) * LANES] = wide[at * LANES : (at + 1) * LANES, :].T

    shifted = [
        wide_b[TOP_BACK - row_off * PITCH : TOP_BACK - row_off * PITCH + ROWS, LANES : 2 * LANES]
        for row_off in range(KSIZE)
    ]
    grad = matmul(wide_t[...], jnp.concatenate(shifted, axis=1))
    for row_off in range(KSIZE):
        learn(1, row_off * SPAN, SPAN, grad[:, row_off * LANES : (row_off + 1) * LANES])
    settle(rows_r, rows_s + rows_e)

    def make_back_a(at, totals):
        grad = conv_chunk(wide_b, TOP_BACK, at, lambda row: weight_f[row * SPAN : (row + 1) * SPAN, :], matmul)
        normed = normed_a[flat_rows(at), :]
        grad_out = grad * act_slope(normed * gain_a + shift_a)
        work[flat_rows(at), :] = grad_out
        return totals[0] + column_sum(grad_out * normed), totals[1] + column_sum(grad_out)

    dgain_a, dshift_a = sweep(make_back_a, (zero_row(LANES), zero_row(LANES)))
    level_a, slope_a, factor_a = dshift_a / count, dgain_a / count, scale_a * gain_a

    def make_first_grad(at, carry):
        grad = (work[flat_rows(at), :] - level_a - normed_a[flat_rows(at), :] * slope_a) * factor_a
        back[flat_rows(at), :] = grad.astype(bf16)
        return carry

    sweep(make_first_grad)
    grad = matmul(back[...].T, x_ref[...])
    for block in range(blocks):
        learn(0, block * LANES, LANES, grad[:, block * LANES : (block + 1) * LANES].T)
    settle(0, rows_r)
    grad = jnp.concatenate([dgain_a, dgain_b, dgain_c, dshift_a, dshift_b, dshift_c], axis=1)
    norm = jnp.concatenate([gains, shifts], axis=1)
    if packed:
        grad = MOMENTUM * held_out[1][...] + grad
    norm_moment[...] = grad
    norm = norm - LEARN_RATE * grad
    if not last:
        for at in range(norm.shape[1] // LANES):
            outs[1][at : at + 1, :] = norm[:, at * LANES : (at + 1) * LANES]
        for copy in stores:
            copy.wait()
        return

    kept_ref, sent_ref = outs
    is_odd = jnp.full((1, 1), core_ref[0], jnp.int32) == 1
    pairs, piece_s, piece_e, piece_r, piece_n = split
    at_e = round_up(piece_s + 1, 8)
    at_r = at_e + piece_e

    def place(pair, start, low, high):
        rows = low.shape[0]
        kept_ref[pair, start : start + rows, :] = jnp.where(is_odd, high, low)
        sent_ref[pair, start : start + rows, :] = jnp.where(is_odd, low, high)

    for pair in range(pairs):
        for part, rows, start in ((1, piece_s, 0), (2, piece_e, at_e), (0, piece_r, at_r)):
            first = spans[part][0] + 2 * pair * rows
            place(pair, start, param_ref[first : first + rows, :], param_ref[first + rows : first + 2 * rows, :])
        low, high = [
            jnp.concatenate(
                [norm[:, at * piece_n : (at + 1) * piece_n], jnp.zeros((1, LANES - piece_n), jnp.float32)], axis=1
            )
            for at in (2 * pair, 2 * pair + 1)
        ]
        rest = jnp.zeros((at_e - piece_s - 1, LANES), jnp.float32)
        place(pair, piece_s, jnp.concatenate([low, rest]), jnp.concatenate([high, rest]))
    for copy in stores:
        copy.wait()


def fold_kernel(bits, *refs):
    spot_ref, kept_ref = refs[:2]
    came, outs, total = refs[2 : 2 + bits[0]], refs[2 + bits[0] : -1], refs[-1]
    values = kept_ref[...]
    for ref in came:
        values = values + ref[...]
    total[...] = values
    ways = len(outs)
    for hop, out in enumerate(outs):
        for at in range(out.shape[0]):
            out[at] = total[at * ways + jnp.bitwise_xor(spot_ref[0], hop)]


def mean_kernel(replicas, spans, *refs):
    outs = refs[-len(spans) :]
    kept_ref, came = refs[0], refs[1 : -len(spans)]
    values = kept_ref[0]
    for ref in came:
        values = values + ref[0]
    values = values * (1.0 / replicas)
    for (start, rows), out in zip(spans, outs):
        width = out.shape[0] // rows
        for at in range(rows):
            out[at * width : (at + 1) * width] = values[start + at, :width]


def copy_kernel(source, target, sem):
    copy = pltpu.make_async_copy(source, target, sem)
    copy.start()
    copy.wait()


def pack_kernel(spans, *refs):
    source, outs = refs[0], refs[-len(spans) :]
    for (start, rows), out in zip(spans, outs):
        if rows == 0:
            out[...] = refs[1][...].astype(jnp.bfloat16)
            continue

        def lay(at, carry, start=start, out=out):
            values = source[pl.ds(pl.multiple_of(start + at * 8, 8), 8), :].astype(jnp.bfloat16)
            base = pl.multiple_of(at * 8 * LANES, 8 * LANES)
            for row in range(8):
                out[0:1, pl.ds(base + row * LANES, LANES)] = values[row : row + 1]
            return carry

        lax.fori_loop(0, rows // 8, lay, 0)


def run_kernel(body, name, operands, outs, scratch=(), flops=0, vmem=SMALL_VMEM):
    def parts(entries, is_plain):
        plain = [entry if is_plain(entry) else entry[0] for entry in entries]
        return plain, [pl.BlockSpec(memory_space=pltpu.VMEM if is_plain(entry) else entry[1]) for entry in entries]

    arrays, in_specs = parts(operands, lambda entry: not isinstance(entry, tuple))
    shapes, out_specs = parts(outs, lambda entry: isinstance(entry[0], tuple) and not isinstance(entry[0][0], tuple))
    moved = sum(array.size * array.dtype.itemsize for array in arrays)
    return list(pl.pallas_call(
        body,
        in_specs=in_specs,
        out_specs=out_specs,
        out_shape=[jax.ShapeDtypeStruct(shape, kind) for shape, kind in shapes],
        scratch_shapes=[pltpu.VMEM(*entry) if isinstance(entry, tuple) else entry for entry in scratch],
        compiler_params=pltpu.CompilerParams(vmem_limit_bytes=vmem),
        cost_estimate=pl.CostEstimate(flops=flops, bytes_accessed=moved, transcendentals=0),
        name=name,
    )(*arrays))


def in_hbm(entry):
    return entry, pltpu.HBM


def in_smem(value):
    return value.astype(jnp.int32).reshape(1), pltpu.SMEM


def swap_all(bit, values):
    return [partner_2(member, "dp", bit) for member in values]


def exchange(spot, first_bit, ways, sends):
    replicas = lax.axis_size("dp")
    return [
        lax.ppermute(sent, "dp", [(at, at ^ (hop << first_bit)) for at in range(replicas)])
        for hop, sent in zip(range(1, ways), sends)
    ]


def scatter_mean(kept, sent, split, beside):
    f32 = jnp.float32
    replicas = lax.axis_size("dp")
    levels = replicas.bit_length() - 1
    place = lax.axis_index("dp")
    pairs, piece_s, piece_e, piece_r, piece_n = split
    rows = kept.shape[1]
    came = exchange(place, 0, 2, [sent])
    (kept,) = run_kernel(
        copy_kernel, "copy", [in_hbm(kept)], [(kept.shape, f32)], [pltpu.SemaphoreType.DMA(())]
    )
    came, kept = lax.optimization_barrier((came, kept))
    left, low, done = pairs, 1, []
    while left > 1:
        width = 2 if low == 1 and levels > 2 else 1
        ways = 1 << width
        spot = in_smem((place >> low) % ways)
        kept, *sends = run_kernel(
            functools.partial(fold_kernel, (len(came),)), "fold", [spot, kept] + came,
            [((left // ways, rows, LANES), f32)] * ways, [((left, rows, LANES), f32)],
        )
        came = exchange(place, low, ways, sends)
        if beside:
            work, *beside = beside
            came, ready = lax.optimization_barrier((came, work()))
            done.append(ready)
        left, low = left // ways, low + width
    at_e = round_up(piece_s + 1, 8)
    spans = ((at_e + piece_e, piece_r), (0, piece_s), (at_e, piece_e), (piece_s, 1))
    sizes = [(rows_of * LANES,) for _, rows_of in spans[:3]] + [(piece_n,)]
    mean = run_kernel(
        functools.partial(mean_kernel, replicas, spans), "mean", [kept] + came, [(size, f32) for size in sizes]
    )
    return done + [work() for work in beside], mean


def scatter_mean_any(arrays):
    replicas = lax.axis_size("dp")
    tables = [member.reshape(replicas, -1) for member in arrays]
    pieces = lax.all_to_all(jnp.concatenate(tables, axis=1), "dp", 0, 0, tiled=True)
    mean = jnp.sum(pieces, axis=0) / replicas
    bounds = [sum(table.shape[1] for table in tables[:at]) for at in range(len(tables) + 1)]
    return tuple(mean[low:high] for low, high in zip(bounds[:-1], bounds[1:]))


def shards(images, cotangent, w_reduce, w_spatial, w_expand, norm_gain, norm_bias, round_index):
    f32, bf16 = jnp.float32, jnp.bfloat16
    replicas = lax.axis_size("dp")
    levels = replicas.bit_length() - 1
    steps, _, pixels, in_ch = images.shape
    weights = [member.reshape(-1, LANES) for member in (w_reduce, w_spatial, w_expand)]
    sizes = [(member.shape, f32) for member in weights]
    rows_r, rows_s, rows_e = (member.shape[0] for member in weights)
    rows = rows_r + rows_s + rows_e
    norm_size = 2 * norm_gain.size
    flat_map = ((pixels, LANES), f32)
    wide_map = ((pixels, in_ch), f32)
    whole = ((rows, LANES), f32)
    norm_rows = ((norm_size // LANES, LANES), f32)
    half_map = ((pixels, in_ch), bf16)
    scratch = [
        half_map, half_map, whole, whole, whole,
        flat_map, flat_map, ((pixels, LANES), bf16), ((ROWS, SPAN), bf16), ((SPAN, ROWS), bf16),
        ((ROWS_BACK, SPAN), bf16), ((ROWS + 16, LANES), f32), ((ROWS_BACK + 16, LANES), f32),
        sizes[2], ((LANES, in_ch), bf16), ((rows_s, LANES), bf16), ((rows_s, LANES), bf16),
        wide_map, wide_map, half_map, flat_map, ((pixels, LANES), bf16), ((in_ch, LANES), bf16),
        pltpu.SemaphoreType.DMA((8,)), pltpu.SemaphoreType.DMA((4,)),
    ]
    flops = 6 * pixels * LANES * (2 * in_ch + rows_s)
    fine = replicas > 1 and all(size[0][0] % replicas == 0 for size in sizes)
    split = (replicas // 2, rows_s // replicas, rows_e // replicas, rows_r // replicas, norm_size // replicas)
    half = ((split[0], round_up(split[1] + 1, 8) + split[2] + split[3], LANES), f32)
    params = [weights[1], weights[0], weights[2], norm_gain, norm_bias]
    moments = []
    for step in range(steps):
        branches = [functools.partial(swap_all, bit) for bit in range(levels)]
        theirs = list(lax.switch((round_index[0] + step) % levels, branches, params))
        if step == 0:
            sides = [[in_hbm(side[at]) for at in (1, 0, 2)] + side[3:] for side in (params, theirs)]
        else:
            sides = [params, [in_hbm(theirs[0]), theirs[1]]]
        operands = [in_hbm(images), in_hbm(cotangent)] + sides[0] + sides[1]
        operands += [in_hbm(member) for member in moments[:1]] + moments[1:]
        moment_outs = [in_hbm(whole), ((1, norm_size), f32)]
        scratch_of = scratch + [whole] if step else [whole] + scratch
        if step == steps - 1 and fine:
            core = in_smem(lax.axis_index("dp") % 2)
            kept, sent, *moments = run_kernel(
                functools.partial(step_kernel, step, True, split), "last_step", [core] + operands,
                [half, half] + moment_outs, scratch_of, flops, VMEM_BYTES,
            )
        else:
            *params, moment, norm_moment = run_kernel(
                functools.partial(step_kernel, step, False, None), "step", operands,
                [in_hbm(whole), norm_rows] + moment_outs, scratch_of, flops, VMEM_BYTES,
            )
            moments = [moment, norm_moment]
    def pack(sources, *spans):
        return run_kernel(
            functools.partial(pack_kernel, spans), "pack", sources,
            [((1, span * LANES if span else norm_size), bf16) for _, span in spans],
        )

    span_r, span_s, span_e = (0, rows_r), (rows_r, rows_s), (rows_r + rows_s, rows_e)
    if fine:
        beside = [
            functools.partial(pack, moments[:1], span_r, span_s), functools.partial(pack, moments, span_e, (0, 0))
        ]
        (first, second), averaged = scatter_mean(kept, sent, split, beside)
        out = first + second
    else:
        flat = [params[0][low:high].reshape(-1) for low, high in ((0, rows_r), (rows_r, rows_r + rows_s), (rows_r + rows_s, rows))]
        out, averaged = pack(moments, span_r, span_s, span_e, (0, 0)), scatter_mean_any(flat + [params[1].reshape(-1)])
    return tuple(averaged) + tuple(out)


def solution(mesh):
    in_specs = (
        P(None, "dp", None, None),
        P(None, "dp", None, None),
        P("dp", None),
        P("dp", None),
        P("dp", None),
        P("dp", None),
        P("dp", None),
        P(),
    )
    out_specs = (
        P("dp"),
        P("dp"),
        P("dp"),
        P("dp"),
        P("dp", None),
        P("dp", None),
        P("dp", None),
        P("dp", None),
    )
    return jax.shard_map(shards, mesh=mesh, in_specs=in_specs, out_specs=out_specs, check_vma=False)
```

```python
import functools

import jax
import jax.numpy as jnp
from jax import lax
from jax.experimental import pallas as pl
from jax.experimental.pallas import tpu as pltpu
from jax.sharding import PartitionSpec as P

HEIGHT = 28
WIDTH = 28
KSIZE = 3

LEARN_RATE = 0.01
MOMENTUM = 0.9
EPSILON = 1e-05

LANES = 128
PITCH = 32
VMEM_BYTES = 60 * 1024 * 1024
SMALL_VMEM = 8 * 1024 * 1024


def round_up(value, unit):
    return (value + unit - 1) // unit * unit


def partner_2(value, axis, distance):
    mask = 2**distance
    pairs = [(source, source ^ mask) for source in range(lax.axis_size(axis))]
    return lax.ppermute(value, axis, pairs)


def matmul(left, right):
    return jnp.dot(left, right, preferred_element_type=jnp.float32)


def contract_cols(left, right):
    return lax.dot_general(left, right, (((1,), (1,)), ((), ())), preferred_element_type=jnp.float32)


def sigmoid(values):
    return 0.5 * jnp.tanh(0.5 * values) + 0.5


def activate(values):
    return values * sigmoid(values)


def act_slope(values):
    sigma = sigmoid(values)
    return sigma * (1.0 + values * (1.0 - sigma))


def column_sum(values):
    return jnp.sum(values, axis=0, keepdims=True)


MAPS = 4
FLAT = MAPS * WIDTH
PITCHED = MAPS * PITCH
CHUNKS = HEIGHT // MAPS
SPAN = KSIZE * LANES
TOP = PITCH
TOP_BACK = 2 * PITCH
ROWS = round_up(HEIGHT * PITCH + 2 * PITCH, LANES)
ROWS_BACK = ROWS + 2 * PITCH


def flat_rows(at):
    return pl.ds(pl.multiple_of(at * FLAT, FLAT), FLAT)


def zero_row(width):
    return jnp.zeros((1, width), jnp.float32)


def sweep(body, init=0, unroll=True):
    return lax.fori_loop(0, CHUNKS, body, init, unroll=unroll)


def statistics(values_ref, total):
    count, width = values_ref.shape
    mean = total / count

    def add(at, held):
        center = values_ref[flat_rows(at), :] - mean
        return held + column_sum(center * center)

    return mean, lax.rsqrt(sweep(add, zero_row(width), width == LANES) / count + EPSILON)


def pad_chunk(pad_ref, top, at, values):
    for row in range(MAPS):
        start = pl.multiple_of(at * PITCHED, PITCHED) + (8 + top + row * PITCH)
        pad_ref[pl.ds(start, WIDTH), :] = values[row * WIDTH : (row + 1) * WIDTH]


def shift_columns(pad_ref, out_ref):
    rows = out_ref.shape[0]
    for col_off in range(KSIZE):
        start = 8 + col_off - KSIZE // 2
        out_ref[:, col_off * LANES : (col_off + 1) * LANES] = pad_ref[start : start + rows, :].astype(jnp.bfloat16)


def conv_chunk(wide_ref, top, at, weight_of, multiply):
    total = None
    for row_off in range(KSIZE):
        start = pl.multiple_of(at * PITCHED, PITCHED) + (top + (row_off - KSIZE // 2) * PITCH)
        piece = multiply(wide_ref[pl.ds(start, PITCHED), :], weight_of(row_off))
        total = piece if total is None else total + piece
    return jnp.concatenate([total[row * PITCH : row * PITCH + WIDTH] for row in range(MAPS)], axis=0)


def mean_of(own, theirs):
    return (own + theirs) * 0.5


def rows_at(ref, start, rows):
    return ref.at[pl.ds(start, rows), :]


def step_kernel(step, last, split, *refs):
    it = iter(refs)
    take = lambda count: [next(it) for _ in range(count)]
    core_ref = next(it) if last else None
    images_ref, cotangent_ref = take(2)
    packed = step > 0
    own, theirs = (take(2) if packed else take(5)) , (take(2) if packed else take(5))
    held_out = take(2) if packed else []
    outs = take(2) if last else take(2)
    moment_out = next(it)
    norm_moment = next(it)
    own_ref = own[0] if packed else next(it)
    (x_ref, upstream_ref, theirs_ref, param_ref, moment_ref,
     normed_a, normed_b, hidden_b, wide, wide_t, wide_b, pad, pad_b, mixed_e, weight_e, weight_s, weight_f,
     third, grad_sum, grad_third, work, back, weight_t, arrived, left) = take(25)
    held_ref = next(it) if packed else None
    count, width = third.shape
    blocks = width // LANES
    rows_r, rows_s, rows_e = width, weight_s.shape[0], width
    spans = ((0, rows_r), (rows_r, rows_s), (rows_r + rows_s, rows_e))
    bf16 = jnp.bfloat16
    view = lambda ref, part: rows_at(ref, *spans[part])
    pending = {}

    def fetch(name, source, target):
        copy = pltpu.make_async_copy(source, target, arrived.at[len(pending)])
        copy.start()
        pending[name] = copy

    def fetch_part(part):
        fetch(("own", part), own[part], view(own_ref, part))
        fetch(("theirs", part), theirs[part], view(theirs_ref, part))

    def ready(part):
        if not packed:
            pending["own", part].wait()
            pending["theirs", part].wait()
        elif part < 2:
            pending["others" if part else "reduce"].wait()

    fetch("x", images_ref.at[step, 0], x_ref)
    if packed:
        later = rows_s + rows_e
        fetch("reduce", rows_at(theirs[0], 0, rows_r), rows_at(theirs_ref, 0, rows_r))
        fetch("others", rows_at(theirs[0], rows_r, later), rows_at(theirs_ref, rows_r, later))
    else:
        for part in range(3):
            fetch_part(part)
    fetch("upstream", cotangent_ref.at[step, 0], upstream_ref)
    if packed:
        fetch("held", held_out[0], held_ref)
    stores = []

    def store(source, target):
        copy = pltpu.make_async_copy(source, target, left.at[len(stores)])
        copy.start()
        stores.append(copy)

    def settle(start, rows):
        store(rows_at(moment_ref, start, rows), rows_at(moment_out, start, rows))
        if not last:
            store(rows_at(param_ref, start, rows), rows_at(outs[0], start, rows))

    if packed:
        rows_of = lambda ref, low: jnp.concatenate([ref[low + at : low + at + 1, :] for at in range(ref.shape[0] // 2)], axis=1)
        half = own[1].shape[0] // 2
        gains = mean_of(rows_of(own[1], 0), rows_of(theirs[1], 0))
        shifts = mean_of(rows_of(own[1], half), rows_of(theirs[1], half))
    else:
        gains = mean_of(own[3][...], theirs[3][...])
        shifts = mean_of(own[4][...], theirs[4][...])
    gain_a, gain_b, gain_c = gains[:, :LANES], gains[:, LANES : 2 * LANES], gains[:, 2 * LANES :]
    shift_a, shift_b, shift_c = shifts[:, :LANES], shifts[:, LANES : 2 * LANES], shifts[:, 2 * LANES :]

    def mixed(part, start, rows):
        span = pl.ds(spans[part][0] + start, rows)
        return mean_of(own_ref[span, :], theirs_ref[span, :])

    def learn(part, start, rows, moment):
        span = pl.ds(spans[part][0] + start, rows)
        if packed:
            moment = MOMENTUM * held_ref[span, :] + moment
        moment_ref[span, :] = moment
        param_ref[span, :] = mixed(part, start, rows) - LEARN_RATE * moment

    pad[...] = jnp.zeros_like(pad)
    pad_b[...] = jnp.zeros_like(pad_b)
    pending["x"].wait()
    ready(0)
    reduce_w = mixed(0, 0, rows_r).astype(bf16)

    def make_first(at, total):
        values = matmul(x_ref[flat_rows(at), :], reduce_w)
        normed_a[flat_rows(at), :] = values
        return total + column_sum(values)

    mean, scale_a = statistics(normed_a, sweep(make_first, zero_row(LANES)))

    def make_hidden_a(at, carry):
        normed = (normed_a[flat_rows(at), :] - mean) * scale_a
        normed_a[flat_rows(at), :] = normed
        pad_chunk(pad, TOP, at, activate(normed * gain_a + shift_a))
        return carry

    sweep(make_hidden_a)
    shift_columns(pad, wide)

    taps = KSIZE * KSIZE
    ready(1)
    for tap in range(taps):
        weights = mixed(1, tap * LANES, LANES).astype(bf16)
        weight_s[tap * LANES : (tap + 1) * LANES, :] = weights
        other = taps - 1 - tap
        weight_f[other * LANES : (other + 1) * LANES, :] = weights.T

    def make_second(at, total):
        values = conv_chunk(wide, TOP, at, lambda row: weight_s[row * SPAN : (row + 1) * SPAN, :], matmul)
        normed_b[flat_rows(at), :] = values
        return total + column_sum(values)

    mean, scale_b = statistics(normed_b, sweep(make_second, zero_row(LANES)))

    def make_hidden_b(at, total):
        normed = (normed_b[flat_rows(at), :] - mean) * scale_b
        normed_b[flat_rows(at), :] = normed
        hidden = activate(normed * gain_b + shift_b).astype(bf16)
        hidden_b[flat_rows(at), :] = hidden
        return total + column_sum(hidden.astype(jnp.float32))

    hidden_mean = sweep(make_hidden_b, zero_row(LANES)) / count

    ready(2)
    mixed_e[...] = mixed(2, 0, rows_e)
    for block in range(blocks):
        weights = mixed_e[pl.ds(block, LANES, stride=blocks), :].astype(bf16)
        weight_e[:, block * LANES : (block + 1) * LANES] = weights
        weight_t[block * LANES : (block + 1) * LANES, :] = weights.T

    rows, rest = [], hidden_mean
    for _ in range(3):
        rows.append(rest.astype(bf16).astype(jnp.float32))
        rest = rest - rows[-1]
    rows = jnp.concatenate(rows + [jnp.zeros((13, LANES), jnp.float32)], axis=0).astype(bf16)
    mean = column_sum(matmul(rows, weight_e[...]))

    def make_third(at, total):
        values = matmul(hidden_b[flat_rows(at), :], weight_e[...]) - mean
        third[flat_rows(at), :] = values
        return total + column_sum(values * values)

    scale_c = lax.rsqrt(sweep(make_third, zero_row(width)) / count + EPSILON)

    def make_sum(at, totals):
        normed = third[flat_rows(at), :] * scale_c
        half_sum = 0.5 * (normed * gain_c + (shift_c + x_ref[flat_rows(at), :].astype(jnp.float32)))
        bend = jnp.tanh(half_sum)
        slope = (1.0 + bend) * (1.0 + half_sum * (1.0 - bend))
        grad = upstream_ref[flat_rows(at), :].astype(jnp.float32) * slope
        grad_sum[flat_rows(at), :] = grad
        third[flat_rows(at), :] = normed
        return totals[0] + column_sum(grad * normed), totals[1] + column_sum(grad)

    pending["upstream"].wait()
    dgain_c, dshift_c = [0.5 * total for total in sweep(make_sum, (zero_row(width), zero_row(width)), False)]
    level, slope, factor = 2.0 * dshift_c / count, 2.0 * dgain_c / count, 0.5 * scale_c * gain_c

    def make_back_c(at, totals):
        grad = (grad_sum[flat_rows(at), :] - level - third[flat_rows(at), :] * slope) * factor
        grad = grad.astype(bf16)
        grad_third[flat_rows(at), :] = grad
        normed = normed_b[flat_rows(at), :]
        grad_out = matmul(grad, weight_t[...]) * act_slope(normed * gain_b + shift_b)
        work[flat_rows(at), :] = grad_out
        return totals[0] + column_sum(grad_out * normed), totals[1] + column_sum(grad_out)

    dgain_b, dshift_b = sweep(make_back_c, (zero_row(LANES), zero_row(LANES)))
    grad = matmul(hidden_b[...].T, grad_third[...])
    for block in range(blocks):
        mixed_e[pl.ds(block, LANES, stride=blocks), :] = grad[:, block * LANES : (block + 1) * LANES]
    if packed:
        pending["held"].wait()
    learn(2, 0, rows_e, mixed_e[...])

    level_b, slope_b, factor_b = dshift_b / count, dgain_b / count, scale_b * gain_b

    def make_back_b(at, carry):
        grad = (work[flat_rows(at), :] - level_b - normed_b[flat_rows(at), :] * slope_b) * factor_b
        pad_chunk(pad_b, TOP_BACK, at, grad)
        return carry

    sweep(make_back_b)
    shift_columns(pad_b, wide_b)

    for at in range(ROWS // LANES):
        wide_t[:, at * LANES : (at + 1) * LANES] = wide[at * LANES : (at + 1) * LANES, :].T

    shifted = [
        wide_b[TOP_BACK - row_off * PITCH : TOP_BACK - row_off * PITCH + ROWS, LANES : 2 * LANES]
        for row_off in range(KSIZE)
    ]
    grad = matmul(wide_t[...], jnp.concatenate(shifted, axis=1))
    for row_off in range(KSIZE):
        learn(1, row_off * SPAN, SPAN, grad[:, row_off * LANES : (row_off + 1) * LANES])
    settle(rows_r, rows_s + rows_e)

    def make_back_a(at, totals):
        grad = conv_chunk(wide_b, TOP_BACK, at, lambda row: weight_f[row * SPAN : (row + 1) * SPAN, :], matmul)
        normed = normed_a[flat_rows(at), :]
        grad_out = grad * act_slope(normed * gain_a + shift_a)
        work[flat_rows(at), :] = grad_out
        return totals[0] + column_sum(grad_out * normed), totals[1] + column_sum(grad_out)

    dgain_a, dshift_a = sweep(make_back_a, (zero_row(LANES), zero_row(LANES)))
    level_a, slope_a, factor_a = dshift_a / count, dgain_a / count, scale_a * gain_a

    def make_first_grad(at, carry):
        grad = (work[flat_rows(at), :] - level_a - normed_a[flat_rows(at), :] * slope_a) * factor_a
        back[flat_rows(at), :] = grad.astype(bf16)
        return carry

    sweep(make_first_grad)
    grad = matmul(back[...].T, x_ref[...])
    for block in range(blocks):
        learn(0, block * LANES, LANES, grad[:, block * LANES : (block + 1) * LANES].T)
    settle(0, rows_r)
    grad = jnp.concatenate([dgain_a, dgain_b, dgain_c, dshift_a, dshift_b, dshift_c], axis=1)
    norm = jnp.concatenate([gains, shifts], axis=1)
    if packed:
        grad = MOMENTUM * held_out[1][...] + grad
    norm_moment[...] = grad
    norm = norm - LEARN_RATE * grad
    if not last:
        for at in range(norm.shape[1] // LANES):
            outs[1][at : at + 1, :] = norm[:, at * LANES : (at + 1) * LANES]
        for copy in stores:
            copy.wait()
        return

    kept_ref, sent_ref = outs
    is_odd = jnp.full((1, 1), core_ref[0], jnp.int32) == 1
    pairs, piece_s, piece_e, piece_r, piece_n = split
    at_e = round_up(piece_s + 1, 8)
    at_r = at_e + piece_e

    def place(pair, start, low, high):
        rows = low.shape[0]
        kept_ref[pair, start : start + rows, :] = jnp.where(is_odd, high, low)
        sent_ref[pair, start : start + rows, :] = jnp.where(is_odd, low, high)

    for pair in range(pairs):
        for part, rows, start in ((1, piece_s, 0), (2, piece_e, at_e), (0, piece_r, at_r)):
            first = spans[part][0] + 2 * pair * rows
            place(pair, start, param_ref[first : first + rows, :], param_ref[first + rows : first + 2 * rows, :])
        low, high = [
            jnp.concatenate(
                [norm[:, at * piece_n : (at + 1) * piece_n], jnp.zeros((1, LANES - piece_n), jnp.float32)], axis=1
            )
            for at in (2 * pair, 2 * pair + 1)
        ]
        rest = jnp.zeros((at_e - piece_s - 1, LANES), jnp.float32)
        place(pair, piece_s, jnp.concatenate([low, rest]), jnp.concatenate([high, rest]))
    for copy in stores:
        copy.wait()


def fold_kernel(bits, *refs):
    spot_ref, kept_ref = refs[:2]
    came, outs, total = refs[2 : 2 + bits[0]], refs[2 + bits[0] : -1], refs[-1]
    values = kept_ref[...]
    for ref in came:
        values = values + ref[...]
    total[...] = values
    ways = len(outs)
    for hop, out in enumerate(outs):
        for at in range(out.shape[0]):
            out[at] = total[at * ways + jnp.bitwise_xor(spot_ref[0], hop)]


def mean_kernel(replicas, spans, *refs):
    outs = refs[-len(spans) :]
    kept_ref, came = refs[0], refs[1 : -len(spans)]
    values = kept_ref[0]
    for ref in came:
        values = values + ref[0]
    values = values * (1.0 / replicas)
    for (start, rows), out in zip(spans, outs):
        width = out.shape[0] // rows
        for at in range(rows):
            out[at * width : (at + 1) * width] = values[start + at, :width]


def copy_kernel(source, target, sem):
    copy = pltpu.make_async_copy(source, target, sem)
    copy.start()
    copy.wait()


def pack_kernel(spans, *refs):
    source, outs = refs[0], refs[-len(spans) :]
    for (start, rows), out in zip(spans, outs):
        if rows == 0:
            out[...] = refs[1][...].astype(jnp.bfloat16)
            continue

        def lay(at, carry, start=start, out=out):
            base = pl.multiple_of(at * 16, 16)
            for row in range(16):
                values = source[pl.ds(start + base + row, 1), :].astype(jnp.bfloat16)
                out[0:1, pl.ds(pl.multiple_of((base + row) * LANES, LANES), LANES)] = values
            return carry

        lax.fori_loop(0, rows // 16, lay, 0)


def run_kernel(body, name, operands, outs, scratch=(), flops=0, vmem=SMALL_VMEM):
    def parts(entries, is_plain):
        plain = [entry if is_plain(entry) else entry[0] for entry in entries]
        return plain, [pl.BlockSpec(memory_space=pltpu.VMEM if is_plain(entry) else entry[1]) for entry in entries]

    arrays, in_specs = parts(operands, lambda entry: not isinstance(entry, tuple))
    shapes, out_specs = parts(outs, lambda entry: isinstance(entry[0], tuple) and not isinstance(entry[0][0], tuple))
    moved = sum(array.size * array.dtype.itemsize for array in arrays)
    return list(pl.pallas_call(
        body,
        in_specs=in_specs,
        out_specs=out_specs,
        out_shape=[jax.ShapeDtypeStruct(shape, kind) for shape, kind in shapes],
        scratch_shapes=[pltpu.VMEM(*entry) if isinstance(entry, tuple) else entry for entry in scratch],
        compiler_params=pltpu.CompilerParams(vmem_limit_bytes=vmem),
        cost_estimate=pl.CostEstimate(flops=flops, bytes_accessed=moved, transcendentals=0),
        name=name,
    )(*arrays))


def in_hbm(entry):
    return entry, pltpu.HBM


def in_smem(value):
    return value.astype(jnp.int32).reshape(1), pltpu.SMEM


def swap_all(bit, values):
    return [partner_2(member, "dp", bit) for member in values]


def exchange(spot, first_bit, ways, sends):
    replicas = lax.axis_size("dp")
    return [
        lax.ppermute(sent, "dp", [(at, at ^ (hop << first_bit)) for at in range(replicas)])
        for hop, sent in zip(range(1, ways), sends)
    ]


def scatter_mean(kept, sent, split, beside):
    f32 = jnp.float32
    replicas = lax.axis_size("dp")
    levels = replicas.bit_length() - 1
    place = lax.axis_index("dp")
    pairs, piece_s, piece_e, piece_r, piece_n = split
    rows = kept.shape[1]
    came = exchange(place, 0, 2, [sent])
    (kept,) = run_kernel(
        copy_kernel, "copy", [in_hbm(kept)], [(kept.shape, f32)], [pltpu.SemaphoreType.DMA(())]
    )
    came, kept = lax.optimization_barrier((came, kept))
    left, low, done = pairs, 1, []
    while left > 1:
        width = 2 if low == 1 and levels > 2 else 1
        ways = 1 << width
        spot = in_smem((place >> low) % ways)
        kept, *sends = run_kernel(
            functools.partial(fold_kernel, (len(came),)), "fold", [spot, kept] + came,
            [((left // ways, rows, LANES), f32)] * ways, [((left, rows, LANES), f32)],
        )
        came = exchange(place, low, ways, sends)
        if beside:
            work, *beside = beside
            came, ready = lax.optimization_barrier((came, work()))
            done.append(ready)
        left, low = left // ways, low + width
    at_e = round_up(piece_s + 1, 8)
    spans = ((at_e + piece_e, piece_r), (0, piece_s), (at_e, piece_e), (piece_s, 1))
    sizes = [(rows_of * LANES,) for _, rows_of in spans[:3]] + [(piece_n,)]
    mean = run_kernel(
        functools.partial(mean_kernel, replicas, spans), "mean", [kept] + came, [(size, f32) for size in sizes]
    )
    return done + [work() for work in beside], mean


def scatter_mean_any(arrays):
    replicas = lax.axis_size("dp")
    tables = [member.reshape(replicas, -1) for member in arrays]
    pieces = lax.all_to_all(jnp.concatenate(tables, axis=1), "dp", 0, 0, tiled=True)
    mean = jnp.sum(pieces, axis=0) / replicas
    bounds = [sum(table.shape[1] for table in tables[:at]) for at in range(len(tables) + 1)]
    return tuple(mean[low:high] for low, high in zip(bounds[:-1], bounds[1:]))


def shards(images, cotangent, w_reduce, w_spatial, w_expand, norm_gain, norm_bias, round_index):
    f32, bf16 = jnp.float32, jnp.bfloat16
    replicas = lax.axis_size("dp")
    levels = replicas.bit_length() - 1
    steps, _, pixels, in_ch = images.shape
    weights = [member.reshape(-1, LANES) for member in (w_reduce, w_spatial, w_expand)]
    sizes = [(member.shape, f32) for member in weights]
    rows_r, rows_s, rows_e = (member.shape[0] for member in weights)
    rows = rows_r + rows_s + rows_e
    norm_size = 2 * norm_gain.size
    flat_map = ((pixels, LANES), f32)
    wide_map = ((pixels, in_ch), f32)
    whole = ((rows, LANES), f32)
    norm_rows = ((norm_size // LANES, LANES), f32)
    half_map = ((pixels, in_ch), bf16)
    scratch = [
        half_map, half_map, whole, whole, whole,
        flat_map, flat_map, ((pixels, LANES), bf16), ((ROWS, SPAN), bf16), ((SPAN, ROWS), bf16),
        ((ROWS_BACK, SPAN), bf16), ((ROWS + 16, LANES), f32), ((ROWS_BACK + 16, LANES), f32),
        sizes[2], ((LANES, in_ch), bf16), ((rows_s, LANES), bf16), ((rows_s, LANES), bf16),
        wide_map, wide_map, half_map, flat_map, ((pixels, LANES), bf16), ((in_ch, LANES), bf16),
        pltpu.SemaphoreType.DMA((8,)), pltpu.SemaphoreType.DMA((4,)),
    ]
    flops = 6 * pixels * LANES * (2 * in_ch + rows_s)
    fine = replicas > 1 and all(size[0][0] % replicas == 0 for size in sizes)
    split = (replicas // 2, rows_s // replicas, rows_e // replicas, rows_r // replicas, norm_size // replicas)
    half = ((split[0], round_up(split[1] + 1, 8) + split[2] + split[3], LANES), f32)
    params = [weights[1], weights[0], weights[2], norm_gain, norm_bias]
    moments = []
    for step in range(steps):
        branches = [functools.partial(swap_all, bit) for bit in range(levels)]
        theirs = list(lax.switch((round_index[0] + step) % levels, branches, params))
        if step == 0:
            sides = [[in_hbm(side[at]) for at in (1, 0, 2)] + side[3:] for side in (params, theirs)]
        else:
            sides = [params, [in_hbm(theirs[0]), theirs[1]]]
        operands = [in_hbm(images), in_hbm(cotangent)] + sides[0] + sides[1]
        operands += [in_hbm(member) for member in moments[:1]] + moments[1:]
        moment_outs = [in_hbm(whole), ((1, norm_size), f32)]
        scratch_of = scratch + [whole] if step else [whole] + scratch
        if step == steps - 1 and fine:
            core = in_smem(lax.axis_index("dp") % 2)
            kept, sent, *moments = run_kernel(
                functools.partial(step_kernel, step, True, split), "last_step", [core] + operands,
                [half, half] + moment_outs, scratch_of, flops, VMEM_BYTES,
            )
        else:
            *params, moment, norm_moment = run_kernel(
                functools.partial(step_kernel, step, False, None), "step", operands,
                [in_hbm(whole), norm_rows] + moment_outs, scratch_of, flops, VMEM_BYTES,
            )
            moments = [moment, norm_moment]
    def pack(sources, *spans):
        return run_kernel(
            functools.partial(pack_kernel, spans), "pack", sources,
            [((1, span * LANES if span else norm_size), bf16) for _, span in spans],
        )

    span_r, span_s, span_e = (0, rows_r), (rows_r, rows_s), (rows_r + rows_s, rows_e)
    if fine:
        beside = [
            functools.partial(pack, moments[:1], span_r, span_s), functools.partial(pack, moments, span_e, (0, 0))
        ]
        (first, second), averaged = scatter_mean(kept, sent, split, beside)
        out = first + second
    else:
        flat = [params[0][low:high].reshape(-1) for low, high in ((0, rows_r), (rows_r, rows_r + rows_s), (rows_r + rows_s, rows))]
        out, averaged = pack(moments, span_r, span_s, span_e, (0, 0)), scatter_mean_any(flat + [params[1].reshape(-1)])
    return tuple(averaged) + tuple(out)


def solution(mesh):
    in_specs = (
        P(None, "dp", None, None),
        P(None, "dp", None, None),
        P("dp", None),
        P("dp", None),
        P("dp", None),
        P("dp", None),
        P("dp", None),
        P(),
    )
    out_specs = (
        P("dp"),
        P("dp"),
        P("dp"),
        P("dp"),
        P("dp", None),
        P("dp", None),
        P("dp", None),
        P("dp", None),
    )
    return jax.shard_map(shards, mesh=mesh, in_specs=in_specs, out_specs=out_specs, check_vma=False)
```

```python
import functools

import jax
import jax.numpy as jnp
from jax import lax
from jax.experimental import pallas as pl
from jax.experimental.pallas import tpu as pltpu
from jax.sharding import PartitionSpec as P

HEIGHT = 28
WIDTH = 28
KSIZE = 3

LEARN_RATE = 0.01
MOMENTUM = 0.9
EPSILON = 1e-05

LANES = 128
PITCH = 32
VMEM_BYTES = 60 * 1024 * 1024
SMALL_VMEM = 8 * 1024 * 1024


def round_up(value, unit):
    return (value + unit - 1) // unit * unit


def partner_2(value, axis, distance):
    mask = 2**distance
    pairs = [(source, source ^ mask) for source in range(lax.axis_size(axis))]
    return lax.ppermute(value, axis, pairs)


def matmul(left, right):
    return jnp.dot(left, right, preferred_element_type=jnp.float32)


def contract_cols(left, right):
    return lax.dot_general(left, right, (((1,), (1,)), ((), ())), preferred_element_type=jnp.float32)


def activate_half(half):
    return half * (1.0 + jnp.tanh(half))


def twice_slope(half):
    bend = jnp.tanh(half)
    return (1.0 + bend) * (1.0 + half * (1.0 - bend))


def column_sum(values):
    return jnp.sum(values, axis=0, keepdims=True)


MAPS = 4
FLAT = MAPS * WIDTH
PITCHED = MAPS * PITCH
CHUNKS = HEIGHT // MAPS
SPAN = KSIZE * LANES
TOP = PITCH
TOP_BACK = 2 * PITCH
ROWS = round_up(HEIGHT * PITCH + 2 * PITCH, LANES)
ROWS_BACK = ROWS + 2 * PITCH


def flat_rows(at):
    return pl.ds(pl.multiple_of(at * FLAT, FLAT), FLAT)


def zero_row(width):
    return jnp.zeros((1, width), jnp.float32)


def sweep(body, init=0, unroll=True):
    return lax.fori_loop(0, CHUNKS, body, init, unroll=unroll)


def fold_rows(values):
    rows, width = values.shape
    return jnp.sum(values.reshape(rows // 8, 8, width), axis=0)


def zero_rows(width):
    return jnp.zeros((8, width), jnp.float32)


def statistics(values_ref, total):
    count, width = values_ref.shape
    mean = column_sum(total) / count

    def add(at, held):
        center = values_ref[flat_rows(at), :] - mean
        return held + fold_rows(center * center)

    return mean, lax.rsqrt(column_sum(sweep(add, zero_rows(width))) / count + EPSILON)


def pad_chunk(pad_ref, top, at, values):
    for row in range(MAPS):
        start = pl.multiple_of(at * PITCHED, PITCHED) + (8 + top + row * PITCH)
        pad_ref[pl.ds(start, WIDTH), :] = values[row * WIDTH : (row + 1) * WIDTH]


def shift_columns(pad_ref, out_ref):
    rows = out_ref.shape[0]
    for col_off in range(KSIZE):
        start = 8 + col_off - KSIZE // 2
        out_ref[:, col_off * LANES : (col_off + 1) * LANES] = pad_ref[start : start + rows, :].astype(jnp.bfloat16)


def conv_chunk(wide_ref, top, at, weight_of, multiply):
    total = None
    for row_off in range(KSIZE):
        start = pl.multiple_of(at * PITCHED, PITCHED) + (top + (row_off - KSIZE // 2) * PITCH)
        piece = multiply(wide_ref[pl.ds(start, PITCHED), :], weight_of(row_off))
        total = piece if total is None else total + piece
    return jnp.concatenate([total[row * PITCH : row * PITCH + WIDTH] for row in range(MAPS)], axis=0)


def mean_of(own, theirs):
    return (own + theirs) * 0.5


def rows_at(ref, start, rows):
    return ref.at[pl.ds(start, rows), :]


def step_kernel(step, last, split, *refs):
    it = iter(refs)
    take = lambda count: [next(it) for _ in range(count)]
    core_ref = next(it) if last else None
    images_ref, cotangent_ref = take(2)
    packed = step > 0
    own, theirs = (take(2) if packed else take(5)) , (take(2) if packed else take(5))
    held_out = take(2) if packed else []
    outs = take(2) if last else take(2)
    moment_out = next(it)
    norm_moment = next(it)
    own_ref = own[0] if packed else next(it)
    (x_ref, upstream_ref, theirs_ref, param_ref, moment_ref,
     normed_a, normed_b, hidden_b, wide, wide_t, wide_b, pad, pad_b, mixed_e, weight_e, weight_s, weight_f,
     third, grad_sum, grad_third, work, back, weight_t, arrived, left) = take(25)
    held_ref = next(it) if packed else None
    count, width = third.shape
    blocks = width // LANES
    rows_r, rows_s, rows_e = width, weight_s.shape[0], width
    spans = ((0, rows_r), (rows_r, rows_s), (rows_r + rows_s, rows_e))
    bf16 = jnp.bfloat16
    view = lambda ref, part: rows_at(ref, *spans[part])
    pending = {}

    def fetch(name, source, target):
        copy = pltpu.make_async_copy(source, target, arrived.at[len(pending)])
        copy.start()
        pending[name] = copy

    def fetch_part(part):
        fetch(("own", part), own[part], view(own_ref, part))
        fetch(("theirs", part), theirs[part], view(theirs_ref, part))

    def ready(part):
        if not packed:
            pending["own", part].wait()
            pending["theirs", part].wait()
        elif part < 2:
            pending["others" if part else "reduce"].wait()

    fetch("x", images_ref.at[step, 0], x_ref)
    if packed:
        later = rows_s + rows_e
        fetch("reduce", rows_at(theirs[0], 0, rows_r), rows_at(theirs_ref, 0, rows_r))
        fetch("others", rows_at(theirs[0], rows_r, later), rows_at(theirs_ref, rows_r, later))
    else:
        for part in range(3):
            fetch_part(part)
    fetch("upstream", cotangent_ref.at[step, 0], upstream_ref)
    if packed:
        fetch("held", held_out[0], held_ref)
    stores = []

    def store(source, target):
        copy = pltpu.make_async_copy(source, target, left.at[len(stores)])
        copy.start()
        stores.append(copy)

    def settle(start, rows):
        store(rows_at(moment_ref, start, rows), rows_at(moment_out, start, rows))
        if not last:
            store(rows_at(param_ref, start, rows), rows_at(outs[0], start, rows))

    if packed:
        rows_of = lambda ref, low: jnp.concatenate([ref[low + at : low + at + 1, :] for at in range(ref.shape[0] // 2)], axis=1)
        half = own[1].shape[0] // 2
        gains = mean_of(rows_of(own[1], 0), rows_of(theirs[1], 0))
        shifts = mean_of(rows_of(own[1], half), rows_of(theirs[1], half))
    else:
        gains = mean_of(own[3][...], theirs[3][...])
        shifts = mean_of(own[4][...], theirs[4][...])
    gain_a, gain_b, gain_c = gains[:, :LANES], gains[:, LANES : 2 * LANES], gains[:, 2 * LANES :]
    shift_a, shift_b, shift_c = shifts[:, :LANES], shifts[:, LANES : 2 * LANES], shifts[:, 2 * LANES :]

    half_a, half_b = (0.5 * gain_a, 0.5 * shift_a), (0.5 * gain_b, 0.5 * shift_b)

    def mixed(part, start, rows):
        span = pl.ds(spans[part][0] + start, rows)
        return mean_of(own_ref[span, :], theirs_ref[span, :])

    def learn(part, start, rows, moment):
        span = pl.ds(spans[part][0] + start, rows)
        if packed:
            moment = MOMENTUM * held_ref[span, :] + moment
        moment_ref[span, :] = moment
        param_ref[span, :] = mixed(part, start, rows) - LEARN_RATE * moment

    pad[...] = jnp.zeros_like(pad)
    pad_b[...] = jnp.zeros_like(pad_b)
    pending["x"].wait()
    ready(0)
    reduce_w = mixed(0, 0, rows_r).astype(bf16)

    def make_first(at, total):
        values = matmul(x_ref[flat_rows(at), :], reduce_w)
        normed_a[flat_rows(at), :] = values
        return total + fold_rows(values)

    mean, scale_a = statistics(normed_a, sweep(make_first, zero_rows(LANES)))

    def make_hidden_a(at, carry):
        normed = (normed_a[flat_rows(at), :] - mean) * scale_a
        normed_a[flat_rows(at), :] = normed
        pad_chunk(pad, TOP, at, activate_half(normed * half_a[0] + half_a[1]))
        return carry

    sweep(make_hidden_a)
    shift_columns(pad, wide)

    taps = KSIZE * KSIZE
    ready(1)
    for tap in range(taps):
        weights = mixed(1, tap * LANES, LANES).astype(bf16)
        weight_s[tap * LANES : (tap + 1) * LANES, :] = weights
        other = taps - 1 - tap
        weight_f[other * LANES : (other + 1) * LANES, :] = weights.T

    def make_second(at, total):
        values = conv_chunk(wide, TOP, at, lambda row: weight_s[row * SPAN : (row + 1) * SPAN, :], matmul)
        normed_b[flat_rows(at), :] = values
        return total + fold_rows(values)

    mean, scale_b = statistics(normed_b, sweep(make_second, zero_rows(LANES)))

    def make_hidden_b(at, total):
        normed = (normed_b[flat_rows(at), :] - mean) * scale_b
        normed_b[flat_rows(at), :] = normed
        hidden = activate_half(normed * half_b[0] + half_b[1]).astype(bf16)
        hidden_b[flat_rows(at), :] = hidden
        return total + fold_rows(hidden.astype(jnp.float32))

    hidden_mean = column_sum(sweep(make_hidden_b, zero_rows(LANES))) / count

    ready(2)
    mixed_e[...] = mixed(2, 0, rows_e)
    for block in range(blocks):
        weights = mixed_e[pl.ds(block, LANES, stride=blocks), :].astype(bf16)
        weight_e[:, block * LANES : (block + 1) * LANES] = weights
        weight_t[block * LANES : (block + 1) * LANES, :] = weights.T

    rows, rest = [], hidden_mean
    for _ in range(3):
        rows.append(rest.astype(bf16).astype(jnp.float32))
        rest = rest - rows[-1]
    rows = jnp.concatenate(rows + [jnp.zeros((13, LANES), jnp.float32)], axis=0).astype(bf16)
    mean = column_sum(matmul(rows, weight_e[...]))

    def make_third(at, total):
        values = matmul(hidden_b[flat_rows(at), :], weight_e[...]) - mean
        third[flat_rows(at), :] = values
        return total + fold_rows(values * values)

    scale_c = lax.rsqrt(column_sum(sweep(make_third, zero_rows(width))) / count + EPSILON)
    stretch = scale_c * gain_c

    def make_sum(at, totals):
        values = third[flat_rows(at), :]
        half = 0.5 * (values * stretch + (shift_c + x_ref[flat_rows(at), :].astype(jnp.float32)))
        grad = upstream_ref[flat_rows(at), :].astype(jnp.float32) * twice_slope(half)
        grad_sum[flat_rows(at), :] = grad
        return totals[0] + fold_rows(grad * values), totals[1] + fold_rows(grad)

    pending["upstream"].wait()
    totals = sweep(make_sum, (zero_rows(width), zero_rows(width)), False)
    dgain_c, dshift_c = 0.5 * scale_c * column_sum(totals[0]), 0.5 * column_sum(totals[1])
    level, slope, factor = 2.0 * dshift_c / count, 2.0 * scale_c * dgain_c / count, 0.5 * stretch

    def make_back_c(at, totals):
        grad = (grad_sum[flat_rows(at), :] - level - third[flat_rows(at), :] * slope) * factor
        grad = grad.astype(bf16)
        grad_third[flat_rows(at), :] = grad
        normed = normed_b[flat_rows(at), :]
        grad_out = matmul(grad, weight_t[...]) * twice_slope(normed * half_b[0] + half_b[1])
        work[flat_rows(at), :] = grad_out
        return totals[0] + fold_rows(grad_out * normed), totals[1] + fold_rows(grad_out)

    dgain_b, dshift_b = [0.5 * column_sum(total) for total in sweep(make_back_c, (zero_rows(LANES), zero_rows(LANES)))]
    grad = matmul(hidden_b[...].T, grad_third[...])
    for block in range(blocks):
        mixed_e[pl.ds(block, LANES, stride=blocks), :] = grad[:, block * LANES : (block + 1) * LANES]
    if packed:
        pending["held"].wait()
    learn(2, 0, rows_e, mixed_e[...])

    level_b, slope_b, factor_b = 2.0 * dshift_b / count, 2.0 * dgain_b / count, 0.5 * scale_b * gain_b

    def make_back_b(at, carry):
        grad = (work[flat_rows(at), :] - level_b - normed_b[flat_rows(at), :] * slope_b) * factor_b
        pad_chunk(pad_b, TOP_BACK, at, grad)
        return carry

    sweep(make_back_b)
    shift_columns(pad_b, wide_b)

    for at in range(ROWS // LANES):
        wide_t[:, at * LANES : (at + 1) * LANES] = wide[at * LANES : (at + 1) * LANES, :].T

    shifted = [
        wide_b[TOP_BACK - row_off * PITCH : TOP_BACK - row_off * PITCH + ROWS, LANES : 2 * LANES]
        for row_off in range(KSIZE)
    ]
    grad = matmul(wide_t[...], jnp.concatenate(shifted, axis=1))
    for row_off in range(KSIZE):
        learn(1, row_off * SPAN, SPAN, grad[:, row_off * LANES : (row_off + 1) * LANES])
    settle(rows_r, rows_s + rows_e)

    def make_back_a(at, totals):
        grad = conv_chunk(wide_b, TOP_BACK, at, lambda row: weight_f[row * SPAN : (row + 1) * SPAN, :], matmul)
        normed = normed_a[flat_rows(at), :]
        grad_out = grad * twice_slope(normed * half_a[0] + half_a[1])
        work[flat_rows(at), :] = grad_out
        return totals[0] + fold_rows(grad_out * normed), totals[1] + fold_rows(grad_out)

    dgain_a, dshift_a = [0.5 * column_sum(total) for total in sweep(make_back_a, (zero_rows(LANES), zero_rows(LANES)))]
    level_a, slope_a, factor_a = 2.0 * dshift_a / count, 2.0 * dgain_a / count, 0.5 * scale_a * gain_a

    def make_first_grad(at, carry):
        grad = (work[flat_rows(at), :] - level_a - normed_a[flat_rows(at), :] * slope_a) * factor_a
        back[flat_rows(at), :] = grad.astype(bf16)
        return carry

    sweep(make_first_grad)
    grad = matmul(back[...].T, x_ref[...])
    for block in range(blocks):
        learn(0, block * LANES, LANES, grad[:, block * LANES : (block + 1) * LANES].T)
    settle(0, rows_r)
    grad = jnp.concatenate([dgain_a, dgain_b, dgain_c, dshift_a, dshift_b, dshift_c], axis=1)
    norm = jnp.concatenate([gains, shifts], axis=1)
    if packed:
        grad = MOMENTUM * held_out[1][...] + grad
    norm_moment[...] = grad
    norm = norm - LEARN_RATE * grad
    if not last:
        for at in range(norm.shape[1] // LANES):
            outs[1][at : at + 1, :] = norm[:, at * LANES : (at + 1) * LANES]
        for copy in stores:
            copy.wait()
        return

    kept_ref, sent_ref = outs
    is_odd = jnp.full((1, 1), core_ref[0], jnp.int32) == 1
    pairs, piece_s, piece_e, piece_r, piece_n = split
    at_e = round_up(piece_s + 1, 8)
    at_r = at_e + piece_e

    def place(pair, start, low, high):
        rows = low.shape[0]
        kept_ref[pair, start : start + rows, :] = jnp.where(is_odd, high, low)
        sent_ref[pair, start : start + rows, :] = jnp.where(is_odd, low, high)

    for pair in range(pairs):
        for part, rows, start in ((1, piece_s, 0), (2, piece_e, at_e), (0, piece_r, at_r)):
            first = spans[part][0] + 2 * pair * rows
            place(pair, start, param_ref[first : first + rows, :], param_ref[first + rows : first + 2 * rows, :])
        low, high = [
            jnp.concatenate(
                [norm[:, at * piece_n : (at + 1) * piece_n], jnp.zeros((1, LANES - piece_n), jnp.float32)], axis=1
            )
            for at in (2 * pair, 2 * pair + 1)
        ]
        rest = jnp.zeros((at_e - piece_s - 1, LANES), jnp.float32)
        place(pair, piece_s, jnp.concatenate([low, rest]), jnp.concatenate([high, rest]))
    for copy in stores:
        copy.wait()


def fold_kernel(bits, *refs):
    spot_ref, kept_ref = refs[:2]
    came, outs, total = refs[2 : 2 + bits[0]], refs[2 + bits[0] : -1], refs[-1]
    values = kept_ref[...]
    for ref in came:
        values = values + ref[...]
    total[...] = values
    ways = len(outs)
    for hop, out in enumerate(outs):
        for at in range(out.shape[0]):
            out[at] = total[at * ways + jnp.bitwise_xor(spot_ref[0], hop)]


def mean_kernel(replicas, spans, *refs):
    outs = refs[-len(spans) :]
    kept_ref, came = refs[0], refs[1 : -len(spans)]
    values = kept_ref[0]
    for ref in came:
        values = values + ref[0]
    values = values * (1.0 / replicas)
    for (start, rows), out in zip(spans, outs):
        width = out.shape[0] // rows
        for at in range(rows):
            out[at * width : (at + 1) * width] = values[start + at, :width]


def copy_kernel(source, target, sem):
    copy = pltpu.make_async_copy(source, target, sem)
    copy.start()
    copy.wait()


def pack_kernel(spans, *refs):
    source, outs = refs[0], refs[-len(spans) :]
    for (start, rows), out in zip(spans, outs):
        if rows == 0:
            out[...] = refs[1][...].astype(jnp.bfloat16)
            continue

        def lay(at, carry, start=start, out=out):
            base = pl.multiple_of(at * 16, 16)
            for row in range(16):
                values = source[pl.ds(start + base + row, 1), :].astype(jnp.bfloat16)
                out[0:1, pl.ds(pl.multiple_of((base + row) * LANES, LANES), LANES)] = values
            return carry

        lax.fori_loop(0, rows // 16, lay, 0)


def run_kernel(body, name, operands, outs, scratch=(), flops=0, vmem=SMALL_VMEM):
    def parts(entries, is_plain):
        plain = [entry if is_plain(entry) else entry[0] for entry in entries]
        return plain, [pl.BlockSpec(memory_space=pltpu.VMEM if is_plain(entry) else entry[1]) for entry in entries]

    arrays, in_specs = parts(operands, lambda entry: not isinstance(entry, tuple))
    shapes, out_specs = parts(outs, lambda entry: isinstance(entry[0], tuple) and not isinstance(entry[0][0], tuple))
    moved = sum(array.size * array.dtype.itemsize for array in arrays)
    return list(pl.pallas_call(
        body,
        in_specs=in_specs,
        out_specs=out_specs,
        out_shape=[jax.ShapeDtypeStruct(shape, kind) for shape, kind in shapes],
        scratch_shapes=[pltpu.VMEM(*entry) if isinstance(entry, tuple) else entry for entry in scratch],
        compiler_params=pltpu.CompilerParams(vmem_limit_bytes=vmem),
        cost_estimate=pl.CostEstimate(flops=flops, bytes_accessed=moved, transcendentals=0),
        name=name,
    )(*arrays))


def in_hbm(entry):
    return entry, pltpu.HBM


def in_smem(value):
    return value.astype(jnp.int32).reshape(1), pltpu.SMEM


def swap_all(bit, values):
    return [partner_2(member, "dp", bit) for member in values]


def exchange(spot, first_bit, ways, sends):
    replicas = lax.axis_size("dp")
    return [
        lax.ppermute(sent, "dp", [(at, at ^ (hop << first_bit)) for at in range(replicas)])
        for hop, sent in zip(range(1, ways), sends)
    ]


def scatter_mean(kept, sent, split, beside):
    f32 = jnp.float32
    replicas = lax.axis_size("dp")
    levels = replicas.bit_length() - 1
    place = lax.axis_index("dp")
    pairs, piece_s, piece_e, piece_r, piece_n = split
    rows = kept.shape[1]
    came = exchange(place, 0, 2, [sent])
    (kept,) = run_kernel(
        copy_kernel, "copy", [in_hbm(kept)], [(kept.shape, f32)], [pltpu.SemaphoreType.DMA(())]
    )
    came, kept = lax.optimization_barrier((came, kept))
    left, low, done = pairs, 1, []
    while left > 1:
        width = 2 if low == 1 and levels > 2 else 1
        ways = 1 << width
        spot = in_smem((place >> low) % ways)
        kept, *sends = run_kernel(
            functools.partial(fold_kernel, (len(came),)), "fold", [spot, kept] + came,
            [((left // ways, rows, LANES), f32)] * ways, [((left, rows, LANES), f32)],
        )
        came = exchange(place, low, ways, sends)
        if beside:
            work, *beside = beside
            came, ready = lax.optimization_barrier((came, work()))
            done.append(ready)
        left, low = left // ways, low + width
    at_e = round_up(piece_s + 1, 8)
    spans = ((at_e + piece_e, piece_r), (0, piece_s), (at_e, piece_e), (piece_s, 1))
    sizes = [(rows_of * LANES,) for _, rows_of in spans[:3]] + [(piece_n,)]
    mean = run_kernel(
        functools.partial(mean_kernel, replicas, spans), "mean", [kept] + came, [(size, f32) for size in sizes]
    )
    return done + [work() for work in beside], mean


def scatter_mean_any(arrays):
    replicas = lax.axis_size("dp")
    tables = [member.reshape(replicas, -1) for member in arrays]
    pieces = lax.all_to_all(jnp.concatenate(tables, axis=1), "dp", 0, 0, tiled=True)
    mean = jnp.sum(pieces, axis=0) / replicas
    bounds = [sum(table.shape[1] for table in tables[:at]) for at in range(len(tables) + 1)]
    return tuple(mean[low:high] for low, high in zip(bounds[:-1], bounds[1:]))


def shards(images, cotangent, w_reduce, w_spatial, w_expand, norm_gain, norm_bias, round_index):
    f32, bf16 = jnp.float32, jnp.bfloat16
    replicas = lax.axis_size("dp")
    levels = replicas.bit_length() - 1
    steps, _, pixels, in_ch = images.shape
    weights = [member.reshape(-1, LANES) for member in (w_reduce, w_spatial, w_expand)]
    sizes = [(member.shape, f32) for member in weights]
    rows_r, rows_s, rows_e = (member.shape[0] for member in weights)
    rows = rows_r + rows_s + rows_e
    norm_size = 2 * norm_gain.size
    flat_map = ((pixels, LANES), f32)
    wide_map = ((pixels, in_ch), f32)
    whole = ((rows, LANES), f32)
    norm_rows = ((norm_size // LANES, LANES), f32)
    half_map = ((pixels, in_ch), bf16)
    scratch = [
        half_map, half_map, whole, whole, whole,
        flat_map, flat_map, ((pixels, LANES), bf16), ((ROWS, SPAN), bf16), ((SPAN, ROWS), bf16),
        ((ROWS_BACK, SPAN), bf16), ((ROWS + 16, LANES), f32), ((ROWS_BACK + 16, LANES), f32),
        sizes[2], ((LANES, in_ch), bf16), ((rows_s, LANES), bf16), ((rows_s, LANES), bf16),
        wide_map, wide_map, half_map, flat_map, ((pixels, LANES), bf16), ((in_ch, LANES), bf16),
        pltpu.SemaphoreType.DMA((8,)), pltpu.SemaphoreType.DMA((4,)),
    ]
    flops = 6 * pixels * LANES * (2 * in_ch + rows_s)
    fine = replicas > 1 and all(size[0][0] % replicas == 0 for size in sizes)
    split = (replicas // 2, rows_s // replicas, rows_e // replicas, rows_r // replicas, norm_size // replicas)
    half = ((split[0], round_up(split[1] + 1, 8) + split[2] + split[3], LANES), f32)
    params = [weights[1], weights[0], weights[2], norm_gain, norm_bias]
    moments = []
    for step in range(steps):
        branches = [functools.partial(swap_all, bit) for bit in range(levels)]
        theirs = list(lax.switch((round_index[0] + step) % levels, branches, params))
        if step == 0:
            sides = [[in_hbm(side[at]) for at in (1, 0, 2)] + side[3:] for side in (params, theirs)]
        else:
            sides = [params, [in_hbm(theirs[0]), theirs[1]]]
        operands = [in_hbm(images), in_hbm(cotangent)] + sides[0] + sides[1]
        operands += [in_hbm(member) for member in moments[:1]] + moments[1:]
        moment_outs = [in_hbm(whole), ((1, norm_size), f32)]
        scratch_of = scratch + [whole] if step else [whole] + scratch
        if step == steps - 1 and fine:
            core = in_smem(lax.axis_index("dp") % 2)
            kept, sent, *moments = run_kernel(
                functools.partial(step_kernel, step, True, split), "last_step", [core] + operands,
                [half, half] + moment_outs, scratch_of, flops, VMEM_BYTES,
            )
        else:
            *params, moment, norm_moment = run_kernel(
                functools.partial(step_kernel, step, False, None), "step", operands,
                [in_hbm(whole), norm_rows] + moment_outs, scratch_of, flops, VMEM_BYTES,
            )
            moments = [moment, norm_moment]
    def pack(sources, *spans):
        return run_kernel(
            functools.partial(pack_kernel, spans), "pack", sources,
            [((1, span * LANES if span else norm_size), bf16) for _, span in spans],
        )

    span_r, span_s, span_e = (0, rows_r), (rows_r, rows_s), (rows_r + rows_s, rows_e)
    if fine:
        beside = [
            functools.partial(pack, moments[:1], span_r, span_s), functools.partial(pack, moments, span_e, (0, 0))
        ]
        (first, second), averaged = scatter_mean(kept, sent, split, beside)
        out = first + second
    else:
        flat = [params[0][low:high].reshape(-1) for low, high in ((0, rows_r), (rows_r, rows_r + rows_s), (rows_r + rows_s, rows))]
        out, averaged = pack(moments, span_r, span_s, span_e, (0, 0)), scatter_mean_any(flat + [params[1].reshape(-1)])
    return tuple(averaged) + tuple(out)


def solution(mesh):
    in_specs = (
        P(None, "dp", None, None),
        P(None, "dp", None, None),
        P("dp", None),
        P("dp", None),
        P("dp", None),
        P("dp", None),
        P("dp", None),
        P(),
    )
    out_specs = (
        P("dp"),
        P("dp"),
        P("dp"),
        P("dp"),
        P("dp", None),
        P("dp", None),
        P("dp", None),
        P("dp", None),
    )
    return jax.shard_map(shards, mesh=mesh, in_specs=in_specs, out_specs=out_specs, check_vma=False)
```

```python
import functools

import jax
import jax.numpy as jnp
from jax import lax
from jax.experimental import pallas as pl
from jax.experimental.pallas import tpu as pltpu
from jax.sharding import PartitionSpec as P

HEIGHT = 28
WIDTH = 28
KSIZE = 3

LEARN_RATE = 0.01
MOMENTUM = 0.9
EPSILON = 1e-05

LANES = 128
PITCH = 32
VMEM_BYTES = 60 * 1024 * 1024
SMALL_VMEM = 8 * 1024 * 1024


def round_up(value, unit):
    return (value + unit - 1) // unit * unit


def partner_2(value, axis, distance):
    mask = 2**distance
    pairs = [(source, source ^ mask) for source in range(lax.axis_size(axis))]
    return lax.ppermute(value, axis, pairs)


def matmul(left, right):
    return jnp.dot(left, right, preferred_element_type=jnp.float32)


def contract_cols(left, right):
    return lax.dot_general(left, right, (((1,), (1,)), ((), ())), preferred_element_type=jnp.float32)


def activate_half(half):
    return half * (1.0 + jnp.tanh(half))


def twice_slope(half):
    bend = jnp.tanh(half)
    return (1.0 + bend) * (1.0 + half * (1.0 - bend))


def column_sum(values):
    return jnp.sum(values, axis=0, keepdims=True)


MAPS = 4
THIN = 16
FLAT = MAPS * WIDTH
PITCHED = MAPS * PITCH
CHUNKS = HEIGHT // MAPS
SPAN = KSIZE * LANES
TOP = PITCH
TOP_BACK = 2 * PITCH
ROWS = round_up(HEIGHT * PITCH + 2 * PITCH, LANES)
ROWS_BACK = ROWS + 2 * PITCH


def flat_rows(at):
    return pl.ds(pl.multiple_of(at * FLAT, FLAT), FLAT)


def zero_row(width):
    return jnp.zeros((1, width), jnp.float32)


def sweep(body, init=0, unroll=True):
    return lax.fori_loop(0, CHUNKS, body, init, unroll=unroll)


def fold_rows(values):
    rows, width = values.shape
    return jnp.sum(values.reshape(rows // 8, 8, width), axis=0)


def zero_rows(width):
    return jnp.zeros((8, width), jnp.float32)


def statistics(values_ref, total):
    count, width = values_ref.shape
    mean = column_sum(total) / count

    def add(at, held):
        center = values_ref[flat_rows(at), :] - mean
        return held + fold_rows(center * center)

    return mean, lax.rsqrt(column_sum(sweep(add, zero_rows(width))) / count + EPSILON)


def pad_chunk(pad_ref, top, at, values):
    for row in range(MAPS):
        start = pl.multiple_of(at * PITCHED, PITCHED) + (8 + top + row * PITCH)
        pad_ref[pl.ds(start, WIDTH), :] = values[row * WIDTH : (row + 1) * WIDTH]


def shift_columns(pad_ref, out_ref):
    rows = out_ref.shape[0]
    for col_off in range(KSIZE):
        start = 8 + col_off - KSIZE // 2
        out_ref[:, col_off * LANES : (col_off + 1) * LANES] = pad_ref[start : start + rows, :].astype(jnp.bfloat16)


def conv_chunk(wide_ref, top, at, weight_of, multiply):
    total = None
    for row_off in range(KSIZE):
        start = pl.multiple_of(at * PITCHED, PITCHED) + (top + (row_off - KSIZE // 2) * PITCH)
        piece = multiply(wide_ref[pl.ds(start, PITCHED), :], weight_of(row_off))
        total = piece if total is None else total + piece
    return jnp.concatenate([total[row * PITCH : row * PITCH + WIDTH] for row in range(MAPS)], axis=0)


def mean_of(own, theirs):
    return (own + theirs) * 0.5


def rows_at(ref, start, rows):
    return ref.at[pl.ds(start, rows), :]


def step_kernel(step, last, split, *refs):
    it = iter(refs)
    take = lambda count: [next(it) for _ in range(count)]
    core_ref = next(it) if last else None
    images_ref, cotangent_ref = take(2)
    packed = step > 0
    own, theirs = (take(2) if packed else take(5)) , (take(2) if packed else take(5))
    held_out = take(2) if packed else []
    outs = take(2) if last else take(2)
    moment_out = next(it)
    norm_moment = next(it)
    own_ref = own[0] if packed else next(it)
    (x_ref, upstream_ref, theirs_ref, param_ref, moment_ref,
     normed_a, normed_b, hidden_b, wide, wide_t, wide_b, pad, pad_b, mixed_e, weight_e, weight_s, weight_f,
     third, grad_sum, grad_third, work, back, weight_t, arrived, left) = take(25)
    held_ref = next(it) if packed else None
    count, width = third.shape
    blocks = width // LANES
    rows_r, rows_s, rows_e = width, weight_s.shape[0], width
    spans = ((0, rows_r), (rows_r, rows_s), (rows_r + rows_s, rows_e))
    bf16 = jnp.bfloat16
    view = lambda ref, part: rows_at(ref, *spans[part])
    pending = {}

    def fetch(name, source, target):
        copy = pltpu.make_async_copy(source, target, arrived.at[len(pending)])
        copy.start()
        pending[name] = copy

    def fetch_part(part):
        fetch(("own", part), own[part], view(own_ref, part))
        fetch(("theirs", part), theirs[part], view(theirs_ref, part))

    def ready(part):
        if not packed:
            pending["own", part].wait()
            pending["theirs", part].wait()
        elif part < 2:
            pending["others" if part else "reduce"].wait()

    fetch("x", images_ref.at[step, 0], x_ref)
    if packed:
        later = rows_s + rows_e
        fetch("reduce", rows_at(theirs[0], 0, rows_r), rows_at(theirs_ref, 0, rows_r))
        fetch("others", rows_at(theirs[0], rows_r, later), rows_at(theirs_ref, rows_r, later))
    else:
        for part in range(3):
            fetch_part(part)
    fetch("upstream", cotangent_ref.at[step, 0], upstream_ref)
    if packed:
        fetch("held", held_out[0], held_ref)
    stores = []

    def store(source, target):
        copy = pltpu.make_async_copy(source, target, left.at[len(stores)])
        copy.start()
        stores.append(copy)

    def settle(start, rows):
        store(rows_at(moment_ref, start, rows), rows_at(moment_out, start, rows))
        if not last:
            store(rows_at(param_ref, start, rows), rows_at(outs[0], start, rows))

    if packed:
        rows_of = lambda ref, low: jnp.concatenate([ref[low + at : low + at + 1, :] for at in range(ref.shape[0] // 2)], axis=1)
        half = own[1].shape[0] // 2
        gains = mean_of(rows_of(own[1], 0), rows_of(theirs[1], 0))
        shifts = mean_of(rows_of(own[1], half), rows_of(theirs[1], half))
    else:
        gains = mean_of(own[3][...], theirs[3][...])
        shifts = mean_of(own[4][...], theirs[4][...])
    gain_a, gain_b, gain_c = gains[:, :LANES], gains[:, LANES : 2 * LANES], gains[:, 2 * LANES :]
    shift_a, shift_b, shift_c = shifts[:, :LANES], shifts[:, LANES : 2 * LANES], shifts[:, 2 * LANES :]

    half_a, half_b = (0.5 * gain_a, 0.5 * shift_a), (0.5 * gain_b, 0.5 * shift_b)

    def mixed(part, start, rows):
        span = pl.ds(spans[part][0] + start, rows)
        return mean_of(own_ref[span, :], theirs_ref[span, :])

    def learn(part, start, rows, moment):
        span = pl.ds(spans[part][0] + start, rows)
        if packed:
            moment = MOMENTUM * held_ref[span, :] + moment
        moment_ref[span, :] = moment
        param_ref[span, :] = mixed(part, start, rows) - LEARN_RATE * moment

    pad[...] = jnp.zeros_like(pad)
    pad_b[...] = jnp.zeros_like(pad_b)
    pending["x"].wait()
    ready(0)
    reduce_w = mixed(0, 0, rows_r).astype(bf16)

    def make_first(at, total):
        values = matmul(x_ref[flat_rows(at), :], reduce_w)
        normed_a[flat_rows(at), :] = values
        return total + fold_rows(values)

    mean, scale_a = statistics(normed_a, sweep(make_first, zero_rows(LANES)))

    def make_hidden_a(at, carry):
        normed = (normed_a[flat_rows(at), :] - mean) * scale_a
        normed_a[flat_rows(at), :] = normed
        pad_chunk(pad, TOP, at, activate_half(normed * half_a[0] + half_a[1]))
        return carry

    sweep(make_hidden_a)
    shift_columns(pad, wide)

    taps = KSIZE * KSIZE
    ready(1)
    for tap in range(taps):
        weights = mixed(1, tap * LANES, LANES).astype(bf16)
        weight_s[tap * LANES : (tap + 1) * LANES, :] = weights
        other = taps - 1 - tap
        weight_f[other * LANES : (other + 1) * LANES, :] = weights.T

    def make_second(at, total):
        values = conv_chunk(wide, TOP, at, lambda row: weight_s[row * SPAN : (row + 1) * SPAN, :], matmul)
        normed_b[flat_rows(at), :] = values
        return total + fold_rows(values)

    mean, scale_b = statistics(normed_b, sweep(make_second, zero_rows(LANES)))

    def make_hidden_b(at, total):
        normed = (normed_b[flat_rows(at), :] - mean) * scale_b
        normed_b[flat_rows(at), :] = normed
        hidden = activate_half(normed * half_b[0] + half_b[1]).astype(bf16)
        hidden_b[flat_rows(at), :] = hidden
        return total + fold_rows(hidden.astype(jnp.float32))

    hidden_mean = column_sum(sweep(make_hidden_b, zero_rows(LANES))) / count

    ready(2)
    mixed_e[...] = mixed(2, 0, rows_e)
    for block in range(blocks):
        weights = mixed_e[pl.ds(block, LANES, stride=blocks), :].astype(bf16)
        weight_e[:, block * LANES : (block + 1) * LANES] = weights
        weight_t[block * LANES : (block + 1) * LANES, :] = weights.T

    rows, rest = [], hidden_mean
    for _ in range(3):
        rows.append(rest.astype(bf16).astype(jnp.float32))
        rest = rest - rows[-1]
    rows = jnp.concatenate(rows + [jnp.zeros((13, LANES), jnp.float32)], axis=0).astype(bf16)
    mean = column_sum(matmul(rows, weight_e[...]))

    def make_third(at, total):
        values = matmul(hidden_b[flat_rows(at), :], weight_e[...]) - mean
        third[flat_rows(at), :] = values
        return total + fold_rows(values * values)

    scale_c = lax.rsqrt(column_sum(sweep(make_third, zero_rows(width))) / count + EPSILON)
    stretch = scale_c * gain_c

    def make_sum(at, totals):
        size = THIN if packed else FLAT
        for piece in range(FLAT // size):
            rows = pl.ds(pl.multiple_of(at * FLAT + piece * size, size), size)
            values = third[rows, :]
            half = 0.5 * (values * stretch + (shift_c + x_ref[rows, :].astype(jnp.float32)))
            grad = upstream_ref[rows, :].astype(jnp.float32) * twice_slope(half)
            grad_sum[rows, :] = grad
            totals = totals[0] + fold_rows(grad * values), totals[1] + fold_rows(grad)
        return totals

    pending["upstream"].wait()
    totals = sweep(make_sum, (zero_rows(width), zero_rows(width)), False)
    dgain_c, dshift_c = 0.5 * scale_c * column_sum(totals[0]), 0.5 * column_sum(totals[1])
    level, slope, factor = 2.0 * dshift_c / count, 2.0 * scale_c * dgain_c / count, 0.5 * stretch

    def make_back_c(at, totals):
        size = FLAT if packed else THIN
        for piece in range(FLAT // size):
            rows = pl.ds(pl.multiple_of(at * FLAT + piece * size, size), size)
            grad = (grad_sum[rows, :] - level - third[rows, :] * slope) * factor
            grad_third[rows, :] = grad.astype(bf16)
        normed = normed_b[flat_rows(at), :]
        grad_out = matmul(grad_third[flat_rows(at), :], weight_t[...]) * twice_slope(normed * half_b[0] + half_b[1])
        work[flat_rows(at), :] = grad_out
        return totals[0] + fold_rows(grad_out * normed), totals[1] + fold_rows(grad_out)

    dgain_b, dshift_b = [0.5 * column_sum(total) for total in sweep(make_back_c, (zero_rows(LANES), zero_rows(LANES)))]
    grad = matmul(hidden_b[...].T, grad_third[...])
    for block in range(blocks):
        mixed_e[pl.ds(block, LANES, stride=blocks), :] = grad[:, block * LANES : (block + 1) * LANES]
    if packed:
        pending["held"].wait()
    learn(2, 0, rows_e, mixed_e[...])

    level_b, slope_b, factor_b = 2.0 * dshift_b / count, 2.0 * dgain_b / count, 0.5 * scale_b * gain_b

    def make_back_b(at, carry):
        grad = (work[flat_rows(at), :] - level_b - normed_b[flat_rows(at), :] * slope_b) * factor_b
        pad_chunk(pad_b, TOP_BACK, at, grad)
        return carry

    sweep(make_back_b)
    shift_columns(pad_b, wide_b)

    for at in range(ROWS // LANES):
        wide_t[:, at * LANES : (at + 1) * LANES] = wide[at * LANES : (at + 1) * LANES, :].T

    shifted = [
        wide_b[TOP_BACK - row_off * PITCH : TOP_BACK - row_off * PITCH + ROWS, LANES : 2 * LANES]
        for row_off in range(KSIZE)
    ]
    grad = matmul(wide_t[...], jnp.concatenate(shifted, axis=1))
    for row_off in range(KSIZE):
        learn(1, row_off * SPAN, SPAN, grad[:, row_off * LANES : (row_off + 1) * LANES])
    settle(rows_r, rows_s + rows_e)

    def make_back_a(at, totals):
        grad = conv_chunk(wide_b, TOP_BACK, at, lambda row: weight_f[row * SPAN : (row + 1) * SPAN, :], matmul)
        normed = normed_a[flat_rows(at), :]
        grad_out = grad * twice_slope(normed * half_a[0] + half_a[1])
        work[flat_rows(at), :] = grad_out
        return totals[0] + fold_rows(grad_out * normed), totals[1] + fold_rows(grad_out)

    dgain_a, dshift_a = [0.5 * column_sum(total) for total in sweep(make_back_a, (zero_rows(LANES), zero_rows(LANES)))]
    level_a, slope_a, factor_a = 2.0 * dshift_a / count, 2.0 * dgain_a / count, 0.5 * scale_a * gain_a

    def make_first_grad(at, carry):
        grad = (work[flat_rows(at), :] - level_a - normed_a[flat_rows(at), :] * slope_a) * factor_a
        back[flat_rows(at), :] = grad.astype(bf16)
        return carry

    sweep(make_first_grad)
    grad = matmul(back[...].T, x_ref[...])
    for block in range(blocks):
        learn(0, block * LANES, LANES, grad[:, block * LANES : (block + 1) * LANES].T)
    settle(0, rows_r)
    grad = jnp.concatenate([dgain_a, dgain_b, dgain_c, dshift_a, dshift_b, dshift_c], axis=1)
    norm = jnp.concatenate([gains, shifts], axis=1)
    if packed:
        grad = MOMENTUM * held_out[1][...] + grad
    norm_moment[...] = grad
    norm = norm - LEARN_RATE * grad
    if not last:
        for at in range(norm.shape[1] // LANES):
            outs[1][at : at + 1, :] = norm[:, at * LANES : (at + 1) * LANES]
        for copy in stores:
            copy.wait()
        return

    kept_ref, sent_ref = outs
    is_odd = jnp.full((1, 1), core_ref[0], jnp.int32) == 1
    pairs, piece_s, piece_e, piece_r, piece_n = split
    at_e = round_up(piece_s + 1, 8)
    at_r = at_e + piece_e

    def place(pair, start, low, high):
        rows = low.shape[0]
        kept_ref[pair, start : start + rows, :] = jnp.where(is_odd, high, low)
        sent_ref[pair, start : start + rows, :] = jnp.where(is_odd, low, high)

    for pair in range(pairs):
        for part, rows, start in ((1, piece_s, 0), (2, piece_e, at_e), (0, piece_r, at_r)):
            first = spans[part][0] + 2 * pair * rows
            place(pair, start, param_ref[first : first + rows, :], param_ref[first + rows : first + 2 * rows, :])
        low, high = [
            jnp.concatenate(
                [norm[:, at * piece_n : (at + 1) * piece_n], jnp.zeros((1, LANES - piece_n), jnp.float32)], axis=1
            )
            for at in (2 * pair, 2 * pair + 1)
        ]
        rest = jnp.zeros((at_e - piece_s - 1, LANES), jnp.float32)
        place(pair, piece_s, jnp.concatenate([low, rest]), jnp.concatenate([high, rest]))
    for copy in stores:
        copy.wait()


def fold_kernel(bits, *refs):
    spot_ref, kept_ref = refs[:2]
    came, outs, total = refs[2 : 2 + bits[0]], refs[2 + bits[0] : -1], refs[-1]
    values = kept_ref[...]
    for ref in came:
        values = values + ref[...]
    total[...] = values
    ways = len(outs)
    for hop, out in enumerate(outs):
        for at in range(out.shape[0]):
            out[at] = total[at * ways + jnp.bitwise_xor(spot_ref[0], hop)]


def mean_kernel(replicas, spans, *refs):
    outs = refs[-len(spans) :]
    kept_ref, came = refs[0], refs[1 : -len(spans)]
    values = kept_ref[0]
    for ref in came:
        values = values + ref[0]
    values = values * (1.0 / replicas)
    for (start, rows), out in zip(spans, outs):
        width = out.shape[0] // rows
        for at in range(rows):
            out[at * width : (at + 1) * width] = values[start + at, :width]


def copy_kernel(source, target, sem):
    copy = pltpu.make_async_copy(source, target, sem)
    copy.start()
    copy.wait()


def pack_kernel(spans, *refs):
    source, outs = refs[0], refs[-len(spans) :]
    for (start, rows), out in zip(spans, outs):
        if rows == 0:
            out[...] = refs[1][...].astype(jnp.bfloat16)
            continue

        def lay(at, carry, start=start, out=out):
            base = pl.multiple_of(at * 16, 16)
            for row in range(16):
                values = source[pl.ds(start + base + row, 1), :].astype(jnp.bfloat16)
                out[0:1, pl.ds(pl.multiple_of((base + row) * LANES, LANES), LANES)] = values
            return carry

        lax.fori_loop(0, rows // 16, lay, 0)


def run_kernel(body, name, operands, outs, scratch=(), flops=0, vmem=SMALL_VMEM):
    def parts(entries, is_plain):
        plain = [entry if is_plain(entry) else entry[0] for entry in entries]
        return plain, [pl.BlockSpec(memory_space=pltpu.VMEM if is_plain(entry) else entry[1]) for entry in entries]

    arrays, in_specs = parts(operands, lambda entry: not isinstance(entry, tuple))
    shapes, out_specs = parts(outs, lambda entry: isinstance(entry[0], tuple) and not isinstance(entry[0][0], tuple))
    moved = sum(array.size * array.dtype.itemsize for array in arrays)
    return list(pl.pallas_call(
        body,
        in_specs=in_specs,
        out_specs=out_specs,
        out_shape=[jax.ShapeDtypeStruct(shape, kind) for shape, kind in shapes],
        scratch_shapes=[pltpu.VMEM(*entry) if isinstance(entry, tuple) else entry for entry in scratch],
        compiler_params=pltpu.CompilerParams(vmem_limit_bytes=vmem),
        cost_estimate=pl.CostEstimate(flops=flops, bytes_accessed=moved, transcendentals=0),
        name=name,
    )(*arrays))


def in_hbm(entry):
    return entry, pltpu.HBM


def in_smem(value):
    return value.astype(jnp.int32).reshape(1), pltpu.SMEM


def swap_all(bit, values):
    return [partner_2(member, "dp", bit) for member in values]


def exchange(spot, first_bit, ways, sends):
    replicas = lax.axis_size("dp")
    return [
        lax.ppermute(sent, "dp", [(at, at ^ (hop << first_bit)) for at in range(replicas)])
        for hop, sent in zip(range(1, ways), sends)
    ]


def scatter_mean(kept, sent, split, beside):
    f32 = jnp.float32
    replicas = lax.axis_size("dp")
    levels = replicas.bit_length() - 1
    place = lax.axis_index("dp")
    pairs, piece_s, piece_e, piece_r, piece_n = split
    rows = kept.shape[1]
    came = exchange(place, 0, 2, [sent])
    (kept,) = run_kernel(
        copy_kernel, "copy", [in_hbm(kept)], [(kept.shape, f32)], [pltpu.SemaphoreType.DMA(())]
    )
    came, kept = lax.optimization_barrier((came, kept))
    left, low, done = pairs, 1, []
    while left > 1:
        width = 2 if low == 1 and levels > 2 else 1
        ways = 1 << width
        spot = in_smem((place >> low) % ways)
        kept, *sends = run_kernel(
            functools.partial(fold_kernel, (len(came),)), "fold", [spot, kept] + came,
            [((left // ways, rows, LANES), f32)] * ways, [((left, rows, LANES), f32)],
        )
        came = exchange(place, low, ways, sends)
        if beside:
            work, *beside = beside
            came, ready = lax.optimization_barrier((came, work()))
            done.append(ready)
        left, low = left // ways, low + width
    at_e = round_up(piece_s + 1, 8)
    spans = ((at_e + piece_e, piece_r), (0, piece_s), (at_e, piece_e), (piece_s, 1))
    sizes = [(rows_of * LANES,) for _, rows_of in spans[:3]] + [(piece_n,)]
    mean = run_kernel(
        functools.partial(mean_kernel, replicas, spans), "mean", [kept] + came, [(size, f32) for size in sizes]
    )
    return done + [work() for work in beside], mean


def scatter_mean_any(arrays):
    replicas = lax.axis_size("dp")
    tables = [member.reshape(replicas, -1) for member in arrays]
    pieces = lax.all_to_all(jnp.concatenate(tables, axis=1), "dp", 0, 0, tiled=True)
    mean = jnp.sum(pieces, axis=0) / replicas
    bounds = [sum(table.shape[1] for table in tables[:at]) for at in range(len(tables) + 1)]
    return tuple(mean[low:high] for low, high in zip(bounds[:-1], bounds[1:]))


def shards(images, cotangent, w_reduce, w_spatial, w_expand, norm_gain, norm_bias, round_index):
    f32, bf16 = jnp.float32, jnp.bfloat16
    replicas = lax.axis_size("dp")
    levels = replicas.bit_length() - 1
    steps, _, pixels, in_ch = images.shape
    weights = [member.reshape(-1, LANES) for member in (w_reduce, w_spatial, w_expand)]
    sizes = [(member.shape, f32) for member in weights]
    rows_r, rows_s, rows_e = (member.shape[0] for member in weights)
    rows = rows_r + rows_s + rows_e
    norm_size = 2 * norm_gain.size
    flat_map = ((pixels, LANES), f32)
    wide_map = ((pixels, in_ch), f32)
    whole = ((rows, LANES), f32)
    norm_rows = ((norm_size // LANES, LANES), f32)
    half_map = ((pixels, in_ch), bf16)
    scratch = [
        half_map, half_map, whole, whole, whole,
        flat_map, flat_map, ((pixels, LANES), bf16), ((ROWS, SPAN), bf16), ((SPAN, ROWS), bf16),
        ((ROWS_BACK, SPAN), bf16), ((ROWS + 16, LANES), f32), ((ROWS_BACK + 16, LANES), f32),
        sizes[2], ((LANES, in_ch), bf16), ((rows_s, LANES), bf16), ((rows_s, LANES), bf16),
        wide_map, wide_map, half_map, flat_map, ((pixels, LANES), bf16), ((in_ch, LANES), bf16),
        pltpu.SemaphoreType.DMA((8,)), pltpu.SemaphoreType.DMA((4,)),
    ]
    flops = 6 * pixels * LANES * (2 * in_ch + rows_s)
    fine = replicas > 1 and all(size[0][0] % replicas == 0 for size in sizes)
    split = (replicas // 2, rows_s // replicas, rows_e // replicas, rows_r // replicas, norm_size // replicas)
    half = ((split[0], round_up(split[1] + 1, 8) + split[2] + split[3], LANES), f32)
    params = [weights[1], weights[0], weights[2], norm_gain, norm_bias]
    moments = []
    for step in range(steps):
        branches = [functools.partial(swap_all, bit) for bit in range(levels)]
        theirs = list(lax.switch((round_index[0] + step) % levels, branches, params))
        if step == 0:
            sides = [[in_hbm(side[at]) for at in (1, 0, 2)] + side[3:] for side in (params, theirs)]
        else:
            sides = [params, [in_hbm(theirs[0]), theirs[1]]]
        operands = [in_hbm(images), in_hbm(cotangent)] + sides[0] + sides[1]
        operands += [in_hbm(member) for member in moments[:1]] + moments[1:]
        moment_outs = [in_hbm(whole), ((1, norm_size), f32)]
        scratch_of = scratch + [whole] if step else [whole] + scratch
        if step == steps - 1 and fine:
            core = in_smem(lax.axis_index("dp") % 2)
            kept, sent, *moments = run_kernel(
                functools.partial(step_kernel, step, True, split), "last_step", [core] + operands,
                [half, half] + moment_outs, scratch_of, flops, VMEM_BYTES,
            )
        else:
            *params, moment, norm_moment = run_kernel(
                functools.partial(step_kernel, step, False, None), "step", operands,
                [in_hbm(whole), norm_rows] + moment_outs, scratch_of, flops, VMEM_BYTES,
            )
            moments = [moment, norm_moment]
    def pack(sources, *spans):
        return run_kernel(
            functools.partial(pack_kernel, spans), "pack", sources,
            [((1, span * LANES if span else norm_size), bf16) for _, span in spans],
        )

    span_r, span_s, span_e = (0, rows_r), (rows_r, rows_s), (rows_r + rows_s, rows_e)
    if fine:
        beside = [
            functools.partial(pack, moments[:1], span_r, span_s), functools.partial(pack, moments, span_e, (0, 0))
        ]
        (first, second), averaged = scatter_mean(kept, sent, split, beside)
        out = first + second
    else:
        flat = [params[0][low:high].reshape(-1) for low, high in ((0, rows_r), (rows_r, rows_r + rows_s), (rows_r + rows_s, rows))]
        out, averaged = pack(moments, span_r, span_s, span_e, (0, 0)), scatter_mean_any(flat + [params[1].reshape(-1)])
    return tuple(averaged) + tuple(out)


def solution(mesh):
    in_specs = (
        P(None, "dp", None, None),
        P(None, "dp", None, None),
        P("dp", None),
        P("dp", None),
        P("dp", None),
        P("dp", None),
        P("dp", None),
        P(),
    )
    out_specs = (
        P("dp"),
        P("dp"),
        P("dp"),
        P("dp"),
        P("dp", None),
        P("dp", None),
        P("dp", None),
        P("dp", None),
    )
    return jax.shard_map(shards, mesh=mesh, in_specs=in_specs, out_specs=out_specs, check_vma=False)
```

```python
import functools

import jax
import jax.numpy as jnp
from jax import lax
from jax.experimental import pallas as pl
from jax.experimental.pallas import tpu as pltpu
from jax.sharding import PartitionSpec as P

HEIGHT = 28
WIDTH = 28
KSIZE = 3

LEARN_RATE = 0.01
MOMENTUM = 0.9
EPSILON = 1e-05

LANES = 128
PITCH = 32
VMEM_BYTES = 60 * 1024 * 1024
SMALL_VMEM = 8 * 1024 * 1024


def round_up(value, unit):
    return (value + unit - 1) // unit * unit


def partner_2(value, axis, distance):
    mask = 2**distance
    pairs = [(source, source ^ mask) for source in range(lax.axis_size(axis))]
    return lax.ppermute(value, axis, pairs)


def matmul(left, right):
    return jnp.dot(left, right, preferred_element_type=jnp.float32)


def contract_cols(left, right):
    return lax.dot_general(left, right, (((1,), (1,)), ((), ())), preferred_element_type=jnp.float32)


def activate_half(half):
    return half * (1.0 + jnp.tanh(half))


def twice_slope(half):
    bend = jnp.tanh(half)
    return (1.0 + bend) * (1.0 + half * (1.0 - bend))


def column_sum(values):
    return jnp.sum(values, axis=0, keepdims=True)


MAPS = 4
FLAT = MAPS * WIDTH
PITCHED = MAPS * PITCH
CHUNKS = HEIGHT // MAPS
SPAN = KSIZE * LANES
TOP = PITCH
TOP_BACK = 2 * PITCH
ROWS = round_up(HEIGHT * PITCH + 2 * PITCH, LANES)
ROWS_BACK = ROWS + 2 * PITCH


def flat_rows(at):
    return pl.ds(pl.multiple_of(at * FLAT, FLAT), FLAT)


def zero_row(width):
    return jnp.zeros((1, width), jnp.float32)


def sweep(body, init=0, unroll=True):
    return lax.fori_loop(0, CHUNKS, body, init, unroll=unroll)


def fold_rows(values):
    rows, width = values.shape
    return jnp.sum(values.reshape(rows // 8, 8, width), axis=0)


def zero_rows(width):
    return jnp.zeros((8, width), jnp.float32)


def statistics(values_ref, total):
    count, width = values_ref.shape
    mean = column_sum(total) / count

    def add(at, held):
        center = values_ref[flat_rows(at), :] - mean
        return held + fold_rows(center * center)

    return mean, lax.rsqrt(column_sum(sweep(add, zero_rows(width))) / count + EPSILON)


def pad_chunk(pad_ref, top, at, values):
    for row in range(MAPS):
        start = pl.multiple_of(at * PITCHED, PITCHED) + (8 + top + row * PITCH)
        pad_ref[pl.ds(start, WIDTH), :] = values[row * WIDTH : (row + 1) * WIDTH]


def shift_columns(pad_ref, out_ref):
    rows = out_ref.shape[0]
    for col_off in range(KSIZE):
        start = 8 + col_off - KSIZE // 2
        out_ref[:, col_off * LANES : (col_off + 1) * LANES] = pad_ref[start : start + rows, :].astype(jnp.bfloat16)


def conv_chunk(wide_ref, top, at, weight_of, multiply):
    total = None
    for row_off in range(KSIZE):
        start = pl.multiple_of(at * PITCHED, PITCHED) + (top + (row_off - KSIZE // 2) * PITCH)
        piece = multiply(wide_ref[pl.ds(start, PITCHED), :], weight_of(row_off))
        total = piece if total is None else total + piece
    return jnp.concatenate([total[row * PITCH : row * PITCH + WIDTH] for row in range(MAPS)], axis=0)


def mean_of(own, theirs):
    return (own + theirs) * 0.5


def rows_at(ref, start, rows):
    return ref.at[pl.ds(start, rows), :]


def step_kernel(step, last, split, *refs):
    it = iter(refs)
    take = lambda count: [next(it) for _ in range(count)]
    core_ref = next(it) if last else None
    images_ref, cotangent_ref = take(2)
    packed = step > 0
    own, theirs = (take(2) if packed else take(5)) , (take(2) if packed else take(5))
    held_out = take(2) if packed else []
    outs = take(2) if last else take(2)
    moment_out = next(it)
    norm_moment = next(it)
    own_ref = own[0] if packed else next(it)
    (x_ref, upstream_ref, theirs_ref, param_ref, moment_ref,
     normed_a, normed_b, hidden_b, wide, wide_t, wide_b, pad, pad_b, mixed_e, weight_e, weight_s, weight_f,
     third, grad_sum, grad_third, work, back, weight_t, arrived, left) = take(25)
    held_ref = next(it) if packed else None
    count, width = third.shape
    blocks = width // LANES
    rows_r, rows_s, rows_e = width, weight_s.shape[0], width
    spans = ((0, rows_r), (rows_r, rows_s), (rows_r + rows_s, rows_e))
    bf16 = jnp.bfloat16
    view = lambda ref, part: rows_at(ref, *spans[part])
    pending = {}

    def fetch(name, source, target):
        copy = pltpu.make_async_copy(source, target, arrived.at[len(pending)])
        copy.start()
        pending[name] = copy

    def fetch_part(part):
        fetch(("own", part), own[part], view(own_ref, part))
        fetch(("theirs", part), theirs[part], view(theirs_ref, part))

    def ready(part):
        if not packed:
            pending["own", part].wait()
            pending["theirs", part].wait()
        elif part < 2:
            pending["others" if part else "reduce"].wait()

    fetch("x", images_ref.at[step, 0], x_ref)
    if packed:
        later = rows_s + rows_e
        fetch("reduce", rows_at(theirs[0], 0, rows_r), rows_at(theirs_ref, 0, rows_r))
        fetch("others", rows_at(theirs[0], rows_r, later), rows_at(theirs_ref, rows_r, later))
    else:
        for part in range(3):
            fetch_part(part)
    fetch("upstream", cotangent_ref.at[step, 0], upstream_ref)
    if packed:
        fetch("held", held_out[0], held_ref)
    stores = []

    def store(source, target):
        copy = pltpu.make_async_copy(source, target, left.at[len(stores)])
        copy.start()
        stores.append(copy)

    def settle(start, rows):
        store(rows_at(moment_ref, start, rows), rows_at(moment_out, start, rows))
        if not last:
            store(rows_at(param_ref, start, rows), rows_at(outs[0], start, rows))

    if packed:
        rows_of = lambda ref, low: jnp.concatenate([ref[low + at : low + at + 1, :] for at in range(ref.shape[0] // 2)], axis=1)
        half = own[1].shape[0] // 2
        gains = mean_of(rows_of(own[1], 0), rows_of(theirs[1], 0))
        shifts = mean_of(rows_of(own[1], half), rows_of(theirs[1], half))
    else:
        gains = mean_of(own[3][...], theirs[3][...])
        shifts = mean_of(own[4][...], theirs[4][...])
    gain_a, gain_b, gain_c = gains[:, :LANES], gains[:, LANES : 2 * LANES], gains[:, 2 * LANES :]
    shift_a, shift_b, shift_c = shifts[:, :LANES], shifts[:, LANES : 2 * LANES], shifts[:, 2 * LANES :]

    half_a, half_b = (0.5 * gain_a, 0.5 * shift_a), (0.5 * gain_b, 0.5 * shift_b)

    def mixed(part, start, rows):
        span = pl.ds(spans[part][0] + start, rows)
        return mean_of(own_ref[span, :], theirs_ref[span, :])

    def learn(part, start, rows, moment):
        span = pl.ds(spans[part][0] + start, rows)
        if packed:
            moment = MOMENTUM * held_ref[span, :] + moment
        moment_ref[span, :] = moment
        param_ref[span, :] = mixed(part, start, rows) - LEARN_RATE * moment

    pad[...] = jnp.zeros_like(pad)
    pad_b[...] = jnp.zeros_like(pad_b)
    pending["x"].wait()
    ready(0)
    reduce_w = mixed(0, 0, rows_r).astype(bf16)

    def make_first(at, total):
        values = matmul(x_ref[flat_rows(at), :], reduce_w)
        normed_a[flat_rows(at), :] = values
        return total + fold_rows(values)

    mean, scale_a = statistics(normed_a, sweep(make_first, zero_rows(LANES)))

    def make_hidden_a(at, carry):
        normed = (normed_a[flat_rows(at), :] - mean) * scale_a
        normed_a[flat_rows(at), :] = normed
        pad_chunk(pad, TOP, at, activate_half(normed * half_a[0] + half_a[1]))
        return carry

    sweep(make_hidden_a)
    shift_columns(pad, wide)

    taps = KSIZE * KSIZE
    ready(1)
    for tap in range(taps):
        weights = mixed(1, tap * LANES, LANES).astype(bf16)
        weight_s[tap * LANES : (tap + 1) * LANES, :] = weights
        other = taps - 1 - tap
        weight_f[other * LANES : (other + 1) * LANES, :] = weights.T

    def make_second(at, total):
        values = conv_chunk(wide, TOP, at, lambda row: weight_s[row * SPAN : (row + 1) * SPAN, :], matmul)
        normed_b[flat_rows(at), :] = values
        return total + fold_rows(values)

    mean, scale_b = statistics(normed_b, sweep(make_second, zero_rows(LANES)))

    def make_hidden_b(at, total):
        normed = (normed_b[flat_rows(at), :] - mean) * scale_b
        normed_b[flat_rows(at), :] = normed
        hidden = activate_half(normed * half_b[0] + half_b[1]).astype(bf16)
        hidden_b[flat_rows(at), :] = hidden
        return total + fold_rows(hidden.astype(jnp.float32))

    hidden_mean = column_sum(sweep(make_hidden_b, zero_rows(LANES))) / count

    ready(2)
    mixed_e[...] = mixed(2, 0, rows_e)
    for block in range(blocks):
        weights = mixed_e[pl.ds(block, LANES, stride=blocks), :].astype(bf16)
        weight_e[:, block * LANES : (block + 1) * LANES] = weights
        weight_t[block * LANES : (block + 1) * LANES, :] = weights.T

    rows, rest = [], hidden_mean
    for _ in range(3):
        rows.append(rest.astype(bf16).astype(jnp.float32))
        rest = rest - rows[-1]
    rows = jnp.concatenate(rows + [jnp.zeros((13, LANES), jnp.float32)], axis=0).astype(bf16)
    mean = column_sum(matmul(rows, weight_e[...]))

    def make_third(at, total):
        values = matmul(hidden_b[flat_rows(at), :], weight_e[...]) - mean
        third[flat_rows(at), :] = values
        return total + fold_rows(values * values)

    scale_c = lax.rsqrt(column_sum(sweep(make_third, zero_rows(width))) / count + EPSILON)
    stretch = scale_c * gain_c

    def make_sum(at, totals):
        values = third[flat_rows(at), :]
        half = 0.5 * (values * stretch + (shift_c + x_ref[flat_rows(at), :].astype(jnp.float32)))
        grad = upstream_ref[flat_rows(at), :].astype(jnp.float32) * twice_slope(half)
        grad_sum[flat_rows(at), :] = grad
        return totals[0] + fold_rows(grad * values), totals[1] + fold_rows(grad)

    pending["upstream"].wait()
    totals = sweep(make_sum, (zero_rows(width), zero_rows(width)), False)
    dgain_c, dshift_c = 0.5 * scale_c * column_sum(totals[0]), 0.5 * column_sum(totals[1])
    level, slope, factor = 2.0 * dshift_c / count, 2.0 * scale_c * dgain_c / count, 0.5 * stretch

    def make_back_c(at, totals):
        grad = (grad_sum[flat_rows(at), :] - level - third[flat_rows(at), :] * slope) * factor
        grad = grad.astype(bf16)
        grad_third[flat_rows(at), :] = grad
        normed = normed_b[flat_rows(at), :]
        grad_out = matmul(grad, weight_t[...]) * twice_slope(normed * half_b[0] + half_b[1])
        work[flat_rows(at), :] = grad_out
        return totals[0] + fold_rows(grad_out * normed), totals[1] + fold_rows(grad_out)

    dgain_b, dshift_b = [0.5 * column_sum(total) for total in sweep(make_back_c, (zero_rows(LANES), zero_rows(LANES)))]
    grad = matmul(hidden_b[...].T, grad_third[...])
    for block in range(blocks):
        mixed_e[pl.ds(block, LANES, stride=blocks), :] = grad[:, block * LANES : (block + 1) * LANES]
    if packed:
        pending["held"].wait()
    learn(2, 0, rows_e, mixed_e[...])

    level_b, slope_b, factor_b = 2.0 * dshift_b / count, 2.0 * dgain_b / count, 0.5 * scale_b * gain_b

    def make_back_b(at, carry):
        grad = (work[flat_rows(at), :] - level_b - normed_b[flat_rows(at), :] * slope_b) * factor_b
        pad_chunk(pad_b, TOP_BACK, at, grad)
        return carry

    sweep(make_back_b)
    shift_columns(pad_b, wide_b)

    for at in range(ROWS // LANES):
        wide_t[:, at * LANES : (at + 1) * LANES] = wide[at * LANES : (at + 1) * LANES, :].T

    shifted = [
        wide_b[TOP_BACK - row_off * PITCH : TOP_BACK - row_off * PITCH + ROWS, LANES : 2 * LANES]
        for row_off in range(KSIZE)
    ]
    grad = matmul(wide_t[...], jnp.concatenate(shifted, axis=1))
    for row_off in range(KSIZE):
        learn(1, row_off * SPAN, SPAN, grad[:, row_off * LANES : (row_off + 1) * LANES])
    settle(rows_r, rows_s + rows_e)

    def make_back_a(at, totals):
        grad = conv_chunk(wide_b, TOP_BACK, at, lambda row: weight_f[row * SPAN : (row + 1) * SPAN, :], matmul)
        normed = normed_a[flat_rows(at), :]
        grad_out = grad * twice_slope(normed * half_a[0] + half_a[1])
        work[flat_rows(at), :] = grad_out
        return totals[0] + fold_rows(grad_out * normed), totals[1] + fold_rows(grad_out)

    dgain_a, dshift_a = [0.5 * column_sum(total) for total in sweep(make_back_a, (zero_rows(LANES), zero_rows(LANES)))]
    level_a, slope_a, factor_a = 2.0 * dshift_a / count, 2.0 * dgain_a / count, 0.5 * scale_a * gain_a

    def make_first_grad(at, carry):
        grad = (work[flat_rows(at), :] - level_a - normed_a[flat_rows(at), :] * slope_a) * factor_a
        back[flat_rows(at), :] = grad.astype(bf16)
        return carry

    sweep(make_first_grad)
    grad = matmul(back[...].T, x_ref[...])
    for block in range(blocks):
        learn(0, block * LANES, LANES, grad[:, block * LANES : (block + 1) * LANES].T)
    settle(0, rows_r)
    grad = jnp.concatenate([dgain_a, dgain_b, dgain_c, dshift_a, dshift_b, dshift_c], axis=1)
    norm = jnp.concatenate([gains, shifts], axis=1)
    if packed:
        grad = MOMENTUM * held_out[1][...] + grad
    norm_moment[...] = grad
    norm = norm - LEARN_RATE * grad
    if not last:
        for at in range(norm.shape[1] // LANES):
            outs[1][at : at + 1, :] = norm[:, at * LANES : (at + 1) * LANES]
        for copy in stores:
            copy.wait()
        return

    kept_ref, sent_ref = outs
    is_odd = jnp.full((1, 1), core_ref[0], jnp.int32) == 1
    pairs, piece_s, piece_e, piece_r, piece_n = split
    at_e = round_up(piece_s + 1, 8)
    at_r = at_e + piece_e

    def place(pair, start, low, high):
        rows = low.shape[0]
        kept_ref[pair, start : start + rows, :] = jnp.where(is_odd, high, low)
        sent_ref[pair, start : start + rows, :] = jnp.where(is_odd, low, high)

    for pair in range(pairs):
        for part, rows, start in ((1, piece_s, 0), (2, piece_e, at_e), (0, piece_r, at_r)):
            first = spans[part][0] + 2 * pair * rows
            place(pair, start, param_ref[first : first + rows, :], param_ref[first + rows : first + 2 * rows, :])
        low, high = [
            jnp.concatenate(
                [norm[:, at * piece_n : (at + 1) * piece_n], jnp.zeros((1, LANES - piece_n), jnp.float32)], axis=1
            )
            for at in (2 * pair, 2 * pair + 1)
        ]
        rest = jnp.zeros((at_e - piece_s - 1, LANES), jnp.float32)
        place(pair, piece_s, jnp.concatenate([low, rest]), jnp.concatenate([high, rest]))
    for copy in stores:
        copy.wait()


def fold_kernel(bits, *refs):
    spot_ref, kept_ref = refs[:2]
    came, outs, total = refs[2 : 2 + bits[0]], refs[2 + bits[0] : -1], refs[-1]
    values = kept_ref[...]
    for ref in came:
        values = values + ref[...]
    total[...] = values
    ways = len(outs)
    for hop, out in enumerate(outs):
        for at in range(out.shape[0]):
            out[at] = total[at * ways + jnp.bitwise_xor(spot_ref[0], hop)]


def mean_kernel(replicas, spans, *refs):
    outs = refs[-len(spans) :]
    kept_ref, came = refs[0], refs[1 : -len(spans)]
    values = kept_ref[0]
    for ref in came:
        values = values + ref[0]
    values = values * (1.0 / replicas)
    for (start, rows), out in zip(spans, outs):
        width = out.shape[0] // rows
        for at in range(rows):
            out[at * width : (at + 1) * width] = values[start + at, :width]


def copy_kernel(source, target, sem):
    copy = pltpu.make_async_copy(source, target, sem)
    copy.start()
    copy.wait()


def pack_kernel(spans, *refs):
    source, outs = refs[0], refs[-len(spans) :]
    for (start, rows), out in zip(spans, outs):
        if rows == 0:
            out[...] = refs[1][...].astype(jnp.bfloat16)
            continue

        def lay(at, carry, start=start, out=out):
            base = pl.multiple_of(at * 16, 16)
            for row in range(16):
                values = source[pl.ds(start + base + row, 1), :].astype(jnp.bfloat16)
                out[0:1, pl.ds(pl.multiple_of((base + row) * LANES, LANES), LANES)] = values
            return carry

        lax.fori_loop(0, rows // 16, lay, 0)


def run_kernel(body, name, operands, outs, scratch=(), flops=0, vmem=SMALL_VMEM):
    def parts(entries, is_plain):
        plain = [entry if is_plain(entry) else entry[0] for entry in entries]
        return plain, [pl.BlockSpec(memory_space=pltpu.VMEM if is_plain(entry) else entry[1]) for entry in entries]

    arrays, in_specs = parts(operands, lambda entry: not isinstance(entry, tuple))
    shapes, out_specs = parts(outs, lambda entry: isinstance(entry[0], tuple) and not isinstance(entry[0][0], tuple))
    moved = sum(array.size * array.dtype.itemsize for array in arrays)
    return list(pl.pallas_call(
        body,
        in_specs=in_specs,
        out_specs=out_specs,
        out_shape=[jax.ShapeDtypeStruct(shape, kind) for shape, kind in shapes],
        scratch_shapes=[pltpu.VMEM(*entry) if isinstance(entry, tuple) else entry for entry in scratch],
        compiler_params=pltpu.CompilerParams(vmem_limit_bytes=vmem),
        cost_estimate=pl.CostEstimate(flops=flops, bytes_accessed=moved, transcendentals=0),
        name=name,
    )(*arrays))


def in_hbm(entry):
    return entry, pltpu.HBM


def in_smem(value):
    return value.astype(jnp.int32).reshape(1), pltpu.SMEM


def swap_all(bit, values):
    return [partner_2(member, "dp", bit) for member in values]


def exchange(spot, first_bit, ways, sends):
    replicas = lax.axis_size("dp")
    came = []
    for hop in [ways - 1] + list(range(1, ways - 1)):
        pairs = [(at, at ^ (hop << first_bit)) for at in range(replicas)]
        came.append(lax.ppermute(sends[hop - 1], "dp", pairs))
    return came


def scatter_mean(kept, sent, split, beside):
    f32 = jnp.float32
    replicas = lax.axis_size("dp")
    levels = replicas.bit_length() - 1
    place = lax.axis_index("dp")
    pairs, piece_s, piece_e, piece_r, piece_n = split
    rows = kept.shape[1]
    came = exchange(place, 0, 2, [sent])
    (kept,) = run_kernel(
        copy_kernel, "copy", [in_hbm(kept)], [(kept.shape, f32)], [pltpu.SemaphoreType.DMA(())]
    )
    came, kept = lax.optimization_barrier((came, kept))
    left, low, done = pairs, 1, []
    while left > 1:
        width = 2 if low == 1 and levels > 2 else 1
        ways = 1 << width
        spot = in_smem((place >> low) % ways)
        kept, *sends = run_kernel(
            functools.partial(fold_kernel, (len(came),)), "fold", [spot, kept] + came,
            [((left // ways, rows, LANES), f32)] * ways, [((left, rows, LANES), f32)],
        )
        came = exchange(place, low, ways, sends)
        if beside:
            work, *beside = beside
            came, ready = lax.optimization_barrier((came, work()))
            done.append(ready)
        left, low = left // ways, low + width
    at_e = round_up(piece_s + 1, 8)
    spans = ((at_e + piece_e, piece_r), (0, piece_s), (at_e, piece_e), (piece_s, 1))
    sizes = [(rows_of * LANES,) for _, rows_of in spans[:3]] + [(piece_n,)]
    mean = run_kernel(
        functools.partial(mean_kernel, replicas, spans), "mean", [kept] + came, [(size, f32) for size in sizes]
    )
    return done + [work() for work in beside], mean


def scatter_mean_any(arrays):
    replicas = lax.axis_size("dp")
    tables = [member.reshape(replicas, -1) for member in arrays]
    pieces = lax.all_to_all(jnp.concatenate(tables, axis=1), "dp", 0, 0, tiled=True)
    mean = jnp.sum(pieces, axis=0) / replicas
    bounds = [sum(table.shape[1] for table in tables[:at]) for at in range(len(tables) + 1)]
    return tuple(mean[low:high] for low, high in zip(bounds[:-1], bounds[1:]))


def shards(images, cotangent, w_reduce, w_spatial, w_expand, norm_gain, norm_bias, round_index):
    f32, bf16 = jnp.float32, jnp.bfloat16
    replicas = lax.axis_size("dp")
    levels = replicas.bit_length() - 1
    steps, _, pixels, in_ch = images.shape
    weights = [member.reshape(-1, LANES) for member in (w_reduce, w_spatial, w_expand)]
    sizes = [(member.shape, f32) for member in weights]
    rows_r, rows_s, rows_e = (member.shape[0] for member in weights)
    rows = rows_r + rows_s + rows_e
    norm_size = 2 * norm_gain.size
    flat_map = ((pixels, LANES), f32)
    wide_map = ((pixels, in_ch), f32)
    whole = ((rows, LANES), f32)
    norm_rows = ((norm_size // LANES, LANES), f32)
    half_map = ((pixels, in_ch), bf16)
    scratch = [
        half_map, half_map, whole, whole, whole,
        flat_map, flat_map, ((pixels, LANES), bf16), ((ROWS, SPAN), bf16), ((SPAN, ROWS), bf16),
        ((ROWS_BACK, SPAN), bf16), ((ROWS + 16, LANES), f32), ((ROWS_BACK + 16, LANES), f32),
        sizes[2], ((LANES, in_ch), bf16), ((rows_s, LANES), bf16), ((rows_s, LANES), bf16),
        wide_map, wide_map, half_map, flat_map, ((pixels, LANES), bf16), ((in_ch, LANES), bf16),
        pltpu.SemaphoreType.DMA((8,)), pltpu.SemaphoreType.DMA((4,)),
    ]
    flops = 6 * pixels * LANES * (2 * in_ch + rows_s)
    fine = replicas > 1 and all(size[0][0] % replicas == 0 for size in sizes)
    split = (replicas // 2, rows_s // replicas, rows_e // replicas, rows_r // replicas, norm_size // replicas)
    half = ((split[0], round_up(split[1] + 1, 8) + split[2] + split[3], LANES), f32)
    params = [weights[1], weights[0], weights[2], norm_gain, norm_bias]
    moments = []
    for step in range(steps):
        branches = [functools.partial(swap_all, bit) for bit in range(levels)]
        theirs = list(lax.switch((round_index[0] + step) % levels, branches, params))
        if step == 0:
            sides = [[in_hbm(side[at]) for at in (1, 0, 2)] + side[3:] for side in (params, theirs)]
        else:
            sides = [params, [in_hbm(theirs[0]), theirs[1]]]
        operands = [in_hbm(images), in_hbm(cotangent)] + sides[0] + sides[1]
        operands += [in_hbm(member) for member in moments[:1]] + moments[1:]
        moment_outs = [in_hbm(whole), ((1, norm_size), f32)]
        scratch_of = scratch + [whole] if step else [whole] + scratch
        if step == steps - 1 and fine:
            core = in_smem(lax.axis_index("dp") % 2)
            kept, sent, *moments = run_kernel(
                functools.partial(step_kernel, step, True, split), "last_step", [core] + operands,
                [half, half] + moment_outs, scratch_of, flops, VMEM_BYTES,
            )
        else:
            *params, moment, norm_moment = run_kernel(
                functools.partial(step_kernel, step, False, None), "step", operands,
                [in_hbm(whole), norm_rows] + moment_outs, scratch_of, flops, VMEM_BYTES,
            )
            moments = [moment, norm_moment]
    def pack(sources, *spans):
        return run_kernel(
            functools.partial(pack_kernel, spans), "pack", sources,
            [((1, span * LANES if span else norm_size), bf16) for _, span in spans],
        )

    span_r, span_s, span_e = (0, rows_r), (rows_r, rows_s), (rows_r + rows_s, rows_e)
    if fine:
        beside = [
            functools.partial(pack, moments[:1], span_r, span_s), functools.partial(pack, moments, span_e, (0, 0))
        ]
        (first, second), averaged = scatter_mean(kept, sent, split, beside)
        out = first + second
    else:
        flat = [params[0][low:high].reshape(-1) for low, high in ((0, rows_r), (rows_r, rows_r + rows_s), (rows_r + rows_s, rows))]
        out, averaged = pack(moments, span_r, span_s, span_e, (0, 0)), scatter_mean_any(flat + [params[1].reshape(-1)])
    return tuple(averaged) + tuple(out)


def solution(mesh):
    in_specs = (
        P(None, "dp", None, None),
        P(None, "dp", None, None),
        P("dp", None),
        P("dp", None),
        P("dp", None),
        P("dp", None),
        P("dp", None),
        P(),
    )
    out_specs = (
        P("dp"),
        P("dp"),
        P("dp"),
        P("dp"),
        P("dp", None),
        P("dp", None),
        P("dp", None),
        P("dp", None),
    )
    return jax.shard_map(shards, mesh=mesh, in_specs=in_specs, out_specs=out_specs, check_vma=False)
```

```python
import functools

import jax
import jax.numpy as jnp
from jax import lax
from jax.experimental import pallas as pl
from jax.experimental.pallas import tpu as pltpu
from jax.sharding import PartitionSpec as P

HEIGHT = 28
WIDTH = 28
KSIZE = 3

LEARN_RATE = 0.01
MOMENTUM = 0.9
EPSILON = 1e-05

LANES = 128
PITCH = 32
VMEM_BYTES = 60 * 1024 * 1024
SMALL_VMEM = 8 * 1024 * 1024


def round_up(value, unit):
    return (value + unit - 1) // unit * unit


def partner_2(value, axis, distance):
    mask = 2**distance
    pairs = [(source, source ^ mask) for source in range(lax.axis_size(axis))]
    return lax.ppermute(value, axis, pairs)


def matmul(left, right):
    return jnp.dot(left, right, preferred_element_type=jnp.float32)


def contract_cols(left, right):
    return lax.dot_general(left, right, (((1,), (1,)), ((), ())), preferred_element_type=jnp.float32)


def activate_half(half):
    return half * (1.0 + jnp.tanh(half))


def twice_slope(half):
    bend = jnp.tanh(half)
    return (1.0 + bend) * (1.0 + half * (1.0 - bend))


def column_sum(values):
    return jnp.sum(values, axis=0, keepdims=True)


MAPS = 4
FLAT = MAPS * WIDTH
PITCHED = MAPS * PITCH
CHUNKS = HEIGHT // MAPS
SPAN = KSIZE * LANES
TOP = PITCH
TOP_BACK = 2 * PITCH
ROWS = round_up(HEIGHT * PITCH + 2 * PITCH, LANES)
ROWS_BACK = ROWS + 2 * PITCH


def flat_rows(at):
    return pl.ds(pl.multiple_of(at * FLAT, FLAT), FLAT)


def zero_row(width):
    return jnp.zeros((1, width), jnp.float32)


def sweep(body, init=0, unroll=True):
    return lax.fori_loop(0, CHUNKS, body, init, unroll=unroll)


def fold_rows(values):
    rows, width = values.shape
    return jnp.sum(values.reshape(rows // 8, 8, width), axis=0)


def zero_rows(width):
    return jnp.zeros((8, width), jnp.float32)


def statistics(values_ref, total):
    count, width = values_ref.shape
    mean = column_sum(total) / count

    def add(at, held):
        center = values_ref[flat_rows(at), :] - mean
        return held + fold_rows(center * center)

    return mean, lax.rsqrt(column_sum(sweep(add, zero_rows(width))) / count + EPSILON)


def pad_chunk(pad_ref, top, at, values):
    for row in range(MAPS):
        start = pl.multiple_of(at * PITCHED, PITCHED) + (8 + top + row * PITCH)
        pad_ref[pl.ds(start, WIDTH), :] = values[row * WIDTH : (row + 1) * WIDTH]


def shift_columns(pad_ref, out_ref):
    rows = out_ref.shape[0]
    for col_off in range(KSIZE):
        start = 8 + col_off - KSIZE // 2
        out_ref[:, col_off * LANES : (col_off + 1) * LANES] = pad_ref[start : start + rows, :].astype(jnp.bfloat16)


def conv_chunk(wide_ref, top, at, weight_of, multiply):
    total = None
    for row_off in range(KSIZE):
        start = pl.multiple_of(at * PITCHED, PITCHED) + (top + (row_off - KSIZE // 2) * PITCH)
        piece = multiply(wide_ref[pl.ds(start, PITCHED), :], weight_of(row_off))
        total = piece if total is None else total + piece
    return jnp.concatenate([total[row * PITCH : row * PITCH + WIDTH] for row in range(MAPS)], axis=0)


def mean_of(own, theirs):
    return (own + theirs) * 0.5


def rows_at(ref, start, rows):
    return ref.at[pl.ds(start, rows), :]


def step_kernel(step, last, split, *refs):
    it = iter(refs)
    take = lambda count: [next(it) for _ in range(count)]
    core_ref = next(it) if last else None
    images_ref, cotangent_ref = take(2)
    packed = step > 0
    own, theirs = (take(2) if packed else take(5)) , (take(2) if packed else take(5))
    held_out = take(2) if packed else []
    outs = take(2) if last else take(2)
    moment_out = next(it)
    norm_moment = next(it)
    own_ref = own[0] if packed else next(it)
    (x_ref, upstream_ref, theirs_ref, param_ref, moment_ref,
     normed_a, normed_b, hidden_b, wide, wide_t, wide_b, pad, pad_b, mixed_e, weight_e, weight_s, weight_f,
     third, grad_sum, grad_third, work, back, weight_t, hidden_t, arrived, left) = take(26)
    held_ref = next(it) if packed else None
    count, width = third.shape
    blocks = width // LANES
    rows_r, rows_s, rows_e = width, weight_s.shape[0], width
    spans = ((0, rows_r), (rows_r, rows_s), (rows_r + rows_s, rows_e))
    bf16 = jnp.bfloat16
    view = lambda ref, part: rows_at(ref, *spans[part])
    pending = {}

    def fetch(name, source, target):
        copy = pltpu.make_async_copy(source, target, arrived.at[len(pending)])
        copy.start()
        pending[name] = copy

    def fetch_part(part):
        fetch(("own", part), own[part], view(own_ref, part))
        fetch(("theirs", part), theirs[part], view(theirs_ref, part))

    def ready(part):
        if not packed:
            pending["own", part].wait()
            pending["theirs", part].wait()
        elif part < 2:
            pending["others" if part else "reduce"].wait()

    fetch("x", images_ref.at[step, 0], x_ref)
    if packed:
        later = rows_s + rows_e
        fetch("reduce", rows_at(theirs[0], 0, rows_r), rows_at(theirs_ref, 0, rows_r))
        fetch("others", rows_at(theirs[0], rows_r, later), rows_at(theirs_ref, rows_r, later))
    else:
        for part in range(3):
            fetch_part(part)
    fetch("upstream", cotangent_ref.at[step, 0], upstream_ref)
    if packed:
        fetch("held", held_out[0], held_ref)
    stores = []

    def store(source, target):
        copy = pltpu.make_async_copy(source, target, left.at[len(stores)])
        copy.start()
        stores.append(copy)

    def settle(start, rows):
        store(rows_at(moment_ref, start, rows), rows_at(moment_out, start, rows))
        if not last:
            store(rows_at(param_ref, start, rows), rows_at(outs[0], start, rows))

    if packed:
        rows_of = lambda ref, low: jnp.concatenate([ref[low + at : low + at + 1, :] for at in range(ref.shape[0] // 2)], axis=1)
        half = own[1].shape[0] // 2
        gains = mean_of(rows_of(own[1], 0), rows_of(theirs[1], 0))
        shifts = mean_of(rows_of(own[1], half), rows_of(theirs[1], half))
    else:
        gains = mean_of(own[3][...], theirs[3][...])
        shifts = mean_of(own[4][...], theirs[4][...])
    gain_a, gain_b, gain_c = gains[:, :LANES], gains[:, LANES : 2 * LANES], gains[:, 2 * LANES :]
    shift_a, shift_b, shift_c = shifts[:, :LANES], shifts[:, LANES : 2 * LANES], shifts[:, 2 * LANES :]

    half_a, half_b = (0.5 * gain_a, 0.5 * shift_a), (0.5 * gain_b, 0.5 * shift_b)

    def mixed(part, start, rows):
        span = pl.ds(spans[part][0] + start, rows)
        return mean_of(own_ref[span, :], theirs_ref[span, :])

    def learn(part, start, rows, moment):
        span = pl.ds(spans[part][0] + start, rows)
        if packed:
            moment = MOMENTUM * held_ref[span, :] + moment
        moment_ref[span, :] = moment
        param_ref[span, :] = mixed(part, start, rows) - LEARN_RATE * moment

    pad[...] = jnp.zeros_like(pad)
    pad_b[...] = jnp.zeros_like(pad_b)
    pending["x"].wait()
    ready(0)
    reduce_w = mixed(0, 0, rows_r).astype(bf16)

    def make_first(at, total):
        values = matmul(x_ref[flat_rows(at), :], reduce_w)
        normed_a[flat_rows(at), :] = values
        return total + fold_rows(values)

    mean, scale_a = statistics(normed_a, sweep(make_first, zero_rows(LANES)))

    def make_hidden_a(at, carry):
        normed = (normed_a[flat_rows(at), :] - mean) * scale_a
        normed_a[flat_rows(at), :] = normed
        pad_chunk(pad, TOP, at, activate_half(normed * half_a[0] + half_a[1]))
        return carry

    sweep(make_hidden_a)
    shift_columns(pad, wide)
    for at in range(ROWS // LANES):
        wide_t[:, at * LANES : (at + 1) * LANES] = wide[at * LANES : (at + 1) * LANES, :].T

    taps = KSIZE * KSIZE
    ready(1)
    for tap in range(taps):
        weights = mixed(1, tap * LANES, LANES).astype(bf16)
        weight_s[tap * LANES : (tap + 1) * LANES, :] = weights
        other = taps - 1 - tap
        weight_f[other * LANES : (other + 1) * LANES, :] = weights.T

    def make_second(at, total):
        values = conv_chunk(wide, TOP, at, lambda row: weight_s[row * SPAN : (row + 1) * SPAN, :], matmul)
        normed_b[flat_rows(at), :] = values
        return total + fold_rows(values)

    mean, scale_b = statistics(normed_b, sweep(make_second, zero_rows(LANES)))

    def make_hidden_b(at, total):
        normed = (normed_b[flat_rows(at), :] - mean) * scale_b
        normed_b[flat_rows(at), :] = normed
        hidden = activate_half(normed * half_b[0] + half_b[1]).astype(bf16)
        hidden_b[flat_rows(at), :] = hidden
        return total + fold_rows(hidden.astype(jnp.float32))

    hidden_mean = column_sum(sweep(make_hidden_b, zero_rows(LANES))) / count
    hidden_t[...] = hidden_b[...].T

    ready(2)
    mixed_e[...] = mixed(2, 0, rows_e)
    for block in range(blocks):
        weights = mixed_e[pl.ds(block, LANES, stride=blocks), :].astype(bf16)
        weight_e[:, block * LANES : (block + 1) * LANES] = weights
        weight_t[block * LANES : (block + 1) * LANES, :] = weights.T

    rows, rest = [], hidden_mean
    for _ in range(3):
        rows.append(rest.astype(bf16).astype(jnp.float32))
        rest = rest - rows[-1]
    rows = jnp.concatenate(rows + [jnp.zeros((13, LANES), jnp.float32)], axis=0).astype(bf16)
    mean = column_sum(matmul(rows, weight_e[...]))

    def make_third(at, total):
        values = matmul(hidden_b[flat_rows(at), :], weight_e[...]) - mean
        third[flat_rows(at), :] = values
        return total + fold_rows(values * values)

    scale_c = lax.rsqrt(column_sum(sweep(make_third, zero_rows(width))) / count + EPSILON)
    stretch = scale_c * gain_c

    def make_sum(at, totals):
        values = third[flat_rows(at), :]
        half = 0.5 * (values * stretch + (shift_c + x_ref[flat_rows(at), :].astype(jnp.float32)))
        grad = upstream_ref[flat_rows(at), :].astype(jnp.float32) * twice_slope(half)
        grad_sum[flat_rows(at), :] = grad
        return totals[0] + fold_rows(grad * values), totals[1] + fold_rows(grad)

    pending["upstream"].wait()
    totals = sweep(make_sum, (zero_rows(width), zero_rows(width)), False)
    dgain_c, dshift_c = 0.5 * scale_c * column_sum(totals[0]), 0.5 * column_sum(totals[1])
    level, slope, factor = 2.0 * dshift_c / count, 2.0 * scale_c * dgain_c / count, 0.5 * stretch

    def make_back_c(at, totals):
        grad = (grad_sum[flat_rows(at), :] - level - third[flat_rows(at), :] * slope) * factor
        grad = grad.astype(bf16)
        grad_third[flat_rows(at), :] = grad
        normed = normed_b[flat_rows(at), :]
        grad_out = matmul(grad, weight_t[...]) * twice_slope(normed * half_b[0] + half_b[1])
        work[flat_rows(at), :] = grad_out
        return totals[0] + fold_rows(grad_out * normed), totals[1] + fold_rows(grad_out)

    dgain_b, dshift_b = [0.5 * column_sum(total) for total in sweep(make_back_c, (zero_rows(LANES), zero_rows(LANES)))]
    grad = matmul(hidden_t[...], grad_third[...])
    for block in range(blocks):
        mixed_e[pl.ds(block, LANES, stride=blocks), :] = grad[:, block * LANES : (block + 1) * LANES]
    if packed:
        pending["held"].wait()
    learn(2, 0, rows_e, mixed_e[...])

    level_b, slope_b, factor_b = 2.0 * dshift_b / count, 2.0 * dgain_b / count, 0.5 * scale_b * gain_b

    def make_back_b(at, carry):
        grad = (work[flat_rows(at), :] - level_b - normed_b[flat_rows(at), :] * slope_b) * factor_b
        pad_chunk(pad_b, TOP_BACK, at, grad)
        return carry

    sweep(make_back_b)
    shift_columns(pad_b, wide_b)


    shifted = [
        wide_b[TOP_BACK - row_off * PITCH : TOP_BACK - row_off * PITCH + ROWS, LANES : 2 * LANES]
        for row_off in range(KSIZE)
    ]
    grad = matmul(wide_t[...], jnp.concatenate(shifted, axis=1))
    for row_off in range(KSIZE):
        learn(1, row_off * SPAN, SPAN, grad[:, row_off * LANES : (row_off + 1) * LANES])
    settle(rows_r, rows_s + rows_e)

    def make_back_a(at, totals):
        grad = conv_chunk(wide_b, TOP_BACK, at, lambda row: weight_f[row * SPAN : (row + 1) * SPAN, :], matmul)
        normed = normed_a[flat_rows(at), :]
        grad_out = grad * twice_slope(normed * half_a[0] + half_a[1])
        work[flat_rows(at), :] = grad_out
        return totals[0] + fold_rows(grad_out * normed), totals[1] + fold_rows(grad_out)

    dgain_a, dshift_a = [0.5 * column_sum(total) for total in sweep(make_back_a, (zero_rows(LANES), zero_rows(LANES)))]
    level_a, slope_a, factor_a = 2.0 * dshift_a / count, 2.0 * dgain_a / count, 0.5 * scale_a * gain_a

    def make_first_grad(at, carry):
        grad = (work[flat_rows(at), :] - level_a - normed_a[flat_rows(at), :] * slope_a) * factor_a
        back[flat_rows(at), :] = grad.astype(bf16)
        return carry

    sweep(make_first_grad)
    grad = matmul(back[...].T, x_ref[...])
    for block in range(blocks):
        learn(0, block * LANES, LANES, grad[:, block * LANES : (block + 1) * LANES].T)
    settle(0, rows_r)
    grad = jnp.concatenate([dgain_a, dgain_b, dgain_c, dshift_a, dshift_b, dshift_c], axis=1)
    norm = jnp.concatenate([gains, shifts], axis=1)
    if packed:
        grad = MOMENTUM * held_out[1][...] + grad
    norm_moment[...] = grad
    norm = norm - LEARN_RATE * grad
    if not last:
        for at in range(norm.shape[1] // LANES):
            outs[1][at : at + 1, :] = norm[:, at * LANES : (at + 1) * LANES]
        for copy in stores:
            copy.wait()
        return

    kept_ref, sent_ref = outs
    is_odd = jnp.full((1, 1), core_ref[0], jnp.int32) == 1
    pairs, piece_s, piece_e, piece_r, piece_n = split
    at_e = round_up(piece_s + 1, 8)
    at_r = at_e + piece_e

    def place(pair, start, low, high):
        rows = low.shape[0]
        kept_ref[pair, start : start + rows, :] = jnp.where(is_odd, high, low)
        sent_ref[pair, start : start + rows, :] = jnp.where(is_odd, low, high)

    for pair in range(pairs):
        for part, rows, start in ((1, piece_s, 0), (2, piece_e, at_e), (0, piece_r, at_r)):
            first = spans[part][0] + 2 * pair * rows
            place(pair, start, param_ref[first : first + rows, :], param_ref[first + rows : first + 2 * rows, :])
        low, high = [
            jnp.concatenate(
                [norm[:, at * piece_n : (at + 1) * piece_n], jnp.zeros((1, LANES - piece_n), jnp.float32)], axis=1
            )
            for at in (2 * pair, 2 * pair + 1)
        ]
        rest = jnp.zeros((at_e - piece_s - 1, LANES), jnp.float32)
        place(pair, piece_s, jnp.concatenate([low, rest]), jnp.concatenate([high, rest]))
    for copy in stores:
        copy.wait()


def fold_kernel(bits, *refs):
    spot_ref, kept_ref = refs[:2]
    came, outs, total = refs[2 : 2 + bits[0]], refs[2 + bits[0] : -1], refs[-1]
    values = kept_ref[...]
    for ref in came:
        values = values + ref[...]
    total[...] = values
    ways = len(outs)
    for hop, out in enumerate(outs):
        for at in range(out.shape[0]):
            out[at] = total[at * ways + jnp.bitwise_xor(spot_ref[0], hop)]


def mean_kernel(replicas, spans, *refs):
    outs = refs[-len(spans) :]
    kept_ref, came = refs[0], refs[1 : -len(spans)]
    values = kept_ref[0]
    for ref in came:
        values = values + ref[0]
    values = values * (1.0 / replicas)
    for (start, rows), out in zip(spans, outs):
        width = out.shape[0] // rows
        for at in range(rows):
            out[at * width : (at + 1) * width] = values[start + at, :width]


def copy_kernel(source, target, sem):
    copy = pltpu.make_async_copy(source, target, sem)
    copy.start()
    copy.wait()


def pack_kernel(spans, *refs):
    source, outs = refs[0], refs[-len(spans) :]
    for (start, rows), out in zip(spans, outs):
        if rows == 0:
            out[...] = refs[1][...].astype(jnp.bfloat16)
            continue

        def lay(at, carry, start=start, out=out):
            base = pl.multiple_of(at * 16, 16)
            for row in range(16):
                values = source[pl.ds(start + base + row, 1), :].astype(jnp.bfloat16)
                out[0:1, pl.ds(pl.multiple_of((base + row) * LANES, LANES), LANES)] = values
            return carry

        lax.fori_loop(0, rows // 16, lay, 0)


def run_kernel(body, name, operands, outs, scratch=(), flops=0, vmem=SMALL_VMEM):
    def parts(entries, is_plain):
        plain = [entry if is_plain(entry) else entry[0] for entry in entries]
        return plain, [pl.BlockSpec(memory_space=pltpu.VMEM if is_plain(entry) else entry[1]) for entry in entries]

    arrays, in_specs = parts(operands, lambda entry: not isinstance(entry, tuple))
    shapes, out_specs = parts(outs, lambda entry: isinstance(entry[0], tuple) and not isinstance(entry[0][0], tuple))
    moved = sum(array.size * array.dtype.itemsize for array in arrays)
    return list(pl.pallas_call(
        body,
        in_specs=in_specs,
        out_specs=out_specs,
        out_shape=[jax.ShapeDtypeStruct(shape, kind) for shape, kind in shapes],
        scratch_shapes=[pltpu.VMEM(*entry) if isinstance(entry, tuple) else entry for entry in scratch],
        compiler_params=pltpu.CompilerParams(vmem_limit_bytes=vmem),
        cost_estimate=pl.CostEstimate(flops=flops, bytes_accessed=moved, transcendentals=0),
        name=name,
    )(*arrays))


def in_hbm(entry):
    return entry, pltpu.HBM


def in_smem(value):
    return value.astype(jnp.int32).reshape(1), pltpu.SMEM


def swap_all(bit, values):
    return [partner_2(member, "dp", bit) for member in values]


def exchange(spot, first_bit, ways, sends):
    replicas = lax.axis_size("dp")
    came = []
    for hop in [ways - 1] + list(range(1, ways - 1)):
        pairs = [(at, at ^ (hop << first_bit)) for at in range(replicas)]
        came.append(lax.ppermute(sends[hop - 1], "dp", pairs))
    return came


def scatter_mean(kept, sent, split, beside):
    f32 = jnp.float32
    replicas = lax.axis_size("dp")
    levels = replicas.bit_length() - 1
    place = lax.axis_index("dp")
    pairs, piece_s, piece_e, piece_r, piece_n = split
    rows = kept.shape[1]
    came = exchange(place, 0, 2, [sent])
    (kept,) = run_kernel(
        copy_kernel, "copy", [in_hbm(kept)], [(kept.shape, f32)], [pltpu.SemaphoreType.DMA(())]
    )
    came, kept = lax.optimization_barrier((came, kept))
    left, low, done = pairs, 1, []
    while left > 1:
        width = 2 if low == 1 and levels > 2 else 1
        ways = 1 << width
        spot = in_smem((place >> low) % ways)
        kept, *sends = run_kernel(
            functools.partial(fold_kernel, (len(came),)), "fold", [spot, kept] + came,
            [((left // ways, rows, LANES), f32)] * ways, [((left, rows, LANES), f32)],
        )
        came = exchange(place, low, ways, sends)
        if beside:
            work, *beside = beside
            came, ready = lax.optimization_barrier((came, work()))
            done.append(ready)
        left, low = left // ways, low + width
    at_e = round_up(piece_s + 1, 8)
    spans = ((at_e + piece_e, piece_r), (0, piece_s), (at_e, piece_e), (piece_s, 1))
    sizes = [(rows_of * LANES,) for _, rows_of in spans[:3]] + [(piece_n,)]
    mean = run_kernel(
        functools.partial(mean_kernel, replicas, spans), "mean", [kept] + came, [(size, f32) for size in sizes]
    )
    return done + [work() for work in beside], mean


def scatter_mean_any(arrays):
    replicas = lax.axis_size("dp")
    tables = [member.reshape(replicas, -1) for member in arrays]
    pieces = lax.all_to_all(jnp.concatenate(tables, axis=1), "dp", 0, 0, tiled=True)
    mean = jnp.sum(pieces, axis=0) / replicas
    bounds = [sum(table.shape[1] for table in tables[:at]) for at in range(len(tables) + 1)]
    return tuple(mean[low:high] for low, high in zip(bounds[:-1], bounds[1:]))


def shards(images, cotangent, w_reduce, w_spatial, w_expand, norm_gain, norm_bias, round_index):
    f32, bf16 = jnp.float32, jnp.bfloat16
    replicas = lax.axis_size("dp")
    levels = replicas.bit_length() - 1
    steps, _, pixels, in_ch = images.shape
    weights = [member.reshape(-1, LANES) for member in (w_reduce, w_spatial, w_expand)]
    sizes = [(member.shape, f32) for member in weights]
    rows_r, rows_s, rows_e = (member.shape[0] for member in weights)
    rows = rows_r + rows_s + rows_e
    norm_size = 2 * norm_gain.size
    flat_map = ((pixels, LANES), f32)
    wide_map = ((pixels, in_ch), f32)
    whole = ((rows, LANES), f32)
    norm_rows = ((norm_size // LANES, LANES), f32)
    half_map = ((pixels, in_ch), bf16)
    scratch = [
        half_map, half_map, whole, whole, whole,
        flat_map, flat_map, ((pixels, LANES), bf16), ((ROWS, SPAN), bf16), ((SPAN, ROWS), bf16),
        ((ROWS_BACK, SPAN), bf16), ((ROWS + 16, LANES), f32), ((ROWS_BACK + 16, LANES), f32),
        sizes[2], ((LANES, in_ch), bf16), ((rows_s, LANES), bf16), ((rows_s, LANES), bf16),
        wide_map, wide_map, half_map, flat_map, ((pixels, LANES), bf16), ((in_ch, LANES), bf16), ((LANES, pixels), bf16),
        pltpu.SemaphoreType.DMA((8,)), pltpu.SemaphoreType.DMA((4,)),
    ]
    flops = 6 * pixels * LANES * (2 * in_ch + rows_s)
    fine = replicas > 1 and all(size[0][0] % replicas == 0 for size in sizes)
    split = (replicas // 2, rows_s // replicas, rows_e // replicas, rows_r // replicas, norm_size // replicas)
    half = ((split[0], round_up(split[1] + 1, 8) + split[2] + split[3], LANES), f32)
    params = [weights[1], weights[0], weights[2], norm_gain, norm_bias]
    moments = []
    for step in range(steps):
        branches = [functools.partial(swap_all, bit) for bit in range(levels)]
        theirs = list(lax.switch((round_index[0] + step) % levels, branches, params))
        if step == 0:
            sides = [[in_hbm(side[at]) for at in (1, 0, 2)] + side[3:] for side in (params, theirs)]
        else:
            sides = [params, [in_hbm(theirs[0]), theirs[1]]]
        operands = [in_hbm(images), in_hbm(cotangent)] + sides[0] + sides[1]
        operands += [in_hbm(member) for member in moments[:1]] + moments[1:]
        moment_outs = [in_hbm(whole), ((1, norm_size), f32)]
        scratch_of = scratch + [whole] if step else [whole] + scratch
        if step == steps - 1 and fine:
            core = in_smem(lax.axis_index("dp") % 2)
            kept, sent, *moments = run_kernel(
                functools.partial(step_kernel, step, True, split), "last_step", [core] + operands,
                [half, half] + moment_outs, scratch_of, flops, VMEM_BYTES,
            )
        else:
            *params, moment, norm_moment = run_kernel(
                functools.partial(step_kernel, step, False, None), "step", operands,
                [in_hbm(whole), norm_rows] + moment_outs, scratch_of, flops, VMEM_BYTES,
            )
            moments = [moment, norm_moment]
    def pack(sources, *spans):
        return run_kernel(
            functools.partial(pack_kernel, spans), "pack", sources,
            [((1, span * LANES if span else norm_size), bf16) for _, span in spans],
        )

    span_r, span_s, span_e = (0, rows_r), (rows_r, rows_s), (rows_r + rows_s, rows_e)
    if fine:
        beside = [
            functools.partial(pack, moments[:1], span_r, span_s), functools.partial(pack, moments, span_e, (0, 0))
        ]
        (first, second), averaged = scatter_mean(kept, sent, split, beside)
        out = first + second
    else:
        flat = [params[0][low:high].reshape(-1) for low, high in ((0, rows_r), (rows_r, rows_r + rows_s), (rows_r + rows_s, rows))]
        out, averaged = pack(moments, span_r, span_s, span_e, (0, 0)), scatter_mean_any(flat + [params[1].reshape(-1)])
    return tuple(averaged) + tuple(out)


def solution(mesh):
    in_specs = (
        P(None, "dp", None, None),
        P(None, "dp", None, None),
        P("dp", None),
        P("dp", None),
        P("dp", None),
        P("dp", None),
        P("dp", None),
        P(),
    )
    out_specs = (
        P("dp"),
        P("dp"),
        P("dp"),
        P("dp"),
        P("dp", None),
        P("dp", None),
        P("dp", None),
        P("dp", None),
    )
    return jax.shard_map(shards, mesh=mesh, in_specs=in_specs, out_specs=out_specs, check_vma=False)
```

```python
import functools

import jax
import jax.numpy as jnp
from jax import lax
from jax.experimental import pallas as pl
from jax.experimental.pallas import tpu as pltpu
from jax.sharding import PartitionSpec as P

HEIGHT = 28
WIDTH = 28
KSIZE = 3

LEARN_RATE = 0.01
MOMENTUM = 0.9
EPSILON = 1e-05

LANES = 128
PITCH = 32
VMEM_BYTES = 60 * 1024 * 1024
SMALL_VMEM = 8 * 1024 * 1024


def round_up(value, unit):
    return (value + unit - 1) // unit * unit


def partner_2(value, axis, distance):
    mask = 2**distance
    pairs = [(source, source ^ mask) for source in range(lax.axis_size(axis))]
    return lax.ppermute(value, axis, pairs)


def matmul(left, right):
    return jnp.dot(left, right, preferred_element_type=jnp.float32)


def contract_cols(left, right):
    return lax.dot_general(left, right, (((1,), (1,)), ((), ())), preferred_element_type=jnp.float32)


def activate_half(half):
    return half * (1.0 + jnp.tanh(half))


def twice_slope(half):
    bend = jnp.tanh(half)
    return (1.0 + bend) * (1.0 + half * (1.0 - bend))


def column_sum(values):
    return jnp.sum(values, axis=0, keepdims=True)


MAPS = 4
FLAT = MAPS * WIDTH
PITCHED = MAPS * PITCH
CHUNKS = HEIGHT // MAPS
SPAN = KSIZE * LANES
TOP = PITCH
TOP_BACK = 2 * PITCH
ROWS = round_up(HEIGHT * PITCH + 2 * PITCH, LANES)
ROWS_BACK = ROWS + 2 * PITCH


def flat_rows(at):
    return pl.ds(pl.multiple_of(at * FLAT, FLAT), FLAT)


def zero_row(width):
    return jnp.zeros((1, width), jnp.float32)


def sweep(body, init=0, unroll=True):
    return lax.fori_loop(0, CHUNKS, body, init, unroll=unroll)


def fold_rows(values):
    rows, width = values.shape
    return jnp.sum(values.reshape(rows // 8, 8, width), axis=0)


def zero_rows(width):
    return jnp.zeros((8, width), jnp.float32)


def statistics(values_ref, total):
    count, width = values_ref.shape
    mean = column_sum(total) / count

    def add(at, held):
        center = values_ref[flat_rows(at), :] - mean
        return held + fold_rows(center * center)

    return mean, lax.rsqrt(column_sum(sweep(add, zero_rows(width))) / count + EPSILON)


def pad_chunk(pad_ref, top, at, values):
    for row in range(MAPS):
        start = pl.multiple_of(at * PITCHED, PITCHED) + (8 + top + row * PITCH)
        pad_ref[pl.ds(start, WIDTH), :] = values[row * WIDTH : (row + 1) * WIDTH]


def shift_columns(pad_ref, out_ref):
    rows = out_ref.shape[0]
    for col_off in range(KSIZE):
        start = 8 + col_off - KSIZE // 2
        out_ref[:, col_off * LANES : (col_off + 1) * LANES] = pad_ref[start : start + rows, :].astype(jnp.bfloat16)


def conv_chunk(wide_ref, top, at, weight_of, multiply):
    total = None
    for row_off in range(KSIZE):
        start = pl.multiple_of(at * PITCHED, PITCHED) + (top + (row_off - KSIZE // 2) * PITCH)
        piece = multiply(wide_ref[pl.ds(start, PITCHED), :], weight_of(row_off))
        total = piece if total is None else total + piece
    return jnp.concatenate([total[row * PITCH : row * PITCH + WIDTH] for row in range(MAPS)], axis=0)


def mean_of(own, theirs):
    return (own + theirs) * 0.5


def rows_at(ref, start, rows):
    return ref.at[pl.ds(start, rows), :]


def step_kernel(step, last, split, *refs):
    it = iter(refs)
    take = lambda count: [next(it) for _ in range(count)]
    core_ref = next(it) if last else None
    images_ref, cotangent_ref = take(2)
    packed = step > 0
    own, theirs = (take(2) if packed else take(5)) , (take(2) if packed else take(5))
    held_out = take(2) if packed else []
    outs = take(2) if last else take(2)
    moment_out = next(it)
    norm_moment = next(it)
    own_ref = own[0] if packed else next(it)
    (x_ref, upstream_ref, theirs_ref, param_ref, moment_ref,
     normed_a, normed_b, hidden_b, wide, wide_t, wide_b, pad, pad_b, mixed_e, weight_e, weight_s, weight_f,
     third, grad_sum, grad_third, work, back, weight_t, arrived, left) = take(25)
    held_ref = next(it) if packed else None
    norm_out = next(it)
    kept_ref, sent_ref, rows_out = take(2) + [None] if last else [None, None] + take(1)
    smalls = list(it)
    norms = [] if packed else [own[3], theirs[3], own[4], theirs[4]]
    count, width = third.shape
    blocks = width // LANES
    rows_r, rows_s, rows_e = width, weight_s.shape[0], width
    spans = ((0, rows_r), (rows_r, rows_s), (rows_r + rows_s, rows_e))
    bf16 = jnp.bfloat16
    view = lambda ref, part: rows_at(ref, *spans[part])
    pending = {}

    def fetch(name, source, target):
        copy = pltpu.make_async_copy(source, target, arrived.at[len(pending)])
        copy.start()
        pending[name] = copy

    def fetch_part(part):
        fetch(("own", part), own[part], view(own_ref, part))
        fetch(("theirs", part), theirs[part], view(theirs_ref, part))

    def ready(part):
        if not packed:
            pending["own", part].wait()
            pending["theirs", part].wait()
        elif part < 2:
            pending["others" if part else "reduce"].wait()

    fetch("x", images_ref.at[step, 0], x_ref)
    if packed:
        later = rows_s + rows_e
        fetch("reduce", rows_at(theirs[0], 0, rows_r), rows_at(theirs_ref, 0, rows_r))
        fetch("others", rows_at(theirs[0], rows_r, later), rows_at(theirs_ref, rows_r, later))
    else:
        for part in range(3):
            fetch_part(part)
    for at, (source, target) in enumerate(zip([own[1], theirs[1], held_out[1]] if packed else norms, smalls)):
        fetch(("small", at), source, target)
    fetch("upstream", cotangent_ref.at[step, 0], upstream_ref)
    if packed:
        fetch("held", held_out[0], held_ref)
    stores = []

    def store(source, target):
        copy = pltpu.make_async_copy(source, target, left.at[len(stores)])
        copy.start()
        stores.append(copy)

    def settle(start, rows):
        store(rows_at(moment_ref, start, rows), rows_at(moment_out, start, rows))
        if not last:
            store(rows_at(param_ref, start, rows), rows_at(outs[0], start, rows))

    for at in range(len(smalls)):
        pending["small", at].wait()
    if packed:
        rows_of = lambda ref, low: jnp.concatenate([ref[low + at : low + at + 1, :] for at in range(ref.shape[0] // 2)], axis=1)
        half = smalls[0].shape[0] // 2
        gains = mean_of(rows_of(smalls[0], 0), rows_of(smalls[1], 0))
        shifts = mean_of(rows_of(smalls[0], half), rows_of(smalls[1], half))
    else:
        gains = mean_of(smalls[0][...], smalls[1][...])
        shifts = mean_of(smalls[2][...], smalls[3][...])
    gain_a, gain_b, gain_c = gains[:, :LANES], gains[:, LANES : 2 * LANES], gains[:, 2 * LANES :]
    shift_a, shift_b, shift_c = shifts[:, :LANES], shifts[:, LANES : 2 * LANES], shifts[:, 2 * LANES :]

    half_a, half_b = (0.5 * gain_a, 0.5 * shift_a), (0.5 * gain_b, 0.5 * shift_b)

    def mixed(part, start, rows):
        span = pl.ds(spans[part][0] + start, rows)
        return mean_of(own_ref[span, :], theirs_ref[span, :])

    def learn(part, start, rows, moment):
        span = pl.ds(spans[part][0] + start, rows)
        if packed:
            moment = MOMENTUM * held_ref[span, :] + moment
        moment_ref[span, :] = moment
        param_ref[span, :] = mixed(part, start, rows) - LEARN_RATE * moment

    pad[...] = jnp.zeros_like(pad)
    pad_b[...] = jnp.zeros_like(pad_b)
    pending["x"].wait()
    ready(0)
    reduce_w = mixed(0, 0, rows_r).astype(bf16)

    def make_first(at, total):
        values = matmul(x_ref[flat_rows(at), :], reduce_w)
        normed_a[flat_rows(at), :] = values
        return total + fold_rows(values)

    mean, scale_a = statistics(normed_a, sweep(make_first, zero_rows(LANES)))

    def make_hidden_a(at, carry):
        normed = (normed_a[flat_rows(at), :] - mean) * scale_a
        normed_a[flat_rows(at), :] = normed
        pad_chunk(pad, TOP, at, activate_half(normed * half_a[0] + half_a[1]))
        return carry

    sweep(make_hidden_a)
    shift_columns(pad, wide)

    taps = KSIZE * KSIZE
    ready(1)
    for tap in range(taps):
        weights = mixed(1, tap * LANES, LANES).astype(bf16)
        weight_s[tap * LANES : (tap + 1) * LANES, :] = weights
        other = taps - 1 - tap
        weight_f[other * LANES : (other + 1) * LANES, :] = weights.T

    def make_second(at, total):
        values = conv_chunk(wide, TOP, at, lambda row: weight_s[row * SPAN : (row + 1) * SPAN, :], matmul)
        normed_b[flat_rows(at), :] = values
        return total + fold_rows(values)

    mean, scale_b = statistics(normed_b, sweep(make_second, zero_rows(LANES)))

    def make_hidden_b(at, total):
        normed = (normed_b[flat_rows(at), :] - mean) * scale_b
        normed_b[flat_rows(at), :] = normed
        hidden = activate_half(normed * half_b[0] + half_b[1]).astype(bf16)
        hidden_b[flat_rows(at), :] = hidden
        return total + fold_rows(hidden.astype(jnp.float32))

    hidden_mean = column_sum(sweep(make_hidden_b, zero_rows(LANES))) / count

    ready(2)
    mixed_e[...] = mixed(2, 0, rows_e)
    for block in range(blocks):
        weights = mixed_e[pl.ds(block, LANES, stride=blocks), :].astype(bf16)
        weight_e[:, block * LANES : (block + 1) * LANES] = weights
        weight_t[block * LANES : (block + 1) * LANES, :] = weights.T

    rows, rest = [], hidden_mean
    for _ in range(3):
        rows.append(rest.astype(bf16).astype(jnp.float32))
        rest = rest - rows[-1]
    rows = jnp.concatenate(rows + [jnp.zeros((13, LANES), jnp.float32)], axis=0).astype(bf16)
    mean = column_sum(matmul(rows, weight_e[...]))

    def make_third(at, total):
        values = matmul(hidden_b[flat_rows(at), :], weight_e[...]) - mean
        third[flat_rows(at), :] = values
        return total + fold_rows(values * values)

    scale_c = lax.rsqrt(column_sum(sweep(make_third, zero_rows(width))) / count + EPSILON)
    stretch = scale_c * gain_c

    def make_sum(at, totals):
        values = third[flat_rows(at), :]
        half = 0.5 * (values * stretch + (shift_c + x_ref[flat_rows(at), :].astype(jnp.float32)))
        grad = upstream_ref[flat_rows(at), :].astype(jnp.float32) * twice_slope(half)
        grad_sum[flat_rows(at), :] = grad
        return totals[0] + fold_rows(grad * values), totals[1] + fold_rows(grad)

    pending["upstream"].wait()
    totals = sweep(make_sum, (zero_rows(width), zero_rows(width)), False)
    dgain_c, dshift_c = 0.5 * scale_c * column_sum(totals[0]), 0.5 * column_sum(totals[1])
    level, slope, factor = 2.0 * dshift_c / count, 2.0 * scale_c * dgain_c / count, 0.5 * stretch

    def make_back_c(at, totals):
        grad = (grad_sum[flat_rows(at), :] - level - third[flat_rows(at), :] * slope) * factor
        grad = grad.astype(bf16)
        grad_third[flat_rows(at), :] = grad
        normed = normed_b[flat_rows(at), :]
        grad_out = matmul(grad, weight_t[...]) * twice_slope(normed * half_b[0] + half_b[1])
        work[flat_rows(at), :] = grad_out
        return totals[0] + fold_rows(grad_out * normed), totals[1] + fold_rows(grad_out)

    dgain_b, dshift_b = [0.5 * column_sum(total) for total in sweep(make_back_c, (zero_rows(LANES), zero_rows(LANES)))]
    grad = matmul(hidden_b[...].T, grad_third[...])
    for block in range(blocks):
        mixed_e[pl.ds(block, LANES, stride=blocks), :] = grad[:, block * LANES : (block + 1) * LANES]
    if packed:
        pending["held"].wait()
    learn(2, 0, rows_e, mixed_e[...])

    level_b, slope_b, factor_b = 2.0 * dshift_b / count, 2.0 * dgain_b / count, 0.5 * scale_b * gain_b

    def make_back_b(at, carry):
        grad = (work[flat_rows(at), :] - level_b - normed_b[flat_rows(at), :] * slope_b) * factor_b
        pad_chunk(pad_b, TOP_BACK, at, grad)
        return carry

    sweep(make_back_b)
    shift_columns(pad_b, wide_b)

    for at in range(ROWS // LANES):
        wide_t[:, at * LANES : (at + 1) * LANES] = wide[at * LANES : (at + 1) * LANES, :].T

    shifted = [
        wide_b[TOP_BACK - row_off * PITCH : TOP_BACK - row_off * PITCH + ROWS, LANES : 2 * LANES]
        for row_off in range(KSIZE)
    ]
    grad = matmul(wide_t[...], jnp.concatenate(shifted, axis=1))
    for row_off in range(KSIZE):
        learn(1, row_off * SPAN, SPAN, grad[:, row_off * LANES : (row_off + 1) * LANES])
    settle(rows_r, rows_s + rows_e)

    def make_back_a(at, totals):
        grad = conv_chunk(wide_b, TOP_BACK, at, lambda row: weight_f[row * SPAN : (row + 1) * SPAN, :], matmul)
        normed = normed_a[flat_rows(at), :]
        grad_out = grad * twice_slope(normed * half_a[0] + half_a[1])
        work[flat_rows(at), :] = grad_out
        return totals[0] + fold_rows(grad_out * normed), totals[1] + fold_rows(grad_out)

    dgain_a, dshift_a = [0.5 * column_sum(total) for total in sweep(make_back_a, (zero_rows(LANES), zero_rows(LANES)))]
    level_a, slope_a, factor_a = 2.0 * dshift_a / count, 2.0 * dgain_a / count, 0.5 * scale_a * gain_a

    def make_first_grad(at, carry):
        grad = (work[flat_rows(at), :] - level_a - normed_a[flat_rows(at), :] * slope_a) * factor_a
        back[flat_rows(at), :] = grad.astype(bf16)
        return carry

    sweep(make_first_grad)
    grad = matmul(back[...].T, x_ref[...])
    for block in range(blocks):
        learn(0, block * LANES, LANES, grad[:, block * LANES : (block + 1) * LANES].T)
    settle(0, rows_r)
    grad = jnp.concatenate([dgain_a, dgain_b, dgain_c, dshift_a, dshift_b, dshift_c], axis=1)
    norm = jnp.concatenate([gains, shifts], axis=1)
    if packed:
        grad = MOMENTUM * smalls[2][...] + grad
    norm_out[...] = grad
    store(norm_out, norm_moment)
    norm = norm - LEARN_RATE * grad
    if not last:
        for at in range(norm.shape[1] // LANES):
            rows_out[at : at + 1, :] = norm[:, at * LANES : (at + 1) * LANES]
        store(rows_out, outs[1])
        for copy in stores:
            copy.wait()
        return

    is_odd = jnp.full((1, 1), core_ref[0], jnp.int32) == 1
    pairs, piece_s, piece_e, piece_r, piece_n = split
    at_e = round_up(piece_s + 1, 8)
    at_r = at_e + piece_e

    def place(pair, start, low, high):
        rows = low.shape[0]
        kept_ref[pair, start : start + rows, :] = jnp.where(is_odd, high, low)
        sent_ref[pair, start : start + rows, :] = jnp.where(is_odd, low, high)

    for pair in range(pairs):
        for part, rows, start in ((1, piece_s, 0), (2, piece_e, at_e), (0, piece_r, at_r)):
            first = spans[part][0] + 2 * pair * rows
            place(pair, start, param_ref[first : first + rows, :], param_ref[first + rows : first + 2 * rows, :])
        low, high = [
            jnp.concatenate(
                [norm[:, at * piece_n : (at + 1) * piece_n], jnp.zeros((1, LANES - piece_n), jnp.float32)], axis=1
            )
            for at in (2 * pair, 2 * pair + 1)
        ]
        rest = jnp.zeros((at_e - piece_s - 1, LANES), jnp.float32)
        place(pair, piece_s, jnp.concatenate([low, rest]), jnp.concatenate([high, rest]))
    store(sent_ref, outs[1])
    store(kept_ref, outs[0])
    for copy in stores:
        copy.wait()


def fold_kernel(bits, *refs):
    spot_ref, kept_ref = refs[:2]
    came, outs, total = refs[2 : 2 + bits[0]], refs[2 + bits[0] : -1], refs[-1]
    values = kept_ref[...]
    for ref in came:
        values = values + ref[...]
    total[...] = values
    ways = len(outs)
    for hop, out in enumerate(outs):
        for at in range(out.shape[0]):
            out[at] = total[at * ways + jnp.bitwise_xor(spot_ref[0], hop)]


def mean_kernel(replicas, spans, *refs):
    outs = refs[-len(spans) :]
    kept_ref, came = refs[0], refs[1 : -len(spans)]
    values = kept_ref[0]
    for ref in came:
        values = values + ref[0]
    values = values * (1.0 / replicas)
    for (start, rows), out in zip(spans, outs):
        width = out.shape[0] // rows
        for at in range(rows):
            out[at * width : (at + 1) * width] = values[start + at, :width]


def copy_kernel(source, target, sem):
    copy = pltpu.make_async_copy(source, target, sem)
    copy.start()
    copy.wait()


def pack_kernel(spans, *refs):
    source, outs = refs[0], refs[-len(spans) :]
    for (start, rows), out in zip(spans, outs):
        if rows == 0:
            out[...] = refs[1][...].astype(jnp.bfloat16)
            continue

        def lay(at, carry, start=start, out=out):
            base = pl.multiple_of(at * 16, 16)
            for row in range(16):
                values = source[pl.ds(start + base + row, 1), :].astype(jnp.bfloat16)
                out[0:1, pl.ds(pl.multiple_of((base + row) * LANES, LANES), LANES)] = values
            return carry

        lax.fori_loop(0, rows // 16, lay, 0)


def run_kernel(body, name, operands, outs, scratch=(), flops=0, vmem=SMALL_VMEM):
    def parts(entries, is_plain):
        plain = [entry if is_plain(entry) else entry[0] for entry in entries]
        return plain, [pl.BlockSpec(memory_space=pltpu.VMEM if is_plain(entry) else entry[1]) for entry in entries]

    arrays, in_specs = parts(operands, lambda entry: not isinstance(entry, tuple))
    shapes, out_specs = parts(outs, lambda entry: isinstance(entry[0], tuple) and not isinstance(entry[0][0], tuple))
    moved = sum(array.size * array.dtype.itemsize for array in arrays)
    return list(pl.pallas_call(
        body,
        in_specs=in_specs,
        out_specs=out_specs,
        out_shape=[jax.ShapeDtypeStruct(shape, kind) for shape, kind in shapes],
        scratch_shapes=[pltpu.VMEM(*entry) if isinstance(entry, tuple) else entry for entry in scratch],
        compiler_params=pltpu.CompilerParams(vmem_limit_bytes=vmem),
        cost_estimate=pl.CostEstimate(flops=flops, bytes_accessed=moved, transcendentals=0),
        name=name,
    )(*arrays))


def in_hbm(entry):
    return entry, pltpu.HBM


def in_smem(value):
    return value.astype(jnp.int32).reshape(1), pltpu.SMEM


def swap_all(bit, values):
    return [partner_2(member, "dp", bit) for member in values]


def exchange(spot, first_bit, ways, sends):
    replicas = lax.axis_size("dp")
    came = []
    for hop in [ways - 1] + list(range(1, ways - 1)):
        pairs = [(at, at ^ (hop << first_bit)) for at in range(replicas)]
        came.append(lax.ppermute(sends[hop - 1], "dp", pairs))
    return came


def scatter_mean(kept, sent, split, beside):
    f32 = jnp.float32
    replicas = lax.axis_size("dp")
    levels = replicas.bit_length() - 1
    place = lax.axis_index("dp")
    pairs, piece_s, piece_e, piece_r, piece_n = split
    rows = kept.shape[1]
    came = exchange(place, 0, 2, [sent])
    (kept,) = run_kernel(
        copy_kernel, "copy", [in_hbm(kept)], [(kept.shape, f32)], [pltpu.SemaphoreType.DMA(())]
    )
    came, kept = lax.optimization_barrier((came, kept))
    left, low, done = pairs, 1, []
    while left > 1:
        width = 2 if low == 1 and levels > 2 else 1
        ways = 1 << width
        spot = in_smem((place >> low) % ways)
        kept, *sends = run_kernel(
            functools.partial(fold_kernel, (len(came),)), "fold", [spot, kept] + came,
            [((left // ways, rows, LANES), f32)] * ways, [((left, rows, LANES), f32)],
        )
        came = exchange(place, low, ways, sends)
        if beside:
            work, *beside = beside
            came, ready = lax.optimization_barrier((came, work()))
            done.append(ready)
        left, low = left // ways, low + width
    at_e = round_up(piece_s + 1, 8)
    spans = ((at_e + piece_e, piece_r), (0, piece_s), (at_e, piece_e), (piece_s, 1))
    sizes = [(rows_of * LANES,) for _, rows_of in spans[:3]] + [(piece_n,)]
    mean = run_kernel(
        functools.partial(mean_kernel, replicas, spans), "mean", [kept] + came, [(size, f32) for size in sizes]
    )
    return done + [work() for work in beside], mean


def scatter_mean_any(arrays):
    replicas = lax.axis_size("dp")
    tables = [member.reshape(replicas, -1) for member in arrays]
    pieces = lax.all_to_all(jnp.concatenate(tables, axis=1), "dp", 0, 0, tiled=True)
    mean = jnp.sum(pieces, axis=0) / replicas
    bounds = [sum(table.shape[1] for table in tables[:at]) for at in range(len(tables) + 1)]
    return tuple(mean[low:high] for low, high in zip(bounds[:-1], bounds[1:]))


def shards(images, cotangent, w_reduce, w_spatial, w_expand, norm_gain, norm_bias, round_index):
    f32, bf16 = jnp.float32, jnp.bfloat16
    replicas = lax.axis_size("dp")
    levels = replicas.bit_length() - 1
    steps, _, pixels, in_ch = images.shape
    weights = [member.reshape(-1, LANES) for member in (w_reduce, w_spatial, w_expand)]
    sizes = [(member.shape, f32) for member in weights]
    rows_r, rows_s, rows_e = (member.shape[0] for member in weights)
    rows = rows_r + rows_s + rows_e
    norm_size = 2 * norm_gain.size
    flat_map = ((pixels, LANES), f32)
    wide_map = ((pixels, in_ch), f32)
    whole = ((rows, LANES), f32)
    norm_rows = ((norm_size // LANES, LANES), f32)
    half_map = ((pixels, in_ch), bf16)
    scratch = [
        half_map, half_map, whole, whole, whole,
        flat_map, flat_map, ((pixels, LANES), bf16), ((ROWS, SPAN), bf16), ((SPAN, ROWS), bf16),
        ((ROWS_BACK, SPAN), bf16), ((ROWS + 16, LANES), f32), ((ROWS_BACK + 16, LANES), f32),
        sizes[2], ((LANES, in_ch), bf16), ((rows_s, LANES), bf16), ((rows_s, LANES), bf16),
        wide_map, wide_map, half_map, flat_map, ((pixels, LANES), bf16), ((in_ch, LANES), bf16),
        pltpu.SemaphoreType.DMA((12,)), pltpu.SemaphoreType.DMA((6,)),
    ]
    flops = 6 * pixels * LANES * (2 * in_ch + rows_s)
    fine = replicas > 1 and all(size[0][0] % replicas == 0 for size in sizes)
    split = (replicas // 2, rows_s // replicas, rows_e // replicas, rows_r // replicas, norm_size // replicas)
    half = ((split[0], round_up(split[1] + 1, 8) + split[2] + split[3], LANES), f32)
    params = [weights[1], weights[0], weights[2], norm_gain, norm_bias]
    moments = []
    for step in range(steps):
        branches = [functools.partial(swap_all, bit) for bit in range(levels)]
        theirs = list(lax.switch((round_index[0] + step) % levels, branches, params))
        if step == 0:
            sides = [[in_hbm(side[at]) for at in (1, 0, 2, 3, 4)] for side in (params, theirs)]
        else:
            sides = [[params[0], in_hbm(params[1])], [in_hbm(member) for member in theirs]]
        operands = [in_hbm(images), in_hbm(cotangent)] + sides[0] + sides[1]
        operands += [in_hbm(member) for member in moments]
        norm_flat = ((1, norm_size), f32)
        moment_outs = [in_hbm(whole), in_hbm(norm_flat)]
        scratch_of = scratch + [whole] if step else [whole] + scratch
        last = step == steps - 1 and fine
        scratch_of += [norm_flat] + ([half, half] if last else [norm_rows])
        scratch_of += [norm_rows, norm_rows, norm_flat] if step else [(norm_gain.shape, f32)] * 4
        if last:
            core = in_smem(lax.axis_index("dp") % 2)
            kept, sent, *moments = run_kernel(
                functools.partial(step_kernel, step, True, split), "last_step", [core] + operands,
                [in_hbm(half), in_hbm(half)] + moment_outs, scratch_of, flops, VMEM_BYTES,
            )
        else:
            *params, moment, norm_moment = run_kernel(
                functools.partial(step_kernel, step, False, None), "step", operands,
                [in_hbm(whole), in_hbm(norm_rows)] + moment_outs, scratch_of, flops, VMEM_BYTES,
            )
            moments = [moment, norm_moment]
    def pack(sources, *spans):
        return run_kernel(
            functools.partial(pack_kernel, spans), "pack", sources,
            [((1, span * LANES if span else norm_size), bf16) for _, span in spans],
        )

    span_r, span_s, span_e = (0, rows_r), (rows_r, rows_s), (rows_r + rows_s, rows_e)
    if fine:
        beside = [
            functools.partial(pack, moments[:1], span_r, span_s), functools.partial(pack, moments, span_e, (0, 0))
        ]
        (first, second), averaged = scatter_mean(kept, sent, split, beside)
        out = first + second
    else:
        flat = [params[0][low:high].reshape(-1) for low, high in ((0, rows_r), (rows_r, rows_r + rows_s), (rows_r + rows_s, rows))]
        out, averaged = pack(moments, span_r, span_s, span_e, (0, 0)), scatter_mean_any(flat + [params[1].reshape(-1)])
    return tuple(averaged) + tuple(out)


def solution(mesh):
    in_specs = (
        P(None, "dp", None, None),
        P(None, "dp", None, None),
        P("dp", None),
        P("dp", None),
        P("dp", None),
        P("dp", None),
        P("dp", None),
        P(),
    )
    out_specs = (
        P("dp"),
        P("dp"),
        P("dp"),
        P("dp"),
        P("dp", None),
        P("dp", None),
        P("dp", None),
        P("dp", None),
    )
    return jax.shard_map(shards, mesh=mesh, in_specs=in_specs, out_specs=out_specs, check_vma=False)
```

```python
import functools

import jax
import jax.numpy as jnp
from jax import lax
from jax.experimental import pallas as pl
from jax.experimental.pallas import tpu as pltpu
from jax.sharding import PartitionSpec as P

HEIGHT = 28
WIDTH = 28
KSIZE = 3

LEARN_RATE = 0.01
MOMENTUM = 0.9
EPSILON = 1e-05

LANES = 128
PITCH = 32
VMEM_BYTES = 60 * 1024 * 1024
SMALL_VMEM = 8 * 1024 * 1024


def round_up(value, unit):
    return (value + unit - 1) // unit * unit


def partner_2(value, axis, distance):
    mask = 2**distance
    pairs = [(source, source ^ mask) for source in range(lax.axis_size(axis))]
    return lax.ppermute(value, axis, pairs)


def matmul(left, right):
    return jnp.dot(left, right, preferred_element_type=jnp.float32)


def contract_cols(left, right):
    return lax.dot_general(left, right, (((1,), (1,)), ((), ())), preferred_element_type=jnp.float32)


def activate_half(half):
    return half * (1.0 + jnp.tanh(half))


def twice_slope(half):
    bend = jnp.tanh(half)
    return (1.0 + bend) * (1.0 + half * (1.0 - bend))


def column_sum(values):
    return jnp.sum(values, axis=0, keepdims=True)


MAPS = 4
FLAT = MAPS * WIDTH
PITCHED = MAPS * PITCH
CHUNKS = HEIGHT // MAPS
SPAN = KSIZE * LANES
TOP = PITCH
TOP_BACK = 2 * PITCH
ROWS = round_up(HEIGHT * PITCH + 2 * PITCH, LANES)
ROWS_BACK = ROWS + 2 * PITCH


def flat_rows(at):
    return pl.ds(pl.multiple_of(at * FLAT, FLAT), FLAT)


def zero_row(width):
    return jnp.zeros((1, width), jnp.float32)


def sweep(body, init=0, unroll=True):
    return lax.fori_loop(0, CHUNKS, body, init, unroll=unroll)


def fold_rows(values):
    rows, width = values.shape
    return jnp.sum(values.reshape(rows // 8, 8, width), axis=0)


def zero_rows(width):
    return jnp.zeros((8, width), jnp.float32)


def statistics(values_ref, total):
    count, width = values_ref.shape
    mean = column_sum(total) / count

    def add(at, held):
        center = values_ref[flat_rows(at), :] - mean
        return held + fold_rows(center * center)

    return mean, lax.rsqrt(column_sum(sweep(add, zero_rows(width))) / count + EPSILON)


def pad_chunk(pad_ref, top, at, values):
    for row in range(MAPS):
        start = pl.multiple_of(at * PITCHED, PITCHED) + (8 + top + row * PITCH)
        pad_ref[pl.ds(start, WIDTH), :] = values[row * WIDTH : (row + 1) * WIDTH]


def shift_columns(pad_ref, out_ref):
    rows = out_ref.shape[0]
    for col_off in range(KSIZE):
        start = 8 + col_off - KSIZE // 2
        out_ref[:, col_off * LANES : (col_off + 1) * LANES] = pad_ref[start : start + rows, :].astype(jnp.bfloat16)


def conv_chunk(wide_ref, top, at, weight_of, multiply):
    total = None
    for row_off in range(KSIZE):
        start = pl.multiple_of(at * PITCHED, PITCHED) + (top + (row_off - KSIZE // 2) * PITCH)
        piece = multiply(wide_ref[pl.ds(start, PITCHED), :], weight_of(row_off))
        total = piece if total is None else total + piece
    return jnp.concatenate([total[row * PITCH : row * PITCH + WIDTH] for row in range(MAPS)], axis=0)


def mean_of(own, theirs):
    return (own + theirs) * 0.5


def rows_at(ref, start, rows):
    return ref.at[pl.ds(start, rows), :]


def step_kernel(step, last, split, *refs):
    it = iter(refs)
    take = lambda count: [next(it) for _ in range(count)]
    core_ref = next(it) if last else None
    images_ref, cotangent_ref = take(2)
    packed = step > 0
    own, theirs = (take(2) if packed else take(5)) , (take(2) if packed else take(5))
    held_out = take(2) if packed else []
    outs = take(2) if last else take(2)
    moment_out = next(it)
    norm_moment = next(it)
    own_ref = own[0] if packed else next(it)
    (x_ref, upstream_ref, theirs_ref, param_ref, moment_ref,
     normed_a, normed_b, hidden_b, wide, wide_t, wide_b, pad, pad_b, mixed_e, weight_e, weight_s, weight_f,
     third, grad_sum, grad_third, work, back, weight_t, arrived, left) = take(25)
    held_ref = next(it) if packed else None
    norm_out = next(it)
    kept_ref, sent_ref, rows_out = take(2) + [None] if last else [None, None] + take(1)
    smalls = list(it)
    norms = [] if packed else [own[3], theirs[3], own[4], theirs[4]]
    count, width = third.shape
    blocks = width // LANES
    rows_r, rows_s, rows_e = width, weight_s.shape[0], width
    spans = ((0, rows_r), (rows_r, rows_s), (rows_r + rows_s, rows_e))
    bf16 = jnp.bfloat16
    view = lambda ref, part: rows_at(ref, *spans[part])
    pending = {}

    def fetch(name, source, target):
        copy = pltpu.make_async_copy(source, target, arrived.at[len(pending)])
        copy.start()
        pending[name] = copy

    def fetch_part(part):
        fetch(("own", part), own[part], view(own_ref, part))
        fetch(("theirs", part), theirs[part], view(theirs_ref, part))

    def ready(part):
        if not packed:
            pending["own", part].wait()
            pending["theirs", part].wait()
        elif part < 2:
            pending["others" if part else "reduce"].wait()

    fetch("x", images_ref.at[step, 0], x_ref)
    if packed:
        fetch("reduce", rows_at(theirs[0], 0, rows_r), rows_at(theirs_ref, 0, rows_r))
    else:
        fetch_part(0)
    for at, (source, target) in enumerate(zip([own[1], theirs[1], held_out[1]] if packed else norms, smalls)):
        fetch(("small", at), source, target)
    if packed:
        later = rows_s + rows_e
        fetch("others", rows_at(theirs[0], rows_r, later), rows_at(theirs_ref, rows_r, later))
    else:
        fetch_part(1)
        fetch_part(2)
    fetch("upstream", cotangent_ref.at[step, 0], upstream_ref)
    if packed:
        fetch("held", held_out[0], held_ref)
    stores = []

    def store(source, target):
        copy = pltpu.make_async_copy(source, target, left.at[len(stores)])
        copy.start()
        stores.append(copy)

    def settle(start, rows):
        store(rows_at(moment_ref, start, rows), rows_at(moment_out, start, rows))
        if not last:
            store(rows_at(param_ref, start, rows), rows_at(outs[0], start, rows))

    for at in range(len(smalls)):
        pending["small", at].wait()
    if packed:
        rows_of = lambda ref, low: jnp.concatenate([ref[low + at : low + at + 1, :] for at in range(ref.shape[0] // 2)], axis=1)
        half = smalls[0].shape[0] // 2
        gains = mean_of(rows_of(smalls[0], 0), rows_of(smalls[1], 0))
        shifts = mean_of(rows_of(smalls[0], half), rows_of(smalls[1], half))
    else:
        gains = mean_of(smalls[0][...], smalls[1][...])
        shifts = mean_of(smalls[2][...], smalls[3][...])
    gain_a, gain_b, gain_c = gains[:, :LANES], gains[:, LANES : 2 * LANES], gains[:, 2 * LANES :]
    shift_a, shift_b, shift_c = shifts[:, :LANES], shifts[:, LANES : 2 * LANES], shifts[:, 2 * LANES :]

    half_a, half_b = (0.5 * gain_a, 0.5 * shift_a), (0.5 * gain_b, 0.5 * shift_b)

    def mixed(part, start, rows):
        span = pl.ds(spans[part][0] + start, rows)
        return mean_of(own_ref[span, :], theirs_ref[span, :])

    def learn(part, start, rows, moment):
        span = pl.ds(spans[part][0] + start, rows)
        if packed:
            moment = MOMENTUM * held_ref[span, :] + moment
        moment_ref[span, :] = moment
        param_ref[span, :] = mixed(part, start, rows) - LEARN_RATE * moment

    pad[...] = jnp.zeros_like(pad)
    pad_b[...] = jnp.zeros_like(pad_b)
    pending["x"].wait()
    ready(0)
    reduce_w = mixed(0, 0, rows_r).astype(bf16)

    def make_first(at, total):
        values = matmul(x_ref[flat_rows(at), :], reduce_w)
        normed_a[flat_rows(at), :] = values
        return total + fold_rows(values)

    mean, scale_a = statistics(normed_a, sweep(make_first, zero_rows(LANES)))

    def make_hidden_a(at, carry):
        normed = (normed_a[flat_rows(at), :] - mean) * scale_a
        normed_a[flat_rows(at), :] = normed
        pad_chunk(pad, TOP, at, activate_half(normed * half_a[0] + half_a[1]))
        return carry

    sweep(make_hidden_a)
    shift_columns(pad, wide)

    taps = KSIZE * KSIZE
    ready(1)
    for tap in range(taps):
        weights = mixed(1, tap * LANES, LANES).astype(bf16)
        weight_s[tap * LANES : (tap + 1) * LANES, :] = weights
        other = taps - 1 - tap
        weight_f[other * LANES : (other + 1) * LANES, :] = weights.T

    def make_second(at, total):
        values = conv_chunk(wide, TOP, at, lambda row: weight_s[row * SPAN : (row + 1) * SPAN, :], matmul)
        normed_b[flat_rows(at), :] = values
        return total + fold_rows(values)

    mean, scale_b = statistics(normed_b, sweep(make_second, zero_rows(LANES)))

    def make_hidden_b(at, total):
        normed = (normed_b[flat_rows(at), :] - mean) * scale_b
        normed_b[flat_rows(at), :] = normed
        hidden = activate_half(normed * half_b[0] + half_b[1]).astype(bf16)
        hidden_b[flat_rows(at), :] = hidden
        return total + fold_rows(hidden.astype(jnp.float32))

    hidden_mean = column_sum(sweep(make_hidden_b, zero_rows(LANES))) / count

    ready(2)
    mixed_e[...] = mixed(2, 0, rows_e)
    for block in range(blocks):
        weights = mixed_e[pl.ds(block, LANES, stride=blocks), :].astype(bf16)
        weight_e[:, block * LANES : (block + 1) * LANES] = weights
        weight_t[block * LANES : (block + 1) * LANES, :] = weights.T

    rows, rest = [], hidden_mean
    for _ in range(3):
        rows.append(rest.astype(bf16).astype(jnp.float32))
        rest = rest - rows[-1]
    rows = jnp.concatenate(rows + [jnp.zeros((13, LANES), jnp.float32)], axis=0).astype(bf16)
    mean = column_sum(matmul(rows, weight_e[...]))

    def make_third(at, total):
        values = matmul(hidden_b[flat_rows(at), :], weight_e[...]) - mean
        third[flat_rows(at), :] = values
        return total + fold_rows(values * values)

    scale_c = lax.rsqrt(column_sum(sweep(make_third, zero_rows(width))) / count + EPSILON)
    stretch = scale_c * gain_c

    def make_sum(at, totals):
        values = third[flat_rows(at), :]
        half = 0.5 * (values * stretch + (shift_c + x_ref[flat_rows(at), :].astype(jnp.float32)))
        grad = upstream_ref[flat_rows(at), :].astype(jnp.float32) * twice_slope(half)
        grad_sum[flat_rows(at), :] = grad
        return totals[0] + fold_rows(grad * values), totals[1] + fold_rows(grad)

    pending["upstream"].wait()
    totals = sweep(make_sum, (zero_rows(width), zero_rows(width)), False)
    dgain_c, dshift_c = 0.5 * scale_c * column_sum(totals[0]), 0.5 * column_sum(totals[1])
    level, slope, factor = 2.0 * dshift_c / count, 2.0 * scale_c * dgain_c / count, 0.5 * stretch

    def make_back_c(at, totals):
        grad = (grad_sum[flat_rows(at), :] - level - third[flat_rows(at), :] * slope) * factor
        grad = grad.astype(bf16)
        grad_third[flat_rows(at), :] = grad
        normed = normed_b[flat_rows(at), :]
        grad_out = matmul(grad, weight_t[...]) * twice_slope(normed * half_b[0] + half_b[1])
        work[flat_rows(at), :] = grad_out
        return totals[0] + fold_rows(grad_out * normed), totals[1] + fold_rows(grad_out)

    dgain_b, dshift_b = [0.5 * column_sum(total) for total in sweep(make_back_c, (zero_rows(LANES), zero_rows(LANES)))]
    grad = matmul(hidden_b[...].T, grad_third[...])
    for block in range(blocks):
        mixed_e[pl.ds(block, LANES, stride=blocks), :] = grad[:, block * LANES : (block + 1) * LANES]
    if packed:
        pending["held"].wait()
    learn(2, 0, rows_e, mixed_e[...])

    level_b, slope_b, factor_b = 2.0 * dshift_b / count, 2.0 * dgain_b / count, 0.5 * scale_b * gain_b

    def make_back_b(at, carry):
        grad = (work[flat_rows(at), :] - level_b - normed_b[flat_rows(at), :] * slope_b) * factor_b
        pad_chunk(pad_b, TOP_BACK, at, grad)
        return carry

    sweep(make_back_b)
    shift_columns(pad_b, wide_b)

    for at in range(ROWS // LANES):
        wide_t[:, at * LANES : (at + 1) * LANES] = wide[at * LANES : (at + 1) * LANES, :].T

    shifted = [
        wide_b[TOP_BACK - row_off * PITCH : TOP_BACK - row_off * PITCH + ROWS, LANES : 2 * LANES]
        for row_off in range(KSIZE)
    ]
    grad = matmul(wide_t[...], jnp.concatenate(shifted, axis=1))
    for row_off in range(KSIZE):
        learn(1, row_off * SPAN, SPAN, grad[:, row_off * LANES : (row_off + 1) * LANES])
    settle(rows_r, rows_s + rows_e)

    def make_back_a(at, totals):
        grad = conv_chunk(wide_b, TOP_BACK, at, lambda row: weight_f[row * SPAN : (row + 1) * SPAN, :], matmul)
        normed = normed_a[flat_rows(at), :]
        grad_out = grad * twice_slope(normed * half_a[0] + half_a[1])
        work[flat_rows(at), :] = grad_out
        return totals[0] + fold_rows(grad_out * normed), totals[1] + fold_rows(grad_out)

    dgain_a, dshift_a = [0.5 * column_sum(total) for total in sweep(make_back_a, (zero_rows(LANES), zero_rows(LANES)))]
    level_a, slope_a, factor_a = 2.0 * dshift_a / count, 2.0 * dgain_a / count, 0.5 * scale_a * gain_a

    def make_first_grad(at, carry):
        grad = (work[flat_rows(at), :] - level_a - normed_a[flat_rows(at), :] * slope_a) * factor_a
        back[flat_rows(at), :] = grad.astype(bf16)
        return carry

    sweep(make_first_grad)
    grad = matmul(back[...].T, x_ref[...])
    for block in range(blocks):
        learn(0, block * LANES, LANES, grad[:, block * LANES : (block + 1) * LANES].T)
    settle(0, rows_r)
    grad = jnp.concatenate([dgain_a, dgain_b, dgain_c, dshift_a, dshift_b, dshift_c], axis=1)
    norm = jnp.concatenate([gains, shifts], axis=1)
    if packed:
        grad = MOMENTUM * smalls[2][...] + grad
    norm_out[...] = grad
    store(norm_out, norm_moment)
    norm = norm - LEARN_RATE * grad
    if not last:
        for at in range(norm.shape[1] // LANES):
            rows_out[at : at + 1, :] = norm[:, at * LANES : (at + 1) * LANES]
        store(rows_out, outs[1])
        for copy in stores:
            copy.wait()
        return

    is_odd = jnp.full((1, 1), core_ref[0], jnp.int32) == 1
    pairs, piece_s, piece_e, piece_r, piece_n = split
    at_e = round_up(piece_s + 1, 8)
    at_r = at_e + piece_e

    def place(pair, start, low, high):
        rows = low.shape[0]
        kept_ref[pair, start : start + rows, :] = jnp.where(is_odd, high, low)
        sent_ref[pair, start : start + rows, :] = jnp.where(is_odd, low, high)

    for pair in range(pairs):
        for part, rows, start in ((1, piece_s, 0), (2, piece_e, at_e), (0, piece_r, at_r)):
            first = spans[part][0] + 2 * pair * rows
            place(pair, start, param_ref[first : first + rows, :], param_ref[first + rows : first + 2 * rows, :])
        low, high = [
            jnp.concatenate(
                [norm[:, at * piece_n : (at + 1) * piece_n], jnp.zeros((1, LANES - piece_n), jnp.float32)], axis=1
            )
            for at in (2 * pair, 2 * pair + 1)
        ]
        rest = jnp.zeros((at_e - piece_s - 1, LANES), jnp.float32)
        place(pair, piece_s, jnp.concatenate([low, rest]), jnp.concatenate([high, rest]))
    store(sent_ref, outs[1])
    store(kept_ref, outs[0])
    for copy in stores:
        copy.wait()


def fold_kernel(bits, *refs):
    spot_ref, kept_ref = refs[:2]
    came, outs, total = refs[2 : 2 + bits[0]], refs[2 + bits[0] : -1], refs[-1]
    values = kept_ref[...]
    for ref in came:
        values = values + ref[...]
    total[...] = values
    ways = len(outs)
    for hop, out in enumerate(outs):
        for at in range(out.shape[0]):
            out[at] = total[at * ways + jnp.bitwise_xor(spot_ref[0], hop)]


def mean_kernel(replicas, spans, *refs):
    outs = refs[-len(spans) :]
    kept_ref, came = refs[0], refs[1 : -len(spans)]
    values = kept_ref[0]
    for ref in came:
        values = values + ref[0]
    values = values * (1.0 / replicas)
    for (start, rows), out in zip(spans, outs):
        width = out.shape[0] // rows
        for at in range(rows):
            out[at * width : (at + 1) * width] = values[start + at, :width]


def copy_kernel(source, target, sem):
    copy = pltpu.make_async_copy(source, target, sem)
    copy.start()
    copy.wait()


def pack_kernel(spans, *refs):
    source, outs = refs[0], refs[-len(spans) :]
    for (start, rows), out in zip(spans, outs):
        if rows == 0:
            out[...] = refs[1][...].astype(jnp.bfloat16)
            continue

        def lay(at, carry, start=start, out=out):
            base = pl.multiple_of(at * 16, 16)
            for row in range(16):
                values = source[pl.ds(start + base + row, 1), :].astype(jnp.bfloat16)
                out[0:1, pl.ds(pl.multiple_of((base + row) * LANES, LANES), LANES)] = values
            return carry

        lax.fori_loop(0, rows // 16, lay, 0)


def run_kernel(body, name, operands, outs, scratch=(), flops=0, vmem=SMALL_VMEM):
    def parts(entries, is_plain):
        plain = [entry if is_plain(entry) else entry[0] for entry in entries]
        return plain, [pl.BlockSpec(memory_space=pltpu.VMEM if is_plain(entry) else entry[1]) for entry in entries]

    arrays, in_specs = parts(operands, lambda entry: not isinstance(entry, tuple))
    shapes, out_specs = parts(outs, lambda entry: isinstance(entry[0], tuple) and not isinstance(entry[0][0], tuple))
    moved = sum(array.size * array.dtype.itemsize for array in arrays)
    return list(pl.pallas_call(
        body,
        in_specs=in_specs,
        out_specs=out_specs,
        out_shape=[jax.ShapeDtypeStruct(shape, kind) for shape, kind in shapes],
        scratch_shapes=[pltpu.VMEM(*entry) if isinstance(entry, tuple) else entry for entry in scratch],
        compiler_params=pltpu.CompilerParams(vmem_limit_bytes=vmem),
        cost_estimate=pl.CostEstimate(flops=flops, bytes_accessed=moved, transcendentals=0),
        name=name,
    )(*arrays))


def in_hbm(entry):
    return entry, pltpu.HBM


def in_smem(value):
    return value.astype(jnp.int32).reshape(1), pltpu.SMEM


def swap_all(bit, values):
    return [partner_2(member, "dp", bit) for member in values]


def exchange(spot, first_bit, ways, sends):
    replicas = lax.axis_size("dp")
    came = []
    for hop in [ways - 1] + list(range(1, ways - 1)):
        pairs = [(at, at ^ (hop << first_bit)) for at in range(replicas)]
        came.append(lax.ppermute(sends[hop - 1], "dp", pairs))
    return came


def scatter_mean(kept, sent, split, beside):
    f32 = jnp.float32
    replicas = lax.axis_size("dp")
    levels = replicas.bit_length() - 1
    place = lax.axis_index("dp")
    pairs, piece_s, piece_e, piece_r, piece_n = split
    rows = kept.shape[1]
    came = exchange(place, 0, 2, [sent])
    (kept,) = run_kernel(
        copy_kernel, "copy", [in_hbm(kept)], [(kept.shape, f32)], [pltpu.SemaphoreType.DMA(())]
    )
    came, kept = lax.optimization_barrier((came, kept))
    left, low, done = pairs, 1, []
    while left > 1:
        width = 2 if low == 1 and levels > 2 else 1
        ways = 1 << width
        spot = in_smem((place >> low) % ways)
        kept, *sends = run_kernel(
            functools.partial(fold_kernel, (len(came),)), "fold", [spot, kept] + came,
            [((left // ways, rows, LANES), f32)] * ways, [((left, rows, LANES), f32)],
        )
        came = exchange(place, low, ways, sends)
        if beside:
            work, *beside = beside
            came, ready = lax.optimization_barrier((came, work()))
            done.append(ready)
        left, low = left // ways, low + width
    at_e = round_up(piece_s + 1, 8)
    spans = ((at_e + piece_e, piece_r), (0, piece_s), (at_e, piece_e), (piece_s, 1))
    sizes = [(rows_of * LANES,) for _, rows_of in spans[:3]] + [(piece_n,)]
    mean = run_kernel(
        functools.partial(mean_kernel, replicas, spans), "mean", [kept] + came, [(size, f32) for size in sizes]
    )
    return done + [work() for work in beside], mean


def scatter_mean_any(arrays):
    replicas = lax.axis_size("dp")
    tables = [member.reshape(replicas, -1) for member in arrays]
    pieces = lax.all_to_all(jnp.concatenate(tables, axis=1), "dp", 0, 0, tiled=True)
    mean = jnp.sum(pieces, axis=0) / replicas
    bounds = [sum(table.shape[1] for table in tables[:at]) for at in range(len(tables) + 1)]
    return tuple(mean[low:high] for low, high in zip(bounds[:-1], bounds[1:]))


def shards(images, cotangent, w_reduce, w_spatial, w_expand, norm_gain, norm_bias, round_index):
    f32, bf16 = jnp.float32, jnp.bfloat16
    replicas = lax.axis_size("dp")
    levels = replicas.bit_length() - 1
    steps, _, pixels, in_ch = images.shape
    weights = [member.reshape(-1, LANES) for member in (w_reduce, w_spatial, w_expand)]
    sizes = [(member.shape, f32) for member in weights]
    rows_r, rows_s, rows_e = (member.shape[0] for member in weights)
    rows = rows_r + rows_s + rows_e
    norm_size = 2 * norm_gain.size
    flat_map = ((pixels, LANES), f32)
    wide_map = ((pixels, in_ch), f32)
    whole = ((rows, LANES), f32)
    norm_rows = ((norm_size // LANES, LANES), f32)
    half_map = ((pixels, in_ch), bf16)
    scratch = [
        half_map, half_map, whole, whole, whole,
        flat_map, flat_map, ((pixels, LANES), bf16), ((ROWS, SPAN), bf16), ((SPAN, ROWS), bf16),
        ((ROWS_BACK, SPAN), bf16), ((ROWS + 16, LANES), f32), ((ROWS_BACK + 16, LANES), f32),
        sizes[2], ((LANES, in_ch), bf16), ((rows_s, LANES), bf16), ((rows_s, LANES), bf16),
        wide_map, wide_map, half_map, flat_map, ((pixels, LANES), bf16), ((in_ch, LANES), bf16),
        pltpu.SemaphoreType.DMA((12,)), pltpu.SemaphoreType.DMA((6,)),
    ]
    flops = 6 * pixels * LANES * (2 * in_ch + rows_s)
    fine = replicas > 1 and all(size[0][0] % replicas == 0 for size in sizes)
    split = (replicas // 2, rows_s // replicas, rows_e // replicas, rows_r // replicas, norm_size // replicas)
    half = ((split[0], round_up(split[1] + 1, 8) + split[2] + split[3], LANES), f32)
    params = [weights[1], weights[0], weights[2], norm_gain, norm_bias]
    moments = []
    for step in range(steps):
        branches = [functools.partial(swap_all, bit) for bit in range(levels)]
        theirs = list(lax.switch((round_index[0] + step) % levels, branches, params))
        if step == 0:
            sides = [[in_hbm(side[at]) for at in (1, 0, 2, 3, 4)] for side in (params, theirs)]
        else:
            sides = [[params[0], in_hbm(params[1])], [in_hbm(member) for member in theirs]]
        operands = [in_hbm(images), in_hbm(cotangent)] + sides[0] + sides[1]
        operands += [in_hbm(member) for member in moments]
        norm_flat = ((1, norm_size), f32)
        moment_outs = [in_hbm(whole), in_hbm(norm_flat)]
        scratch_of = scratch + [whole] if step else [whole] + scratch
        last = step == steps - 1 and fine
        scratch_of += [norm_flat] + ([half, half] if last else [norm_rows])
        scratch_of += [norm_rows, norm_rows, norm_flat] if step else [(norm_gain.shape, f32)] * 4
        if last:
            core = in_smem(lax.axis_index("dp") % 2)
            kept, sent, *moments = run_kernel(
                functools.partial(step_kernel, step, True, split), "last_step", [core] + operands,
                [in_hbm(half), in_hbm(half)] + moment_outs, scratch_of, flops, VMEM_BYTES,
            )
        else:
            *params, moment, norm_moment = run_kernel(
                functools.partial(step_kernel, step, False, None), "step", operands,
                [in_hbm(whole), in_hbm(norm_rows)] + moment_outs, scratch_of, flops, VMEM_BYTES,
            )
            moments = [moment, norm_moment]
    def pack(sources, *spans):
        return run_kernel(
            functools.partial(pack_kernel, spans), "pack", sources,
            [((1, span * LANES if span else norm_size), bf16) for _, span in spans],
        )

    span_r, span_s, span_e = (0, rows_r), (rows_r, rows_s), (rows_r + rows_s, rows_e)
    if fine:
        beside = [
            functools.partial(pack, moments[:1], span_r, span_s), functools.partial(pack, moments, span_e, (0, 0))
        ]
        (first, second), averaged = scatter_mean(kept, sent, split, beside)
        out = first + second
    else:
        flat = [params[0][low:high].reshape(-1) for low, high in ((0, rows_r), (rows_r, rows_r + rows_s), (rows_r + rows_s, rows))]
        out, averaged = pack(moments, span_r, span_s, span_e, (0, 0)), scatter_mean_any(flat + [params[1].reshape(-1)])
    return tuple(averaged) + tuple(out)


def solution(mesh):
    in_specs = (
        P(None, "dp", None, None),
        P(None, "dp", None, None),
        P("dp", None),
        P("dp", None),
        P("dp", None),
        P("dp", None),
        P("dp", None),
        P(),
    )
    out_specs = (
        P("dp"),
        P("dp"),
        P("dp"),
        P("dp"),
        P("dp", None),
        P("dp", None),
        P("dp", None),
        P("dp", None),
    )
    return jax.shard_map(shards, mesh=mesh, in_specs=in_specs, out_specs=out_specs, check_vma=False)
```
